32 devices in a mesh: groups: 2 (over x), tp: 16 (over z, y, core).
Axes of the slice: x: 2, y: 2, z: 4, core: 2. Of those that a mesh axis runs over, the one named last changes fastest.
Arguments:
- normed_layer_input: bfloat16 [64, 8192], P(('groups', 'tp')), parts along dimension 0, may hold values from -6 to 6
- hidden_unit_gradient: bfloat16 [64, 28672], P('groups', 'tp'), parts along dimension 0, may hold values from -6 to 6
- gate_weight: bfloat16 [8192, 28672], P(None, 'tp'), may hold values from -0.0625 to 0.0625
- up_weight: bfloat16 [8192, 28672], P(None, 'tp'), may hold values from -0.0625 to 0.0625
- adapter_down_maps: bfloat16 [8192, 2048], P('tp'), may hold values from -0.125 to 0.125
- adapter_up_maps: bfloat16 [2048, 28672], P(None, 'tp'), may hold values from -0.03125 to 0.03125
- token_tenant_index: int32 [64], P('groups'), parts along dimension 0, may hold values from 0 to 31
Outputs:
- grad_input: bfloat16 [64, 8192], P(('groups', 'tp')), parts along dimension 0
- down_map_gradient: bfloat16 [8192, 4096], P('tp', 'groups'), parts along dimension 1
- up_map_gradient: bfloat16 [4096, 28672], P('groups', 'tp'), parts along dimension 0
The draws below stay inside these ranges and needn't reach their ends.
There are 2 independent parts, one for each index of `groups`. The reference program is written for one: setup_inputs(seed, part) draws one part's arguments, and reference() takes and returns one part's arrays. A program takes and returns all parts, laid end to end along the dimension named above; an argument that names none is the same for every part. Nothing has to cross between parts.
All inputs are finite; a program needn't handle non-finite values.
Results may differ from the reference program's by a relative error of at most 0.006.
Values may be sent and summed in bfloat16 or wider, within the bound.
No kernel may reach another device: no remote copies, remote signals or barrier semaphores. Data moves between devices by JAX's collectives and lax.ppermute only.
A program may use at most 192 MiB of HBM per device.

```python
import math
import jax
import jax.numpy as jnp
import numpy as np

MODEL_WIDTH = 8192
HIDDEN_UNITS = 28672
ADAPTER_RANK = 64
TENANT_COUNT = 32
TOKENS = 32


def touch_ends(drawn, rng, least, top_value):
    shape = drawn.shape
    spot = [jax.random.randint(jax.random.fold_in(rng, axis), (), 0, shape[axis]) for axis in range(len(shape))]
    drawn = drawn.at[tuple(spot)].set(least)
    longest = shape.index(max(shape))
    spot[longest] = (spot[longest] + 1) % shape[longest]
    return drawn.at[tuple(spot)].set(top_value)


def raised(result, key, source, target, shards_of, factor):
    def block_of(dim):
        return (jnp.arange(result.shape[dim]) // (result.shape[dim] // shards_of)).reshape((-1,) + (1,) * (result.ndim - 1 - dim))

    near = jax.random.permutation(key, shards_of)[block_of(target)]
    second = (block_of(target) + shards_of // 2) % shards_of
    return jnp.where((block_of(source) == near) | (block_of(source) == second), factor * result, result)


def levels(key, shape, split, least, top_value):
    def one(dim, parts):
        steps = jax.random.uniform(jax.random.fold_in(jax.random.fold_in(key, 6), dim), (parts,), jnp.float32, least / len(split), top_value / len(split))
        return jnp.repeat(jnp.exp(steps), shape[dim] // parts).reshape((-1,) + (1,) * (len(shape) - dim - 1))

    gain = one(*split[0])
    for cut in split[1:]:
        gain = gain * one(*cut)
    return gain


def rank_table(count, lean):
    weights = [(1 << 20) // math.isqrt(grade ** lean) + 1 for grade in range(1, count + 1)]
    scale = 1 + sum(weights) // (1 << 30)
    return np.cumsum(np.array([max(1, weight // scale) for weight in weights]))


def ranked(key, dims, count, skew):
    listing = rank_table(count, skew)
    ticket = jax.random.randint(jax.random.fold_in(key, 1), dims, 0, int(listing[count - 1]))
    standing = jnp.searchsorted(jnp.asarray(listing, jnp.int32), ticket, side="right")
    return jax.random.permutation(jax.random.fold_in(key, 2), count)[standing].astype(jnp.int32)


def gaussian(key, shape, scale, reach, pieces=(), kind=jnp.bfloat16):
    values = jax.random.normal(key, shape, jnp.float32) * scale
    if len(pieces) > 0:
        values = levels(key, shape, pieces, -0.22, 0.18) * values
    return jnp.clip(values, min=-reach, max=reach).astype(kind)


def bell_draw_with(key, shape, deviation, bound, shards, heavy, held_as=jnp.bfloat16):
    drawn = deviation * jax.random.normal(key, shape, jnp.float32)
    if shards:
        drawn = drawn * levels(key, shape, shards, -0.22, 0.18)
    return jnp.clip(raised(drawn, jax.random.fold_in(key, 3), *heavy), -bound, bound).astype(held_as)


def setup_inputs(seed: int = 0, part: int = 0) -> dict:
    key_list = jax.random.split(jax.random.key(seed), 8)
    part_keys = jax.random.split(jax.random.fold_in(key_list[7], part), 8)
    return {
        "normed_layer_input": gaussian(part_keys[0], (TOKENS, MODEL_WIDTH), 1.0, 6.0, ((0, 16),)),
        "hidden_unit_gradient": bell_draw_with(part_keys[1], (TOKENS, HIDDEN_UNITS), 1.0, 6.0, ((1, 16),), (1, 0, 16, 2.0)),
        "gate_weight": gaussian(key_list[2], (MODEL_WIDTH, HIDDEN_UNITS), MODEL_WIDTH ** -0.5, 0.0625, ((1, 16),)),
        "up_weight": gaussian(key_list[3], (MODEL_WIDTH, HIDDEN_UNITS), MODEL_WIDTH ** -0.5, 0.0625, ((1, 16),)),
        "adapter_down_maps": gaussian(key_list[4], (MODEL_WIDTH, TENANT_COUNT * ADAPTER_RANK), (MODEL_WIDTH // 4) ** -0.5, 0.125, ((0, 16),)),
        "adapter_up_maps": gaussian(key_list[5], (TENANT_COUNT * ADAPTER_RANK, HIDDEN_UNITS), HIDDEN_UNITS ** -0.5, 0.03125, ((1, 16),)),
        "token_tenant_index": touch_ends(ranked(part_keys[6], (TOKENS,), TENANT_COUNT, 2), jax.random.fold_in(part_keys[6], 3), 0, TENANT_COUNT - 1).astype(jnp.int32),
    }


adapter_scale = 2.0


def spread_mask(token_tenant_index):
    columns = jnp.arange(TENANT_COUNT * ADAPTER_RANK, dtype=jnp.int32) // ADAPTER_RANK
    return (token_tenant_index[:, None] == columns[None, :]).astype(jnp.float32)


def select_block(wide_rows, tenant_match_mask):
    return (wide_rows * tenant_match_mask).reshape(wide_rows.shape[0], TENANT_COUNT, ADAPTER_RANK).sum(axis=1)


def reference(normed_layer_input, hidden_unit_gradient, gate_weight, up_weight, adapter_down_maps, adapter_up_maps, token_tenant_index):
    tenant_match_mask = spread_mask(token_tenant_index)
    reduced_input = select_block(jnp.dot(normed_layer_input, adapter_down_maps, preferred_element_type=jnp.float32), tenant_match_mask)
    input_spread_rows = (jnp.tile(reduced_input, (1, TENANT_COUNT)) * tenant_match_mask).astype(jnp.bfloat16)
    gate_activation = jnp.dot(normed_layer_input, gate_weight, preferred_element_type=jnp.float32)
    gate_activation = gate_activation + adapter_scale * jnp.dot(input_spread_rows, adapter_up_maps, preferred_element_type=jnp.float32)
    up_val = jnp.dot(normed_layer_input, up_weight, preferred_element_type=jnp.float32)
    sigmoid_gate = jax.nn.sigmoid(gate_activation)
    hidden_grad = hidden_unit_gradient.astype(jnp.float32)
    gate_gradient = (hidden_grad * up_val * sigmoid_gate * (1.0 + gate_activation * (1.0 - sigmoid_gate))).astype(jnp.bfloat16)
    d_up = (hidden_grad * gate_activation * sigmoid_gate).astype(jnp.bfloat16)
    reduced_gradient = select_block(jnp.dot(gate_gradient, adapter_up_maps.T, preferred_element_type=jnp.float32), tenant_match_mask)
    gradient_spread_rows = (jnp.tile(reduced_gradient, (1, TENANT_COUNT)) * tenant_match_mask).astype(jnp.bfloat16)
    down_map_gradient = (adapter_scale * jnp.dot(normed_layer_input.T, gradient_spread_rows, preferred_element_type=jnp.float32)).astype(jnp.bfloat16)
    up_map_gradient = (adapter_scale * jnp.dot(input_spread_rows.T, gate_gradient, preferred_element_type=jnp.float32)).astype(jnp.bfloat16)
    running_sum = jnp.dot(gate_gradient, gate_weight.T, preferred_element_type=jnp.float32)
    running_sum = running_sum + jnp.dot(d_up, up_weight.T, preferred_element_type=jnp.float32)
    running_sum = running_sum + adapter_scale * jnp.dot(gradient_spread_rows, adapter_down_maps.T, preferred_element_type=jnp.float32)
    return running_sum.astype(jnp.bfloat16), down_map_gradient, up_map_gradient
```

```python
import jax
import jax.numpy as jnp
from jax import lax
from jax.sharding import PartitionSpec as P

ADAPTER_RANK = 64
TENANT_COUNT = 32


adapter_scale = 2.0


def select_block(wide_rows, tenant_match_mask):
    return (
        (wide_rows * tenant_match_mask)
        .reshape(wide_rows.shape[0], TENANT_COUNT, ADAPTER_RANK)
        .sum(axis=1)
    )


def contracted_rows(left, right):
    return lax.dot_general(
        left, right, (((0,), (0,)), ((), ())), preferred_element_type=jnp.float32
    )


def contracted_columns(left, right):
    return lax.dot_general(
        left, right, (((1,), (1,)), ((), ())), preferred_element_type=jnp.float32
    )


def spread_rows(low_rows, tenant_match_mask):
    return (jnp.tile(low_rows, (1, TENANT_COUNT)) * tenant_match_mask).astype(jnp.bfloat16)


def from_everyone(block):
    count = lax.axis_size("tp")
    copies = jnp.broadcast_to(block[None], (count,) + block.shape)
    return lax.all_to_all(copies, "tp", split_axis=0, concat_axis=0, tiled=True)


def local(
    normed_layer_input,
    hidden_unit_gradient,
    gate_weight,
    up_weight,
    adapter_down_maps,
    adapter_up_maps,
    token_tenant_index,
):
    count = lax.axis_size("tp")
    own_rows, width = normed_layer_input.shape
    rows = own_rows * count
    columns = lax.broadcasted_iota(jnp.int32, (1, TENANT_COUNT * ADAPTER_RANK), 1) // ADAPTER_RANK
    tenant_match_mask = (token_tenant_index[:, None] == columns).astype(jnp.float32)
    feature_column_span = adapter_down_maps.shape[0]
    col_start = lax.axis_index("tp") * feature_column_span
    whole = from_everyone(normed_layer_input).reshape(rows, width)
    input_column_span = lax.dynamic_slice_in_dim(whole, col_start, feature_column_span, 1)
    input_part = select_block(
        jnp.dot(input_column_span, adapter_down_maps, preferred_element_type=jnp.float32),
        tenant_match_mask,
    )
    reduced_input = from_everyone(input_part).sum(axis=0)
    input_spread_rows = spread_rows(reduced_input, tenant_match_mask)
    gate_activation = jnp.dot(whole, gate_weight, preferred_element_type=jnp.float32)
    up_val = jnp.dot(whole, up_weight, preferred_element_type=jnp.float32)
    gate_activation = gate_activation + adapter_scale * jnp.dot(
        input_spread_rows, adapter_up_maps, preferred_element_type=jnp.float32
    )
    sigmoid_gate = jax.nn.sigmoid(gate_activation)
    hidden_grad = hidden_unit_gradient.astype(jnp.float32)
    gate_gradient = (
        hidden_grad * up_val * sigmoid_gate * (1.0 + gate_activation * (1.0 - sigmoid_gate))
    ).astype(jnp.bfloat16)
    d_up = (hidden_grad * gate_activation * sigmoid_gate).astype(jnp.bfloat16)
    gradient_portion = select_block(
        contracted_columns(gate_gradient, adapter_up_maps), tenant_match_mask
    )
    reduced_gradient = from_everyone(gradient_portion).sum(axis=0)
    gradient_spread_rows = spread_rows(reduced_gradient, tenant_match_mask)
    down_map_gradient = (
        adapter_scale * contracted_rows(input_column_span, gradient_spread_rows)
    ).astype(jnp.bfloat16)
    up_map_gradient = (adapter_scale * contracted_rows(input_spread_rows, gate_gradient)).astype(
        jnp.bfloat16
    )
    adapter_column_span = adapter_scale * contracted_columns(
        gradient_spread_rows, adapter_down_maps
    )
    half = width // 2
    arrived = []
    for start in (0, half):
        part = contracted_columns(
            gate_gradient, gate_weight[start : start + half]
        ) + contracted_columns(d_up, up_weight[start : start + half])
        part = part.astype(jnp.bfloat16)
        if start > 0:
            part = jnp.concatenate([part, adapter_column_span.astype(jnp.bfloat16)], axis=1)
        part = part.reshape(count, own_rows, part.shape[1])
        arrived.append(
            lax.all_to_all(part, "tp", split_axis=0, concat_axis=0, tiled=True).astype(jnp.float32)
        )
    adapter_part = arrived[1][:, :, half:].transpose(1, 0, 2).reshape(own_rows, width)
    running_sum = jnp.concatenate(
        [arrived[0].sum(axis=0), arrived[1][:, :, :half].sum(axis=0)], axis=1
    )
    running_sum = running_sum + adapter_part
    return (running_sum.astype(jnp.bfloat16), down_map_gradient, up_map_gradient)


def solution(mesh):
    placed = (
        P(("groups", "tp"), None),
        P("groups", "tp"),
        P(None, "tp"),
        P(None, "tp"),
        P("tp", None),
        P(None, "tp"),
        P("groups"),
    )
    return jax.shard_map(
        local,
        mesh=mesh,
        in_specs=placed,
        out_specs=(P(("groups", "tp"), None), P("tp", "groups"), P("groups", "tp")),
        check_vma=False,
    )
```

```python
import jax
import jax.numpy as jnp
from jax import lax
from jax.sharding import PartitionSpec as P

ADAPTER_RANK = 64
TENANT_COUNT = 32


adapter_scale = 2.0


def select_block(wide_rows, tenant_match_mask):
    return (
        (wide_rows * tenant_match_mask)
        .reshape(wide_rows.shape[0], TENANT_COUNT, ADAPTER_RANK)
        .sum(axis=1)
    )


def contracted_rows(left, right):
    return lax.dot_general(
        left, right, (((0,), (0,)), ((), ())), preferred_element_type=jnp.float32
    )


def contracted_columns(left, right):
    return lax.dot_general(
        left, right, (((1,), (1,)), ((), ())), preferred_element_type=jnp.float32
    )


def spread_rows(low_rows, tenant_match_mask):
    return (jnp.tile(low_rows, (1, TENANT_COUNT)) * tenant_match_mask).astype(jnp.bfloat16)


def swap(block, hop):
    count = lax.axis_size("tp")
    return lax.ppermute(block, "tp", [(i, i ^ hop) for i in range(count)])


def hops():
    count = lax.axis_size("tp")
    return [1 << bit for bit in range(count.bit_length() - 1)]


def gathered(block):
    count = lax.axis_size("tp")
    held = {0: block}
    for hop in reversed(hops()):
        order = sorted(held)
        stacked = jnp.concatenate([held[p] for p in order], axis=0) if len(order) > 1 else block
        came = swap(stacked, hop)
        size = block.shape[0]
        for k, p in enumerate(order):
            held[p ^ hop] = came[k * size : (k + 1) * size]
    return jnp.concatenate([held[p] for p in range(count)], axis=0)


def summed_directly(block):
    total = block
    for hop in range(1, lax.axis_size("tp")):
        total = total + swap(block, hop)
    return total


def summed_by_doubling(block):
    for hop in hops():
        block = block + swap(block, hop)
    return block


def scattered_sum(part):
    for hop in reversed(hops()):
        rows = part.shape[0] // 2
        came = swap(part[rows:].astype(jnp.bfloat16), hop)
        part = part[:rows] + came.astype(jnp.float32)
    return part


def local(
    normed_layer_input,
    hidden_unit_gradient,
    gate_weight,
    up_weight,
    adapter_down_maps,
    adapter_up_maps,
    token_tenant_index,
):
    count = lax.axis_size("tp")
    own = lax.axis_index("tp")
    own_rows, width = normed_layer_input.shape
    rows = own_rows * count
    row = jnp.arange(rows, dtype=jnp.int32)
    source = ((row // own_rows) ^ own) * own_rows + row % own_rows
    turn = (source[:, None] == row[None, :]).astype(jnp.float32)

    def turned(block):
        return jnp.dot(turn, block, precision=lax.Precision.HIGHEST)

    tenants = jnp.where(source[:, None] == row[None, :], token_tenant_index[None, :], 0).sum(axis=1)
    columns = lax.broadcasted_iota(jnp.int32, (1, TENANT_COUNT * ADAPTER_RANK), 1) // ADAPTER_RANK
    tenant_match_mask = (tenants[:, None] == columns).astype(jnp.float32)
    hidden_grad = jnp.dot(
        turn.astype(jnp.bfloat16), hidden_unit_gradient, preferred_element_type=jnp.float32
    )
    feature_column_span = adapter_down_maps.shape[0]
    col_start = own * feature_column_span
    whole = gathered(normed_layer_input)
    input_column_span = lax.dynamic_slice_in_dim(whole, col_start, feature_column_span, 1)
    input_part = select_block(
        jnp.dot(input_column_span, adapter_down_maps, preferred_element_type=jnp.float32),
        tenant_match_mask,
    )
    reduced_input = turned(summed_directly(turned(input_part)))
    input_spread_rows = spread_rows(reduced_input, tenant_match_mask)
    gate_activation = jnp.dot(whole, gate_weight, preferred_element_type=jnp.float32)
    up_val = jnp.dot(whole, up_weight, preferred_element_type=jnp.float32)
    gate_activation = gate_activation + adapter_scale * jnp.dot(
        input_spread_rows, adapter_up_maps, preferred_element_type=jnp.float32
    )
    sigmoid_gate = jax.nn.sigmoid(gate_activation)
    gate_gradient = (
        hidden_grad * up_val * sigmoid_gate * (1.0 + gate_activation * (1.0 - sigmoid_gate))
    ).astype(jnp.bfloat16)
    d_up = (hidden_grad * gate_activation * sigmoid_gate).astype(jnp.bfloat16)
    gradient_portion = select_block(
        contracted_columns(gate_gradient, adapter_up_maps), tenant_match_mask
    )
    reduced_gradient = turned(summed_by_doubling(turned(gradient_portion)))
    gradient_spread_rows = spread_rows(reduced_gradient, tenant_match_mask)
    down_map_gradient = (
        adapter_scale * contracted_rows(input_column_span, gradient_spread_rows)
    ).astype(jnp.bfloat16)
    up_map_gradient = (adapter_scale * contracted_rows(input_spread_rows, gate_gradient)).astype(
        jnp.bfloat16
    )
    adapter_column_span = adapter_scale * contracted_columns(
        gradient_spread_rows, adapter_down_maps
    )
    half = width // 2
    sums = []
    for start in (0, half):
        part = contracted_columns(
            gate_gradient, gate_weight[start : start + half]
        ) + contracted_columns(d_up, up_weight[start : start + half])
        sums.append(scattered_sum(part))
    adapter_part = lax.all_to_all(
        turned(adapter_column_span).astype(jnp.bfloat16).reshape(count, own_rows, -1),
        "tp", split_axis=0, concat_axis=0, tiled=True,
    ).astype(jnp.float32)
    adapter_part = adapter_part.transpose(1, 0, 2).reshape(own_rows, width)
    running_sum = jnp.concatenate(sums, axis=1) + adapter_part
    return (running_sum.astype(jnp.bfloat16), down_map_gradient, up_map_gradient)


def solution(mesh):
    placed = (
        P(("groups", "tp"), None),
        P("groups", "tp"),
        P(None, "tp"),
        P(None, "tp"),
        P("tp", None),
        P(None, "tp"),
        P("groups"),
    )
    return jax.shard_map(
        local,
        mesh=mesh,
        in_specs=placed,
        out_specs=(P(("groups", "tp"), None), P("tp", "groups"), P("groups", "tp")),
        check_vma=False,
    )
```

```python
import jax
import jax.numpy as jnp
from jax import lax
from jax.experimental import pallas as pl
from jax.experimental.pallas import tpu as pltpu
from jax.sharding import PartitionSpec as P

ADAPTER_RANK = 64
TENANT_COUNT = 32
SPREAD = ADAPTER_RANK * TENANT_COUNT

adapter_scale = 2.0


def block_of(size, largest):
    block = largest
    while size % block:
        block //= 2
    return block


def contracted_rows(left, right):
    return lax.dot_general(
        left, right, (((0,), (0,)), ((), ())), preferred_element_type=jnp.float32
    )


def contracted_columns(left, right):
    return lax.dot_general(
        left, right, (((1,), (1,)), ((), ())), preferred_element_type=jnp.float32
    )


def tenant_mask(tenants, rows):
    columns = lax.broadcasted_iota(jnp.int32, (rows, SPREAD), 1) // ADAPTER_RANK
    return tenants == columns


def select_block(wide_rows, mask):
    kept = jnp.where(mask, wide_rows, 0.0)
    pair = 2 * ADAPTER_RANK
    total = kept[:, :pair]
    for start in range(pair, SPREAD, pair):
        total = total + kept[:, start : start + pair]
    return total[:, :ADAPTER_RANK] + total[:, ADAPTER_RANK:]


def spread_rows(low_rows, mask):
    pair = jnp.concatenate([low_rows, low_rows], axis=1)
    wide = jnp.concatenate([pair] * (TENANT_COUNT // 2), axis=1)
    return jnp.where(mask, wide, 0.0).astype(jnp.bfloat16)


def low_kernel(span_ref, down_ref, tenants_ref, low_ref):
    wide = jnp.dot(span_ref[...], down_ref[...], preferred_element_type=jnp.float32)
    low_ref[...] = select_block(wide, tenant_mask(tenants_ref[...], wide.shape[0]))


def low_part(span, down, tenants):
    rows = span.shape[0]
    return pl.pallas_call(
        low_kernel,
        out_shape=jax.ShapeDtypeStruct((rows, ADAPTER_RANK), jnp.float32),
        compiler_params=pltpu.CompilerParams(vmem_limit_bytes=16 << 20),
        cost_estimate=pl.CostEstimate(
            flops=2 * rows * down.size, bytes_accessed=2 * down.size, transcendentals=0
        ),
        name="low_part",
    )(span, down, tenants)


def forward_kernel(own_ref, other_ref, gate_ref, up_ref, gate_out, up_out):
    @pl.when(pl.program_id(0) == 0)
    def _():
        gate_out[...] = jnp.zeros_like(gate_out)
        up_out[...] = jnp.zeros_like(up_out)

    rows = jnp.concatenate([own_ref[...], other_ref[...]], axis=0)
    gate_out[...] += jnp.dot(rows, gate_ref[...], preferred_element_type=jnp.float32)
    up_out[...] += jnp.dot(rows, up_ref[...], preferred_element_type=jnp.float32)


def forward(own, other, gate_weight, up_weight):
    half, width = own.shape
    hidden = gate_weight.shape[1]
    block = block_of(width, 512)
    result = jax.ShapeDtypeStruct((2 * half, hidden), jnp.float32)
    whole = pl.BlockSpec((2 * half, hidden), lambda k: (0, 0))
    tokens = pl.BlockSpec((half, block), lambda k: (0, k))
    weight = pl.BlockSpec((block, hidden), lambda k: (k, 0))
    return pl.pallas_call(
        forward_kernel,
        grid=(width // block,),
        in_specs=[tokens, tokens, weight, weight],
        out_specs=[whole, whole],
        out_shape=[result, result],
        compiler_params=pltpu.CompilerParams(vmem_limit_bytes=24 << 20),
        cost_estimate=pl.CostEstimate(
            flops=8 * half * gate_weight.size, bytes_accessed=4 * gate_weight.size, transcendentals=0
        ),
        name="forward",
    )(own, other, gate_weight, up_weight)


def activation_kernel(
    gate_ref, up_ref, hidden_ref, low_ref, tenants_ref, maps_ref, dgate_ref, dup_ref, part_ref, spread_ref
):
    rows = gate_ref.shape[0]
    mask = tenant_mask(tenants_ref[...], rows)
    spread = spread_rows(low_ref[...], mask)
    spread_ref[...] = spread
    gate = gate_ref[...] + adapter_scale * jnp.dot(
        spread, maps_ref[...], preferred_element_type=jnp.float32
    )
    s = jax.nn.sigmoid(gate)
    hidden = hidden_ref[...].astype(jnp.float32)
    dgate = (hidden * up_ref[...] * s * (1.0 + gate * (1.0 - s))).astype(jnp.bfloat16)
    dgate_ref[...] = dgate
    dup_ref[...] = (hidden * gate * s).astype(jnp.bfloat16)
    part_ref[...] = select_block(contracted_columns(dgate, maps_ref[...]), mask)


def activation(gate, up, hidden, low, tenants, maps):
    shape = gate.shape
    return pl.pallas_call(
        activation_kernel,
        out_shape=[
            jax.ShapeDtypeStruct(shape, jnp.bfloat16),
            jax.ShapeDtypeStruct(shape, jnp.bfloat16),
            jax.ShapeDtypeStruct((shape[0], ADAPTER_RANK), jnp.float32),
            jax.ShapeDtypeStruct((shape[0], SPREAD), jnp.bfloat16),
        ],
        compiler_params=pltpu.CompilerParams(vmem_limit_bytes=32 << 20),
        cost_estimate=pl.CostEstimate(
            flops=4 * shape[0] * maps.size, bytes_accessed=2 * maps.size, transcendentals=0
        ),
        name="activation",
    )(gate, up, hidden, low, tenants, maps)


def backward_kernel(dgate_ref, dup_ref, gate_ref, up_ref, own_out, other_out):
    half = own_out.shape[0]
    part = contracted_columns(dgate_ref[...], gate_ref[...])
    part = part + contracted_columns(dup_ref[...], up_ref[...])
    own_out[...] = part[:half]
    other_out[...] = part[half:].astype(jnp.bfloat16)


def backward(dgate, dup, gate_weight, up_weight, start, width):
    rows, hidden = dgate.shape
    half = rows // 2
    block = block_of(width, 512)
    first = start // block
    gradient = pl.BlockSpec((rows, hidden), lambda k: (0, 0))
    weight = pl.BlockSpec((block, hidden), lambda k: (k + first, 0))
    out = pl.BlockSpec((half, block), lambda k: (0, k))
    return pl.pallas_call(
        backward_kernel,
        grid=(width // block,),
        in_specs=[gradient, gradient, weight, weight],
        out_specs=[out, out],
        out_shape=[
            jax.ShapeDtypeStruct((half, width), jnp.float32),
            jax.ShapeDtypeStruct((half, width), jnp.bfloat16),
        ],
        compiler_params=pltpu.CompilerParams(vmem_limit_bytes=24 << 20),
        cost_estimate=pl.CostEstimate(
            flops=4 * rows * hidden * width, bytes_accessed=4 * hidden * width, transcendentals=0
        ),
        name="backward",
    )(dgate, dup, gate_weight, up_weight)


def outer_kernel(left_ref, right_ref, out_ref):
    out_ref[...] = (adapter_scale * contracted_rows(left_ref[...], right_ref[...])).astype(
        jnp.bfloat16
    )


def outer(left, right, name):
    rows, height = left.shape
    width = right.shape[1]
    block = block_of(height, 256)
    if block % 128:
        block = height
    return pl.pallas_call(
        outer_kernel,
        grid=(height // block,),
        in_specs=[
            pl.BlockSpec((rows, block), lambda k: (0, k)),
            pl.BlockSpec((rows, width), lambda k: (0, 0)),
        ],
        out_specs=pl.BlockSpec((block, width), lambda k: (k, 0)),
        out_shape=jax.ShapeDtypeStruct((height, width), jnp.bfloat16),
        compiler_params=pltpu.CompilerParams(vmem_limit_bytes=24 << 20),
        cost_estimate=pl.CostEstimate(
            flops=2 * rows * height * width, bytes_accessed=2 * height * width, transcendentals=0
        ),
        name=name,
    )(left, right)


def same_core_groups():
    count = lax.axis_size("tp")
    return [list(range(core, count, 2)) for core in range(2)]


def between_same_cores(blocks):
    return lax.all_to_all(
        blocks, "tp", split_axis=0, concat_axis=0, tiled=True, axis_index_groups=same_core_groups()
    )


def other_core(block):
    return lax.ppermute(block, "tp", [(i, i ^ 1) for i in range(lax.axis_size("tp"))])


def summed(block):
    copies = jnp.broadcast_to(block[None], (lax.axis_size("tp"),) + block.shape)
    return lax.all_to_all(copies, "tp", split_axis=0, concat_axis=0, tiled=True).sum(axis=0)


def local(
    normed_layer_input,
    hidden_unit_gradient,
    gate_weight,
    up_weight,
    adapter_down_maps,
    adapter_up_maps,
    token_tenant_index,
):
    count = lax.axis_size("tp")
    chips = count // 2
    own = lax.axis_index("tp")
    core = own % 2
    own_rows, width = normed_layer_input.shape
    rows = own_rows * count
    half = rows // 2
    span = adapter_down_maps.shape[0]

    def turned(block):
        blocks = block.reshape((chips, 2, own_rows) + block.shape[1:])
        blocks = jnp.where(core == 0, blocks, blocks[:, ::-1])
        return blocks.swapaxes(0, 1).reshape(block.shape)

    def returned(block):
        blocks = block.reshape((2, chips, own_rows) + block.shape[1:]).swapaxes(0, 1)
        return jnp.where(core == 0, blocks, blocks[:, ::-1]).reshape(block.shape)

    hidden = turned(hidden_unit_gradient)
    tenants = turned(token_tenant_index)[:, None]

    own_tokens = between_same_cores(
        jnp.broadcast_to(normed_layer_input[None], (chips, own_rows, width))
    ).reshape(half, width)
    other_tokens = other_core(own_tokens)
    input_span = jnp.concatenate(
        [lax.dynamic_slice_in_dim(x, own * span, span, 1) for x in (own_tokens, other_tokens)], axis=0
    )
    low = turned(summed(returned(low_part(input_span, adapter_down_maps, tenants))))
    gate, up = forward(own_tokens, other_tokens, gate_weight, up_weight)
    dgate, dup, low_grad, input_spread = activation(
        gate, up, hidden, low, tenants, adapter_up_maps
    )
    low_grad = turned(summed(returned(low_grad)))
    grad_spread = spread_rows(low_grad, tenant_mask(tenants, rows))
    adapter = (adapter_scale * contracted_columns(grad_spread, adapter_down_maps)).astype(
        jnp.bfloat16
    )

    chunk = width // 2
    arrived = []
    for start in (0, chunk):
        own_part, other_part = backward(dgate, dup, gate_weight, up_weight, start, chunk)
        if start > 0:
            other_part = jnp.concatenate([other_part, adapter[half:]], axis=1)
        came = other_core(other_part)
        part = (own_part + came[:, :chunk].astype(jnp.float32)).astype(jnp.bfloat16)
        if start > 0:
            part = jnp.concatenate([part, adapter[:half], came[:, chunk:]], axis=1)
        part = between_same_cores(part.reshape(chips, own_rows, part.shape[1]))
        arrived.append(part.astype(jnp.float32))
    down_map_gradient = outer(input_span, grad_spread, "down_maps")
    up_map_gradient = outer(input_spread, dgate, "up_maps")
    pair = arrived[1][:, :, chunk:].reshape(chips, own_rows, 2, span)
    pair = jnp.where(core == 0, pair, pair[:, :, ::-1])
    total = jnp.concatenate(
        [arrived[0].sum(axis=0), arrived[1][:, :, :chunk].sum(axis=0)], axis=1
    )
    total = total + pair.transpose(1, 0, 2, 3).reshape(own_rows, width)
    return (total.astype(jnp.bfloat16), down_map_gradient, up_map_gradient)


def solution(mesh):
    placed = (
        P(("groups", "tp"), None),
        P("groups", "tp"),
        P(None, "tp"),
        P(None, "tp"),
        P("tp", None),
        P(None, "tp"),
        P("groups"),
    )
    return jax.shard_map(
        local,
        mesh=mesh,
        in_specs=placed,
        out_specs=(P(("groups", "tp"), None), P("tp", "groups"), P("groups", "tp")),
        check_vma=False,
    )
```

```python
import jax
import jax.numpy as jnp
from jax import lax
from jax.experimental import pallas as pl
from jax.experimental.pallas import tpu as pltpu
from jax.sharding import PartitionSpec as P

ADAPTER_RANK = 64
TENANT_COUNT = 32
SPREAD = ADAPTER_RANK * TENANT_COUNT

adapter_scale = 2.0


def block_of(size, largest):
    block = largest
    while size % block:
        block //= 2
    return block


def contracted_rows(left, right):
    return lax.dot_general(
        left, right, (((0,), (0,)), ((), ())), preferred_element_type=jnp.float32
    )


def contracted_columns(left, right):
    return lax.dot_general(
        left, right, (((1,), (1,)), ((), ())), preferred_element_type=jnp.float32
    )


def tenant_mask(tenants, rows):
    columns = lax.broadcasted_iota(jnp.int32, (rows, SPREAD), 1) // ADAPTER_RANK
    return tenants == columns


def select_block(wide_rows, mask):
    kept = jnp.where(mask, wide_rows, 0.0)
    pair = 2 * ADAPTER_RANK
    total = kept[:, :pair]
    for start in range(pair, SPREAD, pair):
        total = total + kept[:, start : start + pair]
    return total[:, :ADAPTER_RANK] + total[:, ADAPTER_RANK:]


def spread_rows(low_rows, mask):
    pair = jnp.concatenate([low_rows, low_rows], axis=1)
    wide = jnp.concatenate([pair] * (TENANT_COUNT // 2), axis=1)
    return jnp.where(mask, wide, 0.0).astype(jnp.bfloat16)


def packed(low):
    half = low.shape[0] // 2
    return jnp.concatenate([low[:half], low[half:]], axis=1)


def unpacked_sum(core, copies_ref):
    sums = []
    for parity in range(2):
        total = copies_ref[parity]
        for k in range(parity + 2, copies_ref.shape[0], 2):
            total = total + copies_ref[k]
        sums.append(total)
    same = jnp.where(core == 0, sums[0], sums[1])
    other = jnp.where(core == 0, sums[1], sums[0])
    first = same[:, :ADAPTER_RANK] + other[:, ADAPTER_RANK:]
    second = same[:, ADAPTER_RANK:] + other[:, :ADAPTER_RANK]
    return jnp.concatenate([first, second], axis=0)


def write_copies(copies_ref, low):
    tile = packed(low)
    for k in range(copies_ref.shape[0]):
        copies_ref[k] = tile


def low_kernel(span_ref, down_ref, tenants_ref, copies_ref):
    wide = jnp.dot(span_ref[...], down_ref[...], preferred_element_type=jnp.float32)
    write_copies(copies_ref, select_block(wide, tenant_mask(tenants_ref[...], wide.shape[0])))


def low_part(span, down, tenants, count):
    rows = span.shape[0]
    return pl.pallas_call(
        low_kernel,
        out_shape=jax.ShapeDtypeStruct((count, rows // 2, 2 * ADAPTER_RANK), jnp.float32),
        compiler_params=pltpu.CompilerParams(vmem_limit_bytes=40 << 20),
        cost_estimate=pl.CostEstimate(
            flops=2 * rows * down.size, bytes_accessed=2 * down.size, transcendentals=0
        ),
        name="low_part",
    )(span, down, tenants)


def forward_kernel(own_ref, other_ref, gate_ref, up_ref, gate_out, up_out):
    @pl.when(pl.program_id(0) == 0)
    def _():
        gate_out[...] = jnp.zeros_like(gate_out)
        up_out[...] = jnp.zeros_like(up_out)

    rows = jnp.concatenate([own_ref[...], other_ref[...]], axis=0)
    gate_out[...] += jnp.dot(rows, gate_ref[...], preferred_element_type=jnp.float32)
    up_out[...] += jnp.dot(rows, up_ref[...], preferred_element_type=jnp.float32)


def forward(own, other, gate_weight, up_weight):
    half, width = own.shape
    hidden = gate_weight.shape[1]
    block = block_of(width, 512)
    result = jax.ShapeDtypeStruct((2 * half, hidden), jnp.float32)
    whole = pl.BlockSpec((2 * half, hidden), lambda k: (0, 0))
    tokens = pl.BlockSpec((half, block), lambda k: (0, k))
    weight = pl.BlockSpec((block, hidden), lambda k: (k, 0))
    return pl.pallas_call(
        forward_kernel,
        grid=(width // block,),
        in_specs=[tokens, tokens, weight, weight],
        out_specs=[whole, whole],
        out_shape=[result, result],
        compiler_params=pltpu.CompilerParams(vmem_limit_bytes=52 << 20),
        cost_estimate=pl.CostEstimate(
            flops=8 * half * gate_weight.size, bytes_accessed=4 * gate_weight.size, transcendentals=0
        ),
        name="forward",
    )(own, other, gate_weight, up_weight)


def activation_kernel(
    core_ref, gate_ref, up_ref, hidden_ref, low_ref, tenants_ref, maps_ref,
    dgate_ref, dgate_turned_ref, dup_turned_ref, copies_ref, spread_ref,
):
    rows = gate_ref.shape[0]
    mask = tenant_mask(tenants_ref[...], rows)
    spread = spread_rows(unpacked_sum(core_ref[0], low_ref), mask)
    spread_ref[...] = spread
    gate = gate_ref[...] + adapter_scale * jnp.dot(
        spread, maps_ref[...], preferred_element_type=jnp.float32
    )
    s = jax.nn.sigmoid(gate)
    hidden = hidden_ref[...].astype(jnp.float32)
    dgate = (hidden * up_ref[...] * s * (1.0 + gate * (1.0 - s))).astype(jnp.bfloat16)
    dup = (hidden * gate * s).astype(jnp.bfloat16)
    dgate_ref[...] = dgate
    lanes = dgate_turned_ref.shape[1]
    for value, out_ref in ((dgate, dgate_turned_ref), (dup, dup_turned_ref)):
        value = value.astype(jnp.float32)
        if lanes > rows:
            value = jnp.concatenate(
                [value, jnp.zeros((lanes - rows, value.shape[1]), jnp.float32)], axis=0
            )
        out_ref[...] = value.T.astype(jnp.bfloat16)
    write_copies(copies_ref, select_block(contracted_columns(dgate, maps_ref[...]), mask))


VMEM = pl.BlockSpec(memory_space=pltpu.VMEM)
SMEM = pl.BlockSpec(memory_space=pltpu.SMEM)


def activation(core, gate, up, hidden, low, tenants, maps):
    rows, width = gate.shape
    lanes = max(rows, 128)
    return pl.pallas_call(
        activation_kernel,
        in_specs=[SMEM] + [VMEM] * 6,
        out_shape=[
            jax.ShapeDtypeStruct((rows, width), jnp.bfloat16),
            jax.ShapeDtypeStruct((width, lanes), jnp.bfloat16),
            jax.ShapeDtypeStruct((width, lanes), jnp.bfloat16),
            jax.ShapeDtypeStruct(low.shape, jnp.float32),
            jax.ShapeDtypeStruct((rows, SPREAD), jnp.bfloat16),
        ],
        compiler_params=pltpu.CompilerParams(vmem_limit_bytes=48 << 20),
        cost_estimate=pl.CostEstimate(
            flops=4 * rows * maps.size, bytes_accessed=2 * maps.size, transcendentals=0
        ),
        name="activation",
    )(core, gate, up, hidden, low, tenants, maps)


def adapter_kernel(
    core_ref, low_ref, tenants_ref, span_ref, down_ref, own_out, other_out, gradient_ref
):
    rows = tenants_ref.shape[0]
    spread = spread_rows(
        unpacked_sum(core_ref[0], low_ref), tenant_mask(tenants_ref[...], rows)
    )
    part = (adapter_scale * contracted_columns(spread, down_ref[...])).astype(jnp.bfloat16)
    own_out[...] = part[: rows // 2]
    other_out[...] = part[rows // 2 :]
    gradient_ref[...] = (adapter_scale * contracted_rows(span_ref[...], spread)).astype(
        jnp.bfloat16
    )


def adapter_part(core, low, tenants, input_span, down):
    rows, span = input_span.shape
    half = jax.ShapeDtypeStruct((rows // 2, span), jnp.bfloat16)
    return pl.pallas_call(
        adapter_kernel,
        in_specs=[SMEM] + [VMEM] * 4,
        out_shape=[half, half, jax.ShapeDtypeStruct(down.shape, jnp.bfloat16)],
        compiler_params=pltpu.CompilerParams(vmem_limit_bytes=40 << 20),
        cost_estimate=pl.CostEstimate(
            flops=4 * rows * down.size, bytes_accessed=4 * down.size, transcendentals=0
        ),
        name="adapter_part",
    )(core, low, tenants, input_span, down)


def backward_kernel(dgate_ref, dup_ref, gate_ref, up_ref, own_out, other_out):
    half = own_out.shape[0]
    part = jnp.dot(gate_ref[...], dgate_ref[...], preferred_element_type=jnp.float32)
    part = part + jnp.dot(up_ref[...], dup_ref[...], preferred_element_type=jnp.float32)
    part = part.T
    own_out[...] = part[:half]
    other_out[...] = part[half : 2 * half].astype(jnp.bfloat16)


def backward(rows, dgate, dup, gate_weight, up_weight, start, width):
    hidden, lanes = dgate.shape
    half = rows // 2
    block = block_of(width, 512)
    first = start // block
    gradient = pl.BlockSpec((hidden, lanes), lambda k: (0, 0))
    weight = pl.BlockSpec((block, hidden), lambda k: (k + first, 0))
    out = pl.BlockSpec((half, block), lambda k: (0, k))
    return pl.pallas_call(
        backward_kernel,
        grid=(width // block,),
        in_specs=[gradient, gradient, weight, weight],
        out_specs=[out, out],
        out_shape=[
            jax.ShapeDtypeStruct((half, width), jnp.float32),
            jax.ShapeDtypeStruct((half, width), jnp.bfloat16),
        ],
        compiler_params=pltpu.CompilerParams(vmem_limit_bytes=60 << 20),
        cost_estimate=pl.CostEstimate(
            flops=4 * rows * hidden * width, bytes_accessed=4 * hidden * width, transcendentals=0
        ),
        name="backward",
    )(dgate, dup, gate_weight, up_weight)


PARTS = 8


def merge_kernel(
    core_ref, own0, own1, came0, came1, adapter_own, adapter_came, out_ref, sums, tiles
):
    chips, tile, lanes = out_ref.shape
    tokens = tile // PARTS
    chunk = own0.shape[1]
    per_part = (lanes - 128) // 128
    blocks = PARTS * per_part

    def put(first, value):
        for k in range(value.shape[1] // 128):
            sums[first + k] = value[:, k * 128 : (k + 1) * 128]

    put(0, own0[...] + came0[...].astype(jnp.float32))
    put(chunk // 128, own1[...] + came1[...].astype(jnp.float32))
    mine = adapter_own[...].astype(jnp.float32)
    came = adapter_came[...].astype(jnp.float32)
    put(
        blocks,
        jnp.where(
            core_ref[0] == 0,
            jnp.concatenate([mine, came], axis=1),
            jnp.concatenate([came, mine], axis=1),
        ),
    )
    if sums.shape[0] < blocks + PARTS:
        tiles[per_part] = jnp.zeros(tiles.shape[1:], jnp.float32)
    for token in range(tokens):
        of_token = pl.ds(token, chips, stride=tokens)
        for part in range(PARTS):
            to = pl.ds(token * PARTS + part, chips, stride=tile)
            for k in range(per_part):
                tiles[k, to, :] = sums[part * per_part + k, of_token, :]
            if blocks + part < sums.shape[0]:
                tiles[per_part, to, :] = sums[blocks + part, of_token, :]
    for k in range(lanes // 128):
        out_ref[:, :, k * 128 : (k + 1) * 128] = (
            tiles[k].astype(jnp.bfloat16).reshape(chips, tile, 128)
        )


def merge(core, own, came, adapter_own, adapter_came, own_rows):
    half, chunk = own[0].shape
    width = 2 * chunk
    pair = 2 * adapter_own.shape[1]
    lanes = width // PARTS + 128
    chips, tile = half // own_rows, own_rows * PARTS
    return pl.pallas_call(
        merge_kernel,
        in_specs=[SMEM] + [VMEM] * 6,
        out_shape=jax.ShapeDtypeStruct((chips, tile, lanes), jnp.bfloat16),
        scratch_shapes=[
            pltpu.VMEM(((width + pair) // 128, half, 128), jnp.float32),
            pltpu.VMEM((lanes // 128, chips * tile, 128), jnp.float32),
        ],
        compiler_params=pltpu.CompilerParams(vmem_limit_bytes=40 << 20),
        name="merge",
    )(core, own[0], own[1], came[0], came[1], adapter_own, adapter_came)


def final_kernel(pair, came_ref, out_ref, total, adapter):
    chips, tile, lanes = came_ref.shape
    tokens = tile // PARTS
    blocks = (lanes - 128) // 128
    for k in range(blocks):
        at = slice(k * 128, (k + 1) * 128)
        value = came_ref[0, :, at].astype(jnp.float32)
        for chip in range(1, chips):
            value = value + came_ref[chip, :, at].astype(jnp.float32)
        total[k] = value
    adapter[...] = came_ref[:, :, lanes - 128 :].astype(jnp.float32).reshape(adapter.shape)
    of_pair = pair // 128
    for token in range(tokens):
        rows = slice(token * PARTS, (token + 1) * PARTS)
        for k in range(blocks):
            chip, part = divmod(k, of_pair)
            source = pl.ds(
                chip * tile + token * PARTS + part, PARTS, stride=blocks // of_pair * tile
            )
            total[k, rows, :] += adapter[source, :]
    for part in range(PARTS):
        for k in range(blocks):
            at = (part * blocks + k) * 128
            out_ref[:, at : at + 128] = total[k, pl.ds(part, tokens, stride=PARTS), :].astype(
                jnp.bfloat16
            )


def final(came, pair):
    chips, tile, lanes = came.shape
    piece = lanes - 128
    return pl.pallas_call(
        lambda *refs: final_kernel(pair, *refs),
        out_shape=jax.ShapeDtypeStruct((tile // PARTS, piece * PARTS), jnp.bfloat16),
        scratch_shapes=[
            pltpu.VMEM((piece // 128, tile, 128), jnp.float32),
            pltpu.VMEM((chips * tile, 128), jnp.float32),
        ],
        compiler_params=pltpu.CompilerParams(vmem_limit_bytes=40 << 20),
        name="final",
    )(came)


def outer_kernel(left_ref, right_ref, out_ref):
    out_ref[...] = (adapter_scale * contracted_rows(left_ref[...], right_ref[...])).astype(
        jnp.bfloat16
    )


def outer(left, right, name):
    rows, height = left.shape
    width = right.shape[1]
    block = block_of(height, 256)
    if block % 128:
        block = height
    return pl.pallas_call(
        outer_kernel,
        grid=(height // block,),
        in_specs=[
            pl.BlockSpec((rows, block), lambda k: (0, k)),
            pl.BlockSpec((rows, width), lambda k: (0, 0)),
        ],
        out_specs=pl.BlockSpec((block, width), lambda k: (k, 0)),
        out_shape=jax.ShapeDtypeStruct((height, width), jnp.bfloat16),
        compiler_params=pltpu.CompilerParams(vmem_limit_bytes=24 << 20),
        cost_estimate=pl.CostEstimate(
            flops=2 * rows * height * width, bytes_accessed=2 * height * width, transcendentals=0
        ),
        name=name,
    )(left, right)


def same_core_groups():
    count = lax.axis_size("tp")
    return [list(range(core, count, 2)) for core in range(2)]


def between_same_cores(blocks):
    return lax.all_to_all(
        blocks, "tp", split_axis=0, concat_axis=0, tiled=True, axis_index_groups=same_core_groups()
    )


def other_core(block):
    return lax.ppermute(block, "tp", [(i, i ^ 1) for i in range(lax.axis_size("tp"))])


def local(
    normed_layer_input,
    hidden_unit_gradient,
    gate_weight,
    up_weight,
    adapter_down_maps,
    adapter_up_maps,
    token_tenant_index,
):
    count = lax.axis_size("tp")
    chips = count // 2
    own = lax.axis_index("tp")
    core = own % 2
    own_rows, width = normed_layer_input.shape
    rows = own_rows * count
    half = rows // 2
    span = adapter_down_maps.shape[0]

    def turned(block):
        blocks = block.reshape((chips, 2, own_rows) + block.shape[1:])
        blocks = jnp.where(core == 0, blocks, blocks[:, ::-1])
        return blocks.swapaxes(0, 1).reshape(block.shape)

    def between_all(blocks):
        return lax.all_to_all(blocks, "tp", split_axis=0, concat_axis=0, tiled=True)

    hidden = turned(hidden_unit_gradient)
    tenants = turned(token_tenant_index)[:, None]
    core = core.reshape(1)

    own_tokens = between_same_cores(
        jnp.broadcast_to(normed_layer_input[None], (chips, own_rows, width))
    ).reshape(half, width)
    other_tokens = other_core(own_tokens)
    input_span = jnp.concatenate(
        [lax.dynamic_slice_in_dim(x, own * span, span, 1) for x in (own_tokens, other_tokens)], axis=0
    )
    low = between_all(low_part(input_span, adapter_down_maps, tenants, count))
    gate, up = forward(own_tokens, other_tokens, gate_weight, up_weight)
    dgate, dgate_turned, dup_turned, low_grad, input_spread = activation(
        core, gate, up, hidden, low, tenants, adapter_up_maps
    )
    low_grad = between_all(low_grad)

    chunk = width // 2
    own0, other0 = backward(rows, dgate_turned, dup_turned, gate_weight, up_weight, 0, chunk)
    came0 = other_core(other0)
    adapter_own, adapter_other, down_map_gradient = adapter_part(
        core, low_grad, tenants, input_span, adapter_down_maps
    )
    dgate_turned, dup_turned, adapter_other = lax.optimization_barrier(
        (dgate_turned, dup_turned, adapter_other)
    )
    adapter_came = other_core(adapter_other)
    own1, other1 = backward(rows, dgate_turned, dup_turned, gate_weight, up_weight, chunk, chunk)
    came1 = other_core(other1)
    merged = merge(core, (own0, own1), (came0, came1), adapter_own, adapter_came, own_rows)
    arrived = between_same_cores(merged)
    up_map_gradient = outer(input_spread, dgate, "up_maps")
    return (final(arrived, 2 * span), down_map_gradient, up_map_gradient)


def solution(mesh):
    placed = (
        P(("groups", "tp"), None),
        P("groups", "tp"),
        P(None, "tp"),
        P(None, "tp"),
        P("tp", None),
        P(None, "tp"),
        P("groups"),
    )
    return jax.shard_map(
        local,
        mesh=mesh,
        in_specs=placed,
        out_specs=(P(("groups", "tp"), None), P("tp", "groups"), P("groups", "tp")),
        check_vma=False,
    )
```

```python
import jax
import jax.numpy as jnp
from jax import lax
from jax.experimental import pallas as pl
from jax.experimental.pallas import tpu as pltpu
from jax.sharding import PartitionSpec as P

ADAPTER_RANK = 64
TENANT_COUNT = 32
SPREAD = ADAPTER_RANK * TENANT_COUNT

adapter_scale = 2.0


def block_of(size, largest):
    block = largest
    while size % block:
        block //= 2
    return block


def contracted_rows(left, right):
    return lax.dot_general(
        left, right, (((0,), (0,)), ((), ())), preferred_element_type=jnp.float32
    )


def contracted_columns(left, right):
    return lax.dot_general(
        left, right, (((1,), (1,)), ((), ())), preferred_element_type=jnp.float32
    )


def tenant_mask(tenants, rows):
    columns = lax.broadcasted_iota(jnp.int32, (rows, SPREAD), 1) // ADAPTER_RANK
    return tenants == columns


def select_block(wide_rows, mask):
    kept = jnp.where(mask, wide_rows, 0.0)
    pair = 2 * ADAPTER_RANK
    total = kept[:, :pair]
    for start in range(pair, SPREAD, pair):
        total = total + kept[:, start : start + pair]
    return total[:, :ADAPTER_RANK] + total[:, ADAPTER_RANK:]


def spread_rows(low_rows, mask):
    pair = jnp.concatenate([low_rows, low_rows], axis=1)
    wide = jnp.concatenate([pair] * (TENANT_COUNT // 2), axis=1)
    return jnp.where(mask, wide, 0.0).astype(jnp.bfloat16)


VMEM = pl.BlockSpec(memory_space=pltpu.VMEM)
SMEM = pl.BlockSpec(memory_space=pltpu.SMEM)
ANY = pl.BlockSpec(memory_space=pl.ANY)
HBM = pl.BlockSpec(memory_space=pltpu.HBM)
CUTS = 4
COPIES = 4


def with_fetches(kernel, wanted, operands, out_shapes, vmem_mib, flops, name, after=()):
    sources = []
    for weight, _ in wanted:
        if not any(weight is known for known in sources):
            sources.append(weight)
    places = [
        next(i for i, known in enumerate(sources) if known is weight) for weight, _ in wanted
    ]
    n_in, n_out = len(operands), len(out_shapes)

    def body(*refs):
        ins = refs[:n_in]
        hbm = refs[n_in : n_in + len(sources)]
        rest = refs[n_in + len(sources) + len(after) :]
        outs, pieces = rest[:n_out], rest[n_out : n_out + len(wanted)]
        scratch = rest[n_out + len(wanted) :]
        copies = []
        for n, (place, (_, cut)) in enumerate(zip(places, wanted)):
            part = pieces[n].shape[0] // COPIES
            for k in range(COPIES):
                copies.append(
                    pltpu.make_async_copy(
                        hbm[place].at[pl.ds(cut * part * COPIES + k * part, part)],
                        pieces[n].at[pl.ds(k * part, part)],
                        scratch[0].at[n * COPIES + k],
                    )
                )
        for copy in copies:
            copy.start()
        kernel(*ins, *outs)
        for copy in copies:
            copy.wait()

    piece_shapes = [
        pltpu.VMEM((weight.shape[0] // (CUTS if cut is not None else 1), weight.shape[1]), weight.dtype)
        for weight, cut in wanted
    ]
    wanted = [(weight, cut or 0) for weight, cut in wanted]
    moved = sum(2 * shape.shape[0] * shape.shape[1] for shape in piece_shapes)
    return pl.pallas_call(
        body,
        in_specs=[VMEM] * n_in + [HBM] * len(sources) + [ANY] * len(after),
        out_specs=[VMEM] * n_out + [ANY] * len(wanted),
        out_shape=list(out_shapes) + piece_shapes,
        scratch_shapes=[pltpu.SemaphoreType.DMA((COPIES * len(wanted),))] if wanted else [],
        compiler_params=pltpu.CompilerParams(vmem_limit_bytes=vmem_mib << 20),
        cost_estimate=pl.CostEstimate(flops=flops, bytes_accessed=moved, transcendentals=0),
        name=name,
    )(*operands, *[pltpu.with_memory_space_constraint(w, pltpu.HBM) for w in sources], *after)


def stacked(blocks, after=()):
    rows = sum(block.shape[0] for block in blocks)

    def stack_kernel(*refs):
        refs[-1][...] = jnp.concatenate([ref[...] for ref in refs[: len(blocks)]], axis=0)

    return pl.pallas_call(
        stack_kernel,
        in_specs=[VMEM] * len(blocks) + [ANY] * len(after),
        out_shape=jax.ShapeDtypeStruct((rows, blocks[0].shape[1]), blocks[0].dtype),
        compiler_params=pltpu.CompilerParams(vmem_limit_bytes=8 << 20),
        name="stacked",
    )(*blocks, *after)


def turned_rows(source, block):
    rows = source.shape[0]
    pick = source == lax.broadcasted_iota(jnp.int32, (rows, rows), 1)
    if block.dtype == jnp.bfloat16:
        return jnp.dot(pick.astype(jnp.bfloat16), block, preferred_element_type=jnp.float32)
    return jnp.dot(pick.astype(jnp.float32), block, precision=lax.Precision.HIGHEST)


def returned_rows(source_row, block):
    rows = source_row.shape[1]
    pick = source_row == lax.broadcasted_iota(jnp.int32, (rows, rows), 0)
    return jnp.dot(pick.astype(jnp.float32), block, precision=lax.Precision.HIGHEST)


def held_mask(source, tenants_row):
    rows = source.shape[0]
    pick = source == lax.broadcasted_iota(jnp.int32, (rows, rows), 1)
    tenants = jnp.sum(jnp.where(pick, tenants_row, 0).astype(jnp.float32), axis=1, keepdims=True)
    return tenant_mask(tenants.astype(jnp.int32), rows)


def low_kernel(span_ref, down_ref, tenants_ref, source_ref, source_row_ref, low_ref):
    wide = jnp.dot(span_ref[...], down_ref[...], preferred_element_type=jnp.float32)
    low = select_block(wide, held_mask(source_ref[...], tenants_ref[...]))
    low_ref[...] = returned_rows(source_row_ref[...], low)


def low_part(span, down, tenants, source, source_row):
    rows = span.shape[0]
    return pl.pallas_call(
        low_kernel,
        out_shape=jax.ShapeDtypeStruct((rows, ADAPTER_RANK), jnp.float32),
        compiler_params=pltpu.CompilerParams(vmem_limit_bytes=10 << 20),
        cost_estimate=pl.CostEstimate(
            flops=2 * rows * down.size, bytes_accessed=2 * down.size, transcendentals=0
        ),
        name="low_part",
    )(span, down, tenants, source, source_row)


def forward_kernel(cut, blocks, first, refs):
    x = refs[:blocks]
    gate_ref, up_ref = refs[blocks : blocks + 2]
    gate_out, up_out = refs[-2:]
    depth = gate_ref.shape[0]
    at = slice(cut * depth, (cut + 1) * depth)
    rows = jnp.concatenate([ref[:, at] for ref in x], axis=0)
    gate = jnp.dot(rows, gate_ref[...], preferred_element_type=jnp.float32)
    up = jnp.dot(rows, up_ref[...], preferred_element_type=jnp.float32)
    if not first:
        gate = gate + refs[blocks + 2][...]
        up = up + refs[blocks + 3][...]
    gate_out[...] = gate
    up_out[...] = up


def forward(cut, x, pieces, sums, wanted, after):
    rows = sum(block.shape[0] for block in x)
    depth, hidden = pieces[0].shape
    result = jax.ShapeDtypeStruct((rows, hidden), jnp.float32)
    return with_fetches(
        lambda *refs: forward_kernel(cut, len(x), not sums, refs),
        wanted,
        [*x, *pieces, *sums],
        [result, result],
        8,
        4 * rows * depth * hidden,
        "forward",
        after,
    )


def activation_kernel(
    gate_ref, up_ref, hidden_ref, low_ref, tenants_ref, source_ref, source_row_ref, maps_ref,
    dgate_ref, dup_ref, part_ref, spread_ref,
):
    source = source_ref[...]
    mask = held_mask(source, tenants_ref[...])
    spread = spread_rows(turned_rows(source, low_ref[...]), mask)
    spread_ref[...] = spread
    gate = gate_ref[...] + adapter_scale * jnp.dot(
        spread, maps_ref[...], preferred_element_type=jnp.float32
    )
    s = jax.nn.sigmoid(gate)
    hidden = turned_rows(source, hidden_ref[...])
    dgate = (hidden * up_ref[...] * s * (1.0 + gate * (1.0 - s))).astype(jnp.bfloat16)
    dgate_ref[...] = dgate
    dup_ref[...] = (hidden * gate * s).astype(jnp.bfloat16)
    part = select_block(contracted_columns(dgate, maps_ref[...]), mask)
    part_ref[...] = returned_rows(source_row_ref[...], part)


def activation(gate, up, hidden, low, tenants, source, source_row, maps, wanted):
    rows, width = gate.shape
    value = jax.ShapeDtypeStruct((rows, width), jnp.bfloat16)
    return with_fetches(
        activation_kernel,
        wanted,
        [gate, up, hidden, low, tenants, source, source_row, maps],
        [
            value,
            value,
            jax.ShapeDtypeStruct((rows, ADAPTER_RANK), jnp.float32),
            jax.ShapeDtypeStruct((rows, SPREAD), jnp.bfloat16),
        ],
        10,
        4 * rows * maps.size,
        "activation",
    )


def adapter_kernel(low_ref, tenants_ref, source_ref, down_ref, own_out, other_out, spread_ref):
    source = source_ref[...]
    half = own_out.shape[0]
    spread = spread_rows(
        turned_rows(source, low_ref[...]), held_mask(source, tenants_ref[...])
    )
    spread_ref[...] = spread
    part = (adapter_scale * contracted_columns(spread, down_ref[...])).astype(jnp.bfloat16)
    own_out[...] = part[:half]
    other_out[...] = part[half:]


def adapter_part(low, tenants, source, down):
    rows, span = low.shape[0], down.shape[0]
    half = jax.ShapeDtypeStruct((rows // 2, span), jnp.bfloat16)
    return pl.pallas_call(
        adapter_kernel,
        out_shape=[half, half, jax.ShapeDtypeStruct((rows, SPREAD), jnp.bfloat16)],
        compiler_params=pltpu.CompilerParams(vmem_limit_bytes=10 << 20),
        cost_estimate=pl.CostEstimate(
            flops=2 * rows * down.size, bytes_accessed=2 * down.size, transcendentals=0
        ),
        name="adapter_part",
    )(low, tenants, source, down)


def backward_kernel(dgate_ref, dup_ref, gate_ref, up_ref, own_out, other_out):
    half = own_out.shape[0]
    part = contracted_columns(dgate_ref[...], gate_ref[...])
    part = part + contracted_columns(dup_ref[...], up_ref[...])
    own_out[...] = part[:half]
    other_out[...] = part[half:].astype(jnp.bfloat16)


def backward(dgate, dup, pieces, wanted, after):
    rows, hidden = dgate.shape
    depth = pieces[0].shape[0]
    return with_fetches(
        backward_kernel,
        wanted,
        [dgate, dup, *pieces],
        [
            jax.ShapeDtypeStruct((rows // 2, depth), jnp.float32),
            jax.ShapeDtypeStruct((rows // 2, depth), jnp.bfloat16),
        ],
        8,
        4 * rows * hidden * depth,
        "backward",
        after,
    )


PARTS = 8


def merge_kernel(chip_ref, core_ref, *refs):
    own, came = refs[:CUTS], refs[CUTS : 2 * CUTS]
    adapter_own, adapter_came, out_ref, sums, tiles = refs[2 * CUTS :]
    chips, tile, lanes = out_ref.shape
    tokens = tile // PARTS
    per_part = (lanes - 128) // 128
    blocks = PARTS * per_part

    def put(first, value):
        for k in range(value.shape[1] // 128):
            sums[first + k] = value[:, k * 128 : (k + 1) * 128]

    for cut in range(CUTS):
        put(cut * blocks // CUTS, own[cut][...] + came[cut][...].astype(jnp.float32))
    mine = adapter_own[...].astype(jnp.float32)
    other = adapter_came[...].astype(jnp.float32)
    put(
        blocks,
        jnp.where(
            core_ref[0] == 0,
            jnp.concatenate([mine, other], axis=1),
            jnp.concatenate([other, mine], axis=1),
        ),
    )
    if sums.shape[0] < blocks + PARTS:
        tiles[per_part] = jnp.zeros(tiles.shape[1:], jnp.float32)
    for token in range(tokens):
        of_token = pl.ds(token, chips, stride=tokens)
        for part in range(PARTS):
            to = pl.ds(token * PARTS + part, chips, stride=tile)
            for k in range(per_part):
                tiles[k, to, :] = sums[part * per_part + k, of_token, :]
            if blocks + part < sums.shape[0]:
                tiles[per_part, to, :] = sums[blocks + part, of_token, :]
    for position in range(chips):
        chip = chip_ref[position]
        for k in range(lanes // 128):
            out_ref[chip, :, k * 128 : (k + 1) * 128] = tiles[
                k, position * tile : (position + 1) * tile, :
            ].astype(jnp.bfloat16)


def merge(chip_table, core, own, came, adapter_own, adapter_came, own_rows):
    half, depth = own[0].shape
    width = CUTS * depth
    pair = 2 * adapter_own.shape[1]
    lanes = width // PARTS + 128
    chips, tile = half // own_rows, own_rows * PARTS
    return pl.pallas_call(
        merge_kernel,
        in_specs=[SMEM] * 2 + [VMEM] * (2 * CUTS + 2),
        out_shape=jax.ShapeDtypeStruct((chips, tile, lanes), jnp.bfloat16),
        scratch_shapes=[
            pltpu.VMEM(((width + pair) // 128, half, 128), jnp.float32),
            pltpu.VMEM((lanes // 128, chips * tile, 128), jnp.float32),
        ],
        compiler_params=pltpu.CompilerParams(vmem_limit_bytes=40 << 20),
        name="merge",
    )(chip_table, core, *own, *came, adapter_own, adapter_came)


def final_kernel(pair, came_ref, out_ref, total, adapter):
    chips, tile, lanes = came_ref.shape
    tokens = tile // PARTS
    blocks = (lanes - 128) // 128
    for k in range(blocks):
        at = slice(k * 128, (k + 1) * 128)
        value = came_ref[0, :, at].astype(jnp.float32)
        for chip in range(1, chips):
            value = value + came_ref[chip, :, at].astype(jnp.float32)
        total[k] = value
    adapter[...] = came_ref[:, :, lanes - 128 :].astype(jnp.float32).reshape(adapter.shape)
    of_pair = pair // 128
    for token in range(tokens):
        rows = slice(token * PARTS, (token + 1) * PARTS)
        for k in range(blocks):
            chip, part = divmod(k, of_pair)
            source = pl.ds(
                chip * tile + token * PARTS + part, PARTS, stride=blocks // of_pair * tile
            )
            total[k, rows, :] += adapter[source, :]
    for part in range(PARTS):
        for k in range(blocks):
            at = (part * blocks + k) * 128
            out_ref[:, at : at + 128] = total[k, pl.ds(part, tokens, stride=PARTS), :].astype(
                jnp.bfloat16
            )


def final(came, pair):
    chips, tile, lanes = came.shape
    piece = lanes - 128
    return pl.pallas_call(
        lambda *refs: final_kernel(pair, *refs),
        out_shape=jax.ShapeDtypeStruct((tile // PARTS, piece * PARTS), jnp.bfloat16),
        scratch_shapes=[
            pltpu.VMEM((piece // 128, tile, 128), jnp.float32),
            pltpu.VMEM((chips * tile, 128), jnp.float32),
        ],
        compiler_params=pltpu.CompilerParams(vmem_limit_bytes=40 << 20),
        name="final",
    )(came)


def outer_kernel(left_ref, right_ref, out_ref):
    out_ref[...] = contracted_rows(
        left_ref[...] * jnp.bfloat16(adapter_scale), right_ref[...]
    ).astype(jnp.bfloat16)


def outer(left, right, name):
    rows, height = left.shape
    width = right.shape[1]
    block = block_of(height, 256)
    if block % 128:
        block = height
    return pl.pallas_call(
        outer_kernel,
        grid=(height // block,),
        in_specs=[
            pl.BlockSpec((rows, block), lambda k: (0, k)),
            pl.BlockSpec((rows, width), lambda k: (0, 0)),
        ],
        out_specs=pl.BlockSpec((block, width), lambda k: (k, 0)),
        out_shape=jax.ShapeDtypeStruct((height, width), jnp.bfloat16),
        compiler_params=pltpu.CompilerParams(vmem_limit_bytes=24 << 20),
        cost_estimate=pl.CostEstimate(
            flops=2 * rows * height * width, bytes_accessed=2 * height * width, transcendentals=0
        ),
        name=name,
    )(left, right)


def same_core_groups():
    count = lax.axis_size("tp")
    return [list(range(core, count, 2)) for core in range(2)]


def between_same_cores(blocks):
    return lax.all_to_all(
        blocks, "tp", split_axis=0, concat_axis=0, tiled=True, axis_index_groups=same_core_groups()
    )


def swapped(block, hop):
    return lax.ppermute(block, "tp", [(i, i ^ hop) for i in range(lax.axis_size("tp"))])


def local(
    normed_layer_input,
    hidden_unit_gradient,
    gate_weight,
    up_weight,
    adapter_down_maps,
    adapter_up_maps,
    token_tenant_index,
):
    count = lax.axis_size("tp")
    own = lax.axis_index("tp")
    own_rows, width = normed_layer_input.shape
    rows = own_rows * count
    span = adapter_down_maps.shape[0]
    hops = [1 << bit for bit in range(count.bit_length() - 1)]

    far, near = hops[-1], hops[-2]
    order = [0, near, far, near | far]
    for hop in reversed(hops[:-2]):
        order = order + [p ^ hop for p in order]
    order = jnp.array(order, jnp.int32)
    held = (order ^ own)[:, None] * own_rows + jnp.arange(own_rows, dtype=jnp.int32)
    source, source_row = held.reshape(rows, 1), held.reshape(1, rows)
    chip_table = (order[: count // 2] ^ own) // 2
    core = (own % 2).reshape(1)
    start = own * span
    tenants = token_tenant_index.reshape(1, rows)
    normed_layer_input, source, source_row, chip_table, core, start, tenants = (
        lax.optimization_barrier(
            (normed_layer_input, source, source_row, chip_table, core, start, tenants)
        )
    )

    def fetched(cut, after):
        return with_fetches(
            lambda *refs: None, [(gate_weight, cut), (up_weight, cut)], [], [], 1, 0, "fetch", after
        )

    pieces = {}
    came = [swapped(normed_layer_input, hop) for hop in (near, far, near | far)]
    pieces[0] = fetched(0, [source, source_row, chip_table, core, tenants])
    block = stacked([normed_layer_input, *came], pieces[0])
    for hop in reversed(hops[2:-2]):
        block = stacked([block, swapped(block, hop)])
    other = swapped(block, hops[1])
    x = [block, other, swapped(block, 1), swapped(other, 1)]
    pieces[1] = fetched(1, [block, *pieces[0]])

    input_span = jnp.concatenate(
        [lax.dynamic_slice_in_dim(part, start, span, 1) for part in x], axis=0
    )
    low = low_part(input_span, adapter_down_maps, tenants, source, source_row)
    sums = []
    wanted = {
        0: [(gate_weight, 2), (up_weight, 2)],
        1: [(gate_weight, 3), (up_weight, 3)],
        2: [(adapter_up_maps, None)],
        3: [],
    }
    step = 0
    for cut in range(CUTS):
        after = [low]
        if step < len(hops):
            low = low + swapped(low, hops[step])
            step += 1
        *sums, = forward(cut, x, pieces[cut], sums, wanted[cut], after)
        sums, extra = sums[:2], sums[2:]
        if cut < 2:
            pieces[cut + 2] = extra
        elif cut == 2:
            maps = extra[0]
    for hop in hops[step:]:
        low = low + swapped(low, hop)
    dgate, dup, low_grad, input_spread, gate1 = activation(
        *sums, hidden_unit_gradient, low, tenants, source, source_row, maps, [(gate_weight, 1)]
    )

    low_grad = low_grad + swapped(low_grad, hops[0])
    step = 1
    parts, arrived = {}, {}
    wanted = {3: [(up_weight, 1), (gate_weight, 0)], 2: [(up_weight, 0)], 1: [], 0: []}
    after = [low_grad]
    for cut in reversed(range(CUTS)):
        if cut > 0:
            after = [low_grad]
            if step < len(hops):
                low_grad = low_grad + swapped(low_grad, hops[step])
                step += 1
        own_part, other_part, *extra = backward(dgate, dup, pieces[cut], wanted[cut], after)
        if cut == 3:
            pieces[1] = [gate1, extra[0]]
            gate0 = extra[1]
        elif cut == 2:
            pieces[0] = [gate0, extra[0]]
        elif cut == 1:
            for hop in hops[step:]:
                low_grad = low_grad + swapped(low_grad, hop)
            adapter_own, adapter_other, grad_spread = adapter_part(
                low_grad, tenants, source, adapter_down_maps
            )
            adapter_came = swapped(adapter_other, 1)
            after = [adapter_other]
        parts[cut] = own_part
        arrived[cut] = swapped(other_part, 1)
    merged = merge(
        chip_table,
        core,
        [parts[cut] for cut in range(CUTS)],
        [arrived[cut] for cut in range(CUTS)],
        adapter_own,
        adapter_came,
        own_rows,
    )
    exchanged = between_same_cores(merged)
    down_map_gradient = outer(input_span, grad_spread, "down_maps")
    up_map_gradient = outer(input_spread, dgate, "up_maps")
    return (final(exchanged, 2 * span), down_map_gradient, up_map_gradient)


def solution(mesh):
    placed = (
        P(("groups", "tp"), None),
        P("groups", "tp"),
        P(None, "tp"),
        P(None, "tp"),
        P("tp", None),
        P(None, "tp"),
        P("groups"),
    )
    return jax.shard_map(
        local,
        mesh=mesh,
        in_specs=placed,
        out_specs=(P(("groups", "tp"), None), P("tp", "groups"), P("groups", "tp")),
        check_vma=False,
    )
```

```python
import jax
import jax.numpy as jnp
from jax import lax
from jax.experimental import pallas as pl
from jax.experimental.pallas import tpu as pltpu
from jax.sharding import PartitionSpec as P

ADAPTER_RANK = 64
TENANT_COUNT = 32
SPREAD = ADAPTER_RANK * TENANT_COUNT

adapter_scale = 2.0


def block_of(size, largest):
    block = largest
    while size % block:
        block //= 2
    return block


def contracted_rows(left, right):
    return lax.dot_general(
        left, right, (((0,), (0,)), ((), ())), preferred_element_type=jnp.float32
    )


def contracted_columns(left, right):
    return lax.dot_general(
        left, right, (((1,), (1,)), ((), ())), preferred_element_type=jnp.float32
    )


def tenant_mask(tenants, rows):
    columns = lax.broadcasted_iota(jnp.int32, (rows, SPREAD), 1) // ADAPTER_RANK
    return tenants == columns


def select_block(wide_rows, mask):
    kept = jnp.where(mask, wide_rows, 0.0)
    pair = 2 * ADAPTER_RANK
    total = kept[:, :pair]
    for start in range(pair, SPREAD, pair):
        total = total + kept[:, start : start + pair]
    return total[:, :ADAPTER_RANK] + total[:, ADAPTER_RANK:]


def spread_rows(low_rows, mask):
    pair = jnp.concatenate([low_rows, low_rows], axis=1)
    wide = jnp.concatenate([pair] * (TENANT_COUNT // 2), axis=1)
    return jnp.where(mask, wide, 0.0).astype(jnp.bfloat16)


VMEM = pl.BlockSpec(memory_space=pltpu.VMEM)
SMEM = pl.BlockSpec(memory_space=pltpu.SMEM)
ANY = pl.BlockSpec(memory_space=pl.ANY)
CUTS = 4
COPIES = 4
SLOTS = 6


def store_call(kernel, store, fetches, operands, out_shapes, flops, name, smem=0, after=()):
    new = isinstance(store, jax.ShapeDtypeStruct)
    depth = store.shape[0] // SLOTS
    part = depth // COPIES
    sources = []
    for array, _, _ in fetches:
        if not any(array is known for known in sources):
            sources.append(array)
    places = [next(i for i, known in enumerate(sources) if known is f[0]) for f in fetches]
    n_in, n_out, n_hbm = len(operands), len(out_shapes), len(sources)

    def body(*refs):
        if not new:
            refs = refs[1:]
        ins, hbm = refs[:n_in], refs[n_in : n_in + n_hbm]
        rest = refs[n_in + n_hbm + len(after) :]
        store_ref, outs, scratch = rest[0], rest[1 : 1 + n_out], rest[1 + n_out :]
        copies = []
        for n, (place, (_, piece, slot)) in enumerate(zip(places, fetches)):
            for k in range(COPIES):
                copies.append(
                    pltpu.make_async_copy(
                        hbm[place].at[pl.ds(piece * depth + k * part, part)],
                        store_ref.at[pl.ds(slot * depth + k * part, part)],
                        scratch[0].at[n * COPIES + k],
                    )
                )
        for copy in copies:
            copy.start()
        kernel(lambda slot: store_ref[slot * depth : (slot + 1) * depth, :], *ins, *outs)
        for copy in copies:
            copy.wait()

    moved = 2 * depth * store.shape[1] * len(fetches)
    return pl.pallas_call(
        body,
        in_specs=([] if new else [VMEM])
        + [SMEM] * smem
        + [VMEM] * (n_in - smem)
        + [ANY] * (n_hbm + len(after)),
        out_specs=[VMEM] * (1 + n_out),
        out_shape=[pltpu.VMEM(store.shape, store.dtype), *out_shapes],
        input_output_aliases={} if new else {0: 0},
        scratch_shapes=[pltpu.SemaphoreType.DMA((COPIES * len(fetches),))] if fetches else [],
        compiler_params=pltpu.CompilerParams(vmem_limit_bytes=13 << 20),
        cost_estimate=pl.CostEstimate(flops=flops, bytes_accessed=moved, transcendentals=0),
        name=name,
    )(
        *([] if new else [store]),
        *operands,
        *[pltpu.with_memory_space_constraint(array, pltpu.HBM) for array in sources],
        *after,
    )


def stacked(blocks, after=()):
    rows = sum(block.shape[0] for block in blocks)

    def stack_kernel(*refs):
        refs[-1][...] = jnp.concatenate([ref[...] for ref in refs[: len(blocks)]], axis=0)

    return pl.pallas_call(
        stack_kernel,
        in_specs=[VMEM] * len(blocks) + [ANY] * len(after),
        out_shape=jax.ShapeDtypeStruct((rows, blocks[0].shape[1]), blocks[0].dtype),
        compiler_params=pltpu.CompilerParams(vmem_limit_bytes=6 << 20),
        name="stacked",
    )(*blocks, *after)


def block_owner(own, block, count):
    bits = count.bit_length() - 1
    hops = [1 << (bits - 2), 1 << (bits - 1)] + [1 << bit for bit in reversed(range(bits - 2))]
    for n, hop in enumerate(hops):
        own = own ^ (((block >> n) & 1) * hop)
    return own


def source_of(own, row, rows, count):
    tokens = rows // count
    return block_owner(own, row // tokens, count) * tokens + row % tokens


def pick_held(own, rows, count):
    held = source_of(own, lax.broadcasted_iota(jnp.int32, (rows, rows), 0), rows, count)
    return held == lax.broadcasted_iota(jnp.int32, (rows, rows), 1)


def pick_given(own, rows, count):
    held = source_of(own, lax.broadcasted_iota(jnp.int32, (rows, rows), 1), rows, count)
    return held == lax.broadcasted_iota(jnp.int32, (rows, rows), 0)


def picked(pick, block):
    if block.dtype == jnp.bfloat16:
        return jnp.dot(pick.astype(jnp.bfloat16), block, preferred_element_type=jnp.float32)
    return jnp.dot(pick.astype(jnp.float32), block, precision=lax.Precision.HIGHEST)


def held_mask(pick, tenants_row):
    tenants = jnp.sum(jnp.where(pick, tenants_row, 0).astype(jnp.float32), axis=1, keepdims=True)
    return tenant_mask(tenants.astype(jnp.int32), pick.shape[0])


def low_kernel(count, aligned, own_ref, down_ref, tenants_ref, *refs):
    x, (span_out, low_ref) = refs[:-2], refs[-2:]
    own = own_ref[0]
    if aligned:
        width = down_ref.shape[0]
        at = pl.ds(pl.multiple_of(own * width, width), width)
        span = jnp.concatenate([ref[:, at] for ref in x], axis=0)
    else:
        span = jnp.concatenate([ref[...] for ref in x], axis=0)
    span_out[...] = span
    rows = span.shape[0]
    wide = jnp.dot(span, down_ref[...], preferred_element_type=jnp.float32)
    low = select_block(wide, held_mask(pick_held(own, rows, count), tenants_ref[...]))
    low_ref[...] = picked(pick_given(own, rows, count), low)


def low_part(own, down, tenants, x, count):
    rows, span = sum(block.shape[0] for block in x), down.shape[0]
    aligned = span % 128 == 0
    if not aligned:
        x = [
            lax.dynamic_slice(
                block, (0, own[0] * span), (block.shape[0], span), allow_negative_indices=False
            )
            for block in x
        ]
    return pl.pallas_call(
        lambda *refs: low_kernel(count, aligned, *refs),
        in_specs=[SMEM] + [VMEM] * (2 + len(x)),
        out_shape=[
            jax.ShapeDtypeStruct((rows, span), x[0].dtype),
            jax.ShapeDtypeStruct((rows, ADAPTER_RANK), jnp.float32),
        ],
        compiler_params=pltpu.CompilerParams(vmem_limit_bytes=6 << 20),
        cost_estimate=pl.CostEstimate(
            flops=2 * rows * down.size, bytes_accessed=2 * down.size, transcendentals=0
        ),
        name="low_part",
    )(own, down, tenants, *x)


def forward_kernel(cut, slots, blocks, first, slot, *refs):
    x = refs[:blocks]
    gate_out, up_out = refs[-2:]
    gate_weight, up_weight = slot(slots[0]), slot(slots[1])
    depth = gate_weight.shape[0]
    at = slice(cut * depth, (cut + 1) * depth)
    rows = jnp.concatenate([ref[:, at] for ref in x], axis=0)
    gate = jnp.dot(rows, gate_weight, preferred_element_type=jnp.float32)
    up = jnp.dot(rows, up_weight, preferred_element_type=jnp.float32)
    if not first:
        gate = gate + refs[blocks][...]
        up = up + refs[blocks + 1][...]
    gate_out[...] = gate
    up_out[...] = up


def forward(cut, slots, x, store, sums, fetches, after):
    rows = sum(block.shape[0] for block in x)
    depth, hidden = store.shape[0] // SLOTS, store.shape[1]
    result = jax.ShapeDtypeStruct((rows, hidden), jnp.float32)
    store, gate, up = store_call(
        lambda *refs: forward_kernel(cut, slots, len(x), not sums, *refs),
        store,
        fetches,
        [*x, *sums],
        [result, result],
        4 * rows * depth * hidden,
        "forward",
        after=after,
    )
    return store, [gate, up]


def activation_kernel(
    count, maps_slot, slot, own_ref, gate_ref, up_ref, hidden_ref, low_ref, tenants_ref,
    dgate_ref, dup_ref, part_ref, spread_ref,
):
    rows = gate_ref.shape[0]
    maps = slot(maps_slot)
    pick = pick_held(own_ref[0], rows, count)
    mask = held_mask(pick, tenants_ref[...])
    spread = spread_rows(picked(pick, low_ref[...]), mask)
    spread_ref[...] = spread
    gate = gate_ref[...] + adapter_scale * jnp.dot(
        spread, maps, preferred_element_type=jnp.float32
    )
    s = jax.nn.sigmoid(gate)
    hidden = picked(pick, hidden_ref[...])
    dgate = (hidden * up_ref[...] * s * (1.0 + gate * (1.0 - s))).astype(jnp.bfloat16)
    dgate_ref[...] = dgate
    dup_ref[...] = (hidden * gate * s).astype(jnp.bfloat16)
    part = select_block(contracted_columns(dgate, maps), mask)
    part_ref[...] = picked(pick_given(own_ref[0], rows, count), part)


def activation(own, maps_slot, store, sums, hidden, low, tenants, count, fetches):
    rows, width = sums[0].shape
    value = jax.ShapeDtypeStruct((rows, width), jnp.bfloat16)
    return store_call(
        lambda *refs: activation_kernel(count, maps_slot, *refs),
        store,
        fetches,
        [own, *sums, hidden, low, tenants],
        [
            value,
            value,
            jax.ShapeDtypeStruct((rows, ADAPTER_RANK), jnp.float32),
            jax.ShapeDtypeStruct((rows, SPREAD), jnp.bfloat16),
        ],
        4 * rows * SPREAD * width,
        "activation",
        smem=1,
    )


def adapter_kernel(count, own_ref, low_ref, tenants_ref, down_ref, own_out, other_out, spread_ref):
    half = own_out.shape[0]
    pick = pick_held(own_ref[0], 2 * half, count)
    spread = spread_rows(picked(pick, low_ref[...]), held_mask(pick, tenants_ref[...]))
    spread_ref[...] = spread
    part = (adapter_scale * contracted_columns(spread, down_ref[...])).astype(jnp.bfloat16)
    own_out[...] = part[:half]
    other_out[...] = part[half:]


def adapter_part(own, low, tenants, down, count):
    rows, span = low.shape[0], down.shape[0]
    half = jax.ShapeDtypeStruct((rows // 2, span), jnp.bfloat16)
    return pl.pallas_call(
        lambda *refs: adapter_kernel(count, *refs),
        in_specs=[SMEM] + [VMEM] * 3,
        out_shape=[half, half, jax.ShapeDtypeStruct((rows, SPREAD), jnp.bfloat16)],
        compiler_params=pltpu.CompilerParams(vmem_limit_bytes=6 << 20),
        cost_estimate=pl.CostEstimate(
            flops=2 * rows * down.size, bytes_accessed=2 * down.size, transcendentals=0
        ),
        name="adapter_part",
    )(own, low, tenants, down)


def backward_kernel(slots, slot, dgate_ref, dup_ref, own_out, other_out):
    half = own_out.shape[0]
    part = contracted_columns(dgate_ref[...], slot(slots[0]))
    part = part + contracted_columns(dup_ref[...], slot(slots[1]))
    own_out[...] = part[:half]
    other_out[...] = part[half:].astype(jnp.bfloat16)


def backward(slots, dgate, dup, store, fetches, after):
    rows, hidden = dgate.shape
    depth = store.shape[0] // SLOTS
    return store_call(
        lambda *refs: backward_kernel(slots, *refs),
        store,
        fetches,
        [dgate, dup],
        [
            jax.ShapeDtypeStruct((rows // 2, depth), jnp.float32),
            jax.ShapeDtypeStruct((rows // 2, depth), jnp.bfloat16),
        ],
        4 * rows * hidden * depth,
        "backward",
        after=after,
    )


PARTS = 8


def merge_kernel(count, own_ref, *refs):
    own, came = refs[:CUTS], refs[CUTS : 2 * CUTS]
    adapter_own, adapter_came, out_ref, sums, tiles = refs[2 * CUTS :]
    chips, tile, lanes = out_ref.shape
    tokens = tile // PARTS
    per_part = (lanes - 128) // 128
    blocks = PARTS * per_part

    def put(first, value):
        for k in range(value.shape[1] // 128):
            sums[first + k] = value[:, k * 128 : (k + 1) * 128]

    for cut in range(CUTS):
        put(cut * blocks // CUTS, own[cut][...] + came[cut][...].astype(jnp.float32))
    mine = adapter_own[...].astype(jnp.float32)
    other = adapter_came[...].astype(jnp.float32)
    put(
        blocks,
        jnp.where(
            own_ref[0] % 2 == 0,
            jnp.concatenate([mine, other], axis=1),
            jnp.concatenate([other, mine], axis=1),
        ),
    )
    if sums.shape[0] < blocks + PARTS:
        tiles[per_part] = jnp.zeros(tiles.shape[1:], jnp.float32)
    for token in range(tokens):
        of_token = pl.ds(token, chips, stride=tokens)
        for part in range(PARTS):
            to = pl.ds(token * PARTS + part, chips, stride=tile)
            for k in range(per_part):
                tiles[k, to, :] = sums[part * per_part + k, of_token, :]
            if blocks + part < sums.shape[0]:
                tiles[per_part, to, :] = sums[blocks + part, of_token, :]
    for position in range(chips):
        chip = block_owner(own_ref[0], position, count) // 2
        for k in range(lanes // 128):
            out_ref[chip, :, k * 128 : (k + 1) * 128] = tiles[
                k, position * tile : (position + 1) * tile, :
            ].astype(jnp.bfloat16)


def merge(device, own, came, adapter_own, adapter_came, own_rows):
    half, depth = own[0].shape
    width = CUTS * depth
    pair = 2 * adapter_own.shape[1]
    lanes = width // PARTS + 128
    chips, tile = half // own_rows, own_rows * PARTS
    return pl.pallas_call(
        lambda *refs: merge_kernel(2 * chips, *refs),
        in_specs=[SMEM] + [VMEM] * (2 * CUTS + 2),
        out_shape=jax.ShapeDtypeStruct((chips, tile, lanes), jnp.bfloat16),
        scratch_shapes=[
            pltpu.VMEM(((width + pair) // 128, half, 128), jnp.float32),
            pltpu.VMEM((lanes // 128, chips * tile, 128), jnp.float32),
        ],
        compiler_params=pltpu.CompilerParams(vmem_limit_bytes=40 << 20),
        name="merge",
    )(device, *own, *came, adapter_own, adapter_came)


def final_kernel(pair, came_ref, out_ref, total, adapter):
    chips, tile, lanes = came_ref.shape
    tokens = tile // PARTS
    blocks = (lanes - 128) // 128
    for k in range(blocks):
        at = slice(k * 128, (k + 1) * 128)
        value = came_ref[0, :, at].astype(jnp.float32)
        for chip in range(1, chips):
            value = value + came_ref[chip, :, at].astype(jnp.float32)
        total[k] = value
    adapter[...] = came_ref[:, :, lanes - 128 :].astype(jnp.float32).reshape(adapter.shape)
    of_pair = pair // 128
    for token in range(tokens):
        rows = slice(token * PARTS, (token + 1) * PARTS)
        for k in range(blocks):
            chip, part = divmod(k, of_pair)
            source = pl.ds(
                chip * tile + token * PARTS + part, PARTS, stride=blocks // of_pair * tile
            )
            total[k, rows, :] += adapter[source, :]
    for part in range(PARTS):
        for k in range(blocks):
            at = (part * blocks + k) * 128
            out_ref[:, at : at + 128] = total[k, pl.ds(part, tokens, stride=PARTS), :].astype(
                jnp.bfloat16
            )


def final(came, pair):
    chips, tile, lanes = came.shape
    piece = lanes - 128
    return pl.pallas_call(
        lambda *refs: final_kernel(pair, *refs),
        out_shape=jax.ShapeDtypeStruct((tile // PARTS, piece * PARTS), jnp.bfloat16),
        scratch_shapes=[
            pltpu.VMEM((piece // 128, tile, 128), jnp.float32),
            pltpu.VMEM((chips * tile, 128), jnp.float32),
        ],
        compiler_params=pltpu.CompilerParams(vmem_limit_bytes=40 << 20),
        name="final",
    )(came)


def outer_kernel(left_ref, right_ref, out_ref):
    out_ref[...] = contracted_rows(
        left_ref[...] * jnp.bfloat16(adapter_scale), right_ref[...]
    ).astype(jnp.bfloat16)


def outer(left, right, name):
    rows, height = left.shape
    width = right.shape[1]
    block = block_of(height, 256)
    if block % 128:
        block = height
    return pl.pallas_call(
        outer_kernel,
        grid=(height // block,),
        in_specs=[
            pl.BlockSpec((rows, block), lambda k: (0, k)),
            pl.BlockSpec((rows, width), lambda k: (0, 0)),
        ],
        out_specs=pl.BlockSpec((block, width), lambda k: (k, 0)),
        out_shape=jax.ShapeDtypeStruct((height, width), jnp.bfloat16),
        compiler_params=pltpu.CompilerParams(vmem_limit_bytes=24 << 20),
        cost_estimate=pl.CostEstimate(
            flops=2 * rows * height * width, bytes_accessed=2 * height * width, transcendentals=0
        ),
        name=name,
    )(left, right)


def same_core_groups():
    count = lax.axis_size("tp")
    return [list(range(core, count, 2)) for core in range(2)]


def between_same_cores(blocks):
    return lax.all_to_all(
        blocks, "tp", split_axis=0, concat_axis=0, tiled=True, axis_index_groups=same_core_groups()
    )


def swapped(block, hop):
    return lax.ppermute(block, "tp", [(i, i ^ hop) for i in range(lax.axis_size("tp"))])


def local(
    normed_layer_input,
    hidden_unit_gradient,
    gate_weight,
    up_weight,
    adapter_down_maps,
    adapter_up_maps,
    token_tenant_index,
):
    count = lax.axis_size("tp")
    own = lax.axis_index("tp").astype(jnp.int32).reshape(1)
    own_rows, width = normed_layer_input.shape
    rows = own_rows * count
    hops = [1 << bit for bit in range(count.bit_length() - 1)]
    tenants = token_tenant_index.reshape(1, rows)

    def pair(cut, first, second):
        return [(gate_weight, cut, first), (up_weight, cut, second)]

    def mark(slot, token_ref):
        token_ref[...] = jnp.zeros_like(token_ref)

    token = jax.ShapeDtypeStruct((8, 128), jnp.float32)
    store = jax.ShapeDtypeStruct(
        (SLOTS * width // CUTS, gate_weight.shape[1]), gate_weight.dtype
    )
    far, near = hops[-1], hops[-2]
    came = [swapped(normed_layer_input, hop) for hop in (near, far, near | far)]
    store, token = store_call(mark, store, pair(0, 0, 1), [], [token], 0, "fetch", after=[own])
    block = stacked([normed_layer_input, *came], [token])
    for hop in reversed(hops[2:-2]):
        block = stacked([block, swapped(block, hop)])
    other = swapped(block, hops[1])
    x = [block, other, swapped(block, 1), swapped(other, 1)]
    store, token = store_call(mark, store, pair(1, 2, 3), [], [token], 0, "fetch", after=[block])

    input_span, low = low_part(own, adapter_down_maps, tenants, x, count)
    sums = []
    slots = {0: (0, 1), 1: (2, 3), 2: (4, 5), 3: (0, 1)}
    fetches = {
        0: pair(2, 4, 5), 1: pair(3, 0, 1), 2: [(adapter_up_maps, 0, 2)], 3: [(gate_weight, 1, 3)]
    }
    step = 0
    for cut in range(CUTS):
        after = [low]
        if step < len(hops):
            low = low + swapped(low, hops[step])
            step += 1
        store, sums = forward(cut, slots[cut], x, store, sums, fetches[cut], after)
    for hop in hops[step:]:
        low = low + swapped(low, hop)
    store, dgate, dup, low_grad, input_spread = activation(
        own, 2, store, sums, hidden_unit_gradient, low, tenants, count, []
    )

    low_grad = low_grad + swapped(low_grad, hops[0])
    step = 1
    parts, arrived = {}, {}
    slots = {3: (0, 1), 2: (4, 5), 1: (3, 2), 0: (0, 1)}
    fetches = {3: [(up_weight, 1, 2)], 2: pair(0, 0, 1), 1: [], 0: []}
    for cut in reversed(range(CUTS)):
        if cut > 0:
            after = [low_grad]
            if step < len(hops):
                low_grad = low_grad + swapped(low_grad, hops[step])
                step += 1
        store, own_part, other_part = backward(slots[cut], dgate, dup, store, fetches[cut], after)
        if cut == 1:
            for hop in hops[step:]:
                low_grad = low_grad + swapped(low_grad, hop)
            adapter_own, adapter_other, grad_spread = adapter_part(
                own, low_grad, tenants, adapter_down_maps, count
            )
            adapter_came = swapped(adapter_other, 1)
            after = [adapter_other]
        parts[cut] = own_part
        arrived[cut] = swapped(other_part, 1)
    merged = merge(
        own,
        [parts[cut] for cut in range(CUTS)],
        [arrived[cut] for cut in range(CUTS)],
        adapter_own,
        adapter_came,
        own_rows,
    )
    exchanged = between_same_cores(merged)
    down_map_gradient = outer(input_span, grad_spread, "down_maps")
    up_map_gradient = outer(input_spread, dgate, "up_maps")
    return (final(exchanged, 2 * input_span.shape[1]), down_map_gradient, up_map_gradient)


def solution(mesh):
    placed = (
        P(("groups", "tp"), None),
        P("groups", "tp"),
        P(None, "tp"),
        P(None, "tp"),
        P("tp", None),
        P(None, "tp"),
        P("groups"),
    )
    return jax.shard_map(
        local,
        mesh=mesh,
        in_specs=placed,
        out_specs=(P(("groups", "tp"), None), P("tp", "groups"), P("groups", "tp")),
        check_vma=False,
    )
```

```python
import jax
import jax.numpy as jnp
from jax import lax
from jax.experimental import pallas as pl
from jax.experimental.pallas import tpu as pltpu
from jax.sharding import PartitionSpec as P

ADAPTER_RANK = 64
TENANT_COUNT = 32
SPREAD = ADAPTER_RANK * TENANT_COUNT

adapter_scale = 2.0


def block_of(size, largest):
    block = largest
    while size % block:
        block //= 2
    return block


def contracted_rows(left, right):
    return lax.dot_general(
        left, right, (((0,), (0,)), ((), ())), preferred_element_type=jnp.float32
    )


def contracted_columns(left, right):
    return lax.dot_general(
        left, right, (((1,), (1,)), ((), ())), preferred_element_type=jnp.float32
    )


def tenant_mask(tenants, rows):
    columns = lax.broadcasted_iota(jnp.int32, (rows, SPREAD), 1) // ADAPTER_RANK
    return tenants == columns


def select_block(wide_rows, mask):
    kept = jnp.where(mask, wide_rows, 0.0)
    pair = 2 * ADAPTER_RANK
    total = kept[:, :pair]
    for start in range(pair, SPREAD, pair):
        total = total + kept[:, start : start + pair]
    return total[:, :ADAPTER_RANK] + total[:, ADAPTER_RANK:]


def spread_rows(low_rows, mask):
    pair = jnp.concatenate([low_rows, low_rows], axis=1)
    wide = jnp.concatenate([pair] * (TENANT_COUNT // 2), axis=1)
    return jnp.where(mask, wide, 0.0).astype(jnp.bfloat16)


VMEM = pl.BlockSpec(memory_space=pltpu.VMEM)
ANY = pl.BlockSpec(memory_space=pl.ANY)
CUTS = 4
COPIES = 4
SLOTS = 6
STORE_GRANT = 10 << 20


def store_call(kernel, store, fetches, operands, out_shapes, flops, name, after=()):
    new = isinstance(store, jax.ShapeDtypeStruct)
    depth = store.shape[0] // SLOTS
    part = depth // COPIES
    sources = []
    for array, _, _ in fetches:
        if not any(array is known for known in sources):
            sources.append(array)
    places = [next(i for i, known in enumerate(sources) if known is f[0]) for f in fetches]
    n_in, n_out, n_hbm = len(operands), len(out_shapes), len(sources)

    def body(*refs):
        if not new:
            refs = refs[1:]
        ins, hbm = refs[:n_in], refs[n_in : n_in + n_hbm]
        rest = refs[n_in + n_hbm + len(after) :]
        store_ref, outs, scratch = rest[0], rest[1 : 1 + n_out], rest[1 + n_out :]
        copies = []
        for n, (place, (_, piece, slot)) in enumerate(zip(places, fetches)):
            for k in range(COPIES):
                copies.append(
                    pltpu.make_async_copy(
                        hbm[place].at[pl.ds(piece * depth + k * part, part)],
                        store_ref.at[pl.ds(slot * depth + k * part, part)],
                        scratch[0].at[n * COPIES + k],
                    )
                )
        for copy in copies:
            copy.start()
        kernel(lambda slot: store_ref[slot * depth : (slot + 1) * depth, :], *ins, *outs)
        for copy in copies:
            copy.wait()

    moved = 2 * depth * store.shape[1] * len(fetches)
    return pl.pallas_call(
        body,
        in_specs=[VMEM] * (n_in + (not new)) + [ANY] * (n_hbm + len(after)),
        out_specs=[VMEM] * (1 + n_out),
        out_shape=[pltpu.VMEM(store.shape, store.dtype), *out_shapes],
        input_output_aliases={} if new else {0: 0},
        scratch_shapes=[pltpu.SemaphoreType.DMA((COPIES * len(fetches),))] if fetches else [],
        compiler_params=pltpu.CompilerParams(vmem_limit_bytes=STORE_GRANT),
        cost_estimate=pl.CostEstimate(flops=flops, bytes_accessed=moved, transcendentals=0),
        name=name,
    )(
        *([] if new else [store]),
        *operands,
        *[pltpu.with_memory_space_constraint(array, pltpu.HBM) for array in sources],
        *after,
    )


def stacked(blocks, after=()):
    rows = sum(block.shape[0] for block in blocks)

    def stack_kernel(*refs):
        refs[-1][...] = jnp.concatenate([ref[...] for ref in refs[: len(blocks)]], axis=0)

    return pl.pallas_call(
        stack_kernel,
        in_specs=[VMEM] * len(blocks) + [ANY] * len(after),
        out_shape=jax.ShapeDtypeStruct((rows, blocks[0].shape[1]), blocks[0].dtype),
        compiler_params=pltpu.CompilerParams(vmem_limit_bytes=4 << 20),
        name="stacked",
    )(*blocks, *after)


def block_owner(own, block, count):
    bits = count.bit_length() - 1
    hops = [1 << (bits - 2), 1 << (bits - 1)] + [1 << bit for bit in reversed(range(bits - 2))]
    for n, hop in enumerate(hops):
        own = own ^ (((block >> n) & 1) * hop)
    return own


def source_of(own, row, rows, count):
    tokens = rows // count
    return block_owner(own, row // tokens, count) * tokens + row % tokens


def pick_held(own, rows, count):
    held = source_of(own, lax.broadcasted_iota(jnp.int32, (rows, rows), 0), rows, count)
    return held == lax.broadcasted_iota(jnp.int32, (rows, rows), 1)


def pick_given(own, rows, count):
    held = source_of(own, lax.broadcasted_iota(jnp.int32, (rows, rows), 1), rows, count)
    return held == lax.broadcasted_iota(jnp.int32, (rows, rows), 0)


def picked(pick, block):
    if block.dtype == jnp.bfloat16:
        return jnp.dot(pick.astype(jnp.bfloat16), block, preferred_element_type=jnp.float32)
    return jnp.dot(pick.astype(jnp.float32), block, precision=lax.Precision.HIGHEST)


def held_mask(pick, tenants_row):
    tenants = jnp.sum(jnp.where(pick, tenants_row, 0).astype(jnp.float32), axis=1, keepdims=True)
    return tenant_mask(tenants.astype(jnp.int32), pick.shape[0])


def low_kernel(count, aligned, down_ref, tenants_ref, *refs):
    x, (span_out, low_ref) = refs[:-2], refs[-2:]
    own = lax.axis_index("tp")
    if aligned:
        width = down_ref.shape[0]
        at = pl.ds(pl.multiple_of(own * width, width), width)
        span = jnp.concatenate([ref[:, at] for ref in x], axis=0)
    else:
        span = jnp.concatenate([ref[...] for ref in x], axis=0)
    span_out[...] = span
    rows = span.shape[0]
    wide = jnp.dot(span, down_ref[...], preferred_element_type=jnp.float32)
    low = select_block(wide, held_mask(pick_held(own, rows, count), tenants_ref[...]))
    low_ref[...] = picked(pick_given(own, rows, count), low)


def low_part(down, tenants, x, count):
    rows, span = sum(block.shape[0] for block in x), down.shape[0]
    aligned = span % 128 == 0
    if not aligned:
        x = [
            lax.dynamic_slice(
                block,
                (0, lax.axis_index("tp") * span),
                (block.shape[0], span),
                allow_negative_indices=False,
            )
            for block in x
        ]
    return pl.pallas_call(
        lambda *refs: low_kernel(count, aligned, *refs),
        out_shape=[
            jax.ShapeDtypeStruct((rows, span), x[0].dtype),
            jax.ShapeDtypeStruct((rows, ADAPTER_RANK), jnp.float32),
        ],
        compiler_params=pltpu.CompilerParams(vmem_limit_bytes=4 << 20),
        cost_estimate=pl.CostEstimate(
            flops=2 * rows * down.size, bytes_accessed=2 * down.size, transcendentals=0
        ),
        name="low_part",
    )(down, tenants, *x)


def forward_kernel(cut, slots, blocks, first, slot, *refs):
    x = refs[:blocks]
    gate_out, up_out = refs[-2:]
    gate_weight, up_weight = slot(slots[0]), slot(slots[1])
    depth = gate_weight.shape[0]
    at = slice(cut * depth, (cut + 1) * depth)
    rows = jnp.concatenate([ref[:, at] for ref in x], axis=0)
    gate = jnp.dot(rows, gate_weight, preferred_element_type=jnp.float32)
    up = jnp.dot(rows, up_weight, preferred_element_type=jnp.float32)
    if not first:
        gate = gate + refs[blocks][...]
        up = up + refs[blocks + 1][...]
    gate_out[...] = gate
    up_out[...] = up


def forward(cut, slots, x, store, sums, fetches, after):
    rows = sum(block.shape[0] for block in x)
    depth, hidden = store.shape[0] // SLOTS, store.shape[1]
    result = jax.ShapeDtypeStruct((rows, hidden), jnp.float32)
    store, gate, up = store_call(
        lambda *refs: forward_kernel(cut, slots, len(x), not sums, *refs),
        store,
        fetches,
        [*x, *sums],
        [result, result],
        4 * rows * depth * hidden,
        "forward",
        after=after,
    )
    return store, [gate, up]


def activation_kernel(
    count, maps_slot, slot, gate_ref, up_ref, hidden_ref, low_ref, tenants_ref,
    dgate_ref, dup_ref, part_ref, spread_ref,
):
    rows = gate_ref.shape[0]
    maps = slot(maps_slot)
    own = lax.axis_index("tp")
    pick = pick_held(own, rows, count)
    mask = held_mask(pick, tenants_ref[...])
    spread = spread_rows(picked(pick, low_ref[...]), mask)
    spread_ref[...] = spread
    gate = gate_ref[...] + adapter_scale * jnp.dot(
        spread, maps, preferred_element_type=jnp.float32
    )
    s = jax.nn.sigmoid(gate)
    hidden = picked(pick, hidden_ref[...])
    dgate = (hidden * up_ref[...] * s * (1.0 + gate * (1.0 - s))).astype(jnp.bfloat16)
    dgate_ref[...] = dgate
    dup_ref[...] = (hidden * gate * s).astype(jnp.bfloat16)
    part = select_block(contracted_columns(dgate, maps), mask)
    part_ref[...] = picked(pick_given(own, rows, count), part)


def activation(maps_slot, store, sums, hidden, low, tenants, count, fetches):
    rows, width = sums[0].shape
    value = jax.ShapeDtypeStruct((rows, width), jnp.bfloat16)
    return store_call(
        lambda *refs: activation_kernel(count, maps_slot, *refs),
        store,
        fetches,
        [*sums, hidden, low, tenants],
        [
            value,
            value,
            jax.ShapeDtypeStruct((rows, ADAPTER_RANK), jnp.float32),
            jax.ShapeDtypeStruct((rows, SPREAD), jnp.bfloat16),
        ],
        4 * rows * SPREAD * width,
        "activation",
    )


def adapter_kernel(count, low_ref, tenants_ref, down_ref, own_out, other_out, spread_ref):
    half = own_out.shape[0]
    pick = pick_held(lax.axis_index("tp"), 2 * half, count)
    spread = spread_rows(picked(pick, low_ref[...]), held_mask(pick, tenants_ref[...]))
    spread_ref[...] = spread
    part = (adapter_scale * contracted_columns(spread, down_ref[...])).astype(jnp.bfloat16)
    own_out[...] = part[:half]
    other_out[...] = part[half:]


def adapter_part(low, tenants, down, count):
    rows, span = low.shape[0], down.shape[0]
    half = jax.ShapeDtypeStruct((rows // 2, span), jnp.bfloat16)
    return pl.pallas_call(
        lambda *refs: adapter_kernel(count, *refs),
        out_shape=[half, half, jax.ShapeDtypeStruct((rows, SPREAD), jnp.bfloat16)],
        compiler_params=pltpu.CompilerParams(vmem_limit_bytes=4 << 20),
        cost_estimate=pl.CostEstimate(
            flops=2 * rows * down.size, bytes_accessed=2 * down.size, transcendentals=0
        ),
        name="adapter_part",
    )(low, tenants, down)


def backward_kernel(slots, slot, dgate_ref, dup_ref, own_out, other_out):
    half = own_out.shape[0]
    part = contracted_columns(dgate_ref[...], slot(slots[0]))
    part = part + contracted_columns(dup_ref[...], slot(slots[1]))
    own_out[...] = part[:half]
    other_out[...] = part[half:].astype(jnp.bfloat16)


def backward(slots, dgate, dup, store, fetches, after):
    rows, hidden = dgate.shape
    depth = store.shape[0] // SLOTS
    return store_call(
        lambda *refs: backward_kernel(slots, *refs),
        store,
        fetches,
        [dgate, dup],
        [
            jax.ShapeDtypeStruct((rows // 2, depth), jnp.float32),
            jax.ShapeDtypeStruct((rows // 2, depth), jnp.bfloat16),
        ],
        4 * rows * hidden * depth,
        "backward",
        after=after,
    )


PARTS = 8


def merge_kernel(count, *refs):
    device = lax.axis_index("tp")
    own, came = refs[:CUTS], refs[CUTS : 2 * CUTS]
    adapter_own, adapter_came, out_ref, sums, tiles = refs[2 * CUTS :]
    chips, tile, lanes = out_ref.shape
    tokens = tile // PARTS
    per_part = (lanes - 128) // 128
    blocks = PARTS * per_part

    def put(first, value):
        for k in range(value.shape[1] // 128):
            sums[first + k] = value[:, k * 128 : (k + 1) * 128]

    for cut in range(CUTS):
        put(cut * blocks // CUTS, own[cut][...] + came[cut][...].astype(jnp.float32))
    mine = adapter_own[...].astype(jnp.float32)
    other = adapter_came[...].astype(jnp.float32)
    put(
        blocks,
        jnp.where(
            device % 2 == 0,
            jnp.concatenate([mine, other], axis=1),
            jnp.concatenate([other, mine], axis=1),
        ),
    )
    if sums.shape[0] < blocks + PARTS:
        tiles[per_part] = jnp.zeros(tiles.shape[1:], jnp.float32)
    for token in range(tokens):
        of_token = pl.ds(token, chips, stride=tokens)
        for part in range(PARTS):
            to = pl.ds(token * PARTS + part, chips, stride=tile)
            for k in range(per_part):
                tiles[k, to, :] = sums[part * per_part + k, of_token, :]
            if blocks + part < sums.shape[0]:
                tiles[per_part, to, :] = sums[blocks + part, of_token, :]
    for position in range(chips):
        chip = block_owner(device, position, count) // 2
        for k in range(lanes // 128):
            out_ref[chip, :, k * 128 : (k + 1) * 128] = tiles[
                k, position * tile : (position + 1) * tile, :
            ].astype(jnp.bfloat16)


def merge(own, came, adapter_own, adapter_came, own_rows):
    half, depth = own[0].shape
    width = CUTS * depth
    pair = 2 * adapter_own.shape[1]
    lanes = width // PARTS + 128
    chips, tile = half // own_rows, own_rows * PARTS
    return pl.pallas_call(
        lambda *refs: merge_kernel(2 * chips, *refs),
        out_shape=jax.ShapeDtypeStruct((chips, tile, lanes), jnp.bfloat16),
        scratch_shapes=[
            pltpu.VMEM(((width + pair) // 128, half, 128), jnp.float32),
            pltpu.VMEM((lanes // 128, chips * tile, 128), jnp.float32),
        ],
        compiler_params=pltpu.CompilerParams(vmem_limit_bytes=40 << 20),
        name="merge",
    )(*own, *came, adapter_own, adapter_came)


def final_kernel(pair, came_ref, out_ref, total, adapter):
    chips, tile, lanes = came_ref.shape
    tokens = tile // PARTS
    blocks = (lanes - 128) // 128
    for k in range(blocks):
        at = slice(k * 128, (k + 1) * 128)
        value = came_ref[0, :, at].astype(jnp.float32)
        for chip in range(1, chips):
            value = value + came_ref[chip, :, at].astype(jnp.float32)
        total[k] = value
    adapter[...] = came_ref[:, :, lanes - 128 :].astype(jnp.float32).reshape(adapter.shape)
    of_pair = pair // 128
    for token in range(tokens):
        rows = slice(token * PARTS, (token + 1) * PARTS)
        for k in range(blocks):
            chip, part = divmod(k, of_pair)
            source = pl.ds(
                chip * tile + token * PARTS + part, PARTS, stride=blocks // of_pair * tile
            )
            total[k, rows, :] += adapter[source, :]
    for part in range(PARTS):
        for k in range(blocks):
            at = (part * blocks + k) * 128
            out_ref[:, at : at + 128] = total[k, pl.ds(part, tokens, stride=PARTS), :].astype(
                jnp.bfloat16
            )


def final(came, pair):
    chips, tile, lanes = came.shape
    piece = lanes - 128
    return pl.pallas_call(
        lambda *refs: final_kernel(pair, *refs),
        out_shape=jax.ShapeDtypeStruct((tile // PARTS, piece * PARTS), jnp.bfloat16),
        scratch_shapes=[
            pltpu.VMEM((piece // 128, tile, 128), jnp.float32),
            pltpu.VMEM((chips * tile, 128), jnp.float32),
        ],
        compiler_params=pltpu.CompilerParams(vmem_limit_bytes=40 << 20),
        name="final",
    )(came)


def outer_kernel(left_ref, right_ref, out_ref):
    out_ref[...] = contracted_rows(
        left_ref[...] * jnp.bfloat16(adapter_scale), right_ref[...]
    ).astype(jnp.bfloat16)


def outer(left, right, name):
    rows, height = left.shape
    width = right.shape[1]
    block = block_of(height, 512)
    if block % 128:
        block = height
    return pl.pallas_call(
        outer_kernel,
        grid=(height // block,),
        in_specs=[
            pl.BlockSpec((rows, block), lambda k: (0, k)),
            pl.BlockSpec((rows, width), lambda k: (0, 0)),
        ],
        out_specs=pl.BlockSpec((block, width), lambda k: (k, 0)),
        out_shape=jax.ShapeDtypeStruct((height, width), jnp.bfloat16),
        compiler_params=pltpu.CompilerParams(vmem_limit_bytes=24 << 20),
        cost_estimate=pl.CostEstimate(
            flops=2 * rows * height * width, bytes_accessed=2 * height * width, transcendentals=0
        ),
        name=name,
    )(left, right)


def same_core_groups():
    count = lax.axis_size("tp")
    return [list(range(core, count, 2)) for core in range(2)]


def between_same_cores(blocks):
    return lax.all_to_all(
        blocks, "tp", split_axis=0, concat_axis=0, tiled=True, axis_index_groups=same_core_groups()
    )


def add_kernel(left_ref, right_ref, out_ref):
    out_ref[...] = left_ref[...] + right_ref[...]


def plus(left, right):
    return pl.pallas_call(
        add_kernel,
        out_shape=jax.ShapeDtypeStruct(left.shape, left.dtype),
        compiler_params=pltpu.CompilerParams(vmem_limit_bytes=2 << 20),
        name="plus",
    )(left, right)


def swapped(block, hop):
    return lax.ppermute(block, "tp", [(i, i ^ hop) for i in range(lax.axis_size("tp"))])


def local(
    normed_layer_input,
    hidden_unit_gradient,
    gate_weight,
    up_weight,
    adapter_down_maps,
    adapter_up_maps,
    token_tenant_index,
):
    count = lax.axis_size("tp")
    own_rows, width = normed_layer_input.shape
    rows = own_rows * count
    hops = [1 << bit for bit in range(count.bit_length() - 1)]
    tenants = token_tenant_index.reshape(1, rows)

    def pair(cut, first, second):
        return [(gate_weight, cut, first), (up_weight, cut, second)]

    def mark(slot, token_ref):
        token_ref[...] = jnp.zeros_like(token_ref)

    mark_shape = jax.ShapeDtypeStruct((8, 128), jnp.float32)
    store = jax.ShapeDtypeStruct(
        (SLOTS * width // CUTS, gate_weight.shape[1]), gate_weight.dtype
    )
    far, near = hops[-1], hops[-2]
    came = [swapped(normed_layer_input, hop) for hop in (near, far, near | far)]
    store, token = store_call(mark, store, pair(0, 0, 1), [], [mark_shape], 0, "fetch")
    block = stacked([normed_layer_input, *came], [token])
    for hop in reversed(hops[2:-2]):
        block = stacked([block, swapped(block, hop)])
    other = swapped(block, hops[1])
    x = [block, other, swapped(block, 1), swapped(other, 1)]
    store, token = store_call(
        mark, store, [(gate_weight, 1, 2)], [], [mark_shape], 0, "fetch", after=[block]
    )
    store, token = store_call(
        mark, store, [(up_weight, 1, 3)], [], [mark_shape], 0, "fetch", after=[other]
    )

    input_span, low = low_part(adapter_down_maps, tenants, x, count)
    sums = []
    slots = {0: (0, 1), 1: (2, 3), 2: (4, 5), 3: (0, 1)}
    fetches = {
        0: pair(2, 4, 5), 1: pair(3, 0, 1), 2: [(adapter_up_maps, 0, 2)], 3: [(gate_weight, 1, 3)]
    }
    step = 0
    for cut in range(CUTS):
        after = [low]
        if step < len(hops):
            low = plus(low, swapped(low, hops[step]))
            step += 1
        store, sums = forward(cut, slots[cut], x, store, sums, fetches[cut], after)
    for hop in hops[step:]:
        low = plus(low, swapped(low, hop))
    store, dgate, dup, low_grad, input_spread = activation(
        2, store, sums, hidden_unit_gradient, low, tenants, count, []
    )

    low_grad = plus(low_grad, swapped(low_grad, hops[0]))
    step = 1
    parts, arrived = {}, {}
    slots = {3: (0, 1), 2: (4, 5), 1: (3, 2), 0: (0, 1)}
    fetches = {3: [(up_weight, 1, 2)], 2: pair(0, 0, 1), 1: [], 0: []}
    for cut in reversed(range(CUTS)):
        if cut > 0:
            after = [low_grad]
            if step < len(hops):
                low_grad = plus(low_grad, swapped(low_grad, hops[step]))
                step += 1
        store, own_part, other_part = backward(slots[cut], dgate, dup, store, fetches[cut], after)
        if cut == 1:
            for hop in hops[step:]:
                low_grad = plus(low_grad, swapped(low_grad, hop))
            adapter_own, adapter_other, grad_spread = adapter_part(
                low_grad, tenants, adapter_down_maps, count
            )
            adapter_came = swapped(adapter_other, 1)
            after = [adapter_other]
        parts[cut] = own_part
        arrived[cut] = swapped(other_part, 1)
    merged = merge(
        [parts[cut] for cut in range(CUTS)],
        [arrived[cut] for cut in range(CUTS)],
        adapter_own,
        adapter_came,
        own_rows,
    )
    exchanged = between_same_cores(merged)
    down_map_gradient = outer(input_span, grad_spread, "down_maps")
    up_map_gradient = outer(input_spread, dgate, "up_maps")
    return (final(exchanged, 2 * input_span.shape[1]), down_map_gradient, up_map_gradient)


def solution(mesh):
    placed = (
        P(("groups", "tp"), None),
        P("groups", "tp"),
        P(None, "tp"),
        P(None, "tp"),
        P("tp", None),
        P(None, "tp"),
        P("groups"),
    )
    return jax.shard_map(
        local,
        mesh=mesh,
        in_specs=placed,
        out_specs=(P(("groups", "tp"), None), P("tp", "groups"), P("groups", "tp")),
        check_vma=False,
    )
```

```python
import jax
import jax.numpy as jnp
from jax import lax
from jax.experimental import pallas as pl
from jax.experimental.pallas import tpu as pltpu
from jax.sharding import PartitionSpec as P

ADAPTER_RANK = 64
TENANT_COUNT = 32
SPREAD = ADAPTER_RANK * TENANT_COUNT

adapter_scale = 2.0


def block_of(size, largest):
    block = largest
    while size % block:
        block //= 2
    return block


def contracted_rows(left, right):
    return lax.dot_general(
        left, right, (((0,), (0,)), ((), ())), preferred_element_type=jnp.float32
    )


def contracted_columns(left, right):
    return lax.dot_general(
        left, right, (((1,), (1,)), ((), ())), preferred_element_type=jnp.float32
    )


def tenant_mask(tenants, rows):
    columns = lax.broadcasted_iota(jnp.int32, (rows, SPREAD), 1) // ADAPTER_RANK
    return tenants == columns


def select_block(wide_rows, mask):
    kept = jnp.where(mask, wide_rows, 0.0)
    pair = 2 * ADAPTER_RANK
    total = kept[:, :pair]
    for start in range(pair, SPREAD, pair):
        total = total + kept[:, start : start + pair]
    return total[:, :ADAPTER_RANK] + total[:, ADAPTER_RANK:]


def spread_rows(low_rows, mask):
    pair = jnp.concatenate([low_rows, low_rows], axis=1)
    wide = jnp.concatenate([pair] * (TENANT_COUNT // 2), axis=1)
    return jnp.where(mask, wide, 0.0).astype(jnp.bfloat16)


VMEM = pl.BlockSpec(memory_space=pltpu.VMEM)
ANY = pl.BlockSpec(memory_space=pl.ANY)
CUTS = 4
COPIES = 8
SLOTS = 6
STORE_GRANT = 10 << 20


def store_call(kernel, store, fetches, operands, out_shapes, flops, name, after=()):
    new = isinstance(store, jax.ShapeDtypeStruct)
    depth = store.shape[0] // SLOTS
    part = depth // COPIES
    sources = []
    for array, _, _ in fetches:
        if not any(array is known for known in sources):
            sources.append(array)
    places = [next(i for i, known in enumerate(sources) if known is f[0]) for f in fetches]
    n_in, n_out, n_hbm = len(operands), len(out_shapes), len(sources)

    def body(*refs):
        if not new:
            refs = refs[1:]
        ins, hbm = refs[:n_in], refs[n_in : n_in + n_hbm]
        rest = refs[n_in + n_hbm + len(after) :]
        store_ref, outs, scratch = rest[0], rest[1 : 1 + n_out], rest[1 + n_out :]
        copies = []
        for n, (place, (_, piece, slot)) in enumerate(zip(places, fetches)):
            for k in range(COPIES):
                copies.append(
                    pltpu.make_async_copy(
                        hbm[place].at[pl.ds(piece * depth + k * part, part)],
                        store_ref.at[pl.ds(slot * depth + k * part, part)],
                        scratch[0].at[n * COPIES + k],
                    )
                )
        for copy in copies:
            copy.start()
        kernel(lambda slot: store_ref[slot * depth : (slot + 1) * depth, :], *ins, *outs)
        for copy in copies:
            copy.wait()

    moved = 2 * depth * store.shape[1] * len(fetches)
    return pl.pallas_call(
        body,
        in_specs=[VMEM] * (n_in + (not new)) + [ANY] * (n_hbm + len(after)),
        out_specs=[VMEM] * (1 + n_out),
        out_shape=[pltpu.VMEM(store.shape, store.dtype), *out_shapes],
        input_output_aliases={} if new else {0: 0},
        scratch_shapes=[pltpu.SemaphoreType.DMA((COPIES * len(fetches),))] if fetches else [],
        compiler_params=pltpu.CompilerParams(vmem_limit_bytes=STORE_GRANT),
        cost_estimate=pl.CostEstimate(flops=flops, bytes_accessed=moved, transcendentals=0),
        name=name,
    )(
        *([] if new else [store]),
        *operands,
        *[pltpu.with_memory_space_constraint(array, pltpu.HBM) for array in sources],
        *after,
    )


def stacked(blocks, after=()):
    rows = sum(block.shape[0] for block in blocks)

    def stack_kernel(*refs):
        refs[-1][...] = jnp.concatenate([ref[...] for ref in refs[: len(blocks)]], axis=0)

    return pl.pallas_call(
        stack_kernel,
        in_specs=[VMEM] * len(blocks) + [ANY] * len(after),
        out_shape=jax.ShapeDtypeStruct((rows, blocks[0].shape[1]), blocks[0].dtype),
        compiler_params=pltpu.CompilerParams(vmem_limit_bytes=4 << 20),
        name="stacked",
    )(*blocks, *after)


def block_owner(own, block, count):
    bits = count.bit_length() - 1
    hops = [1 << (bits - 2), 1 << (bits - 1)] + [1 << bit for bit in reversed(range(bits - 2))]
    for n, hop in enumerate(hops):
        own = own ^ (((block >> n) & 1) * hop)
    return own


def source_of(own, row, rows, count):
    tokens = rows // count
    return block_owner(own, row // tokens, count) * tokens + row % tokens


def pick_held(own, rows, count):
    held = source_of(own, lax.broadcasted_iota(jnp.int32, (rows, rows), 0), rows, count)
    return held == lax.broadcasted_iota(jnp.int32, (rows, rows), 1)


def pick_given(own, rows, count):
    held = source_of(own, lax.broadcasted_iota(jnp.int32, (rows, rows), 1), rows, count)
    return held == lax.broadcasted_iota(jnp.int32, (rows, rows), 0)


def picked(pick, block):
    if block.dtype == jnp.bfloat16:
        return jnp.dot(pick.astype(jnp.bfloat16), block, preferred_element_type=jnp.float32)
    return jnp.dot(pick.astype(jnp.float32), block, precision=lax.Precision.HIGHEST)


def held_mask(pick, tenants_row):
    tenants = jnp.sum(jnp.where(pick, tenants_row, 0).astype(jnp.float32), axis=1, keepdims=True)
    return tenant_mask(tenants.astype(jnp.int32), pick.shape[0])


def low_kernel(count, aligned, down_ref, tenants_ref, *refs):
    x, (span_out, low_ref) = refs[:-2], refs[-2:]
    own = lax.axis_index("tp")
    if aligned:
        width = down_ref.shape[0]
        at = pl.ds(pl.multiple_of(own * width, width), width)
        span = jnp.concatenate([ref[:, at] for ref in x], axis=0)
    else:
        span = jnp.concatenate([ref[...] for ref in x], axis=0)
    span_out[...] = span
    rows = span.shape[0]
    wide = jnp.dot(span, down_ref[...], preferred_element_type=jnp.float32)
    low = select_block(wide, held_mask(pick_held(own, rows, count), tenants_ref[...]))
    low_ref[...] = picked(pick_given(own, rows, count), low)


def low_part(down, tenants, x, count):
    rows, span = sum(block.shape[0] for block in x), down.shape[0]
    aligned = span % 128 == 0
    if not aligned:
        x = [
            lax.dynamic_slice(
                block,
                (0, lax.axis_index("tp") * span),
                (block.shape[0], span),
                allow_negative_indices=False,
            )
            for block in x
        ]
    return pl.pallas_call(
        lambda *refs: low_kernel(count, aligned, *refs),
        out_shape=[
            jax.ShapeDtypeStruct((rows, span), x[0].dtype),
            jax.ShapeDtypeStruct((rows, ADAPTER_RANK), jnp.float32),
        ],
        compiler_params=pltpu.CompilerParams(vmem_limit_bytes=4 << 20),
        cost_estimate=pl.CostEstimate(
            flops=2 * rows * down.size, bytes_accessed=2 * down.size, transcendentals=0
        ),
        name="low_part",
    )(down, tenants, *x)


def forward_kernel(cut, slots, blocks, first, slot, *refs):
    x = refs[:blocks]
    gate_out, up_out = refs[-2:]
    gate_weight, up_weight = slot(slots[0]), slot(slots[1])
    depth = gate_weight.shape[0]
    at = slice(cut * depth, (cut + 1) * depth)
    rows = jnp.concatenate([ref[:, at] for ref in x], axis=0)
    gate = jnp.dot(rows, gate_weight, preferred_element_type=jnp.float32)
    up = jnp.dot(rows, up_weight, preferred_element_type=jnp.float32)
    if not first:
        gate = gate + refs[blocks][...]
        up = up + refs[blocks + 1][...]
    gate_out[...] = gate
    up_out[...] = up


def forward(cut, slots, x, store, sums, fetches, after):
    rows = sum(block.shape[0] for block in x)
    depth, hidden = store.shape[0] // SLOTS, store.shape[1]
    result = jax.ShapeDtypeStruct((rows, hidden), jnp.float32)
    store, gate, up = store_call(
        lambda *refs: forward_kernel(cut, slots, len(x), not sums, *refs),
        store,
        fetches,
        [*x, *sums],
        [result, result],
        4 * rows * depth * hidden,
        "forward",
        after=after,
    )
    return store, [gate, up]


def activation_kernel(
    count, maps_slot, slot, gate_ref, up_ref, hidden_ref, low_ref, tenants_ref,
    dgate_ref, dup_ref, part_ref, spread_ref,
):
    rows = gate_ref.shape[0]
    maps = slot(maps_slot)
    own = lax.axis_index("tp")
    pick = pick_held(own, rows, count)
    mask = held_mask(pick, tenants_ref[...])
    spread = spread_rows(picked(pick, low_ref[...]), mask)
    spread_ref[...] = spread
    gate = gate_ref[...] + adapter_scale * jnp.dot(
        spread, maps, preferred_element_type=jnp.float32
    )
    s = jax.nn.sigmoid(gate)
    hidden = picked(pick, hidden_ref[...])
    dgate = (hidden * up_ref[...] * s * (1.0 + gate * (1.0 - s))).astype(jnp.bfloat16)
    dgate_ref[...] = dgate
    dup_ref[...] = (hidden * gate * s).astype(jnp.bfloat16)
    part = select_block(contracted_columns(dgate, maps), mask)
    part_ref[...] = picked(pick_given(own, rows, count), part)


def activation(maps_slot, store, sums, hidden, low, tenants, count, fetches):
    rows, width = sums[0].shape
    value = jax.ShapeDtypeStruct((rows, width), jnp.bfloat16)
    return store_call(
        lambda *refs: activation_kernel(count, maps_slot, *refs),
        store,
        fetches,
        [*sums, hidden, low, tenants],
        [
            value,
            value,
            jax.ShapeDtypeStruct((rows, ADAPTER_RANK), jnp.float32),
            jax.ShapeDtypeStruct((rows, SPREAD), jnp.bfloat16),
        ],
        4 * rows * SPREAD * width,
        "activation",
    )


def adapter_kernel(count, low_ref, tenants_ref, down_ref, own_out, other_out, spread_ref):
    half = own_out.shape[0]
    pick = pick_held(lax.axis_index("tp"), 2 * half, count)
    spread = spread_rows(picked(pick, low_ref[...]), held_mask(pick, tenants_ref[...]))
    spread_ref[...] = spread
    part = (adapter_scale * contracted_columns(spread, down_ref[...])).astype(jnp.bfloat16)
    own_out[...] = part[:half]
    other_out[...] = part[half:]


def adapter_part(low, tenants, down, count):
    rows, span = low.shape[0], down.shape[0]
    half = jax.ShapeDtypeStruct((rows // 2, span), jnp.bfloat16)
    return pl.pallas_call(
        lambda *refs: adapter_kernel(count, *refs),
        out_shape=[half, half, jax.ShapeDtypeStruct((rows, SPREAD), jnp.bfloat16)],
        compiler_params=pltpu.CompilerParams(vmem_limit_bytes=4 << 20),
        cost_estimate=pl.CostEstimate(
            flops=2 * rows * down.size, bytes_accessed=2 * down.size, transcendentals=0
        ),
        name="adapter_part",
    )(low, tenants, down)


def backward_kernel(slots, slot, dgate_ref, dup_ref, own_out, other_out):
    half = own_out.shape[0]
    part = contracted_columns(dgate_ref[...], slot(slots[0]))
    part = part + contracted_columns(dup_ref[...], slot(slots[1]))
    own_out[...] = part[:half]
    other_out[...] = part[half:].astype(jnp.bfloat16)


def backward(slots, dgate, dup, store, fetches, after):
    rows, hidden = dgate.shape
    depth = store.shape[0] // SLOTS
    return store_call(
        lambda *refs: backward_kernel(slots, *refs),
        store,
        fetches,
        [dgate, dup],
        [
            jax.ShapeDtypeStruct((rows // 2, depth), jnp.float32),
            jax.ShapeDtypeStruct((rows // 2, depth), jnp.bfloat16),
        ],
        4 * rows * hidden * depth,
        "backward",
        after=after,
    )


PARTS = 8


def merge_kernel(count, *refs):
    device = lax.axis_index("tp")
    own, came = refs[:CUTS], refs[CUTS : 2 * CUTS]
    adapter_own, adapter_came, out_ref, sums, tiles = refs[2 * CUTS :]
    chips, tile, lanes = out_ref.shape
    tokens = tile // PARTS
    per_part = (lanes - 128) // 128
    blocks = PARTS * per_part

    def put(first, value):
        for k in range(value.shape[1] // 128):
            sums[first + k] = value[:, k * 128 : (k + 1) * 128]

    for cut in range(CUTS):
        put(cut * blocks // CUTS, own[cut][...] + came[cut][...].astype(jnp.float32))
    mine = adapter_own[...].astype(jnp.float32)
    other = adapter_came[...].astype(jnp.float32)
    put(
        blocks,
        jnp.where(
            device % 2 == 0,
            jnp.concatenate([mine, other], axis=1),
            jnp.concatenate([other, mine], axis=1),
        ),
    )
    if sums.shape[0] < blocks + PARTS:
        tiles[per_part] = jnp.zeros(tiles.shape[1:], jnp.float32)
    for token in range(tokens):
        of_token = pl.ds(token, chips, stride=tokens)
        for part in range(PARTS):
            to = pl.ds(token * PARTS + part, chips, stride=tile)
            for k in range(per_part):
                tiles[k, to, :] = sums[part * per_part + k, of_token, :]
            if blocks + part < sums.shape[0]:
                tiles[per_part, to, :] = sums[blocks + part, of_token, :]
    for position in range(chips):
        chip = block_owner(device, position, count) // 2
        for k in range(lanes // 128):
            out_ref[chip, :, k * 128 : (k + 1) * 128] = tiles[
                k, position * tile : (position + 1) * tile, :
            ].astype(jnp.bfloat16)


def merge(own, came, adapter_own, adapter_came, own_rows):
    half, depth = own[0].shape
    width = CUTS * depth
    pair = 2 * adapter_own.shape[1]
    lanes = width // PARTS + 128
    chips, tile = half // own_rows, own_rows * PARTS
    return pl.pallas_call(
        lambda *refs: merge_kernel(2 * chips, *refs),
        out_shape=jax.ShapeDtypeStruct((chips, tile, lanes), jnp.bfloat16),
        scratch_shapes=[
            pltpu.VMEM(((width + pair) // 128, half, 128), jnp.float32),
            pltpu.VMEM((lanes // 128, chips * tile, 128), jnp.float32),
        ],
        compiler_params=pltpu.CompilerParams(vmem_limit_bytes=40 << 20),
        name="merge",
    )(*own, *came, adapter_own, adapter_came)


def final_kernel(pair, came_ref, out_ref, total, adapter):
    chips, tile, lanes = came_ref.shape
    tokens = tile // PARTS
    blocks = (lanes - 128) // 128
    for k in range(blocks):
        at = slice(k * 128, (k + 1) * 128)
        value = came_ref[0, :, at].astype(jnp.float32)
        for chip in range(1, chips):
            value = value + came_ref[chip, :, at].astype(jnp.float32)
        total[k] = value
    adapter[...] = came_ref[:, :, lanes - 128 :].astype(jnp.float32).reshape(adapter.shape)
    of_pair = pair // 128
    for token in range(tokens):
        rows = slice(token * PARTS, (token + 1) * PARTS)
        for k in range(blocks):
            chip, part = divmod(k, of_pair)
            source = pl.ds(
                chip * tile + token * PARTS + part, PARTS, stride=blocks // of_pair * tile
            )
            total[k, rows, :] += adapter[source, :]
    for part in range(PARTS):
        for k in range(blocks):
            at = (part * blocks + k) * 128
            out_ref[:, at : at + 128] = total[k, pl.ds(part, tokens, stride=PARTS), :].astype(
                jnp.bfloat16
            )


def final(came, pair):
    chips, tile, lanes = came.shape
    piece = lanes - 128
    return pl.pallas_call(
        lambda *refs: final_kernel(pair, *refs),
        out_shape=jax.ShapeDtypeStruct((tile // PARTS, piece * PARTS), jnp.bfloat16),
        scratch_shapes=[
            pltpu.VMEM((piece // 128, tile, 128), jnp.float32),
            pltpu.VMEM((chips * tile, 128), jnp.float32),
        ],
        compiler_params=pltpu.CompilerParams(vmem_limit_bytes=40 << 20),
        name="final",
    )(came)


def outer_kernel(left_ref, right_ref, out_ref):
    out_ref[...] = contracted_rows(
        left_ref[...] * jnp.bfloat16(adapter_scale), right_ref[...]
    ).astype(jnp.bfloat16)


def outer(left, right, name):
    rows, height = left.shape
    width = right.shape[1]
    block = block_of(height, 512)
    if block % 128:
        block = height
    return pl.pallas_call(
        outer_kernel,
        grid=(height // block,),
        in_specs=[
            pl.BlockSpec((rows, block), lambda k: (0, k)),
            pl.BlockSpec((rows, width), lambda k: (0, 0)),
        ],
        out_specs=pl.BlockSpec((block, width), lambda k: (k, 0)),
        out_shape=jax.ShapeDtypeStruct((height, width), jnp.bfloat16),
        compiler_params=pltpu.CompilerParams(vmem_limit_bytes=24 << 20),
        cost_estimate=pl.CostEstimate(
            flops=2 * rows * height * width, bytes_accessed=2 * height * width, transcendentals=0
        ),
        name=name,
    )(left, right)


def same_core_groups():
    count = lax.axis_size("tp")
    return [list(range(core, count, 2)) for core in range(2)]


def between_same_cores(blocks):
    return lax.all_to_all(
        blocks, "tp", split_axis=0, concat_axis=0, tiled=True, axis_index_groups=same_core_groups()
    )


def add_kernel(left_ref, right_ref, out_ref):
    out_ref[...] = left_ref[...] + right_ref[...]


def plus(left, right):
    return pl.pallas_call(
        add_kernel,
        out_shape=jax.ShapeDtypeStruct(left.shape, left.dtype),
        compiler_params=pltpu.CompilerParams(vmem_limit_bytes=2 << 20),
        name="plus",
    )(left, right)


def swapped(block, hop):
    return lax.ppermute(block, "tp", [(i, i ^ hop) for i in range(lax.axis_size("tp"))])


def local(
    normed_layer_input,
    hidden_unit_gradient,
    gate_weight,
    up_weight,
    adapter_down_maps,
    adapter_up_maps,
    token_tenant_index,
):
    count = lax.axis_size("tp")
    own_rows, width = normed_layer_input.shape
    rows = own_rows * count
    hops = [1 << bit for bit in range(count.bit_length() - 1)]
    tenants = token_tenant_index.reshape(1, rows)

    def pair(cut, first, second):
        return [(gate_weight, cut, first), (up_weight, cut, second)]

    def mark(slot, token_ref):
        token_ref[...] = jnp.zeros_like(token_ref)

    mark_shape = jax.ShapeDtypeStruct((8, 128), jnp.float32)
    store = jax.ShapeDtypeStruct(
        (SLOTS * width // CUTS, gate_weight.shape[1]), gate_weight.dtype
    )
    far, near = hops[-1], hops[-2]
    came = [swapped(normed_layer_input, hop) for hop in (near, far, near | far)]
    store, token = store_call(mark, store, pair(0, 0, 1), [], [mark_shape], 0, "fetch")
    block = stacked([normed_layer_input, *came], [token])
    for hop in reversed(hops[2:-2]):
        block = stacked([block, swapped(block, hop)])
    other = swapped(block, hops[1])
    store, token = store_call(
        mark, store, [(gate_weight, 1, 2)], [], [mark_shape], 0, "fetch", after=[block]
    )
    block = stacked([block, other], [token])
    x = [block, swapped(block, 1)]
    store, token = store_call(
        mark, store, [(up_weight, 1, 3)], [], [mark_shape], 0, "fetch", after=[block]
    )

    input_span, low = low_part(adapter_down_maps, tenants, x, count)
    sums = []
    slots = {0: (0, 1), 1: (2, 3), 2: (4, 5), 3: (0, 1)}
    fetches = {
        0: pair(2, 4, 5), 1: pair(3, 0, 1), 2: [(adapter_up_maps, 0, 2)], 3: []
    }
    step = 0
    for cut in range(CUTS):
        after = [low]
        if step < len(hops):
            low = plus(low, swapped(low, hops[step]))
            step += 1
        store, sums = forward(cut, slots[cut], x, store, sums, fetches[cut], after)
    for hop in hops[step:]:
        low = plus(low, swapped(low, hop))
    store, dgate, dup, low_grad, input_spread = activation(
        2, store, sums, hidden_unit_gradient, low, tenants, count, []
    )

    low_grad = plus(low_grad, swapped(low_grad, hops[0]))
    step = 1
    parts, arrived = {}, {}
    slots = {3: (0, 1), 2: (4, 5), 1: (2, 3), 0: (0, 1)}
    fetches = {
        3: [(gate_weight, 1, 2)], 2: [(gate_weight, 0, 0)], 1: [(up_weight, 0, 1)], 0: []
    }
    for cut in reversed(range(CUTS)):
        if cut > 0:
            after = [low_grad]
            if step < len(hops):
                low_grad = plus(low_grad, swapped(low_grad, hops[step]))
                step += 1
        store, own_part, other_part = backward(slots[cut], dgate, dup, store, fetches[cut], after)
        if cut == 1:
            for hop in hops[step:]:
                low_grad = plus(low_grad, swapped(low_grad, hop))
            adapter_own, adapter_other, grad_spread = adapter_part(
                low_grad, tenants, adapter_down_maps, count
            )
            adapter_came = swapped(adapter_other, 1)
            after = [adapter_other]
        parts[cut] = own_part
        arrived[cut] = swapped(other_part, 1)
    merged = merge(
        [parts[cut] for cut in range(CUTS)],
        [arrived[cut] for cut in range(CUTS)],
        adapter_own,
        adapter_came,
        own_rows,
    )
    exchanged = between_same_cores(merged)
    down_map_gradient = outer(input_span, grad_spread, "down_maps")
    up_map_gradient = outer(input_spread, dgate, "up_maps")
    return (final(exchanged, 2 * input_span.shape[1]), down_map_gradient, up_map_gradient)


def solution(mesh):
    placed = (
        P(("groups", "tp"), None),
        P("groups", "tp"),
        P(None, "tp"),
        P(None, "tp"),
        P("tp", None),
        P(None, "tp"),
        P("groups"),
    )
    return jax.shard_map(
        local,
        mesh=mesh,
        in_specs=placed,
        out_specs=(P(("groups", "tp"), None), P("tp", "groups"), P("groups", "tp")),
        check_vma=False,
    )
```

```python
import jax
import jax.numpy as jnp
from jax import lax
from jax.experimental import pallas as pl
from jax.experimental.pallas import tpu as pltpu
from jax.sharding import PartitionSpec as P

ADAPTER_RANK = 64
TENANT_COUNT = 32
SPREAD = ADAPTER_RANK * TENANT_COUNT

adapter_scale = 2.0


def block_of(size, largest):
    block = largest
    while size % block:
        block //= 2
    return block


def contracted_rows(left, right):
    return lax.dot_general(
        left, right, (((0,), (0,)), ((), ())), preferred_element_type=jnp.float32
    )


def contracted_columns(left, right):
    return lax.dot_general(
        left, right, (((1,), (1,)), ((), ())), preferred_element_type=jnp.float32
    )


def tenant_mask(tenants, rows):
    columns = lax.broadcasted_iota(jnp.int32, (rows, SPREAD), 1) // ADAPTER_RANK
    return tenants == columns


def select_block(wide_rows, mask):
    kept = jnp.where(mask, wide_rows, 0.0)
    pair = 2 * ADAPTER_RANK
    total = kept[:, :pair]
    for start in range(pair, SPREAD, pair):
        total = total + kept[:, start : start + pair]
    return total[:, :ADAPTER_RANK] + total[:, ADAPTER_RANK:]


def spread_rows(low_rows, mask):
    pair = jnp.concatenate([low_rows, low_rows], axis=1)
    wide = jnp.concatenate([pair] * (TENANT_COUNT // 2), axis=1)
    return jnp.where(mask, wide, 0.0).astype(jnp.bfloat16)


VMEM = pl.BlockSpec(memory_space=pltpu.VMEM)
ANY = pl.BlockSpec(memory_space=pl.ANY)
CUTS = 4
COPIES = 8
SLOTS = 6
STORE_GRANT = 10 << 20


def store_call(kernel, store, fetches, operands, out_shapes, flops, name, after=()):
    new = isinstance(store, jax.ShapeDtypeStruct)
    depth = store.shape[0] // SLOTS
    part = depth // COPIES
    sources = []
    for array, _, _ in fetches:
        if not any(array is known for known in sources):
            sources.append(array)
    places = [next(i for i, known in enumerate(sources) if known is f[0]) for f in fetches]
    n_in, n_out, n_hbm = len(operands), len(out_shapes), len(sources)

    def body(*refs):
        if not new:
            refs = refs[1:]
        ins, hbm = refs[:n_in], refs[n_in : n_in + n_hbm]
        rest = refs[n_in + n_hbm + len(after) :]
        store_ref, outs, scratch = rest[0], rest[1 : 1 + n_out], rest[1 + n_out :]
        copies = []
        for n, (place, (_, piece, slot)) in enumerate(zip(places, fetches)):
            for k in range(COPIES):
                copies.append(
                    pltpu.make_async_copy(
                        hbm[place].at[pl.ds(piece * depth + k * part, part)],
                        store_ref.at[pl.ds(slot * depth + k * part, part)],
                        scratch[0].at[n * COPIES + k],
                    )
                )
        for copy in copies:
            copy.start()
        kernel(lambda slot: store_ref[slot * depth : (slot + 1) * depth, :], *ins, *outs)
        for copy in copies:
            copy.wait()

    moved = 2 * depth * store.shape[1] * len(fetches)
    return pl.pallas_call(
        body,
        in_specs=[VMEM] * (n_in + (not new)) + [ANY] * (n_hbm + len(after)),
        out_specs=[VMEM] * (1 + n_out),
        out_shape=[pltpu.VMEM(store.shape, store.dtype), *out_shapes],
        input_output_aliases={} if new else {0: 0},
        scratch_shapes=[pltpu.SemaphoreType.DMA((COPIES * len(fetches),))] if fetches else [],
        compiler_params=pltpu.CompilerParams(vmem_limit_bytes=STORE_GRANT),
        cost_estimate=pl.CostEstimate(flops=flops, bytes_accessed=moved, transcendentals=0),
        name=name,
    )(
        *([] if new else [store]),
        *operands,
        *[pltpu.with_memory_space_constraint(array, pltpu.HBM) for array in sources],
        *after,
    )


def stacked(blocks, after=()):
    rows = sum(block.shape[0] for block in blocks)

    def stack_kernel(*refs):
        refs[-1][...] = jnp.concatenate([ref[...] for ref in refs[: len(blocks)]], axis=0)

    return pl.pallas_call(
        stack_kernel,
        in_specs=[VMEM] * len(blocks) + [ANY] * len(after),
        out_shape=jax.ShapeDtypeStruct((rows, blocks[0].shape[1]), blocks[0].dtype),
        compiler_params=pltpu.CompilerParams(vmem_limit_bytes=4 << 20),
        name="stacked",
    )(*blocks, *after)


def block_owner(own, block, count):
    bits = count.bit_length() - 1
    hops = [1 << (bits - 2), 1 << (bits - 1)] + [1 << bit for bit in reversed(range(bits - 2))]
    for n, hop in enumerate(hops):
        own = own ^ (((block >> n) & 1) * hop)
    return own


def source_of(own, row, rows, count):
    tokens = rows // count
    return block_owner(own, row // tokens, count) * tokens + row % tokens


def pick_held(own, rows, count):
    held = source_of(own, lax.broadcasted_iota(jnp.int32, (rows, rows), 0), rows, count)
    return held == lax.broadcasted_iota(jnp.int32, (rows, rows), 1)


def pick_given(own, rows, count):
    held = source_of(own, lax.broadcasted_iota(jnp.int32, (rows, rows), 1), rows, count)
    return held == lax.broadcasted_iota(jnp.int32, (rows, rows), 0)


def picked(pick, block):
    if block.dtype == jnp.bfloat16:
        return jnp.dot(pick.astype(jnp.bfloat16), block, preferred_element_type=jnp.float32)
    return jnp.dot(pick.astype(jnp.float32), block, precision=lax.Precision.HIGHEST)


def held_mask(pick, tenants_row):
    tenants = jnp.sum(jnp.where(pick, tenants_row, 0).astype(jnp.float32), axis=1, keepdims=True)
    return tenant_mask(tenants.astype(jnp.int32), pick.shape[0])


def low_kernel(count, aligned, down_ref, tenants_ref, *refs):
    x, (span_out, low_ref) = refs[:-2], refs[-2:]
    own = lax.axis_index("tp")
    if aligned:
        width = down_ref.shape[0]
        at = pl.ds(pl.multiple_of(own * width, width), width)
        span = jnp.concatenate([ref[:, at] for ref in x], axis=0)
    else:
        span = jnp.concatenate([ref[...] for ref in x], axis=0)
    span_out[...] = span
    rows = span.shape[0]
    wide = jnp.dot(span, down_ref[...], preferred_element_type=jnp.float32)
    low = select_block(wide, held_mask(pick_held(own, rows, count), tenants_ref[...]))
    low_ref[...] = picked(pick_given(own, rows, count), low)


def low_part(down, tenants, x, count):
    rows, span = sum(block.shape[0] for block in x), down.shape[0]
    aligned = span % 128 == 0
    if not aligned:
        x = [
            lax.dynamic_slice(
                block,
                (0, lax.axis_index("tp") * span),
                (block.shape[0], span),
                allow_negative_indices=False,
            )
            for block in x
        ]
    return pl.pallas_call(
        lambda *refs: low_kernel(count, aligned, *refs),
        out_shape=[
            jax.ShapeDtypeStruct((rows, span), x[0].dtype),
            jax.ShapeDtypeStruct((rows, ADAPTER_RANK), jnp.float32),
        ],
        compiler_params=pltpu.CompilerParams(vmem_limit_bytes=4 << 20),
        cost_estimate=pl.CostEstimate(
            flops=2 * rows * down.size, bytes_accessed=2 * down.size, transcendentals=0
        ),
        name="low_part",
    )(down, tenants, *x)


def forward_kernel(cuts, slots, blocks, first, slot, *refs):
    x = refs[:blocks]
    gate_out, up_out = refs[-2:]
    gate, up = (0.0, 0.0) if first else (refs[blocks][...], refs[blocks + 1][...])
    for cut in cuts:
        gate_weight, up_weight = slot(slots[cut][0]), slot(slots[cut][1])
        depth = gate_weight.shape[0]
        at = slice(cut * depth, (cut + 1) * depth)
        rows = jnp.concatenate([ref[:, at] for ref in x], axis=0)
        gate = gate + jnp.dot(rows, gate_weight, preferred_element_type=jnp.float32)
        up = up + jnp.dot(rows, up_weight, preferred_element_type=jnp.float32)
    gate_out[...] = gate
    up_out[...] = up


def forward(cuts, slots, x, store, sums, fetches, after):
    rows = sum(block.shape[0] for block in x)
    depth, hidden = store.shape[0] // SLOTS, store.shape[1]
    result = jax.ShapeDtypeStruct((rows, hidden), jnp.float32)
    store, gate, up = store_call(
        lambda *refs: forward_kernel(cuts, slots, len(x), not sums, *refs),
        store,
        fetches,
        [*x, *sums],
        [result, result],
        4 * rows * depth * hidden * len(cuts),
        "forward",
        after=after,
    )
    return store, [gate, up]


def activation_kernel(
    count, maps_slot, slot, gate_ref, up_ref, hidden_ref, low_ref, tenants_ref,
    dgate_ref, dup_ref, part_ref, spread_ref,
):
    rows = gate_ref.shape[0]
    maps = slot(maps_slot)
    own = lax.axis_index("tp")
    pick = pick_held(own, rows, count)
    mask = held_mask(pick, tenants_ref[...])
    spread = spread_rows(picked(pick, low_ref[...]), mask)
    spread_ref[...] = spread
    gate = gate_ref[...] + adapter_scale * jnp.dot(
        spread, maps, preferred_element_type=jnp.float32
    )
    s = jax.nn.sigmoid(gate)
    hidden = picked(pick, hidden_ref[...])
    dgate = (hidden * up_ref[...] * s * (1.0 + gate * (1.0 - s))).astype(jnp.bfloat16)
    dgate_ref[...] = dgate
    dup_ref[...] = (hidden * gate * s).astype(jnp.bfloat16)
    part = select_block(contracted_columns(dgate, maps), mask)
    part_ref[...] = picked(pick_given(own, rows, count), part)


def activation(maps_slot, store, sums, hidden, low, tenants, count, fetches):
    rows, width = sums[0].shape
    value = jax.ShapeDtypeStruct((rows, width), jnp.bfloat16)
    return store_call(
        lambda *refs: activation_kernel(count, maps_slot, *refs),
        store,
        fetches,
        [*sums, hidden, low, tenants],
        [
            value,
            value,
            jax.ShapeDtypeStruct((rows, ADAPTER_RANK), jnp.float32),
            jax.ShapeDtypeStruct((rows, SPREAD), jnp.bfloat16),
        ],
        4 * rows * SPREAD * width,
        "activation",
    )


def adapter_kernel(count, low_ref, tenants_ref, down_ref, own_out, other_out, spread_ref):
    half = own_out.shape[0]
    pick = pick_held(lax.axis_index("tp"), 2 * half, count)
    spread = spread_rows(picked(pick, low_ref[...]), held_mask(pick, tenants_ref[...]))
    spread_ref[...] = spread
    part = (adapter_scale * contracted_columns(spread, down_ref[...])).astype(jnp.bfloat16)
    own_out[...] = part[:half]
    other_out[...] = part[half:]


def adapter_part(low, tenants, down, count):
    rows, span = low.shape[0], down.shape[0]
    half = jax.ShapeDtypeStruct((rows // 2, span), jnp.bfloat16)
    return pl.pallas_call(
        lambda *refs: adapter_kernel(count, *refs),
        out_shape=[half, half, jax.ShapeDtypeStruct((rows, SPREAD), jnp.bfloat16)],
        compiler_params=pltpu.CompilerParams(vmem_limit_bytes=4 << 20),
        cost_estimate=pl.CostEstimate(
            flops=2 * rows * down.size, bytes_accessed=2 * down.size, transcendentals=0
        ),
        name="adapter_part",
    )(low, tenants, down)


def backward_kernel(slots, slot, dgate_ref, dup_ref, own_out, other_out):
    half = own_out.shape[0]
    part = contracted_columns(dgate_ref[...], slot(slots[0]))
    part = part + contracted_columns(dup_ref[...], slot(slots[1]))
    own_out[...] = part[:half]
    other_out[...] = part[half:].astype(jnp.bfloat16)


def backward(slots, dgate, dup, store, fetches, after):
    rows, hidden = dgate.shape
    depth = store.shape[0] // SLOTS
    return store_call(
        lambda *refs: backward_kernel(slots, *refs),
        store,
        fetches,
        [dgate, dup],
        [
            jax.ShapeDtypeStruct((rows // 2, depth), jnp.float32),
            jax.ShapeDtypeStruct((rows // 2, depth), jnp.bfloat16),
        ],
        4 * rows * hidden * depth,
        "backward",
        after=after,
    )


PARTS = 8


def merge_kernel(count, *refs):
    device = lax.axis_index("tp")
    own, came = refs[:CUTS], refs[CUTS : 2 * CUTS]
    adapter_own, adapter_came, out_ref, sums, tiles = refs[2 * CUTS :]
    chips, tile, lanes = out_ref.shape
    tokens = tile // PARTS
    per_part = lanes // 128
    blocks = PARTS * per_part
    for cut in range(CUTS):
        value = own[cut][...] + came[cut][...].astype(jnp.float32)
        for k in range(blocks // CUTS):
            sums[cut * blocks // CUTS + k] = value[:, k * 128 : (k + 1) * 128]
    mine = adapter_own[...].astype(jnp.float32)
    other = adapter_came[...].astype(jnp.float32)
    pair = jnp.where(
        device % 2 == 0,
        jnp.concatenate([mine, other], axis=1),
        jnp.concatenate([other, mine], axis=1),
    )
    of_chip = blocks // chips
    for k in range(of_chip):
        sums[device // 2 * of_chip + k] += pair[:, k * 128 : (k + 1) * 128]
    for token in range(tokens):
        of_token = pl.ds(token, chips, stride=tokens)
        for part in range(PARTS):
            to = pl.ds(token * PARTS + part, chips, stride=tile)
            for k in range(per_part):
                tiles[k, to, :] = sums[part * per_part + k, of_token, :]
    for position in range(chips):
        chip = block_owner(device, position, count) // 2
        for k in range(per_part):
            out_ref[chip, :, k * 128 : (k + 1) * 128] = tiles[
                k, position * tile : (position + 1) * tile, :
            ].astype(jnp.bfloat16)


def merge(own, came, adapter_own, adapter_came, own_rows):
    half, depth = own[0].shape
    lanes = CUTS * depth // PARTS
    chips, tile = half // own_rows, own_rows * PARTS
    return pl.pallas_call(
        lambda *refs: merge_kernel(2 * chips, *refs),
        out_shape=jax.ShapeDtypeStruct((chips, tile, lanes), jnp.bfloat16),
        scratch_shapes=[
            pltpu.VMEM((CUTS * depth // 128, half, 128), jnp.float32),
            pltpu.VMEM((lanes // 128, chips * tile, 128), jnp.float32),
        ],
        compiler_params=pltpu.CompilerParams(vmem_limit_bytes=40 << 20),
        name="merge",
    )(*own, *came, adapter_own, adapter_came)


def final_kernel(came_ref, out_ref, total):
    chips, tile, lanes = came_ref.shape
    tokens = tile // PARTS
    blocks = lanes // 128
    for k in range(blocks):
        at = slice(k * 128, (k + 1) * 128)
        value = came_ref[0, :, at].astype(jnp.float32)
        for chip in range(1, chips):
            value = value + came_ref[chip, :, at].astype(jnp.float32)
        total[k] = value
    for part in range(PARTS):
        for k in range(blocks):
            at = (part * blocks + k) * 128
            out_ref[:, at : at + 128] = total[k, pl.ds(part, tokens, stride=PARTS), :].astype(
                jnp.bfloat16
            )


def final(came):
    chips, tile, lanes = came.shape
    return pl.pallas_call(
        final_kernel,
        out_shape=jax.ShapeDtypeStruct((tile // PARTS, lanes * PARTS), jnp.bfloat16),
        scratch_shapes=[pltpu.VMEM((lanes // 128, tile, 128), jnp.float32)],
        compiler_params=pltpu.CompilerParams(vmem_limit_bytes=40 << 20),
        name="final",
    )(came)


def outer_kernel(left_ref, right_ref, out_ref):
    out_ref[...] = contracted_rows(
        left_ref[...] * jnp.bfloat16(adapter_scale), right_ref[...]
    ).astype(jnp.bfloat16)


def outer(left, right, name):
    rows, height = left.shape
    width = right.shape[1]
    block = block_of(height, 512)
    if block % 128:
        block = height
    return pl.pallas_call(
        outer_kernel,
        grid=(height // block,),
        in_specs=[
            pl.BlockSpec((rows, block), lambda k: (0, k)),
            pl.BlockSpec((rows, width), lambda k: (0, 0)),
        ],
        out_specs=pl.BlockSpec((block, width), lambda k: (k, 0)),
        out_shape=jax.ShapeDtypeStruct((height, width), jnp.bfloat16),
        compiler_params=pltpu.CompilerParams(vmem_limit_bytes=24 << 20),
        cost_estimate=pl.CostEstimate(
            flops=2 * rows * height * width, bytes_accessed=2 * height * width, transcendentals=0
        ),
        name=name,
    )(left, right)


def same_core_groups():
    count = lax.axis_size("tp")
    return [list(range(core, count, 2)) for core in range(2)]


def between_same_cores(blocks):
    return lax.all_to_all(
        blocks, "tp", split_axis=0, concat_axis=0, tiled=True, axis_index_groups=same_core_groups()
    )


def add_kernel(left_ref, right_ref, out_ref):
    out_ref[...] = left_ref[...] + right_ref[...]


def plus(left, right):
    return pl.pallas_call(
        add_kernel,
        out_shape=jax.ShapeDtypeStruct(left.shape, left.dtype),
        compiler_params=pltpu.CompilerParams(vmem_limit_bytes=2 << 20),
        name="plus",
    )(left, right)


def swapped(block, hop):
    return lax.ppermute(block, "tp", [(i, i ^ hop) for i in range(lax.axis_size("tp"))])


def local(
    normed_layer_input,
    hidden_unit_gradient,
    gate_weight,
    up_weight,
    adapter_down_maps,
    adapter_up_maps,
    token_tenant_index,
):
    count = lax.axis_size("tp")
    own_rows, width = normed_layer_input.shape
    rows = own_rows * count
    hops = [1 << bit for bit in range(count.bit_length() - 1)]
    tenants = token_tenant_index.reshape(1, rows)

    def pair(cut, first, second):
        return [(gate_weight, cut, first), (up_weight, cut, second)]

    def mark(slot, token_ref):
        token_ref[...] = jnp.zeros_like(token_ref)

    mark_shape = jax.ShapeDtypeStruct((8, 128), jnp.float32)
    store = jax.ShapeDtypeStruct(
        (SLOTS * width // CUTS, gate_weight.shape[1]), gate_weight.dtype
    )
    far, near = hops[-1], hops[-2]
    came = [swapped(normed_layer_input, hop) for hop in (near, far, near | far)]
    store, token = store_call(mark, store, pair(0, 0, 1), [], [mark_shape], 0, "fetch")
    block = stacked([normed_layer_input, *came], [token])
    for hop in reversed(hops[2:-2]):
        block = stacked([block, swapped(block, hop)])
    other = swapped(block, hops[1])
    store, token = store_call(
        mark, store, [(gate_weight, 1, 2)], [], [mark_shape], 0, "fetch", after=[block]
    )
    block = stacked([block, other], [token])
    x = [block, swapped(block, 1)]
    store, token = store_call(
        mark, store, [(up_weight, 1, 3)], [], [mark_shape], 0, "fetch", after=[block]
    )

    input_span, low = low_part(adapter_down_maps, tenants, x, count)
    sums = []
    slots = {0: (0, 1), 1: (2, 3), 2: (4, 5), 3: (0, 1)}
    step = 0
    for cuts, fetches in (
        ((0, 1), pair(2, 4, 5)), ((2,), pair(3, 0, 1)), ((3,), [(adapter_up_maps, 0, 2)])
    ):
        after = [low]
        if step < len(hops):
            low = plus(low, swapped(low, hops[step]))
            step += 1
        store, sums = forward(cuts, slots, x, store, sums, fetches, after)
    for hop in hops[step:]:
        low = plus(low, swapped(low, hop))
    store, dgate, dup, low_grad, input_spread = activation(
        2, store, sums, hidden_unit_gradient, low, tenants, count, []
    )

    later_hops = hops[1:] + hops[:1]
    parts, arrived = {}, {}
    slots = {3: (0, 1), 2: (4, 5), 1: (2, 3), 0: (0, 1)}
    fetches = {
        3: [(gate_weight, 1, 2)], 2: [(gate_weight, 0, 0)], 1: [(up_weight, 0, 1)], 0: []
    }
    for cut in reversed(range(CUTS)):
        after = [low_grad]
        turns = later_hops[:1] if cut > 0 else later_hops
        later_hops = later_hops[len(turns) :]
        for hop in turns:
            low_grad = plus(low_grad, swapped(low_grad, hop))
        store, own_part, other_part = backward(slots[cut], dgate, dup, store, fetches[cut], after)
        parts[cut] = own_part
        arrived[cut] = swapped(other_part, 1)
    adapter_own, adapter_other, grad_spread = adapter_part(
        low_grad, tenants, adapter_down_maps, count
    )
    adapter_came = swapped(adapter_other, 1)
    merged = merge(
        [parts[cut] for cut in range(CUTS)],
        [arrived[cut] for cut in range(CUTS)],
        adapter_own,
        adapter_came,
        own_rows,
    )
    exchanged = between_same_cores(merged)
    down_map_gradient = outer(input_span, grad_spread, "down_maps")
    up_map_gradient = outer(input_spread, dgate, "up_maps")
    return (final(exchanged), down_map_gradient, up_map_gradient)


def solution(mesh):
    placed = (
        P(("groups", "tp"), None),
        P("groups", "tp"),
        P(None, "tp"),
        P(None, "tp"),
        P("tp", None),
        P(None, "tp"),
        P("groups"),
    )
    return jax.shard_map(
        local,
        mesh=mesh,
        in_specs=placed,
        out_specs=(P(("groups", "tp"), None), P("tp", "groups"), P("groups", "tp")),
        check_vma=False,
    )
```

```python
import jax
import jax.numpy as jnp
from jax import lax
from jax.experimental import pallas as pl
from jax.experimental.pallas import tpu as pltpu
from jax.sharding import PartitionSpec as P

ADAPTER_RANK = 64
TENANT_COUNT = 32
SPREAD = ADAPTER_RANK * TENANT_COUNT

adapter_scale = 2.0


def block_of(size, largest):
    block = largest
    while size % block:
        block //= 2
    return block


def contracted_rows(left, right):
    return lax.dot_general(
        left, right, (((0,), (0,)), ((), ())), preferred_element_type=jnp.float32
    )


def contracted_columns(left, right):
    return lax.dot_general(
        left, right, (((1,), (1,)), ((), ())), preferred_element_type=jnp.float32
    )


def tenant_mask(tenants, rows):
    columns = lax.broadcasted_iota(jnp.int32, (rows, SPREAD), 1) // ADAPTER_RANK
    return tenants == columns


def select_block(wide_rows, mask):
    kept = jnp.where(mask, wide_rows, 0.0)
    pair = 2 * ADAPTER_RANK
    total = kept[:, :pair]
    for start in range(pair, SPREAD, pair):
        total = total + kept[:, start : start + pair]
    return total[:, :ADAPTER_RANK] + total[:, ADAPTER_RANK:]


def spread_rows(low_rows, mask):
    pair = jnp.concatenate([low_rows, low_rows], axis=1)
    wide = jnp.concatenate([pair] * (TENANT_COUNT // 2), axis=1)
    return jnp.where(mask, wide, 0.0).astype(jnp.bfloat16)


VMEM = pl.BlockSpec(memory_space=pltpu.VMEM)
ANY = pl.BlockSpec(memory_space=pl.ANY)
CUTS = 4
COPIES = 8
SLOTS = 6
STORE_GRANT = 10 << 20


def store_call(
    kernel, store, fetches, operands, out_shapes, flops, name, after=(), kept=None, scratch_shapes=()
):
    new = isinstance(store, jax.ShapeDtypeStruct)
    depth = store.shape[0] // SLOTS
    part = depth // COPIES
    sources = []
    for array, _, _ in fetches:
        if not any(array is known for known in sources):
            sources.append(array)
    places = [next(i for i, known in enumerate(sources) if known is f[0]) for f in fetches]
    n_in, n_out, n_hbm = len(operands), len(out_shapes), len(sources)

    first_kept = isinstance(kept, jax.ShapeDtypeStruct)
    kept_in = [] if kept is None or first_kept else [kept]
    kept_out = [] if kept is None else [pltpu.HBM(kept.shape, kept.dtype)]

    def body(*refs):
        if not new:
            refs = refs[1:]
        ins, hbm = refs[:n_in], refs[n_in : n_in + n_hbm]
        rest = refs[n_in + n_hbm + len(after) + len(kept_in) :]
        n_results = n_out + len(kept_out)
        store_ref, outs, scratch = rest[0], rest[1 : 1 + n_results], rest[1 + n_results :]
        copies = []
        for n, (place, (_, piece, slot)) in enumerate(zip(places, fetches)):
            for k in range(COPIES):
                copies.append(
                    pltpu.make_async_copy(
                        hbm[place].at[pl.ds(piece * depth + k * part, part)],
                        store_ref.at[pl.ds(slot * depth + k * part, part)],
                        scratch[0].at[n * COPIES + k],
                    )
                )
        for copy in copies:
            copy.start()
        own_scratch = scratch[1:] if fetches else scratch
        kernel(
            lambda slot: store_ref[slot * depth : (slot + 1) * depth, :], *ins, *outs, *own_scratch
        )
        for copy in copies:
            copy.wait()

    moved = 2 * depth * store.shape[1] * len(fetches)
    n_before = (not new) + n_in + n_hbm + len(after)
    aliases = {} if new else {0: 0}
    if kept_in:
        aliases[n_before] = 1 + n_out
    semaphores = [pltpu.SemaphoreType.DMA((COPIES * len(fetches),))] if fetches else []
    return pl.pallas_call(
        body,
        in_specs=[VMEM] * (n_in + (not new)) + [ANY] * (n_hbm + len(after) + len(kept_in)),
        out_specs=[VMEM] * (1 + n_out) + [ANY] * len(kept_out),
        out_shape=[pltpu.VMEM(store.shape, store.dtype), *out_shapes, *kept_out],
        input_output_aliases=aliases,
        scratch_shapes=[*semaphores, *scratch_shapes],
        compiler_params=pltpu.CompilerParams(vmem_limit_bytes=STORE_GRANT),
        cost_estimate=pl.CostEstimate(flops=flops, bytes_accessed=moved, transcendentals=0),
        name=name,
    )(
        *([] if new else [store]),
        *operands,
        *[pltpu.with_memory_space_constraint(array, pltpu.HBM) for array in sources],
        *after,
        *kept_in,
    )


def stacked(blocks, after=()):
    rows = sum(block.shape[0] for block in blocks)

    def stack_kernel(*refs):
        refs[-1][...] = jnp.concatenate([ref[...] for ref in refs[: len(blocks)]], axis=0)

    return pl.pallas_call(
        stack_kernel,
        in_specs=[VMEM] * len(blocks) + [ANY] * len(after),
        out_shape=jax.ShapeDtypeStruct((rows, blocks[0].shape[1]), blocks[0].dtype),
        compiler_params=pltpu.CompilerParams(vmem_limit_bytes=4 << 20),
        name="stacked",
    )(*blocks, *after)


def block_owner(own, block, count):
    bits = count.bit_length() - 1
    hops = [1 << (bits - 2), 1 << (bits - 1)] + [1 << bit for bit in reversed(range(bits - 2))]
    for n, hop in enumerate(hops):
        own = own ^ (((block >> n) & 1) * hop)
    return own


def source_of(own, row, rows, count):
    tokens = rows // count
    return block_owner(own, row // tokens, count) * tokens + row % tokens


def pick_held(own, rows, count):
    held = source_of(own, lax.broadcasted_iota(jnp.int32, (rows, rows), 0), rows, count)
    return held == lax.broadcasted_iota(jnp.int32, (rows, rows), 1)


def pick_given(own, rows, count):
    held = source_of(own, lax.broadcasted_iota(jnp.int32, (rows, rows), 1), rows, count)
    return held == lax.broadcasted_iota(jnp.int32, (rows, rows), 0)


def picked(pick, block):
    if block.dtype == jnp.bfloat16:
        return jnp.dot(pick.astype(jnp.bfloat16), block, preferred_element_type=jnp.float32)
    return jnp.dot(pick.astype(jnp.float32), block, precision=lax.Precision.HIGHEST)


def held_mask(pick, tenants_row):
    tenants = jnp.sum(jnp.where(pick, tenants_row, 0).astype(jnp.float32), axis=1, keepdims=True)
    return tenant_mask(tenants.astype(jnp.int32), pick.shape[0])


def low_kernel(count, aligned, down_ref, tenants_ref, *refs):
    x, (span_out, low_ref) = refs[:-2], refs[-2:]
    own = lax.axis_index("tp")
    if aligned:
        width = down_ref.shape[0]
        at = pl.ds(pl.multiple_of(own * width, width), width)
        span = jnp.concatenate([ref[:, at] for ref in x], axis=0)
    else:
        span = jnp.concatenate([ref[...] for ref in x], axis=0)
    span_out[...] = span
    rows = span.shape[0]
    wide = jnp.dot(span, down_ref[...], preferred_element_type=jnp.float32)
    low = select_block(wide, held_mask(pick_held(own, rows, count), tenants_ref[...]))
    low_ref[...] = picked(pick_given(own, rows, count), low)


def low_part(down, tenants, x, count):
    rows, span = sum(block.shape[0] for block in x), down.shape[0]
    aligned = span % 128 == 0
    if not aligned:
        x = [
            lax.dynamic_slice(
                block,
                (0, lax.axis_index("tp") * span),
                (block.shape[0], span),
                allow_negative_indices=False,
            )
            for block in x
        ]
    return pl.pallas_call(
        lambda *refs: low_kernel(count, aligned, *refs),
        out_shape=[
            jax.ShapeDtypeStruct((rows, span), x[0].dtype),
            jax.ShapeDtypeStruct((rows, ADAPTER_RANK), jnp.float32),
        ],
        compiler_params=pltpu.CompilerParams(vmem_limit_bytes=4 << 20),
        cost_estimate=pl.CostEstimate(
            flops=2 * rows * down.size, bytes_accessed=2 * down.size, transcendentals=0
        ),
        name="low_part",
    )(down, tenants, *x)


def forward_kernel(cuts, slots, blocks, first, slot, *refs):
    x = refs[:blocks]
    gate_out, up_out = refs[-2:]
    gate, up = (0.0, 0.0) if first else (refs[blocks][...], refs[blocks + 1][...])
    for cut in cuts:
        gate_weight, up_weight = slot(slots[cut][0]), slot(slots[cut][1])
        depth = gate_weight.shape[0]
        at = slice(cut * depth, (cut + 1) * depth)
        rows = jnp.concatenate([ref[:, at] for ref in x], axis=0)
        gate = gate + jnp.dot(rows, gate_weight, preferred_element_type=jnp.float32)
        up = up + jnp.dot(rows, up_weight, preferred_element_type=jnp.float32)
    gate_out[...] = gate
    up_out[...] = up


def forward(cuts, slots, x, store, sums, fetches, after):
    rows = sum(block.shape[0] for block in x)
    depth, hidden = store.shape[0] // SLOTS, store.shape[1]
    result = jax.ShapeDtypeStruct((rows, hidden), jnp.float32)
    store, gate, up = store_call(
        lambda *refs: forward_kernel(cuts, slots, len(x), not sums, *refs),
        store,
        fetches,
        [*x, *sums],
        [result, result],
        4 * rows * depth * hidden * len(cuts),
        "forward",
        after=after,
    )
    return store, [gate, up]


def activation_kernel(
    count, maps_slot, slot, gate_ref, up_ref, hidden_ref, low_ref, tenants_ref,
    dgate_ref, dup_ref, part_ref, spread_ref,
):
    rows = gate_ref.shape[0]
    maps = slot(maps_slot)
    own = lax.axis_index("tp")
    pick = pick_held(own, rows, count)
    mask = held_mask(pick, tenants_ref[...])
    spread = spread_rows(picked(pick, low_ref[...]), mask)
    spread_ref[...] = spread
    gate = gate_ref[...] + adapter_scale * jnp.dot(
        spread, maps, preferred_element_type=jnp.float32
    )
    s = jax.nn.sigmoid(gate)
    hidden = picked(pick, hidden_ref[...])
    dgate = (hidden * up_ref[...] * s * (1.0 + gate * (1.0 - s))).astype(jnp.bfloat16)
    dgate_ref[...] = dgate
    dup_ref[...] = (hidden * gate * s).astype(jnp.bfloat16)
    part = select_block(contracted_columns(dgate, maps), mask)
    part_ref[...] = picked(pick_given(own, rows, count), part)


def activation(maps_slot, store, sums, hidden, low, tenants, count, fetches):
    rows, width = sums[0].shape
    value = jax.ShapeDtypeStruct((rows, width), jnp.bfloat16)
    return store_call(
        lambda *refs: activation_kernel(count, maps_slot, *refs),
        store,
        fetches,
        [*sums, hidden, low, tenants],
        [
            value,
            value,
            jax.ShapeDtypeStruct((rows, ADAPTER_RANK), jnp.float32),
            jax.ShapeDtypeStruct((rows, SPREAD), jnp.bfloat16),
        ],
        4 * rows * SPREAD * width,
        "activation",
    )


def adapter_kernel(
    count, low_ref, tenants_ref, down_ref, after_ref, own_out, other_out, spread_ref
):
    del after_ref
    half = own_out.shape[0]
    pick = pick_held(lax.axis_index("tp"), 2 * half, count)
    spread = spread_rows(picked(pick, low_ref[...]), held_mask(pick, tenants_ref[...]))
    spread_ref[...] = spread
    part = (adapter_scale * contracted_columns(spread, down_ref[...])).astype(jnp.bfloat16)
    own_out[...] = part[:half]
    other_out[...] = part[half:]


def adapter_part(low, tenants, down, count, after):
    rows, span = low.shape[0], down.shape[0]
    half = jax.ShapeDtypeStruct((rows // 2, span), jnp.bfloat16)
    return pl.pallas_call(
        lambda *refs: adapter_kernel(count, *refs),
        in_specs=[VMEM] * 3 + [ANY],
        out_shape=[half, half, jax.ShapeDtypeStruct((rows, SPREAD), jnp.bfloat16)],
        compiler_params=pltpu.CompilerParams(vmem_limit_bytes=4 << 20),
        cost_estimate=pl.CostEstimate(
            flops=2 * rows * down.size, bytes_accessed=2 * down.size, transcendentals=0
        ),
        name="adapter_part",
    )(low, tenants, down, after)


def backward_kernel(
    cut, slots, slot, dgate_ref, dup_ref, spread_ref, own_out, other_out, maps_out, maps, sem
):
    half = own_out.shape[0]
    height = maps.shape[0]
    at = slice(cut * height, (cut + 1) * height)
    maps[...] = contracted_rows(
        spread_ref[:, at] * jnp.bfloat16(adapter_scale), dgate_ref[...]
    ).astype(jnp.bfloat16)
    copy = pltpu.make_async_copy(maps, maps_out.at[pl.ds(cut * height, height)], sem)
    copy.start()
    part = contracted_columns(dgate_ref[...], slot(slots[0]))
    part = part + contracted_columns(dup_ref[...], slot(slots[1]))
    own_out[...] = part[:half]
    other_out[...] = part[half:].astype(jnp.bfloat16)
    copy.wait()


def backward(cut, slots, dgate, dup, spread, maps, store, fetches, after):
    rows, hidden = dgate.shape
    depth = store.shape[0] // SLOTS
    return store_call(
        lambda *refs: backward_kernel(cut, slots, *refs),
        store,
        fetches,
        [dgate, dup, spread],
        [
            jax.ShapeDtypeStruct((rows // 2, depth), jnp.float32),
            jax.ShapeDtypeStruct((rows // 2, depth), jnp.bfloat16),
        ],
        4 * rows * hidden * depth,
        "backward",
        after=after,
        kept=maps,
        scratch_shapes=[
            pltpu.VMEM((SPREAD // CUTS, hidden), jnp.bfloat16),
            pltpu.SemaphoreType.DMA,
        ],
    )


PARTS = 8
DIRECT_CHIPS = 8


def merge_kernel(count, *refs):
    device = lax.axis_index("tp")
    own, came = refs[:CUTS], refs[CUTS : 2 * CUTS]
    adapter_own, adapter_came, *outs, sums, tiles = refs[2 * CUTS :]
    tile, lanes = outs[0].shape[-2:]
    chips = tiles.shape[1] // tile
    tokens = tile // PARTS
    per_part = lanes // 128
    blocks = PARTS * per_part
    for cut in range(CUTS):
        value = own[cut][...] + came[cut][...].astype(jnp.float32)
        for k in range(blocks // CUTS):
            sums[cut * blocks // CUTS + k] = value[:, k * 128 : (k + 1) * 128]
    mine = adapter_own[...].astype(jnp.float32)
    other = adapter_came[...].astype(jnp.float32)
    pair = jnp.where(
        device % 2 == 0,
        jnp.concatenate([mine, other], axis=1),
        jnp.concatenate([other, mine], axis=1),
    )
    of_chip = blocks // chips
    for k in range(of_chip):
        sums[device // 2 * of_chip + k] += pair[:, k * 128 : (k + 1) * 128]
    for token in range(tokens):
        of_token = pl.ds(token, chips, stride=tokens)
        for part in range(PARTS):
            to = pl.ds(token * PARTS + part, chips, stride=tile)
            for k in range(per_part):
                tiles[k, to, :] = sums[part * per_part + k, of_token, :]
    for position in range(chips):
        if len(outs) == chips:
            out_ref = outs[position]
        else:
            out_ref = outs[0].at[block_owner(device, position, count) // 2]
        for k in range(per_part):
            out_ref[:, k * 128 : (k + 1) * 128] = tiles[
                k, position * tile : (position + 1) * tile, :
            ].astype(jnp.bfloat16)


def merge(own, came, adapter_own, adapter_came, own_rows):
    half, depth = own[0].shape
    lanes = CUTS * depth // PARTS
    chips, tile = half // own_rows, own_rows * PARTS
    if chips <= DIRECT_CHIPS:
        out_shape = [jax.ShapeDtypeStruct((tile, lanes), jnp.bfloat16)] * chips
    else:
        out_shape = [jax.ShapeDtypeStruct((chips, tile, lanes), jnp.bfloat16)]
    return pl.pallas_call(
        lambda *refs: merge_kernel(2 * chips, *refs),
        out_shape=out_shape,
        scratch_shapes=[
            pltpu.VMEM((CUTS * depth // 128, half, 128), jnp.float32),
            pltpu.VMEM((lanes // 128, chips * tile, 128), jnp.float32),
        ],
        compiler_params=pltpu.CompilerParams(vmem_limit_bytes=40 << 20),
        name="merge",
    )(*own, *came, adapter_own, adapter_came)


def final_kernel(*refs):
    came, (out_ref, total) = refs[:-2], refs[-2:]
    if len(came) == 1:
        came = [came[0].at[chip] for chip in range(came[0].shape[0])]
    tile, lanes = came[0].shape
    tokens = tile // PARTS
    blocks = lanes // 128
    for k in range(blocks):
        at = slice(k * 128, (k + 1) * 128)
        value = came[0][:, at].astype(jnp.float32)
        for ref in came[1:]:
            value = value + ref[:, at].astype(jnp.float32)
        total[k] = value
    for part in range(PARTS):
        for k in range(blocks):
            at = (part * blocks + k) * 128
            out_ref[:, at : at + 128] = total[k, pl.ds(part, tokens, stride=PARTS), :].astype(
                jnp.bfloat16
            )


def final(came):
    tile, lanes = came[0].shape[-2:]
    return pl.pallas_call(
        final_kernel,
        out_shape=jax.ShapeDtypeStruct((tile // PARTS, lanes * PARTS), jnp.bfloat16),
        scratch_shapes=[pltpu.VMEM((lanes // 128, tile, 128), jnp.float32)],
        compiler_params=pltpu.CompilerParams(vmem_limit_bytes=40 << 20),
        name="final",
    )(*came)


def outer_kernel(left_ref, right_ref, out_ref):
    out_ref[...] = contracted_rows(
        left_ref[...] * jnp.bfloat16(adapter_scale), right_ref[...]
    ).astype(jnp.bfloat16)


def outer(left, right, name):
    rows, height = left.shape
    width = right.shape[1]
    block = block_of(height, 512)
    if block % 128:
        block = height
    return pl.pallas_call(
        outer_kernel,
        grid=(height // block,),
        in_specs=[
            pl.BlockSpec((rows, block), lambda k: (0, k)),
            pl.BlockSpec((rows, width), lambda k: (0, 0)),
        ],
        out_specs=pl.BlockSpec((block, width), lambda k: (k, 0)),
        out_shape=jax.ShapeDtypeStruct((height, width), jnp.bfloat16),
        compiler_params=pltpu.CompilerParams(vmem_limit_bytes=24 << 20),
        cost_estimate=pl.CostEstimate(
            flops=2 * rows * height * width, bytes_accessed=2 * height * width, transcendentals=0
        ),
        name=name,
    )(left, right)


def same_core_groups():
    count = lax.axis_size("tp")
    return [list(range(core, count, 2)) for core in range(2)]


def between_same_cores(blocks):
    return lax.all_to_all(
        blocks, "tp", split_axis=0, concat_axis=0, tiled=True, axis_index_groups=same_core_groups()
    )


def add_kernel(left_ref, right_ref, out_ref):
    out_ref[...] = left_ref[...] + right_ref[...]


def plus(left, right):
    return pl.pallas_call(
        add_kernel,
        out_shape=jax.ShapeDtypeStruct(left.shape, left.dtype),
        compiler_params=pltpu.CompilerParams(vmem_limit_bytes=2 << 20),
        name="plus",
    )(left, right)


def swapped(block, hop):
    return lax.ppermute(block, "tp", [(i, i ^ hop) for i in range(lax.axis_size("tp"))])


def local(
    normed_layer_input,
    hidden_unit_gradient,
    gate_weight,
    up_weight,
    adapter_down_maps,
    adapter_up_maps,
    token_tenant_index,
):
    count = lax.axis_size("tp")
    own_rows, width = normed_layer_input.shape
    rows = own_rows * count
    hops = [1 << bit for bit in range(count.bit_length() - 1)]
    tenants = token_tenant_index.reshape(1, rows)

    def pair(cut, first, second):
        return [(gate_weight, cut, first), (up_weight, cut, second)]

    def mark(slot, token_ref):
        token_ref[...] = jnp.zeros_like(token_ref)

    mark_shape = jax.ShapeDtypeStruct((8, 128), jnp.float32)
    store = jax.ShapeDtypeStruct(
        (SLOTS * width // CUTS, gate_weight.shape[1]), gate_weight.dtype
    )
    far, near = hops[-1], hops[-2]
    came = [swapped(normed_layer_input, hop) for hop in (near, far, near | far)]
    store, token = store_call(mark, store, pair(0, 0, 1), [], [mark_shape], 0, "fetch")
    block = stacked([normed_layer_input, *came], [token])
    for hop in reversed(hops[2:-2]):
        block = stacked([block, swapped(block, hop)])
    other = swapped(block, hops[1])
    store, token = store_call(
        mark, store, [(gate_weight, 1, 2)], [], [mark_shape], 0, "fetch", after=[block]
    )
    block = stacked([block, other], [token])
    x = [block, swapped(block, 1)]
    store, token = store_call(
        mark, store, [(up_weight, 1, 3)], [], [mark_shape], 0, "fetch", after=[block]
    )

    input_span, low = low_part(adapter_down_maps, tenants, x, count)
    sums = []
    slots = {0: (0, 1), 1: (2, 3), 2: (4, 5), 3: (0, 1)}
    step = 0
    for cuts, fetches in (
        ((0, 1), pair(2, 4, 5)), ((2,), pair(3, 0, 1)), ((3,), [(adapter_up_maps, 0, 2)])
    ):
        after = [low]
        if step < len(hops):
            low = plus(low, swapped(low, hops[step]))
            step += 1
        store, sums = forward(cuts, slots, x, store, sums, fetches, after)
    for hop in hops[step:]:
        low = plus(low, swapped(low, hop))
    store, dgate, dup, low_grad, input_spread = activation(
        2, store, sums, hidden_unit_gradient, low, tenants, count, []
    )

    later_hops = hops[1:] + hops[:1]
    parts, arrived = {}, {}
    up_map_gradient = jax.ShapeDtypeStruct(adapter_up_maps.shape, jnp.bfloat16)
    slots = {3: (0, 1), 2: (4, 5), 1: (2, 3), 0: (0, 1)}
    fetches = {
        3: [(gate_weight, 1, 2)], 2: [(gate_weight, 0, 0)], 1: [(up_weight, 0, 1)], 0: []
    }
    for cut in reversed(range(CUTS)):
        after = [low_grad]
        turns = later_hops[:1] if cut > 0 else later_hops
        later_hops = later_hops[len(turns) :]
        for hop in turns:
            low_grad = plus(low_grad, swapped(low_grad, hop))
        store, own_part, other_part, up_map_gradient = backward(
            cut, slots[cut], dgate, dup, input_spread, up_map_gradient, store, fetches[cut], after
        )
        parts[cut] = own_part
        arrived[cut] = swapped(other_part, 1)
    adapter_own, adapter_other, grad_spread = adapter_part(
        low_grad, tenants, adapter_down_maps, count, other_part
    )
    adapter_came = swapped(adapter_other, 1)
    merged = merge(
        [parts[cut] for cut in range(CUTS)],
        [arrived[cut] for cut in range(CUTS)],
        adapter_own,
        adapter_came,
        own_rows,
    )
    if count // 2 <= DIRECT_CHIPS:
        hop_of = [block_owner(0, position, count) for position in range(count // 2)]
        farthest = sorted(range(1, count // 2), key=lambda position: -hop_of[position])
        exchanged = [merged[0]] + [swapped(merged[n], hop_of[n]) for n in farthest]
    else:
        exchanged = [between_same_cores(merged[0])]
    down_map_gradient = outer(input_span, grad_spread, "down_maps")
    return (final(exchanged), down_map_gradient, up_map_gradient)


def solution(mesh):
    placed = (
        P(("groups", "tp"), None),
        P("groups", "tp"),
        P(None, "tp"),
        P(None, "tp"),
        P("tp", None),
        P(None, "tp"),
        P("groups"),
    )
    return jax.shard_map(
        local,
        mesh=mesh,
        in_specs=placed,
        out_specs=(P(("groups", "tp"), None), P("tp", "groups"), P("groups", "tp")),
        check_vma=False,
    )
```

```python
import jax
import jax.numpy as jnp
from jax import lax
from jax.experimental import pallas as pl
from jax.experimental.pallas import tpu as pltpu
from jax.sharding import PartitionSpec as P

ADAPTER_RANK = 64
TENANT_COUNT = 32
SPREAD = ADAPTER_RANK * TENANT_COUNT

adapter_scale = 2.0


def block_of(size, largest):
    block = largest
    while size % block:
        block //= 2
    return block


def contracted_rows(left, right):
    return lax.dot_general(
        left, right, (((0,), (0,)), ((), ())), preferred_element_type=jnp.float32
    )


def contracted_columns(left, right):
    return lax.dot_general(
        left, right, (((1,), (1,)), ((), ())), preferred_element_type=jnp.float32
    )


def tenant_mask(tenants, rows):
    columns = lax.broadcasted_iota(jnp.int32, (rows, SPREAD), 1) // ADAPTER_RANK
    return tenants == columns


def select_block(wide_rows, mask):
    kept = jnp.where(mask, wide_rows, 0.0)
    pair = 2 * ADAPTER_RANK
    total = kept[:, :pair]
    for start in range(pair, SPREAD, pair):
        total = total + kept[:, start : start + pair]
    return total[:, :ADAPTER_RANK] + total[:, ADAPTER_RANK:]


def spread_rows(low_rows, mask):
    pair = jnp.concatenate([low_rows, low_rows], axis=1)
    wide = jnp.concatenate([pair] * (TENANT_COUNT // 2), axis=1)
    return jnp.where(mask, wide, 0.0).astype(jnp.bfloat16)


VMEM = pl.BlockSpec(memory_space=pltpu.VMEM)
ANY = pl.BlockSpec(memory_space=pl.ANY)
CUTS = 4
COPIES = 8
SLOTS = 6
STORE_GRANT = 10 << 20


def store_call(kernel, store, fetches, operands, out_shapes, flops, name, after=()):
    new = isinstance(store, jax.ShapeDtypeStruct)
    depth = store.shape[0] // SLOTS
    part = depth // COPIES
    sources = []
    for array, _, _ in fetches:
        if not any(array is known for known in sources):
            sources.append(array)
    places = [next(i for i, known in enumerate(sources) if known is f[0]) for f in fetches]
    n_in, n_out, n_hbm = len(operands), len(out_shapes), len(sources)

    def body(*refs):
        if not new:
            refs = refs[1:]
        ins, hbm = refs[:n_in], refs[n_in : n_in + n_hbm]
        rest = refs[n_in + n_hbm + len(after) :]
        store_ref, outs, scratch = rest[0], rest[1 : 1 + n_out], rest[1 + n_out :]
        copies = []
        for n, (place, (_, piece, slot)) in enumerate(zip(places, fetches)):
            for k in range(COPIES):
                copies.append(
                    pltpu.make_async_copy(
                        hbm[place].at[pl.ds(piece * depth + k * part, part)],
                        store_ref.at[pl.ds(slot * depth + k * part, part)],
                        scratch[0].at[n * COPIES + k],
                    )
                )
        for copy in copies:
            copy.start()
        kernel(lambda slot: store_ref[slot * depth : (slot + 1) * depth, :], *ins, *outs)
        for copy in copies:
            copy.wait()

    moved = 2 * depth * store.shape[1] * len(fetches)
    return pl.pallas_call(
        body,
        in_specs=[VMEM] * (n_in + (not new)) + [ANY] * (n_hbm + len(after)),
        out_specs=[VMEM] * (1 + n_out),
        out_shape=[pltpu.VMEM(store.shape, store.dtype), *out_shapes],
        input_output_aliases={} if new else {0: 0},
        scratch_shapes=[pltpu.SemaphoreType.DMA((COPIES * len(fetches),))] if fetches else [],
        compiler_params=pltpu.CompilerParams(vmem_limit_bytes=STORE_GRANT),
        cost_estimate=pl.CostEstimate(flops=flops, bytes_accessed=moved, transcendentals=0),
        name=name,
    )(
        *([] if new else [store]),
        *operands,
        *[pltpu.with_memory_space_constraint(array, pltpu.HBM) for array in sources],
        *after,
    )


def stacked(blocks, after=()):
    rows = sum(block.shape[0] for block in blocks)

    def stack_kernel(*refs):
        refs[-1][...] = jnp.concatenate([ref[...] for ref in refs[: len(blocks)]], axis=0)

    return pl.pallas_call(
        stack_kernel,
        in_specs=[VMEM] * len(blocks) + [ANY] * len(after),
        out_shape=jax.ShapeDtypeStruct((rows, blocks[0].shape[1]), blocks[0].dtype),
        compiler_params=pltpu.CompilerParams(vmem_limit_bytes=4 << 20),
        name="stacked",
    )(*blocks, *after)


def block_owner(own, block, count):
    bits = count.bit_length() - 1
    hops = [1 << (bits - 2), 1 << (bits - 1)] + [1 << bit for bit in reversed(range(bits - 2))]
    for n, hop in enumerate(hops):
        own = own ^ (((block >> n) & 1) * hop)
    return own


def source_of(own, row, rows, count):
    tokens = rows // count
    return block_owner(own, row // tokens, count) * tokens + row % tokens


def pick_held(own, rows, count):
    held = source_of(own, lax.broadcasted_iota(jnp.int32, (rows, rows), 0), rows, count)
    return held == lax.broadcasted_iota(jnp.int32, (rows, rows), 1)


def pick_given(own, rows, count):
    held = source_of(own, lax.broadcasted_iota(jnp.int32, (rows, rows), 1), rows, count)
    return held == lax.broadcasted_iota(jnp.int32, (rows, rows), 0)


def picked(pick, block):
    if block.dtype == jnp.bfloat16:
        return jnp.dot(pick.astype(jnp.bfloat16), block, preferred_element_type=jnp.float32)
    return jnp.dot(pick.astype(jnp.float32), block, precision=lax.Precision.HIGHEST)


def held_mask(pick, tenants_row):
    tenants = jnp.sum(jnp.where(pick, tenants_row, 0).astype(jnp.float32), axis=1, keepdims=True)
    return tenant_mask(tenants.astype(jnp.int32), pick.shape[0])


def low_kernel(count, aligned, down_ref, tenants_ref, *refs):
    x, (span_out, low_ref) = refs[:-2], refs[-2:]
    own = lax.axis_index("tp")
    if aligned:
        width = down_ref.shape[0]
        at = pl.ds(pl.multiple_of(own * width, width), width)
        span = jnp.concatenate([ref[:, at] for ref in x], axis=0)
    else:
        span = jnp.concatenate([ref[...] for ref in x], axis=0)
    span_out[...] = span
    rows = span.shape[0]
    wide = jnp.dot(span, down_ref[...], preferred_element_type=jnp.float32)
    low = select_block(wide, held_mask(pick_held(own, rows, count), tenants_ref[...]))
    low_ref[...] = picked(pick_given(own, rows, count), low)


def low_part(down, tenants, x, count):
    rows, span = sum(block.shape[0] for block in x), down.shape[0]
    aligned = span % 128 == 0
    if not aligned:
        x = [
            lax.dynamic_slice(
                block,
                (0, lax.axis_index("tp") * span),
                (block.shape[0], span),
                allow_negative_indices=False,
            )
            for block in x
        ]
    return pl.pallas_call(
        lambda *refs: low_kernel(count, aligned, *refs),
        out_shape=[
            jax.ShapeDtypeStruct((rows, span), x[0].dtype),
            jax.ShapeDtypeStruct((rows, ADAPTER_RANK), jnp.float32),
        ],
        compiler_params=pltpu.CompilerParams(vmem_limit_bytes=4 << 20),
        cost_estimate=pl.CostEstimate(
            flops=2 * rows * down.size, bytes_accessed=2 * down.size, transcendentals=0
        ),
        name="low_part",
    )(down, tenants, *x)


def forward_kernel(cuts, slots, blocks, first, slot, *refs):
    x = refs[:blocks]
    gate_out, up_out = refs[-2:]
    gate, up = (0.0, 0.0) if first else (refs[blocks][...], refs[blocks + 1][...])
    for cut in cuts:
        gate_weight, up_weight = slot(slots[cut][0]), slot(slots[cut][1])
        depth = gate_weight.shape[0]
        at = slice(cut * depth, (cut + 1) * depth)
        rows = jnp.concatenate([ref[:, at] for ref in x], axis=0)
        gate = gate + jnp.dot(rows, gate_weight, preferred_element_type=jnp.float32)
        up = up + jnp.dot(rows, up_weight, preferred_element_type=jnp.float32)
    gate_out[...] = gate
    up_out[...] = up


def forward(cuts, slots, x, store, sums, fetches, after):
    rows = sum(block.shape[0] for block in x)
    depth, hidden = store.shape[0] // SLOTS, store.shape[1]
    result = jax.ShapeDtypeStruct((rows, hidden), jnp.float32)
    store, gate, up = store_call(
        lambda *refs: forward_kernel(cuts, slots, len(x), not sums, *refs),
        store,
        fetches,
        [*x, *sums],
        [result, result],
        4 * rows * depth * hidden * len(cuts),
        "forward",
        after=after,
    )
    return store, [gate, up]


def activation_kernel(
    count, maps_slot, slot, gate_ref, up_ref, hidden_ref, low_ref, tenants_ref,
    dgate_ref, dup_ref, part_ref, spread_ref,
):
    rows = gate_ref.shape[0]
    maps = slot(maps_slot)
    own = lax.axis_index("tp")
    pick = pick_held(own, rows, count)
    mask = held_mask(pick, tenants_ref[...])
    spread = spread_rows(picked(pick, low_ref[...]), mask)
    spread_ref[...] = spread
    gate = gate_ref[...] + adapter_scale * jnp.dot(
        spread, maps, preferred_element_type=jnp.float32
    )
    s = jax.nn.sigmoid(gate)
    hidden = picked(pick, hidden_ref[...])
    dgate = (hidden * up_ref[...] * s * (1.0 + gate * (1.0 - s))).astype(jnp.bfloat16)
    dgate_ref[...] = dgate
    dup_ref[...] = (hidden * gate * s).astype(jnp.bfloat16)
    part = select_block(contracted_columns(dgate, maps), mask)
    part_ref[...] = picked(pick_given(own, rows, count), part)


def activation(maps_slot, store, sums, hidden, low, tenants, count, fetches):
    rows, width = sums[0].shape
    value = jax.ShapeDtypeStruct((rows, width), jnp.bfloat16)
    return store_call(
        lambda *refs: activation_kernel(count, maps_slot, *refs),
        store,
        fetches,
        [*sums, hidden, low, tenants],
        [
            value,
            value,
            jax.ShapeDtypeStruct((rows, ADAPTER_RANK), jnp.float32),
            jax.ShapeDtypeStruct((rows, SPREAD), jnp.bfloat16),
        ],
        4 * rows * SPREAD * width,
        "activation",
    )


def adapter_kernel(count, low_ref, tenants_ref, down_ref, own_out, other_out, spread_ref):
    half = own_out.shape[0]
    pick = pick_held(lax.axis_index("tp"), 2 * half, count)
    spread = spread_rows(picked(pick, low_ref[...]), held_mask(pick, tenants_ref[...]))
    spread_ref[...] = spread
    part = (adapter_scale * contracted_columns(spread, down_ref[...])).astype(jnp.bfloat16)
    own_out[...] = part[:half]
    other_out[...] = part[half:]


def adapter_part(low, tenants, down, count):
    rows, span = low.shape[0], down.shape[0]
    half = jax.ShapeDtypeStruct((rows // 2, span), jnp.bfloat16)
    return pl.pallas_call(
        lambda *refs: adapter_kernel(count, *refs),
        out_shape=[half, half, jax.ShapeDtypeStruct((rows, SPREAD), jnp.bfloat16)],
        compiler_params=pltpu.CompilerParams(vmem_limit_bytes=4 << 20),
        cost_estimate=pl.CostEstimate(
            flops=2 * rows * down.size, bytes_accessed=2 * down.size, transcendentals=0
        ),
        name="adapter_part",
    )(low, tenants, down)


def backward_kernel(slots, start, height, slot, dgate_ref, dup_ref, own_out, other_out):
    half = own_out.shape[0]
    at = slice(start, start + height)
    part = contracted_columns(dgate_ref[...], slot(slots[0])[at, :])
    part = part + contracted_columns(dup_ref[...], slot(slots[1])[at, :])
    own_out[...] = part[:half]
    other_out[...] = part[half:].astype(jnp.bfloat16)


def backward(slots, start, height, dgate, dup, store, fetches, after):
    rows, hidden = dgate.shape
    return store_call(
        lambda *refs: backward_kernel(slots, start, height, *refs),
        store,
        fetches,
        [dgate, dup],
        [
            jax.ShapeDtypeStruct((rows // 2, height), jnp.float32),
            jax.ShapeDtypeStruct((rows // 2, height), jnp.bfloat16),
        ],
        4 * rows * hidden * height,
        "backward",
        after=after,
    )


def first_halves_kernel(count, adapter_own, adapter_came, *refs):
    keep_ref, send_ref, sums = refs[-3:]
    pieces = refs[:-3]
    half = keep_ref.shape[0]
    device = lax.axis_index("tp")
    at = 0
    for own, came in zip(pieces[::2], pieces[1::2]):
        width = own.shape[1]
        sums[:, at : at + width] = own[...] + came[...].astype(jnp.float32)
        at += width
    mine = adapter_own[...].astype(jnp.float32)
    other = adapter_came[...].astype(jnp.float32)
    pair = jnp.where(
        device % 2 == 0,
        jnp.concatenate([mine, other], axis=1),
        jnp.concatenate([other, mine], axis=1),
    )
    width = pair.shape[1]
    sums[:, pl.ds(pl.multiple_of(device // 2 * width, width), width)] += pair
    keep_ref[...] = sums[:half, :]
    send_ref[...] = sums[half:, :].astype(jnp.bfloat16)


def first_halves(pieces, adapter_own, adapter_came, count):
    rows = adapter_own.shape[0]
    width = sum(own.shape[1] for own, _ in pieces)
    return pl.pallas_call(
        lambda *refs: first_halves_kernel(count, *refs),
        out_shape=[
            jax.ShapeDtypeStruct((rows // 2, width), jnp.float32),
            jax.ShapeDtypeStruct((rows // 2, width), jnp.bfloat16),
        ],
        scratch_shapes=[pltpu.VMEM((rows, width), jnp.float32)],
        compiler_params=pltpu.CompilerParams(vmem_limit_bytes=40 << 20),
        name="first_halves",
    )(adapter_own, adapter_came, *[array for pair in pieces for array in pair])


def halves(keep, came, after):
    rows, width = keep.shape

    def halves_kernel(keep_ref, came_ref, after_ref, keep_out, send_out):
        del after_ref
        total = keep_ref[...] + came_ref[...].astype(jnp.float32)
        keep_out[...] = total[: rows // 2]
        send_out[...] = total[rows // 2 :].astype(jnp.bfloat16)

    return pl.pallas_call(
        halves_kernel,
        in_specs=[VMEM, VMEM, ANY],
        out_shape=[
            jax.ShapeDtypeStruct((rows // 2, width), jnp.float32),
            jax.ShapeDtypeStruct((rows // 2, width), jnp.bfloat16),
        ],
        compiler_params=pltpu.CompilerParams(vmem_limit_bytes=40 << 20),
        name="halves",
    )(keep, came, after)


def final(keep, came, after):
    def final_kernel(keep_ref, came_ref, after_ref, out_ref):
        del after_ref
        out_ref[...] = (keep_ref[...] + came_ref[...].astype(jnp.float32)).astype(jnp.bfloat16)

    return pl.pallas_call(
        final_kernel,
        in_specs=[VMEM, VMEM, ANY],
        out_shape=jax.ShapeDtypeStruct(keep.shape, jnp.bfloat16),
        compiler_params=pltpu.CompilerParams(vmem_limit_bytes=40 << 20),
        name="final",
    )(keep, came, after)


def outer_kernel(left_ref, right_ref, *refs):
    out_ref, token_ref = refs[-2:]
    out_ref[...] = contracted_rows(
        left_ref[...] * jnp.bfloat16(adapter_scale), right_ref[...]
    ).astype(jnp.bfloat16)
    token_ref[...] = jnp.zeros_like(token_ref)


def outer(left, right, name, after, parts=1, part=0, earlier=None):
    rows, height = left.shape
    width = right.shape[1]
    block = block_of(height // parts, 512)
    if block % 128:
        block = height // parts
    steps = height // parts // block
    first = part * steps
    kept = [] if earlier is None else [earlier]
    return pl.pallas_call(
        outer_kernel,
        grid=(steps,),
        in_specs=[
            pl.BlockSpec((rows, block), lambda k: (0, k + first)),
            pl.BlockSpec((rows, width), lambda k: (0, 0)),
            ANY,
        ]
        + [ANY] * len(kept),
        out_specs=[
            pl.BlockSpec((block, width), lambda k: (k + first, 0)),
            pl.BlockSpec((8, 128), lambda k: (0, 0)),
        ],
        out_shape=[
            jax.ShapeDtypeStruct((height, width), jnp.bfloat16),
            jax.ShapeDtypeStruct((8, 128), jnp.float32),
        ],
        input_output_aliases={3: 0} if kept else {},
        compiler_params=pltpu.CompilerParams(vmem_limit_bytes=24 << 20),
        cost_estimate=pl.CostEstimate(
            flops=2 * rows * (height // parts) * width,
            bytes_accessed=2 * (height // parts) * width,
            transcendentals=0,
        ),
        name=name,
    )(left, right, after, *kept)


def add_kernel(left_ref, right_ref, out_ref):
    out_ref[...] = left_ref[...] + right_ref[...]


def plus(left, right):
    return pl.pallas_call(
        add_kernel,
        out_shape=jax.ShapeDtypeStruct(left.shape, left.dtype),
        compiler_params=pltpu.CompilerParams(vmem_limit_bytes=2 << 20),
        name="plus",
    )(left, right)


def swapped(block, hop):
    return lax.ppermute(block, "tp", [(i, i ^ hop) for i in range(lax.axis_size("tp"))])


def local(
    normed_layer_input,
    hidden_unit_gradient,
    gate_weight,
    up_weight,
    adapter_down_maps,
    adapter_up_maps,
    token_tenant_index,
):
    count = lax.axis_size("tp")
    own_rows, width = normed_layer_input.shape
    rows = own_rows * count
    hops = [1 << bit for bit in range(count.bit_length() - 1)]
    tenants = token_tenant_index.reshape(1, rows)

    def pair(cut, first, second):
        return [(gate_weight, cut, first), (up_weight, cut, second)]

    def mark(slot, token_ref):
        token_ref[...] = jnp.zeros_like(token_ref)

    mark_shape = jax.ShapeDtypeStruct((8, 128), jnp.float32)
    store = jax.ShapeDtypeStruct(
        (SLOTS * width // CUTS, gate_weight.shape[1]), gate_weight.dtype
    )
    far, near = hops[-1], hops[-2]
    came = [swapped(normed_layer_input, hop) for hop in (near, far, near | far)]
    store, token = store_call(mark, store, pair(0, 0, 1), [], [mark_shape], 0, "fetch")
    block = stacked([normed_layer_input, *came], [token])
    for hop in reversed(hops[2:-2]):
        block = stacked([block, swapped(block, hop)])
    other = swapped(block, hops[1])
    store, token = store_call(
        mark, store, [(gate_weight, 1, 2)], [], [mark_shape], 0, "fetch", after=[block]
    )
    block = stacked([block, other], [token])
    x = [block, swapped(block, 1)]
    store, token = store_call(
        mark, store, [(up_weight, 1, 3)], [], [mark_shape], 0, "fetch", after=[block]
    )

    input_span, low = low_part(adapter_down_maps, tenants, x, count)
    sums = []
    slots = {0: (0, 1), 1: (2, 3), 2: (4, 5), 3: (0, 1)}
    step = 0
    for cuts, fetches in (
        ((0, 1), pair(2, 4, 5)), ((2,), pair(3, 0, 1)), ((3,), [(adapter_up_maps, 0, 2)])
    ):
        after = [low]
        if step < len(hops):
            low = plus(low, swapped(low, hops[step]))
            step += 1
        store, sums = forward(cuts, slots, x, store, sums, fetches, after)
    for hop in hops[step:]:
        low = plus(low, swapped(low, hop))
    store, dgate, dup, low_grad, input_spread = activation(
        2, store, sums, hidden_unit_gradient, low, tenants, count, []
    )

    later_hops = hops[1:] + hops[:1]
    depth = width // CUTS
    part_list = [
        (3, (0, 1), 0, depth, [(gate_weight, 1, 2)]),
        (2, (4, 5), 0, depth, [(gate_weight, 0, 0)]),
        (1, (2, 3), 0, depth, [(up_weight, 0, 1)]),
        (0, (0, 1), 0, depth // 2, []),
        (0, (0, 1), depth // 2, depth // 2, []),
    ]
    columns = {}
    for n, (piece, slots, first, height, fetches) in enumerate(part_list):
        after = [low_grad]
        if n == len(part_list) - 1:
            adapter_own, adapter_other, grad_spread = adapter_part(
                low_grad, tenants, adapter_down_maps, count
            )
            adapter_came = swapped(adapter_other, 1)
            after = [adapter_other]
        else:
            turns = later_hops[:1] if n < len(part_list) - 2 else later_hops
            later_hops = later_hops[len(turns) :]
            for hop in turns:
                low_grad = plus(low_grad, swapped(low_grad, hop))
        store, own_part, other_part = backward(
            slots, first, height, dgate, dup, store, fetches, after
        )
        columns[piece * depth + first] = (own_part, swapped(other_part, 1))

    keep, send = first_halves(
        [columns[start] for start in sorted(columns)], adapter_own, adapter_came, count
    )
    halvings = [block_owner(0, 1 << bit, count) for bit in reversed(range(len(hops) - 1))]
    up_map_gradient = None
    for n, hop in enumerate(halvings[:-1]):
        came = swapped(send, hop)
        beside = send
        if n < 2:
            up_map_gradient, beside = outer(
                input_spread, dgate, "up_maps", send, 2, n, up_map_gradient
            )
        keep, send = halves(keep, came, beside)
    came = swapped(send, halvings[-1])
    down_map_gradient, beside = outer(input_span, grad_spread, "down_maps", send)
    return (final(keep, came, beside), down_map_gradient, up_map_gradient)


def solution(mesh):
    placed = (
        P(("groups", "tp"), None),
        P("groups", "tp"),
        P(None, "tp"),
        P(None, "tp"),
        P("tp", None),
        P(None, "tp"),
        P("groups"),
    )
    return jax.shard_map(
        local,
        mesh=mesh,
        in_specs=placed,
        out_specs=(P(("groups", "tp"), None), P("tp", "groups"), P("groups", "tp")),
        check_vma=False,
    )
```

```python
import jax
import jax.numpy as jnp
from jax import lax
from jax.experimental import pallas as pl
from jax.experimental.pallas import tpu as pltpu
from jax.sharding import PartitionSpec as P

ADAPTER_RANK = 64
TENANT_COUNT = 32
SPREAD = ADAPTER_RANK * TENANT_COUNT

adapter_scale = 2.0


def block_of(size, largest):
    block = largest
    while size % block:
        block //= 2
    return block


def contracted_rows(left, right):
    return lax.dot_general(
        left, right, (((0,), (0,)), ((), ())), preferred_element_type=jnp.float32
    )


def contracted_columns(left, right):
    return lax.dot_general(
        left, right, (((1,), (1,)), ((), ())), preferred_element_type=jnp.float32
    )


def tenant_mask(tenants, rows):
    columns = lax.broadcasted_iota(jnp.int32, (rows, SPREAD), 1) // ADAPTER_RANK
    return tenants == columns


def select_block(wide_rows, mask):
    kept = jnp.where(mask, wide_rows, 0.0)
    pair = 2 * ADAPTER_RANK
    total = kept[:, :pair]
    for start in range(pair, SPREAD, pair):
        total = total + kept[:, start : start + pair]
    return total[:, :ADAPTER_RANK] + total[:, ADAPTER_RANK:]


def spread_rows(low_rows, mask):
    pair = jnp.concatenate([low_rows, low_rows], axis=1)
    wide = jnp.concatenate([pair] * (TENANT_COUNT // 2), axis=1)
    return jnp.where(mask, wide, 0.0).astype(jnp.bfloat16)


VMEM = pl.BlockSpec(memory_space=pltpu.VMEM)
ANY = pl.BlockSpec(memory_space=pl.ANY)
CUTS = 4
COPIES = 8
STRIP = 256
SLOTS = 6
STORE_GRANT = 10 << 20


def store_call(kernel, store, fetches, operands, out_shapes, flops, name, after=()):
    new = isinstance(store, jax.ShapeDtypeStruct)
    depth = store.shape[0] // SLOTS
    part = depth // COPIES
    sources = []
    for array, *_ in fetches:
        if not any(array is known for known in sources):
            sources.append(array)
    places = [next(i for i, known in enumerate(sources) if known is f[0]) for f in fetches]
    n_in, n_out, n_hbm = len(operands), len(out_shapes), len(sources)

    def body(*refs):
        if not new:
            refs = refs[1:]
        ins, hbm = refs[:n_in], refs[n_in : n_in + n_hbm]
        rest = refs[n_in + n_hbm + len(after) :]
        store_ref, outs, scratch = rest[0], rest[1 : 1 + n_out], rest[1 + n_out :]
        copies = []
        for n, (place, (_, piece, slot, *half)) in enumerate(zip(places, fetches)):
            for k in range(COPIES):
                if half and k // (COPIES // 2) != half[0]:
                    continue
                copies.append(
                    pltpu.make_async_copy(
                        hbm[place].at[pl.ds(piece * depth + k * part, part)],
                        store_ref.at[pl.ds(slot * depth + k * part, part)],
                        scratch[0].at[n * COPIES + k],
                    )
                )
        for copy in copies:
            copy.start()
        def rows_of(slot, at=slice(0, depth)):
            return store_ref[slot * depth + at.start : slot * depth + at.stop, :]

        kernel(rows_of, *ins, *outs)
        for copy in copies:
            copy.wait()

    moved = 2 * depth * store.shape[1] * len(fetches)
    return pl.pallas_call(
        body,
        in_specs=[VMEM] * (n_in + (not new)) + [ANY] * (n_hbm + len(after)),
        out_specs=[VMEM] * (1 + n_out),
        out_shape=[pltpu.VMEM(store.shape, store.dtype), *out_shapes],
        input_output_aliases={} if new else {0: 0},
        scratch_shapes=[pltpu.SemaphoreType.DMA((COPIES * len(fetches),))] if fetches else [],
        compiler_params=pltpu.CompilerParams(vmem_limit_bytes=STORE_GRANT),
        cost_estimate=pl.CostEstimate(flops=flops, bytes_accessed=moved, transcendentals=0),
        name=name,
    )(
        *([] if new else [store]),
        *operands,
        *[pltpu.with_memory_space_constraint(array, pltpu.HBM) for array in sources],
        *after,
    )


def stacked(blocks, after=()):
    rows = sum(block.shape[0] for block in blocks)

    def stack_kernel(*refs):
        refs[-1][...] = jnp.concatenate([ref[...] for ref in refs[: len(blocks)]], axis=0)

    return pl.pallas_call(
        stack_kernel,
        in_specs=[VMEM] * len(blocks) + [ANY] * len(after),
        out_shape=jax.ShapeDtypeStruct((rows, blocks[0].shape[1]), blocks[0].dtype),
        compiler_params=pltpu.CompilerParams(vmem_limit_bytes=4 << 20),
        name="stacked",
    )(*blocks, *after)


def block_owner(own, block, count):
    bits = count.bit_length() - 1
    hops = [1 << (bits - 2), 1 << (bits - 1)] + [1 << bit for bit in reversed(range(bits - 2))]
    for n, hop in enumerate(hops):
        own = own ^ (((block >> n) & 1) * hop)
    return own


def source_of(own, row, rows, count):
    tokens = rows // count
    return block_owner(own, row // tokens, count) * tokens + row % tokens


def pick_held(own, rows, count):
    held = source_of(own, lax.broadcasted_iota(jnp.int32, (rows, rows), 0), rows, count)
    return held == lax.broadcasted_iota(jnp.int32, (rows, rows), 1)


def pick_given(own, rows, count):
    held = source_of(own, lax.broadcasted_iota(jnp.int32, (rows, rows), 1), rows, count)
    return held == lax.broadcasted_iota(jnp.int32, (rows, rows), 0)


def picked(pick, block):
    if block.dtype == jnp.bfloat16:
        return jnp.dot(pick.astype(jnp.bfloat16), block, preferred_element_type=jnp.float32)
    return jnp.dot(pick.astype(jnp.float32), block, precision=lax.Precision.HIGHEST)


def held_mask(pick, tenants_row):
    tenants = jnp.sum(jnp.where(pick, tenants_row, 0).astype(jnp.float32), axis=1, keepdims=True)
    return tenant_mask(tenants.astype(jnp.int32), pick.shape[0])


def low_kernel(count, aligned, down_ref, tenants_ref, *refs):
    x, (span_out, low_ref) = refs[:-3], refs[-2:]
    own = lax.axis_index("tp")
    if aligned:
        width = down_ref.shape[0]
        at = pl.ds(pl.multiple_of(own * width, width), width)
        span = jnp.concatenate([ref[:, at] for ref in x], axis=0)
    else:
        span = jnp.concatenate([ref[...] for ref in x], axis=0)
    span_out[...] = span
    rows = span.shape[0]
    wide = jnp.dot(span, down_ref[...], preferred_element_type=jnp.float32)
    low = select_block(wide, held_mask(pick_held(own, rows, count), tenants_ref[...]))
    low_ref[...] = picked(pick_given(own, rows, count), low)


def low_part(down, tenants, x, count, after):
    rows, span = sum(block.shape[0] for block in x), down.shape[0]
    aligned = span % 128 == 0
    if not aligned:
        x = [
            lax.dynamic_slice(
                block,
                (0, lax.axis_index("tp") * span),
                (block.shape[0], span),
                allow_negative_indices=False,
            )
            for block in x
        ]
    return pl.pallas_call(
        lambda *refs: low_kernel(count, aligned, *refs),
        in_specs=[VMEM] * (2 + len(x)) + [ANY],
        out_shape=[
            jax.ShapeDtypeStruct((rows, span), x[0].dtype),
            jax.ShapeDtypeStruct((rows, ADAPTER_RANK), jnp.float32),
        ],
        compiler_params=pltpu.CompilerParams(vmem_limit_bytes=4 << 20),
        cost_estimate=pl.CostEstimate(
            flops=2 * rows * down.size, bytes_accessed=2 * down.size, transcendentals=0
        ),
        name="low_part",
    )(down, tenants, *x, after)


def forward_kernel(cuts, slots, blocks, first, slot, *refs):
    x = refs[:blocks]
    gate_out, up_out = refs[-2:]
    gate, up = (0.0, 0.0) if first else (refs[blocks][...], refs[blocks + 1][...])
    for cut in cuts:
        gate_weight, up_weight = slot(slots[cut][0]), slot(slots[cut][1])
        depth = gate_weight.shape[0]
        at = slice(cut * depth, (cut + 1) * depth)
        rows = jnp.concatenate([ref[:, at] for ref in x], axis=0)
        gate = gate + jnp.dot(rows, gate_weight, preferred_element_type=jnp.float32)
        up = up + jnp.dot(rows, up_weight, preferred_element_type=jnp.float32)
    gate_out[...] = gate
    up_out[...] = up


def forward(cuts, slots, x, store, sums, fetches, after):
    rows = sum(block.shape[0] for block in x)
    depth, hidden = store.shape[0] // SLOTS, store.shape[1]
    result = jax.ShapeDtypeStruct((rows, hidden), jnp.float32)
    store, gate, up = store_call(
        lambda *refs: forward_kernel(cuts, slots, len(x), not sums, *refs),
        store,
        fetches,
        [*x, *sums],
        [result, result],
        4 * rows * depth * hidden * len(cuts),
        "forward",
        after=after,
    )
    return store, [gate, up]


def activation_kernel(
    count, maps_slot, slot, gate_ref, up_ref, hidden_ref, low_ref, tenants_ref,
    dgate_ref, dup_ref, part_ref, spread_ref,
):
    rows = gate_ref.shape[0]
    maps = slot(maps_slot)
    own = lax.axis_index("tp")
    pick = pick_held(own, rows, count)
    mask = held_mask(pick, tenants_ref[...])
    spread = spread_rows(picked(pick, low_ref[...]), mask)
    spread_ref[...] = spread
    gate = gate_ref[...] + adapter_scale * jnp.dot(
        spread, maps, preferred_element_type=jnp.float32
    )
    s = jax.nn.sigmoid(gate)
    hidden = picked(pick, hidden_ref[...])
    dgate = (hidden * up_ref[...] * s * (1.0 + gate * (1.0 - s))).astype(jnp.bfloat16)
    dgate_ref[...] = dgate
    dup_ref[...] = (hidden * gate * s).astype(jnp.bfloat16)
    part = select_block(contracted_columns(dgate, maps), mask)
    part_ref[...] = picked(pick_given(own, rows, count), part)


def activation(maps_slot, store, sums, hidden, low, tenants, count, fetches):
    rows, width = sums[0].shape
    value = jax.ShapeDtypeStruct((rows, width), jnp.bfloat16)
    return store_call(
        lambda *refs: activation_kernel(count, maps_slot, *refs),
        store,
        fetches,
        [*sums, hidden, low, tenants],
        [
            value,
            value,
            jax.ShapeDtypeStruct((rows, ADAPTER_RANK), jnp.float32),
            jax.ShapeDtypeStruct((rows, SPREAD), jnp.bfloat16),
        ],
        4 * rows * SPREAD * width,
        "activation",
    )


def adapter_kernel(count, low_ref, tenants_ref, down_ref, own_out, other_out, spread_ref):
    half = own_out.shape[0]
    pick = pick_held(lax.axis_index("tp"), 2 * half, count)
    spread = spread_rows(picked(pick, low_ref[...]), held_mask(pick, tenants_ref[...]))
    spread_ref[...] = spread
    part = (adapter_scale * contracted_columns(spread, down_ref[...])).astype(jnp.bfloat16)
    own_out[...] = part[:half]
    other_out[...] = part[half:]


def adapter_part(low, tenants, down, count):
    rows, span = low.shape[0], down.shape[0]
    half = jax.ShapeDtypeStruct((rows // 2, span), jnp.bfloat16)
    return pl.pallas_call(
        lambda *refs: adapter_kernel(count, *refs),
        out_shape=[half, half, jax.ShapeDtypeStruct((rows, SPREAD), jnp.bfloat16)],
        compiler_params=pltpu.CompilerParams(vmem_limit_bytes=4 << 20),
        cost_estimate=pl.CostEstimate(
            flops=2 * rows * down.size, bytes_accessed=2 * down.size, transcendentals=0
        ),
        name="adapter_part",
    )(low, tenants, down)


def backward_kernel(slots, start, height, slot, dgate_ref, dup_ref, own_out, other_out):
    half = own_out.shape[0]
    dgate, dup = dgate_ref[...], dup_ref[...]
    for strip in range(0, height, STRIP):
        at = slice(start + strip, start + strip + STRIP)
        part = contracted_columns(dgate, slot(slots[0], at))
        part = part + contracted_columns(dup, slot(slots[1], at))
        own_out[:, strip : strip + STRIP] = part[:half]
        other_out[:, strip : strip + STRIP] = part[half:].astype(jnp.bfloat16)


def backward(slots, start, height, dgate, dup, store, fetches, after):
    rows, hidden = dgate.shape
    return store_call(
        lambda *refs: backward_kernel(slots, start, height, *refs),
        store,
        fetches,
        [dgate, dup],
        [
            jax.ShapeDtypeStruct((rows // 2, height), jnp.float32),
            jax.ShapeDtypeStruct((rows // 2, height), jnp.bfloat16),
        ],
        4 * rows * hidden * height,
        "backward",
        after=after,
    )


def first_halves_kernel(count, adapter_own, adapter_came, *refs):
    keep_ref, send_ref, sums = refs[-3:]
    pieces = refs[:-3]
    half = keep_ref.shape[0]
    device = lax.axis_index("tp")
    at = 0
    for own, came in zip(pieces[::2], pieces[1::2]):
        width = own.shape[1]
        sums[:, at : at + width] = own[...] + came[...].astype(jnp.float32)
        at += width
    mine = adapter_own[...].astype(jnp.float32)
    other = adapter_came[...].astype(jnp.float32)
    pair = jnp.where(
        device % 2 == 0,
        jnp.concatenate([mine, other], axis=1),
        jnp.concatenate([other, mine], axis=1),
    )
    width = pair.shape[1]
    sums[:, pl.ds(pl.multiple_of(device // 2 * width, width), width)] += pair
    keep_ref[...] = sums[:half, :]
    send_ref[...] = sums[half:, :].astype(jnp.bfloat16)


def first_halves(pieces, adapter_own, adapter_came, count):
    rows = adapter_own.shape[0]
    width = sum(own.shape[1] for own, _ in pieces)
    return pl.pallas_call(
        lambda *refs: first_halves_kernel(count, *refs),
        out_shape=[
            jax.ShapeDtypeStruct((rows // 2, width), jnp.float32),
            jax.ShapeDtypeStruct((rows // 2, width), jnp.bfloat16),
        ],
        scratch_shapes=[pltpu.VMEM((rows, width), jnp.float32)],
        compiler_params=pltpu.CompilerParams(vmem_limit_bytes=40 << 20),
        name="first_halves",
    )(adapter_own, adapter_came, *[array for pair in pieces for array in pair])


def halves(keep, came, after):
    rows, width = keep.shape

    def halves_kernel(keep_ref, came_ref, after_ref, keep_out, send_out):
        del after_ref
        total = keep_ref[...] + came_ref[...].astype(jnp.float32)
        keep_out[...] = total[: rows // 2]
        send_out[...] = total[rows // 2 :].astype(jnp.bfloat16)

    return pl.pallas_call(
        halves_kernel,
        in_specs=[VMEM, VMEM, ANY],
        out_shape=[
            jax.ShapeDtypeStruct((rows // 2, width), jnp.float32),
            jax.ShapeDtypeStruct((rows // 2, width), jnp.bfloat16),
        ],
        compiler_params=pltpu.CompilerParams(vmem_limit_bytes=40 << 20),
        name="halves",
    )(keep, came, after)


def final(keep, came, after):
    def final_kernel(keep_ref, came_ref, after_ref, out_ref):
        del after_ref
        out_ref[...] = (keep_ref[...] + came_ref[...].astype(jnp.float32)).astype(jnp.bfloat16)

    return pl.pallas_call(
        final_kernel,
        in_specs=[VMEM, VMEM, ANY],
        out_shape=jax.ShapeDtypeStruct(keep.shape, jnp.bfloat16),
        compiler_params=pltpu.CompilerParams(vmem_limit_bytes=40 << 20),
        name="final",
    )(keep, came, after)


def outer_kernel(left_ref, right_ref, *refs):
    out_ref, token_ref = refs[-2:]
    out_ref[...] = contracted_rows(
        left_ref[...] * jnp.bfloat16(adapter_scale), right_ref[...]
    ).astype(jnp.bfloat16)
    token_ref[...] = jnp.zeros_like(token_ref)


def outer(left, right, name, after, parts=1, part=0, earlier=None):
    rows, height = left.shape
    width = right.shape[1]
    block = block_of(height // parts, 512)
    if block % 128:
        block = height // parts
    steps = height // parts // block
    first = part * steps
    kept = [] if earlier is None else [earlier]
    return pl.pallas_call(
        outer_kernel,
        grid=(steps,),
        in_specs=[
            pl.BlockSpec((rows, block), lambda k: (0, k + first)),
            pl.BlockSpec((rows, width), lambda k: (0, 0)),
            ANY,
        ]
        + [ANY] * len(kept),
        out_specs=[
            pl.BlockSpec((block, width), lambda k: (k + first, 0)),
            pl.BlockSpec((8, 128), lambda k: (0, 0)),
        ],
        out_shape=[
            jax.ShapeDtypeStruct((height, width), jnp.bfloat16),
            jax.ShapeDtypeStruct((8, 128), jnp.float32),
        ],
        input_output_aliases={3: 0} if kept else {},
        compiler_params=pltpu.CompilerParams(vmem_limit_bytes=24 << 20),
        cost_estimate=pl.CostEstimate(
            flops=2 * rows * (height // parts) * width,
            bytes_accessed=2 * (height // parts) * width,
            transcendentals=0,
        ),
        name=name,
    )(left, right, after, *kept)


def add_kernel(left_ref, right_ref, out_ref):
    out_ref[...] = left_ref[...] + right_ref[...]


def plus(left, right):
    return pl.pallas_call(
        add_kernel,
        out_shape=jax.ShapeDtypeStruct(left.shape, left.dtype),
        compiler_params=pltpu.CompilerParams(vmem_limit_bytes=2 << 20),
        name="plus",
    )(left, right)


def swapped(block, hop):
    return lax.ppermute(block, "tp", [(i, i ^ hop) for i in range(lax.axis_size("tp"))])


def local(
    normed_layer_input,
    hidden_unit_gradient,
    gate_weight,
    up_weight,
    adapter_down_maps,
    adapter_up_maps,
    token_tenant_index,
):
    count = lax.axis_size("tp")
    own_rows, width = normed_layer_input.shape
    rows = own_rows * count
    hops = [1 << bit for bit in range(count.bit_length() - 1)]
    tenants = token_tenant_index.reshape(1, rows)

    def pair(cut, first, second):
        return [(gate_weight, cut, first), (up_weight, cut, second)]

    def mark(slot, token_ref):
        token_ref[...] = jnp.zeros_like(token_ref)

    mark_shape = jax.ShapeDtypeStruct((8, 128), jnp.float32)
    store = jax.ShapeDtypeStruct(
        (SLOTS * width // CUTS, gate_weight.shape[1]), gate_weight.dtype
    )
    far, near = hops[-1], hops[-2]
    came = [swapped(normed_layer_input, hop) for hop in (near, far, near | far)]
    store, token = store_call(mark, store, pair(0, 0, 1), [], [mark_shape], 0, "fetch")
    block = stacked([normed_layer_input, *came], [token])
    for hop in reversed(hops[2:-2]):
        block = stacked([block, swapped(block, hop)])
    other = swapped(block, hops[1])
    store, token = store_call(
        mark, store, [(gate_weight, 1, 2)], [], [mark_shape], 0, "fetch", after=[block]
    )
    block = stacked([block, other], [token])
    x = [block, swapped(block, 1)]
    store, token = store_call(
        mark, store, [(up_weight, 1, 3, 0)], [], [mark_shape], 0, "fetch", after=[block]
    )

    input_span, low = low_part(adapter_down_maps, tenants, x, count, token)
    store, token = store_call(
        mark, store, [(up_weight, 1, 3, 1)], [], [mark_shape], 0, "fetch", after=[low]
    )
    sums = []
    slots = {0: (0, 1), 1: (2, 3), 2: (4, 5), 3: (0, 1)}
    step = 0
    for cuts, fetches in (
        ((0, 1), pair(2, 4, 5)), ((2,), pair(3, 0, 1)), ((3,), [(adapter_up_maps, 0, 2)])
    ):
        after = [low]
        if step < len(hops):
            low = plus(low, swapped(low, hops[step]))
            step += 1
        store, sums = forward(cuts, slots, x, store, sums, fetches, after)
    for hop in hops[step:]:
        low = plus(low, swapped(low, hop))
    store, dgate, dup, low_grad, input_spread = activation(
        2, store, sums, hidden_unit_gradient, low, tenants, count, []
    )

    later_hops = hops[1:] + hops[:1]
    depth = width // CUTS
    part_list = [
        (3, (0, 1), 0, depth, [(gate_weight, 1, 2)]),
        (2, (4, 5), 0, depth, [(gate_weight, 0, 0)]),
        (1, (2, 3), 0, depth, [(up_weight, 0, 1)]),
        (0, (0, 1), 0, depth // 2, []),
        (0, (0, 1), depth // 2, depth // 2, []),
    ]
    columns = {}
    for n, (piece, slots, first, height, fetches) in enumerate(part_list):
        after = [low_grad]
        if n == len(part_list) - 1:
            adapter_own, adapter_other, grad_spread = adapter_part(
                low_grad, tenants, adapter_down_maps, count
            )
            adapter_came = swapped(adapter_other, 1)
            after = [adapter_other]
        else:
            turns = later_hops[:1] if n < len(part_list) - 2 else later_hops
            later_hops = later_hops[len(turns) :]
            for hop in turns:
                low_grad = plus(low_grad, swapped(low_grad, hop))
        store, own_part, other_part = backward(
            slots, first, height, dgate, dup, store, fetches, after
        )
        columns[piece * depth + first] = (own_part, swapped(other_part, 1))

    keep, send = first_halves(
        [columns[start] for start in sorted(columns)], adapter_own, adapter_came, count
    )
    halvings = [block_owner(0, 1 << bit, count) for bit in reversed(range(len(hops) - 1))]
    up_map_gradient = None
    for n, hop in enumerate(halvings[:-1]):
        came = swapped(send, hop)
        beside = send
        if n < 2:
            up_map_gradient, beside = outer(
                input_spread, dgate, "up_maps", send, 2, n, up_map_gradient
            )
        keep, send = halves(keep, came, beside)
    came = swapped(send, halvings[-1])
    down_map_gradient, beside = outer(input_span, grad_spread, "down_maps", send)
    return (final(keep, came, beside), down_map_gradient, up_map_gradient)


def solution(mesh):
    placed = (
        P(("groups", "tp"), None),
        P("groups", "tp"),
        P(None, "tp"),
        P(None, "tp"),
        P("tp", None),
        P(None, "tp"),
        P("groups"),
    )
    return jax.shard_map(
        local,
        mesh=mesh,
        in_specs=placed,
        out_specs=(P(("groups", "tp"), None), P("tp", "groups"), P("groups", "tp")),
        check_vma=False,
    )
```

```python
import jax
import jax.numpy as jnp
from jax import lax
from jax.experimental import pallas as pl
from jax.experimental.pallas import tpu as pltpu
from jax.sharding import PartitionSpec as P

ADAPTER_RANK = 64
TENANT_COUNT = 32
SPREAD = ADAPTER_RANK * TENANT_COUNT

adapter_scale = 2.0


def block_of(size, largest):
    block = largest
    while size % block:
        block //= 2
    return block


def contracted_rows(left, right):
    return lax.dot_general(
        left, right, (((0,), (0,)), ((), ())), preferred_element_type=jnp.float32
    )


def contracted_columns(left, right):
    return lax.dot_general(
        left, right, (((1,), (1,)), ((), ())), preferred_element_type=jnp.float32
    )


def tenant_mask(tenants, rows):
    columns = lax.broadcasted_iota(jnp.int32, (rows, SPREAD), 1) // ADAPTER_RANK
    return tenants == columns


def select_block(wide_rows, mask):
    kept = jnp.where(mask, wide_rows, 0.0)
    pair = 2 * ADAPTER_RANK
    total = kept[:, :pair]
    for start in range(pair, SPREAD, pair):
        total = total + kept[:, start : start + pair]
    return total[:, :ADAPTER_RANK] + total[:, ADAPTER_RANK:]


def spread_rows(low_rows, mask):
    pair = jnp.concatenate([low_rows, low_rows], axis=1)
    wide = jnp.concatenate([pair] * (TENANT_COUNT // 2), axis=1)
    return jnp.where(mask, wide, 0.0).astype(jnp.bfloat16)


VMEM = pl.BlockSpec(memory_space=pltpu.VMEM)
ANY = pl.BlockSpec(memory_space=pl.ANY)
CUTS = 4
COPIES = 8
STRIP = 256
SLOTS = 6
STORE_GRANT = 10 << 20


def store_call(kernel, store, fetches, operands, out_shapes, flops, name, after=()):
    new = isinstance(store, jax.ShapeDtypeStruct)
    depth = store.shape[0] // SLOTS
    part = depth // COPIES
    sources = []
    for array, *_ in fetches:
        if not any(array is known for known in sources):
            sources.append(array)
    places = [next(i for i, known in enumerate(sources) if known is f[0]) for f in fetches]
    n_in, n_out, n_hbm = len(operands), len(out_shapes), len(sources)

    def body(*refs):
        if not new:
            refs = refs[1:]
        ins, hbm = refs[:n_in], refs[n_in : n_in + n_hbm]
        rest = refs[n_in + n_hbm + len(after) :]
        store_ref, outs, scratch = rest[0], rest[1 : 1 + n_out], rest[1 + n_out :]
        copies = []
        for n, (place, (_, piece, slot, *half)) in enumerate(zip(places, fetches)):
            for k in range(COPIES):
                if half and k // (COPIES // 2) != half[0]:
                    continue
                copies.append(
                    pltpu.make_async_copy(
                        hbm[place].at[pl.ds(piece * depth + k * part, part)],
                        store_ref.at[pl.ds(slot * depth + k * part, part)],
                        scratch[0].at[n * COPIES + k],
                    )
                )
        for copy in copies:
            copy.start()
        def rows_of(slot, at=slice(0, depth)):
            return store_ref[slot * depth + at.start : slot * depth + at.stop, :]

        kernel(rows_of, *ins, *outs)
        for copy in copies:
            copy.wait()

    moved = 2 * depth * store.shape[1] * len(fetches)
    return pl.pallas_call(
        body,
        in_specs=[VMEM] * (n_in + (not new)) + [ANY] * (n_hbm + len(after)),
        out_specs=[VMEM] * (1 + n_out),
        out_shape=[pltpu.VMEM(store.shape, store.dtype), *out_shapes],
        input_output_aliases={} if new else {0: 0},
        scratch_shapes=[pltpu.SemaphoreType.DMA((COPIES * len(fetches),))] if fetches else [],
        compiler_params=pltpu.CompilerParams(vmem_limit_bytes=STORE_GRANT),
        cost_estimate=pl.CostEstimate(flops=flops, bytes_accessed=moved, transcendentals=0),
        name=name,
    )(
        *([] if new else [store]),
        *operands,
        *[pltpu.with_memory_space_constraint(array, pltpu.HBM) for array in sources],
        *after,
    )


def stacked(blocks, after=()):
    rows = sum(block.shape[0] for block in blocks)

    def stack_kernel(*refs):
        refs[-1][...] = jnp.concatenate([ref[...] for ref in refs[: len(blocks)]], axis=0)

    return pl.pallas_call(
        stack_kernel,
        in_specs=[VMEM] * len(blocks) + [ANY] * len(after),
        out_shape=jax.ShapeDtypeStruct((rows, blocks[0].shape[1]), blocks[0].dtype),
        compiler_params=pltpu.CompilerParams(vmem_limit_bytes=4 << 20),
        name="stacked",
    )(*blocks, *after)


def block_owner(own, block, count):
    bits = count.bit_length() - 1
    hops = [1 << (bits - 2), 1 << (bits - 1)] + [1 << bit for bit in reversed(range(bits - 2))]
    for n, hop in enumerate(hops):
        own = own ^ (((block >> n) & 1) * hop)
    return own


def source_of(own, row, rows, count):
    tokens = rows // count
    return block_owner(own, row // tokens, count) * tokens + row % tokens


def pick_held(own, rows, count):
    held = source_of(own, lax.broadcasted_iota(jnp.int32, (rows, rows), 0), rows, count)
    return held == lax.broadcasted_iota(jnp.int32, (rows, rows), 1)


def pick_given(own, rows, count):
    held = source_of(own, lax.broadcasted_iota(jnp.int32, (rows, rows), 1), rows, count)
    return held == lax.broadcasted_iota(jnp.int32, (rows, rows), 0)


def picked(pick, block):
    if block.dtype == jnp.bfloat16:
        return jnp.dot(pick.astype(jnp.bfloat16), block, preferred_element_type=jnp.float32)
    return jnp.dot(pick.astype(jnp.float32), block, precision=lax.Precision.HIGHEST)


def held_mask(pick, tenants_row):
    tenants = jnp.sum(jnp.where(pick, tenants_row, 0).astype(jnp.float32), axis=1, keepdims=True)
    return tenant_mask(tenants.astype(jnp.int32), pick.shape[0])


def low_kernel(count, aligned, down_ref, tenants_ref, *refs):
    x, (span_out, low_ref) = refs[:-3], refs[-2:]
    own = lax.axis_index("tp")
    if aligned:
        width = down_ref.shape[0]
        at = pl.ds(pl.multiple_of(own * width, width), width)
        span = jnp.concatenate([ref[:, at] for ref in x], axis=0)
    else:
        span = jnp.concatenate([ref[...] for ref in x], axis=0)
    span_out[...] = span
    rows = span.shape[0]
    wide = jnp.dot(span, down_ref[...], preferred_element_type=jnp.float32)
    low = select_block(wide, held_mask(pick_held(own, rows, count), tenants_ref[...]))
    low_ref[...] = picked(pick_given(own, rows, count), low)


def low_part(down, tenants, x, count, after):
    rows, span = sum(block.shape[0] for block in x), down.shape[0]
    aligned = span % 128 == 0
    if not aligned:
        x = [
            lax.dynamic_slice(
                block,
                (0, lax.axis_index("tp") * span),
                (block.shape[0], span),
                allow_negative_indices=False,
            )
            for block in x
        ]
    return pl.pallas_call(
        lambda *refs: low_kernel(count, aligned, *refs),
        in_specs=[VMEM] * (2 + len(x)) + [ANY],
        out_shape=[
            jax.ShapeDtypeStruct((rows, span), x[0].dtype),
            jax.ShapeDtypeStruct((rows, ADAPTER_RANK), jnp.float32),
        ],
        compiler_params=pltpu.CompilerParams(vmem_limit_bytes=4 << 20),
        cost_estimate=pl.CostEstimate(
            flops=2 * rows * down.size, bytes_accessed=2 * down.size, transcendentals=0
        ),
        name="low_part",
    )(down, tenants, *x, after)


def forward_kernel(cuts, slots, blocks, first, slot, *refs):
    x = refs[:blocks]
    gate_out, up_out = refs[-2:]
    gate, up = (0.0, 0.0) if first else (refs[blocks][...], refs[blocks + 1][...])
    for cut in cuts:
        gate_weight, up_weight = slot(slots[cut][0]), slot(slots[cut][1])
        depth = gate_weight.shape[0]
        at = slice(cut * depth, (cut + 1) * depth)
        rows = jnp.concatenate([ref[:, at] for ref in x], axis=0)
        gate = gate + jnp.dot(rows, gate_weight, preferred_element_type=jnp.float32)
        up = up + jnp.dot(rows, up_weight, preferred_element_type=jnp.float32)
    gate_out[...] = gate
    up_out[...] = up


def forward(cuts, slots, x, store, sums, fetches, after):
    rows = sum(block.shape[0] for block in x)
    depth, hidden = store.shape[0] // SLOTS, store.shape[1]
    result = jax.ShapeDtypeStruct((rows, hidden), jnp.float32)
    store, gate, up = store_call(
        lambda *refs: forward_kernel(cuts, slots, len(x), not sums, *refs),
        store,
        fetches,
        [*x, *sums],
        [result, result],
        4 * rows * depth * hidden * len(cuts),
        "forward",
        after=after,
    )
    return store, [gate, up]


def activation_kernel(
    count, maps_slot, slot, gate_ref, up_ref, hidden_ref, low_ref, tenants_ref,
    dgate_ref, dup_ref, part_ref, spread_ref,
):
    rows = gate_ref.shape[0]
    maps = slot(maps_slot)
    own = lax.axis_index("tp")
    pick = pick_held(own, rows, count)
    mask = held_mask(pick, tenants_ref[...])
    spread = spread_rows(picked(pick, low_ref[...]), mask)
    spread_ref[...] = spread
    gate = gate_ref[...] + adapter_scale * jnp.dot(
        spread, maps, preferred_element_type=jnp.float32
    )
    s = jax.nn.sigmoid(gate)
    hidden = picked(pick, hidden_ref[...])
    dgate = (hidden * up_ref[...] * s * (1.0 + gate * (1.0 - s))).astype(jnp.bfloat16)
    dgate_ref[...] = dgate
    dup_ref[...] = (hidden * gate * s).astype(jnp.bfloat16)
    part = select_block(contracted_columns(dgate, maps), mask)
    part_ref[...] = picked(pick_given(own, rows, count), part)


def activation(maps_slot, store, sums, hidden, low, tenants, count, fetches):
    rows, width = sums[0].shape
    value = jax.ShapeDtypeStruct((rows, width), jnp.bfloat16)
    return store_call(
        lambda *refs: activation_kernel(count, maps_slot, *refs),
        store,
        fetches,
        [*sums, hidden, low, tenants],
        [
            value,
            value,
            jax.ShapeDtypeStruct((rows, ADAPTER_RANK), jnp.float32),
            jax.ShapeDtypeStruct((rows, SPREAD), jnp.bfloat16),
        ],
        4 * rows * SPREAD * width,
        "activation",
    )


def adapter_kernel(count, low_ref, tenants_ref, down_ref, earlier, own_out, other_out, spread_ref):
    half = own_out.shape[0]
    before = earlier.shape[1]
    pick = pick_held(lax.axis_index("tp"), 2 * half, count)
    spread = spread_rows(picked(pick, low_ref[...]), held_mask(pick, tenants_ref[...]))
    spread_ref[...] = spread
    part = (adapter_scale * contracted_columns(spread, down_ref[...])).astype(jnp.bfloat16)
    own_out[...] = part[:half]
    other_out[:, :before] = earlier[...]
    other_out[:, before:] = part[half:]


def adapter_part(low, tenants, down, count, earlier):
    rows, span = low.shape[0], down.shape[0]
    return pl.pallas_call(
        lambda *refs: adapter_kernel(count, *refs),
        out_shape=[
            jax.ShapeDtypeStruct((rows // 2, span), jnp.bfloat16),
            jax.ShapeDtypeStruct((rows // 2, earlier.shape[1] + span), jnp.bfloat16),
            jax.ShapeDtypeStruct((rows, SPREAD), jnp.bfloat16),
        ],
        compiler_params=pltpu.CompilerParams(vmem_limit_bytes=4 << 20),
        cost_estimate=pl.CostEstimate(
            flops=2 * rows * down.size, bytes_accessed=2 * down.size, transcendentals=0
        ),
        name="adapter_part",
    )(low, tenants, down, earlier)


def backward_kernel(slots, start, height, slot, dgate_ref, dup_ref, *refs):
    own_out, other_out = refs[-2:]
    half = own_out.shape[0]
    before = other_out.shape[1] - height
    if before:
        other_out[:, :before] = refs[0][...]
    dgate, dup = dgate_ref[...], dup_ref[...]
    for strip in range(0, height, STRIP):
        at = slice(start + strip, start + strip + STRIP)
        part = contracted_columns(dgate, slot(slots[0], at))
        part = part + contracted_columns(dup, slot(slots[1], at))
        own_out[:, strip : strip + STRIP] = part[:half]
        other_out[:, before + strip : before + strip + STRIP] = part[half:].astype(jnp.bfloat16)


def backward(slots, start, height, dgate, dup, store, fetches, after, earlier=()):
    rows, hidden = dgate.shape
    other_width = height + sum(part.shape[1] for part in earlier)
    return store_call(
        lambda *refs: backward_kernel(slots, start, height, *refs),
        store,
        fetches,
        [dgate, dup, *earlier],
        [
            jax.ShapeDtypeStruct((rows // 2, height), jnp.float32),
            jax.ShapeDtypeStruct((rows // 2, other_width), jnp.bfloat16),
        ],
        4 * rows * hidden * height,
        "backward",
        after=after,
    )


def first_halves_kernel(places, span, adapter_own, *refs):
    keep_ref, send_ref, sums = refs[-3:]
    own, came = refs[: len(places)], refs[len(places) : -3]
    half = keep_ref.shape[0]
    device = lax.axis_index("tp")
    for part, (at, group, start) in zip(own, places):
        width = part.shape[1]
        other = came[group][:, start : start + width].astype(jnp.float32)
        sums[:, at : at + width] = part[...] + other
    mine = adapter_own[...].astype(jnp.float32)
    group, start = span
    other = came[group][:, start : start + mine.shape[1]].astype(jnp.float32)
    pair = jnp.where(
        device % 2 == 0,
        jnp.concatenate([mine, other], axis=1),
        jnp.concatenate([other, mine], axis=1),
    )
    width = pair.shape[1]
    sums[:, pl.ds(pl.multiple_of(device // 2 * width, width), width)] += pair
    keep_ref[...] = sums[:half, :]
    send_ref[...] = sums[half:, :].astype(jnp.bfloat16)


def first_halves(own, places, adapter_own, span, came):
    rows = adapter_own.shape[0]
    width = sum(part.shape[1] for part in own)
    return pl.pallas_call(
        lambda *refs: first_halves_kernel(places, span, *refs),
        out_shape=[
            jax.ShapeDtypeStruct((rows // 2, width), jnp.float32),
            jax.ShapeDtypeStruct((rows // 2, width), jnp.bfloat16),
        ],
        scratch_shapes=[pltpu.VMEM((rows, width), jnp.float32)],
        compiler_params=pltpu.CompilerParams(vmem_limit_bytes=40 << 20),
        name="first_halves",
    )(adapter_own, *own, *came)


def halves(keep, came, after):
    rows, width = keep.shape

    def halves_kernel(keep_ref, came_ref, after_ref, keep_out, send_out):
        del after_ref
        total = keep_ref[...] + came_ref[...].astype(jnp.float32)
        keep_out[...] = total[: rows // 2]
        send_out[...] = total[rows // 2 :].astype(jnp.bfloat16)

    return pl.pallas_call(
        halves_kernel,
        in_specs=[VMEM, VMEM, ANY],
        out_shape=[
            jax.ShapeDtypeStruct((rows // 2, width), jnp.float32),
            jax.ShapeDtypeStruct((rows // 2, width), jnp.bfloat16),
        ],
        compiler_params=pltpu.CompilerParams(vmem_limit_bytes=40 << 20),
        name="halves",
    )(keep, came, after)


def final(keep, came, after):
    def final_kernel(keep_ref, came_ref, after_ref, out_ref):
        del after_ref
        out_ref[...] = (keep_ref[...] + came_ref[...].astype(jnp.float32)).astype(jnp.bfloat16)

    return pl.pallas_call(
        final_kernel,
        in_specs=[VMEM, VMEM, ANY],
        out_shape=jax.ShapeDtypeStruct(keep.shape, jnp.bfloat16),
        compiler_params=pltpu.CompilerParams(vmem_limit_bytes=40 << 20),
        name="final",
    )(keep, came, after)


def outer_kernel(left_ref, right_ref, *refs):
    out_ref, token_ref = refs[-2:]
    out_ref[...] = contracted_rows(
        left_ref[...] * jnp.bfloat16(adapter_scale), right_ref[...]
    ).astype(jnp.bfloat16)
    token_ref[...] = jnp.zeros_like(token_ref)


def outer(left, right, name, after, parts=1, part=0, earlier=None):
    rows, height = left.shape
    width = right.shape[1]
    block = block_of(height // parts, 512)
    if block % 128:
        block = height // parts
    steps = height // parts // block
    first = part * steps
    kept = [] if earlier is None else [earlier]
    return pl.pallas_call(
        outer_kernel,
        grid=(steps,),
        in_specs=[
            pl.BlockSpec((rows, block), lambda k: (0, k + first)),
            pl.BlockSpec((rows, width), lambda k: (0, 0)),
            ANY,
        ]
        + [ANY] * len(kept),
        out_specs=[
            pl.BlockSpec((block, width), lambda k: (k + first, 0)),
            pl.BlockSpec((8, 128), lambda k: (0, 0)),
        ],
        out_shape=[
            jax.ShapeDtypeStruct((height, width), jnp.bfloat16),
            jax.ShapeDtypeStruct((8, 128), jnp.float32),
        ],
        input_output_aliases={3: 0} if kept else {},
        compiler_params=pltpu.CompilerParams(vmem_limit_bytes=24 << 20),
        cost_estimate=pl.CostEstimate(
            flops=2 * rows * (height // parts) * width,
            bytes_accessed=2 * (height // parts) * width,
            transcendentals=0,
        ),
        name=name,
    )(left, right, after, *kept)


def add_kernel(left_ref, right_ref, out_ref):
    out_ref[...] = left_ref[...] + right_ref[...]


def plus(left, right):
    return pl.pallas_call(
        add_kernel,
        out_shape=jax.ShapeDtypeStruct(left.shape, left.dtype),
        compiler_params=pltpu.CompilerParams(vmem_limit_bytes=2 << 20),
        name="plus",
    )(left, right)


def swapped(block, hop):
    return lax.ppermute(block, "tp", [(i, i ^ hop) for i in range(lax.axis_size("tp"))])


def local(
    normed_layer_input,
    hidden_unit_gradient,
    gate_weight,
    up_weight,
    adapter_down_maps,
    adapter_up_maps,
    token_tenant_index,
):
    count = lax.axis_size("tp")
    own_rows, width = normed_layer_input.shape
    rows = own_rows * count
    hops = [1 << bit for bit in range(count.bit_length() - 1)]
    tenants = token_tenant_index.reshape(1, rows)

    def pair(cut, first, second):
        return [(gate_weight, cut, first), (up_weight, cut, second)]

    def mark(slot, token_ref):
        token_ref[...] = jnp.zeros_like(token_ref)

    mark_shape = jax.ShapeDtypeStruct((8, 128), jnp.float32)
    store = jax.ShapeDtypeStruct(
        (SLOTS * width // CUTS, gate_weight.shape[1]), gate_weight.dtype
    )
    far, near = hops[-1], hops[-2]
    came = [swapped(normed_layer_input, hop) for hop in (near, far, near | far)]
    store, token = store_call(mark, store, pair(0, 0, 1), [], [mark_shape], 0, "fetch")
    block = stacked([normed_layer_input, *came], [token])
    for hop in reversed(hops[2:-2]):
        block = stacked([block, swapped(block, hop)])
    other = swapped(block, hops[1])
    store, token = store_call(
        mark, store, [(gate_weight, 1, 2)], [], [mark_shape], 0, "fetch", after=[block]
    )
    block = stacked([block, other], [token])
    x = [block, swapped(block, 1)]
    store, token = store_call(
        mark, store, [(up_weight, 1, 3, 0)], [], [mark_shape], 0, "fetch", after=[block]
    )

    input_span, low = low_part(adapter_down_maps, tenants, x, count, token)
    store, token = store_call(
        mark, store, [(up_weight, 1, 3, 1)], [], [mark_shape], 0, "fetch", after=[low]
    )
    sums = []
    slots = {0: (0, 1), 1: (2, 3), 2: (4, 5), 3: (0, 1)}
    step = 0
    for cuts, fetches in (
        ((0, 1), pair(2, 4, 5)), ((2,), pair(3, 0, 1)), ((3,), [(adapter_up_maps, 0, 2)])
    ):
        after = [low]
        if step < len(hops):
            low = plus(low, swapped(low, hops[step]))
            step += 1
        store, sums = forward(cuts, slots, x, store, sums, fetches, after)
    for hop in hops[step:]:
        low = plus(low, swapped(low, hop))
    store, dgate, dup, low_grad, input_spread = activation(
        2, store, sums, hidden_unit_gradient, low, tenants, count, []
    )

    later_hops = hops[1:] + hops[:1]
    depth = width // CUTS
    part_list = [
        (3, (0, 1), 0, depth, [(gate_weight, 1, 2)], True),
        (2, (4, 5), 0, depth, [(gate_weight, 0, 0)], False),
        (1, (2, 3), 0, depth, [(up_weight, 0, 1)], True),
        (0, (0, 1), depth // 2, depth // 2, [], True),
        (0, (0, 1), 0, depth // 2, [], False),
    ]
    own_parts, places, came, waiting = [], [], [], []
    for n, (piece, slots, first, height, fetches, waits) in enumerate(part_list):
        after = [low_grad]
        if n == len(part_list) - 1:
            span = (len(came), waiting[0].shape[1])
            adapter_own, to_send, grad_spread = adapter_part(
                low_grad, tenants, adapter_down_maps, count, waiting[0]
            )
            came.append(swapped(to_send, 1))
            after, waiting = [to_send], []
        else:
            turns = later_hops[:1] if n < len(part_list) - 2 else later_hops
            later_hops = later_hops[len(turns) :]
            for hop in turns:
                low_grad = plus(low_grad, swapped(low_grad, hop))
        begin = sum(part.shape[1] for part in waiting)
        store, own_part, other_part = backward(
            slots, first, height, dgate, dup, store, fetches, after, waiting
        )
        own_parts.append(own_part)
        places.append((piece * depth + first, len(came), begin))
        waiting = [other_part]
        if not waits:
            came.append(swapped(other_part, 1))
            waiting = []

    keep, send = first_halves(own_parts, places, adapter_own, span, came)
    halvings = [block_owner(0, 1 << bit, count) for bit in reversed(range(len(hops) - 1))]
    up_map_gradient = None
    for n, hop in enumerate(halvings[:-1]):
        came = swapped(send, hop)
        beside = send
        if n < 2:
            up_map_gradient, beside = outer(
                input_spread, dgate, "up_maps", send, 2, n, up_map_gradient
            )
        keep, send = halves(keep, came, beside)
    came = swapped(send, halvings[-1])
    down_map_gradient, beside = outer(input_span, grad_spread, "down_maps", send)
    return (final(keep, came, beside), down_map_gradient, up_map_gradient)


def solution(mesh):
    placed = (
        P(("groups", "tp"), None),
        P("groups", "tp"),
        P(None, "tp"),
        P(None, "tp"),
        P("tp", None),
        P(None, "tp"),
        P("groups"),
    )
    return jax.shard_map(
        local,
        mesh=mesh,
        in_specs=placed,
        out_specs=(P(("groups", "tp"), None), P("tp", "groups"), P("groups", "tp")),
        check_vma=False,
    )
```

```python
import jax
import jax.numpy as jnp
from jax import lax
from jax.experimental import pallas as pl
from jax.experimental.pallas import tpu as pltpu
from jax.sharding import PartitionSpec as P

ADAPTER_RANK = 64
TENANT_COUNT = 32
SPREAD = ADAPTER_RANK * TENANT_COUNT

adapter_scale = 2.0


def block_of(size, largest):
    block = largest
    while size % block:
        block //= 2
    return block


def contracted_rows(left, right):
    return lax.dot_general(
        left, right, (((0,), (0,)), ((), ())), preferred_element_type=jnp.float32
    )


def contracted_columns(left, right):
    return lax.dot_general(
        left, right, (((1,), (1,)), ((), ())), preferred_element_type=jnp.float32
    )


def tenant_mask(tenants, rows):
    columns = lax.broadcasted_iota(jnp.int32, (rows, SPREAD), 1) // ADAPTER_RANK
    return tenants == columns


def select_block(wide_rows, mask):
    kept = jnp.where(mask, wide_rows, 0.0)
    pair = 2 * ADAPTER_RANK
    total = kept[:, :pair]
    for start in range(pair, SPREAD, pair):
        total = total + kept[:, start : start + pair]
    return total[:, :ADAPTER_RANK] + total[:, ADAPTER_RANK:]


def spread_rows(low_rows, mask):
    pair = jnp.concatenate([low_rows, low_rows], axis=1)
    wide = jnp.concatenate([pair] * (TENANT_COUNT // 2), axis=1)
    return jnp.where(mask, wide, 0.0).astype(jnp.bfloat16)


VMEM = pl.BlockSpec(memory_space=pltpu.VMEM)
ANY = pl.BlockSpec(memory_space=pl.ANY)
CUTS = 4
COPIES = 8
STRIP = 256
SLOTS = 6
STORE_GRANT = 10 << 20


def store_call(kernel, store, fetches, operands, out_shapes, flops, name, after=()):
    new = isinstance(store, jax.ShapeDtypeStruct)
    depth = store.shape[0] // SLOTS
    part = depth // COPIES
    sources = []
    for array, *_ in fetches:
        if not any(array is known for known in sources):
            sources.append(array)
    places = [next(i for i, known in enumerate(sources) if known is f[0]) for f in fetches]
    n_in, n_out, n_hbm = len(operands), len(out_shapes), len(sources)

    def body(*refs):
        if not new:
            refs = refs[1:]
        ins, hbm = refs[:n_in], refs[n_in : n_in + n_hbm]
        rest = refs[n_in + n_hbm + len(after) :]
        store_ref, outs, scratch = rest[0], rest[1 : 1 + n_out], rest[1 + n_out :]
        copies = []
        for n, (place, (_, piece, slot, *half)) in enumerate(zip(places, fetches)):
            for k in range(COPIES):
                if half and k // (COPIES // 2) != half[0]:
                    continue
                copies.append(
                    pltpu.make_async_copy(
                        hbm[place].at[pl.ds(piece * depth + k * part, part)],
                        store_ref.at[pl.ds(slot * depth + k * part, part)],
                        scratch[0].at[n * COPIES + k],
                    )
                )
        for copy in copies:
            copy.start()
        def rows_of(slot, at=slice(0, depth)):
            return store_ref[slot * depth + at.start : slot * depth + at.stop, :]

        kernel(rows_of, *ins, *outs)
        for copy in copies:
            copy.wait()

    moved = 2 * depth * store.shape[1] * len(fetches)
    return pl.pallas_call(
        body,
        in_specs=[VMEM] * (n_in + (not new)) + [ANY] * (n_hbm + len(after)),
        out_specs=[VMEM] * (1 + n_out),
        out_shape=[pltpu.VMEM(store.shape, store.dtype), *out_shapes],
        input_output_aliases={} if new else {0: 0},
        scratch_shapes=[pltpu.SemaphoreType.DMA((COPIES * len(fetches),))] if fetches else [],
        compiler_params=pltpu.CompilerParams(vmem_limit_bytes=STORE_GRANT),
        cost_estimate=pl.CostEstimate(flops=flops, bytes_accessed=moved, transcendentals=0),
        name=name,
    )(
        *([] if new else [store]),
        *operands,
        *[pltpu.with_memory_space_constraint(array, pltpu.HBM) for array in sources],
        *after,
    )


def stacked(blocks, after=()):
    rows = sum(block.shape[0] for block in blocks)

    def stack_kernel(*refs):
        refs[-1][...] = jnp.concatenate([ref[...] for ref in refs[: len(blocks)]], axis=0)

    return pl.pallas_call(
        stack_kernel,
        in_specs=[VMEM] * len(blocks) + [ANY] * len(after),
        out_shape=jax.ShapeDtypeStruct((rows, blocks[0].shape[1]), blocks[0].dtype),
        compiler_params=pltpu.CompilerParams(vmem_limit_bytes=4 << 20),
        name="stacked",
    )(*blocks, *after)


def block_owner(own, block, count):
    bits = count.bit_length() - 1
    hops = [1 << (bits - 2), 1 << (bits - 1)] + [1 << bit for bit in reversed(range(bits - 2))]
    for n, hop in enumerate(hops):
        own = own ^ (((block >> n) & 1) * hop)
    return own


def source_of(own, row, rows, count):
    tokens = rows // count
    return block_owner(own, row // tokens, count) * tokens + row % tokens


def pick_held(own, rows, count):
    held = source_of(own, lax.broadcasted_iota(jnp.int32, (rows, rows), 0), rows, count)
    return held == lax.broadcasted_iota(jnp.int32, (rows, rows), 1)


def pick_given(own, rows, count):
    held = source_of(own, lax.broadcasted_iota(jnp.int32, (rows, rows), 1), rows, count)
    return held == lax.broadcasted_iota(jnp.int32, (rows, rows), 0)


def picked(pick, block):
    if block.dtype == jnp.bfloat16:
        return jnp.dot(pick.astype(jnp.bfloat16), block, preferred_element_type=jnp.float32)
    return jnp.dot(pick.astype(jnp.float32), block, precision=lax.Precision.HIGHEST)


def held_mask(pick, tenants_row):
    tenants = jnp.sum(jnp.where(pick, tenants_row, 0).astype(jnp.float32), axis=1, keepdims=True)
    return tenant_mask(tenants.astype(jnp.int32), pick.shape[0])


def low_kernel(count, aligned, down_ref, tenants_ref, *refs):
    x, (span_out, low_ref) = refs[:-3], refs[-2:]
    own = lax.axis_index("tp")
    if aligned:
        width = down_ref.shape[0]
        at = pl.ds(pl.multiple_of(own * width, width), width)
        span = jnp.concatenate([ref[:, at] for ref in x], axis=0)
    else:
        span = jnp.concatenate([ref[...] for ref in x], axis=0)
    span_out[...] = span
    rows = span.shape[0]
    wide = jnp.dot(span, down_ref[...], preferred_element_type=jnp.float32)
    low = select_block(wide, held_mask(pick_held(own, rows, count), tenants_ref[...]))
    low_ref[...] = picked(pick_given(own, rows, count), low)


def low_part(down, tenants, x, count, after):
    rows, span = sum(block.shape[0] for block in x), down.shape[0]
    aligned = span % 128 == 0
    if not aligned:
        x = [
            lax.dynamic_slice(
                block,
                (0, lax.axis_index("tp") * span),
                (block.shape[0], span),
                allow_negative_indices=False,
            )
            for block in x
        ]
    return pl.pallas_call(
        lambda *refs: low_kernel(count, aligned, *refs),
        in_specs=[VMEM] * (2 + len(x)) + [ANY],
        out_shape=[
            jax.ShapeDtypeStruct((rows, span), x[0].dtype),
            jax.ShapeDtypeStruct((rows, ADAPTER_RANK), jnp.float32),
        ],
        compiler_params=pltpu.CompilerParams(vmem_limit_bytes=4 << 20),
        cost_estimate=pl.CostEstimate(
            flops=2 * rows * down.size, bytes_accessed=2 * down.size, transcendentals=0
        ),
        name="low_part",
    )(down, tenants, *x, after)


def forward_kernel(cuts, slots, blocks, first, slot, *refs):
    x = refs[:blocks]
    gate_out, up_out = refs[-2:]
    gate, up = (0.0, 0.0) if first else (refs[blocks][...], refs[blocks + 1][...])
    for cut in cuts:
        gate_weight, up_weight = slot(slots[cut][0]), slot(slots[cut][1])
        depth = gate_weight.shape[0]
        at = slice(cut * depth, (cut + 1) * depth)
        rows = jnp.concatenate([ref[:, at] for ref in x], axis=0)
        gate = gate + jnp.dot(rows, gate_weight, preferred_element_type=jnp.float32)
        up = up + jnp.dot(rows, up_weight, preferred_element_type=jnp.float32)
    gate_out[...] = gate
    up_out[...] = up


def forward(cuts, slots, x, store, sums, fetches, after):
    rows = sum(block.shape[0] for block in x)
    depth, hidden = store.shape[0] // SLOTS, store.shape[1]
    result = jax.ShapeDtypeStruct((rows, hidden), jnp.float32)
    store, gate, up = store_call(
        lambda *refs: forward_kernel(cuts, slots, len(x), not sums, *refs),
        store,
        fetches,
        [*x, *sums],
        [result, result],
        4 * rows * depth * hidden * len(cuts),
        "forward",
        after=after,
    )
    return store, [gate, up]


def activation_kernel(
    count, maps_slot, slot, gate_ref, up_ref, hidden_ref, low_ref, tenants_ref,
    dgate_ref, dup_ref, part_ref, spread_ref,
):
    rows = gate_ref.shape[0]
    maps = slot(maps_slot)
    own = lax.axis_index("tp")
    pick = pick_held(own, rows, count)
    mask = held_mask(pick, tenants_ref[...])
    spread = spread_rows(picked(pick, low_ref[...]), mask)
    spread_ref[...] = spread
    gate = gate_ref[...] + adapter_scale * jnp.dot(
        spread, maps, preferred_element_type=jnp.float32
    )
    s = jax.nn.sigmoid(gate)
    hidden = picked(pick, hidden_ref[...])
    dgate = (hidden * up_ref[...] * s * (1.0 + gate * (1.0 - s))).astype(jnp.bfloat16)
    dgate_ref[...] = dgate
    dup_ref[...] = (hidden * gate * s).astype(jnp.bfloat16)
    part = select_block(contracted_columns(dgate, maps), mask)
    part_ref[...] = picked(pick_given(own, rows, count), part)


def activation(maps_slot, store, sums, hidden, low, tenants, count, fetches):
    rows, width = sums[0].shape
    value = jax.ShapeDtypeStruct((rows, width), jnp.bfloat16)
    return store_call(
        lambda *refs: activation_kernel(count, maps_slot, *refs),
        store,
        fetches,
        [*sums, hidden, low, tenants],
        [
            value,
            value,
            jax.ShapeDtypeStruct((rows, ADAPTER_RANK), jnp.float32),
            jax.ShapeDtypeStruct((rows, SPREAD), jnp.bfloat16),
        ],
        4 * rows * SPREAD * width,
        "activation",
    )


def adapter_kernel(count, low_ref, tenants_ref, down_ref, earlier, own_out, other_out, spread_ref):
    half = own_out.shape[0]
    before = earlier.shape[1]
    pick = pick_held(lax.axis_index("tp"), 2 * half, count)
    spread = spread_rows(picked(pick, low_ref[...]), held_mask(pick, tenants_ref[...]))
    spread_ref[...] = spread
    part = (adapter_scale * contracted_columns(spread, down_ref[...])).astype(jnp.bfloat16)
    own_out[...] = part[:half]
    other_out[:, :before] = earlier[...]
    other_out[:, before:] = part[half:]


def adapter_part(low, tenants, down, count, earlier):
    rows, span = low.shape[0], down.shape[0]
    return pl.pallas_call(
        lambda *refs: adapter_kernel(count, *refs),
        out_shape=[
            jax.ShapeDtypeStruct((rows // 2, span), jnp.bfloat16),
            jax.ShapeDtypeStruct((rows // 2, earlier.shape[1] + span), jnp.bfloat16),
            jax.ShapeDtypeStruct((rows, SPREAD), jnp.bfloat16),
        ],
        compiler_params=pltpu.CompilerParams(vmem_limit_bytes=4 << 20),
        cost_estimate=pl.CostEstimate(
            flops=2 * rows * down.size, bytes_accessed=2 * down.size, transcendentals=0
        ),
        name="adapter_part",
    )(low, tenants, down, earlier)


def backward_kernel(slots, start, height, slot, dgate_ref, dup_ref, *refs):
    own_out, other_out = refs[-2:]
    half = own_out.shape[0]
    before = other_out.shape[1] - height
    if before:
        other_out[:, :before] = refs[0][...]
    dgate, dup = dgate_ref[...], dup_ref[...]
    for strip in range(0, height, STRIP):
        at = slice(start + strip, start + strip + STRIP)
        part = contracted_columns(dgate, slot(slots[0], at))
        part = part + contracted_columns(dup, slot(slots[1], at))
        own_out[:, strip : strip + STRIP] = part[:half]
        other_out[:, before + strip : before + strip + STRIP] = part[half:].astype(jnp.bfloat16)


def backward(slots, start, height, dgate, dup, store, fetches, after, earlier=()):
    rows, hidden = dgate.shape
    other_width = height + sum(part.shape[1] for part in earlier)
    return store_call(
        lambda *refs: backward_kernel(slots, start, height, *refs),
        store,
        fetches,
        [dgate, dup, *earlier],
        [
            jax.ShapeDtypeStruct((rows // 2, height), jnp.float32),
            jax.ShapeDtypeStruct((rows // 2, other_width), jnp.bfloat16),
        ],
        4 * rows * hidden * height,
        "backward",
        after=after,
    )


def first_halves_kernel(places, span, adapter_own, *refs):
    keep_ref, send_ref, sums = refs[-3:]
    own, came = refs[: len(places)], refs[len(places) : -3]
    half = keep_ref.shape[0]
    device = lax.axis_index("tp")
    for part, (at, group, start) in zip(own, places):
        width = part.shape[1]
        other = came[group][:, start : start + width].astype(jnp.float32)
        sums[:, at : at + width] = part[...] + other
    mine = adapter_own[...].astype(jnp.float32)
    group, start = span
    other = came[group][:, start : start + mine.shape[1]].astype(jnp.float32)
    pair = jnp.where(
        device % 2 == 0,
        jnp.concatenate([mine, other], axis=1),
        jnp.concatenate([other, mine], axis=1),
    )
    width = pair.shape[1]
    sums[:, pl.ds(pl.multiple_of(device // 2 * width, width), width)] += pair
    keep_ref[...] = sums[:half, :]
    send_ref[...] = sums[half:, :].astype(jnp.bfloat16)


def first_halves(own, places, adapter_own, span, came):
    rows = adapter_own.shape[0]
    width = sum(part.shape[1] for part in own)
    return pl.pallas_call(
        lambda *refs: first_halves_kernel(places, span, *refs),
        out_shape=[
            jax.ShapeDtypeStruct((rows // 2, width), jnp.float32),
            jax.ShapeDtypeStruct((rows // 2, width), jnp.bfloat16),
        ],
        scratch_shapes=[pltpu.VMEM((rows, width), jnp.float32)],
        compiler_params=pltpu.CompilerParams(vmem_limit_bytes=40 << 20),
        name="first_halves",
    )(adapter_own, *own, *came)


def halves(keep, came, after):
    rows, width = keep.shape

    def halves_kernel(keep_ref, came_ref, *refs):
        keep_out, send_out = refs[-2:]
        total = keep_ref[...] + came_ref[...].astype(jnp.float32)
        keep_out[...] = total[: rows // 2]
        send_out[...] = total[rows // 2 :].astype(jnp.bfloat16)

    return pl.pallas_call(
        halves_kernel,
        in_specs=[VMEM, VMEM] + [ANY] * len(after),
        out_shape=[
            jax.ShapeDtypeStruct((rows // 2, width), jnp.float32),
            jax.ShapeDtypeStruct((rows // 2, width), jnp.bfloat16),
        ],
        compiler_params=pltpu.CompilerParams(vmem_limit_bytes=40 << 20),
        name="halves",
    )(keep, came, *after)


def final(keep, came):
    def final_kernel(keep_ref, came_ref, out_ref):
        out_ref[...] = (keep_ref[...] + came_ref[...].astype(jnp.float32)).astype(jnp.bfloat16)

    return pl.pallas_call(
        final_kernel,
        out_shape=jax.ShapeDtypeStruct(keep.shape, jnp.bfloat16),
        compiler_params=pltpu.CompilerParams(vmem_limit_bytes=40 << 20),
        name="final",
    )(keep, came)


def outer_kernel(left_ref, right_ref, *refs):
    out_ref, token_ref = refs[-2:]
    out_ref[...] = contracted_rows(
        left_ref[...] * jnp.bfloat16(adapter_scale), right_ref[...]
    ).astype(jnp.bfloat16)
    token_ref[...] = jnp.zeros_like(token_ref)


def outer(left, right, name, after, parts=1, span=(0, 1), earlier=None):
    rows, height = left.shape
    width = right.shape[1]
    block = block_of(height // parts, 512)
    if block % 128:
        block = height // parts
    per_part = height // parts // block
    first, steps = span[0] * per_part, (span[1] - span[0]) * per_part
    kept = [] if earlier is None else [earlier]
    return pl.pallas_call(
        outer_kernel,
        grid=(steps,),
        in_specs=[
            pl.BlockSpec((rows, block), lambda k: (0, k + first)),
            pl.BlockSpec((rows, width), lambda k: (0, 0)),
            ANY,
        ]
        + [ANY] * len(kept),
        out_specs=[
            pl.BlockSpec((block, width), lambda k: (k + first, 0)),
            pl.BlockSpec((8, 128), lambda k: (0, 0)),
        ],
        out_shape=[
            jax.ShapeDtypeStruct((height, width), jnp.bfloat16),
            jax.ShapeDtypeStruct((8, 128), jnp.float32),
        ],
        input_output_aliases={3: 0} if kept else {},
        compiler_params=pltpu.CompilerParams(vmem_limit_bytes=24 << 20),
        cost_estimate=pl.CostEstimate(
            flops=2 * rows * steps * block * width,
            bytes_accessed=2 * steps * block * width,
            transcendentals=0,
        ),
        name=name,
    )(left, right, after, *kept)


def add_kernel(left_ref, right_ref, out_ref):
    out_ref[...] = left_ref[...] + right_ref[...]


def plus(left, right):
    return pl.pallas_call(
        add_kernel,
        out_shape=jax.ShapeDtypeStruct(left.shape, left.dtype),
        compiler_params=pltpu.CompilerParams(vmem_limit_bytes=2 << 20),
        name="plus",
    )(left, right)


def swapped(block, hop):
    return lax.ppermute(block, "tp", [(i, i ^ hop) for i in range(lax.axis_size("tp"))])


def local(
    normed_layer_input,
    hidden_unit_gradient,
    gate_weight,
    up_weight,
    adapter_down_maps,
    adapter_up_maps,
    token_tenant_index,
):
    count = lax.axis_size("tp")
    own_rows, width = normed_layer_input.shape
    rows = own_rows * count
    hops = [1 << bit for bit in range(count.bit_length() - 1)]
    tenants = token_tenant_index.reshape(1, rows)

    def pair(cut, first, second):
        return [(gate_weight, cut, first), (up_weight, cut, second)]

    def mark(slot, token_ref):
        token_ref[...] = jnp.zeros_like(token_ref)

    mark_shape = jax.ShapeDtypeStruct((8, 128), jnp.float32)
    store = jax.ShapeDtypeStruct(
        (SLOTS * width // CUTS, gate_weight.shape[1]), gate_weight.dtype
    )
    far, near = hops[-1], hops[-2]
    came = [swapped(normed_layer_input, hop) for hop in (near, far, near | far)]
    store, token = store_call(mark, store, pair(0, 0, 1), [], [mark_shape], 0, "fetch")
    block = stacked([normed_layer_input, *came], [token])
    for hop in reversed(hops[2:-2]):
        block = stacked([block, swapped(block, hop)])
    other = swapped(block, hops[1])
    store, token = store_call(
        mark, store, [(gate_weight, 1, 2)], [], [mark_shape], 0, "fetch", after=[block]
    )
    block = stacked([block, other], [token])
    x = [block, swapped(block, 1)]
    store, token = store_call(
        mark, store, [(up_weight, 1, 3, 0)], [], [mark_shape], 0, "fetch", after=[block]
    )

    input_span, low = low_part(adapter_down_maps, tenants, x, count, token)
    store, token = store_call(
        mark, store, [(up_weight, 1, 3, 1)], [], [mark_shape], 0, "fetch", after=[low]
    )
    sums = []
    slots = {0: (0, 1), 1: (2, 3), 2: (4, 5), 3: (0, 1)}
    step = 0
    for cuts, fetches in (
        ((0, 1), pair(2, 4, 5)), ((2,), pair(3, 0, 1)), ((3,), [(adapter_up_maps, 0, 2)])
    ):
        after = [low]
        if step < len(hops):
            low = plus(low, swapped(low, hops[step]))
            step += 1
        store, sums = forward(cuts, slots, x, store, sums, fetches, after)
    for hop in hops[step:]:
        low = plus(low, swapped(low, hop))
    store, dgate, dup, low_grad, input_spread = activation(
        2, store, sums, hidden_unit_gradient, low, tenants, count, []
    )

    later_hops = hops[1:] + hops[:1]
    depth = width // CUTS
    part_list = [
        (3, (0, 1), 0, depth, [(gate_weight, 1, 2)], True),
        (2, (4, 5), 0, depth, [(gate_weight, 0, 0)], False),
        (1, (2, 3), 0, depth, [(up_weight, 0, 1)], True),
        (0, (0, 1), depth // 2, depth // 2, [], True),
        (0, (0, 1), 0, depth // 2, [], False),
    ]
    own_parts, places, came, waiting = [], [], [], []
    for n, (piece, slots, first, height, fetches, waits) in enumerate(part_list):
        after = [low_grad]
        if n == len(part_list) - 1:
            span = (len(came), waiting[0].shape[1])
            adapter_own, to_send, grad_spread = adapter_part(
                low_grad, tenants, adapter_down_maps, count, waiting[0]
            )
            came.append(swapped(to_send, 1))
            after, waiting = [to_send], []
        else:
            turns = later_hops[:1] if n < len(part_list) - 2 else later_hops
            later_hops = later_hops[len(turns) :]
            for hop in turns:
                low_grad = plus(low_grad, swapped(low_grad, hop))
        begin = sum(part.shape[1] for part in waiting)
        store, own_part, other_part = backward(
            slots, first, height, dgate, dup, store, fetches, after, waiting
        )
        own_parts.append(own_part)
        places.append((piece * depth + first, len(came), begin))
        waiting = [other_part]
        if not waits:
            came.append(swapped(other_part, 1))
            waiting = []

    keep, send = first_halves(own_parts, places, adapter_own, span, came)
    halvings = [block_owner(0, 1 << bit, count) for bit in reversed(range(len(hops) - 1))]
    for n, hop in enumerate(halvings[:-1]):
        came = swapped(send, hop)
        beside = [send]
        if n == 0:
            up_map_gradient, token = outer(input_spread, dgate, "up_maps", send, 4, (0, 3))
            beside = [token]
        elif n == 1:
            up_map_gradient, token = outer(
                input_spread, dgate, "up_maps", send, 4, (3, 4), up_map_gradient
            )
            down_map_gradient, other_token = outer(input_span, grad_spread, "down_maps", send)
            beside = [token, other_token]
        keep, send = halves(keep, came, beside)
    came = swapped(send, halvings[-1])
    return (final(keep, came), down_map_gradient, up_map_gradient)


def solution(mesh):
    placed = (
        P(("groups", "tp"), None),
        P("groups", "tp"),
        P(None, "tp"),
        P(None, "tp"),
        P("tp", None),
        P(None, "tp"),
        P("groups"),
    )
    return jax.shard_map(
        local,
        mesh=mesh,
        in_specs=placed,
        out_specs=(P(("groups", "tp"), None), P("tp", "groups"), P("groups", "tp")),
        check_vma=False,
    )
```

```python
import jax
import jax.numpy as jnp
from jax import lax
from jax.experimental import pallas as pl
from jax.experimental.pallas import tpu as pltpu
from jax.sharding import PartitionSpec as P

ADAPTER_RANK = 64
TENANT_COUNT = 32
SPREAD = ADAPTER_RANK * TENANT_COUNT

adapter_scale = 2.0


def block_of(size, largest):
    block = largest
    while size % block:
        block //= 2
    return block


def contracted_rows(left, right):
    return lax.dot_general(
        left, right, (((0,), (0,)), ((), ())), preferred_element_type=jnp.float32
    )


def contracted_columns(left, right):
    return lax.dot_general(
        left, right, (((1,), (1,)), ((), ())), preferred_element_type=jnp.float32
    )


def tenant_mask(tenants, rows):
    columns = lax.broadcasted_iota(jnp.int32, (rows, SPREAD), 1) // ADAPTER_RANK
    return tenants == columns


def select_block(wide_rows, mask):
    kept = jnp.where(mask, wide_rows, 0.0)
    pair = 2 * ADAPTER_RANK
    total = kept[:, :pair]
    for start in range(pair, SPREAD, pair):
        total = total + kept[:, start : start + pair]
    return total[:, :ADAPTER_RANK] + total[:, ADAPTER_RANK:]


def spread_rows(low_rows, mask):
    pair = jnp.concatenate([low_rows, low_rows], axis=1)
    wide = jnp.concatenate([pair] * (TENANT_COUNT // 2), axis=1)
    return jnp.where(mask, wide, 0.0).astype(jnp.bfloat16)


VMEM = pl.BlockSpec(memory_space=pltpu.VMEM)
ANY = pl.BlockSpec(memory_space=pl.ANY)
CUTS = 4
COPIES = 8
STRIP = 256
SLOTS = 6
STORE_GRANT = 10 << 20


def store_call(kernel, store, fetches, operands, out_shapes, flops, name, after=()):
    new = isinstance(store, jax.ShapeDtypeStruct)
    depth = store.shape[0] // SLOTS
    part = depth // COPIES
    sources = []
    for array, *_ in fetches:
        if not any(array is known for known in sources):
            sources.append(array)
    places = [next(i for i, known in enumerate(sources) if known is f[0]) for f in fetches]
    n_in, n_out, n_hbm = len(operands), len(out_shapes), len(sources)

    def body(*refs):
        if not new:
            refs = refs[1:]
        ins, hbm = refs[:n_in], refs[n_in : n_in + n_hbm]
        rest = refs[n_in + n_hbm + len(after) :]
        store_ref, outs, scratch = rest[0], rest[1 : 1 + n_out], rest[1 + n_out :]
        copies = []
        for n, (place, (_, piece, slot, *half)) in enumerate(zip(places, fetches)):
            for k in range(COPIES):
                if half and k // (COPIES // 2) != half[0]:
                    continue
                copies.append(
                    pltpu.make_async_copy(
                        hbm[place].at[pl.ds(piece * depth + k * part, part)],
                        store_ref.at[pl.ds(slot * depth + k * part, part)],
                        scratch[0].at[n * COPIES + k],
                    )
                )
        for copy in copies:
            copy.start()
        def rows_of(slot, at=slice(0, depth)):
            return store_ref[slot * depth + at.start : slot * depth + at.stop, :]

        kernel(rows_of, *ins, *outs)
        for copy in copies:
            copy.wait()

    moved = 2 * depth * store.shape[1] * len(fetches)
    return pl.pallas_call(
        body,
        in_specs=[VMEM] * (n_in + (not new)) + [ANY] * (n_hbm + len(after)),
        out_specs=[VMEM] * (1 + n_out),
        out_shape=[pltpu.VMEM(store.shape, store.dtype), *out_shapes],
        input_output_aliases={} if new else {0: 0},
        scratch_shapes=[pltpu.SemaphoreType.DMA((COPIES * len(fetches),))] if fetches else [],
        compiler_params=pltpu.CompilerParams(vmem_limit_bytes=STORE_GRANT),
        cost_estimate=pl.CostEstimate(flops=flops, bytes_accessed=moved, transcendentals=0),
        name=name,
    )(
        *([] if new else [store]),
        *operands,
        *[pltpu.with_memory_space_constraint(array, pltpu.HBM) for array in sources],
        *after,
    )


def stacked(blocks, after=()):
    rows = sum(block.shape[0] for block in blocks)

    def stack_kernel(*refs):
        refs[-1][...] = jnp.concatenate([ref[...] for ref in refs[: len(blocks)]], axis=0)

    return pl.pallas_call(
        stack_kernel,
        in_specs=[VMEM] * len(blocks) + [ANY] * len(after),
        out_shape=jax.ShapeDtypeStruct((rows, blocks[0].shape[1]), blocks[0].dtype),
        compiler_params=pltpu.CompilerParams(vmem_limit_bytes=4 << 20),
        name="stacked",
    )(*blocks, *after)


def block_owner(own, block, count):
    bits = count.bit_length() - 1
    hops = [1 << (bits - 2), 1 << (bits - 1)] + [1 << bit for bit in reversed(range(bits - 2))]
    for n, hop in enumerate(hops):
        own = own ^ (((block >> n) & 1) * hop)
    return own


def source_of(own, row, rows, count):
    tokens = rows // count
    return block_owner(own, row // tokens, count) * tokens + row % tokens


def pick_held(own, rows, count):
    held = source_of(own, lax.broadcasted_iota(jnp.int32, (rows, rows), 0), rows, count)
    return held == lax.broadcasted_iota(jnp.int32, (rows, rows), 1)


def pick_given(own, rows, count):
    held = source_of(own, lax.broadcasted_iota(jnp.int32, (rows, rows), 1), rows, count)
    return held == lax.broadcasted_iota(jnp.int32, (rows, rows), 0)


def picked(pick, block):
    if block.dtype == jnp.bfloat16:
        return jnp.dot(pick.astype(jnp.bfloat16), block, preferred_element_type=jnp.float32)
    return jnp.dot(pick.astype(jnp.float32), block, precision=lax.Precision.HIGHEST)


def held_mask(pick, tenants_row):
    tenants = jnp.sum(jnp.where(pick, tenants_row, 0).astype(jnp.float32), axis=1, keepdims=True)
    return tenant_mask(tenants.astype(jnp.int32), pick.shape[0])


def low_kernel(count, aligned, down_ref, tenants_ref, *refs):
    x, (span_out, low_ref) = refs[:-3], refs[-2:]
    own = lax.axis_index("tp")
    if aligned:
        width = down_ref.shape[0]
        at = pl.ds(pl.multiple_of(own * width, width), width)
        span = jnp.concatenate([ref[:, at] for ref in x], axis=0)
    else:
        span = jnp.concatenate([ref[...] for ref in x], axis=0)
    span_out[...] = span
    rows = span.shape[0]
    wide = jnp.dot(span, down_ref[...], preferred_element_type=jnp.float32)
    low = select_block(wide, held_mask(pick_held(own, rows, count), tenants_ref[...]))
    low_ref[...] = picked(pick_given(own, rows, count), low)


def low_part(down, tenants, x, count, after):
    rows, span = sum(block.shape[0] for block in x), down.shape[0]
    aligned = span % 128 == 0
    if not aligned:
        x = [
            lax.dynamic_slice(
                block,
                (0, lax.axis_index("tp") * span),
                (block.shape[0], span),
                allow_negative_indices=False,
            )
            for block in x
        ]
    return pl.pallas_call(
        lambda *refs: low_kernel(count, aligned, *refs),
        in_specs=[VMEM] * (2 + len(x)) + [ANY],
        out_shape=[
            jax.ShapeDtypeStruct((rows, span), x[0].dtype),
            jax.ShapeDtypeStruct((rows, ADAPTER_RANK), jnp.float32),
        ],
        compiler_params=pltpu.CompilerParams(vmem_limit_bytes=4 << 20),
        cost_estimate=pl.CostEstimate(
            flops=2 * rows * down.size, bytes_accessed=2 * down.size, transcendentals=0
        ),
        name="low_part",
    )(down, tenants, *x, after)


def forward_kernel(cuts, slots, blocks, first, slot, *refs):
    x = refs[:blocks]
    gate_out, up_out = refs[-2:]
    gate, up = (0.0, 0.0) if first else (refs[blocks][...], refs[blocks + 1][...])
    for cut in cuts:
        gate_weight, up_weight = slot(slots[cut][0]), slot(slots[cut][1])
        depth = gate_weight.shape[0]
        at = slice(cut * depth, (cut + 1) * depth)
        rows = jnp.concatenate([ref[:, at] for ref in x], axis=0)
        gate = gate + jnp.dot(rows, gate_weight, preferred_element_type=jnp.float32)
        up = up + jnp.dot(rows, up_weight, preferred_element_type=jnp.float32)
    gate_out[...] = gate
    up_out[...] = up


def forward(cuts, slots, x, store, sums, fetches, after):
    rows = sum(block.shape[0] for block in x)
    depth, hidden = store.shape[0] // SLOTS, store.shape[1]
    result = jax.ShapeDtypeStruct((rows, hidden), jnp.float32)
    store, gate, up = store_call(
        lambda *refs: forward_kernel(cuts, slots, len(x), not sums, *refs),
        store,
        fetches,
        [*x, *sums],
        [result, result],
        4 * rows * depth * hidden * len(cuts),
        "forward",
        after=after,
    )
    return store, [gate, up]


def activation_kernel(
    count, maps_slot, slot, gate_ref, up_ref, hidden_ref, low_ref, tenants_ref,
    dgate_ref, dup_ref, part_ref, spread_ref,
):
    rows = gate_ref.shape[0]
    maps = slot(maps_slot)
    own = lax.axis_index("tp")
    pick = pick_held(own, rows, count)
    mask = held_mask(pick, tenants_ref[...])
    spread = spread_rows(picked(pick, low_ref[...]), mask)
    spread_ref[...] = spread
    gate = gate_ref[...] + adapter_scale * jnp.dot(
        spread, maps, preferred_element_type=jnp.float32
    )
    s = jax.nn.sigmoid(gate)
    hidden = picked(pick, hidden_ref[...])
    dgate = (hidden * up_ref[...] * s * (1.0 + gate * (1.0 - s))).astype(jnp.bfloat16)
    dgate_ref[...] = dgate
    dup_ref[...] = (hidden * gate * s).astype(jnp.bfloat16)
    part = select_block(contracted_columns(dgate, maps), mask)
    part_ref[...] = picked(pick_given(own, rows, count), part)


def activation(maps_slot, store, sums, hidden, low, tenants, count, fetches):
    rows, width = sums[0].shape
    value = jax.ShapeDtypeStruct((rows, width), jnp.bfloat16)
    return store_call(
        lambda *refs: activation_kernel(count, maps_slot, *refs),
        store,
        fetches,
        [*sums, hidden, low, tenants],
        [
            value,
            value,
            jax.ShapeDtypeStruct((rows, ADAPTER_RANK), jnp.float32),
            jax.ShapeDtypeStruct((rows, SPREAD), jnp.bfloat16),
        ],
        4 * rows * SPREAD * width,
        "activation",
    )


def adapter_kernel(count, low_ref, tenants_ref, down_ref, earlier, own_out, other_out, spread_ref):
    half = own_out.shape[0]
    before = earlier.shape[1]
    pick = pick_held(lax.axis_index("tp"), 2 * half, count)
    spread = spread_rows(picked(pick, low_ref[...]), held_mask(pick, tenants_ref[...]))
    spread_ref[...] = spread
    part = (adapter_scale * contracted_columns(spread, down_ref[...])).astype(jnp.bfloat16)
    own_out[...] = part[:half]
    other_out[:, :before] = earlier[...]
    other_out[:, before:] = part[half:]


def adapter_part(low, tenants, down, count, earlier):
    rows, span = low.shape[0], down.shape[0]
    return pl.pallas_call(
        lambda *refs: adapter_kernel(count, *refs),
        out_shape=[
            jax.ShapeDtypeStruct((rows // 2, span), jnp.bfloat16),
            jax.ShapeDtypeStruct((rows // 2, earlier.shape[1] + span), jnp.bfloat16),
            jax.ShapeDtypeStruct((rows, SPREAD), jnp.bfloat16),
        ],
        compiler_params=pltpu.CompilerParams(vmem_limit_bytes=4 << 20),
        cost_estimate=pl.CostEstimate(
            flops=2 * rows * down.size, bytes_accessed=2 * down.size, transcendentals=0
        ),
        name="adapter_part",
    )(low, tenants, down, earlier)


def backward_kernel(slots, start, height, slot, dgate_ref, dup_ref, *refs):
    own_out, other_out = refs[-2:]
    half = own_out.shape[0]
    before = other_out.shape[1] - height
    if before:
        other_out[:, :before] = refs[0][...]
    dgate, dup = dgate_ref[...], dup_ref[...]
    for strip in range(0, height, STRIP):
        at = slice(start + strip, start + strip + STRIP)
        part = contracted_columns(dgate, slot(slots[0], at))
        part = part + contracted_columns(dup, slot(slots[1], at))
        own_out[:, strip : strip + STRIP] = part[:half]
        other_out[:, before + strip : before + strip + STRIP] = part[half:].astype(jnp.bfloat16)


def backward(slots, start, height, dgate, dup, store, fetches, after, earlier=()):
    rows, hidden = dgate.shape
    other_width = height + sum(part.shape[1] for part in earlier)
    return store_call(
        lambda *refs: backward_kernel(slots, start, height, *refs),
        store,
        fetches,
        [dgate, dup, *earlier],
        [
            jax.ShapeDtypeStruct((rows // 2, height), jnp.float32),
            jax.ShapeDtypeStruct((rows // 2, other_width), jnp.bfloat16),
        ],
        4 * rows * hidden * height,
        "backward",
        after=after,
    )


def first_halves_kernel(places, span, adapter_own, *refs):
    keep_ref, send_ref, sums = refs[-3:]
    own, came = refs[: len(places)], refs[len(places) : -3]
    half = keep_ref.shape[0]
    device = lax.axis_index("tp")
    for part, (at, group, start) in zip(own, places):
        width = part.shape[1]
        other = came[group][:, start : start + width].astype(jnp.float32)
        sums[:, at : at + width] = part[...] + other
    mine = adapter_own[...].astype(jnp.float32)
    group, start = span
    other = came[group][:, start : start + mine.shape[1]].astype(jnp.float32)
    pair = jnp.where(
        device % 2 == 0,
        jnp.concatenate([mine, other], axis=1),
        jnp.concatenate([other, mine], axis=1),
    )
    width = pair.shape[1]
    sums[:, pl.ds(pl.multiple_of(device // 2 * width, width), width)] += pair
    keep_ref[...] = sums[:half, :]
    send_ref[...] = sums[half:, :].astype(jnp.bfloat16)


def first_halves(own, places, adapter_own, span, came):
    rows = adapter_own.shape[0]
    width = sum(part.shape[1] for part in own)
    return pl.pallas_call(
        lambda *refs: first_halves_kernel(places, span, *refs),
        out_shape=[
            jax.ShapeDtypeStruct((rows // 2, width), jnp.float32),
            jax.ShapeDtypeStruct((rows // 2, width), jnp.bfloat16),
        ],
        scratch_shapes=[pltpu.VMEM((rows, width), jnp.float32)],
        compiler_params=pltpu.CompilerParams(vmem_limit_bytes=40 << 20),
        name="first_halves",
    )(adapter_own, *own, *came)


def halves(keep, came, after):
    rows, width = keep.shape

    def halves_kernel(keep_ref, came_ref, *refs):
        keep_out, send_out = refs[-2:]
        total = keep_ref[...] + came_ref[...].astype(jnp.float32)
        keep_out[...] = total[: rows // 2]
        send_out[...] = total[rows // 2 :].astype(jnp.bfloat16)

    return pl.pallas_call(
        halves_kernel,
        in_specs=[VMEM, VMEM] + [ANY] * len(after),
        out_shape=[
            jax.ShapeDtypeStruct((rows // 2, width), jnp.float32),
            jax.ShapeDtypeStruct((rows // 2, width), jnp.bfloat16),
        ],
        compiler_params=pltpu.CompilerParams(vmem_limit_bytes=40 << 20),
        name="halves",
    )(keep, came, *after)


def quarters(keep, came, after):
    rows, width = keep.shape
    quarter = rows // 4

    def quarters_kernel(keep_ref, came_ref, *refs):
        keep_out, *sends = refs[-4:]
        total = keep_ref[...] + came_ref[...].astype(jnp.float32)
        keep_out[...] = total[:quarter]
        for n, send_out in enumerate(sends, 1):
            send_out[...] = total[n * quarter : (n + 1) * quarter].astype(jnp.bfloat16)

    return pl.pallas_call(
        quarters_kernel,
        in_specs=[VMEM, VMEM] + [ANY] * len(after),
        out_shape=[jax.ShapeDtypeStruct((quarter, width), jnp.float32)]
        + [jax.ShapeDtypeStruct((quarter, width), jnp.bfloat16)] * 3,
        compiler_params=pltpu.CompilerParams(vmem_limit_bytes=40 << 20),
        name="quarters",
    )(keep, came, *after)


def final(keep, came, after):
    def final_kernel(keep_ref, *refs):
        total = keep_ref[...]
        for ref in refs[: len(came)]:
            total = total + ref[...].astype(jnp.float32)
        refs[-1][...] = total.astype(jnp.bfloat16)

    return pl.pallas_call(
        final_kernel,
        in_specs=[VMEM] * (1 + len(came)) + [ANY] * len(after),
        out_shape=jax.ShapeDtypeStruct(keep.shape, jnp.bfloat16),
        compiler_params=pltpu.CompilerParams(vmem_limit_bytes=40 << 20),
        name="final",
    )(keep, *came, *after)


def outer_kernel(left_ref, right_ref, *refs):
    out_ref, token_ref = refs[-2:]
    out_ref[...] = contracted_rows(
        left_ref[...] * jnp.bfloat16(adapter_scale), right_ref[...]
    ).astype(jnp.bfloat16)
    token_ref[...] = jnp.zeros_like(token_ref)


def outer(left, right, name, after, parts=1, span=(0, 1), earlier=None):
    rows, height = left.shape
    width = right.shape[1]
    block = block_of(height // parts, 512)
    if block % 128:
        block = height // parts
    per_part = height // parts // block
    first, steps = span[0] * per_part, (span[1] - span[0]) * per_part
    kept = [] if earlier is None else [earlier]
    return pl.pallas_call(
        outer_kernel,
        grid=(steps,),
        in_specs=[
            pl.BlockSpec((rows, block), lambda k: (0, k + first)),
            pl.BlockSpec((rows, width), lambda k: (0, 0)),
            ANY,
        ]
        + [ANY] * len(kept),
        out_specs=[
            pl.BlockSpec((block, width), lambda k: (k + first, 0)),
            pl.BlockSpec((8, 128), lambda k: (0, 0)),
        ],
        out_shape=[
            jax.ShapeDtypeStruct((height, width), jnp.bfloat16),
            jax.ShapeDtypeStruct((8, 128), jnp.float32),
        ],
        input_output_aliases={3: 0} if kept else {},
        compiler_params=pltpu.CompilerParams(vmem_limit_bytes=24 << 20),
        cost_estimate=pl.CostEstimate(
            flops=2 * rows * steps * block * width,
            bytes_accessed=2 * steps * block * width,
            transcendentals=0,
        ),
        name=name,
    )(left, right, after, *kept)


def add_kernel(left_ref, right_ref, out_ref):
    out_ref[...] = left_ref[...] + right_ref[...]


def plus(left, right):
    return pl.pallas_call(
        add_kernel,
        out_shape=jax.ShapeDtypeStruct(left.shape, left.dtype),
        compiler_params=pltpu.CompilerParams(vmem_limit_bytes=2 << 20),
        name="plus",
    )(left, right)


def swapped(block, hop):
    return lax.ppermute(block, "tp", [(i, i ^ hop) for i in range(lax.axis_size("tp"))])


def local(
    normed_layer_input,
    hidden_unit_gradient,
    gate_weight,
    up_weight,
    adapter_down_maps,
    adapter_up_maps,
    token_tenant_index,
):
    count = lax.axis_size("tp")
    own_rows, width = normed_layer_input.shape
    rows = own_rows * count
    hops = [1 << bit for bit in range(count.bit_length() - 1)]
    tenants = token_tenant_index.reshape(1, rows)

    def pair(cut, first, second):
        return [(gate_weight, cut, first), (up_weight, cut, second)]

    def mark(slot, token_ref):
        token_ref[...] = jnp.zeros_like(token_ref)

    mark_shape = jax.ShapeDtypeStruct((8, 128), jnp.float32)
    store = jax.ShapeDtypeStruct(
        (SLOTS * width // CUTS, gate_weight.shape[1]), gate_weight.dtype
    )
    far, near = hops[-1], hops[-2]
    came = [swapped(normed_layer_input, hop) for hop in (near, far, near | far)]
    store, token = store_call(mark, store, pair(0, 0, 1), [], [mark_shape], 0, "fetch")
    block = stacked([normed_layer_input, *came], [token])
    for hop in reversed(hops[2:-2]):
        block = stacked([block, swapped(block, hop)])
    other = swapped(block, hops[1])
    store, token = store_call(
        mark, store, [(gate_weight, 1, 2)], [], [mark_shape], 0, "fetch", after=[block]
    )
    block = stacked([block, other], [token])
    x = [block, swapped(block, 1)]
    store, token = store_call(
        mark, store, [(up_weight, 1, 3, 0)], [], [mark_shape], 0, "fetch", after=[block]
    )

    input_span, low = low_part(adapter_down_maps, tenants, x, count, token)
    store, token = store_call(
        mark, store, [(up_weight, 1, 3, 1)], [], [mark_shape], 0, "fetch", after=[low]
    )
    sums = []
    slots = {0: (0, 1), 1: (2, 3), 2: (4, 5), 3: (0, 1)}
    step = 0
    for cuts, fetches in (
        ((0, 1), pair(2, 4, 5)), ((2,), pair(3, 0, 1)), ((3,), [(adapter_up_maps, 0, 2)])
    ):
        after = [low]
        if step < len(hops):
            low = plus(low, swapped(low, hops[step]))
            step += 1
        store, sums = forward(cuts, slots, x, store, sums, fetches, after)
    for hop in hops[step:]:
        low = plus(low, swapped(low, hop))
    store, dgate, dup, low_grad, input_spread = activation(
        2, store, sums, hidden_unit_gradient, low, tenants, count, []
    )

    later_hops = hops[1:] + hops[:1]
    depth = width // CUTS
    part_list = [
        (3, (0, 1), 0, depth, [(gate_weight, 1, 2)], True),
        (2, (4, 5), 0, depth, [(gate_weight, 0, 0)], False),
        (1, (2, 3), 0, depth, [(up_weight, 0, 1)], True),
        (0, (0, 1), depth // 2, depth // 2, [], True),
        (0, (0, 1), 0, depth // 2, [], False),
    ]
    own_parts, places, came, waiting = [], [], [], []
    for n, (piece, slots, first, height, fetches, waits) in enumerate(part_list):
        after = [low_grad]
        if n == len(part_list) - 1:
            span = (len(came), waiting[0].shape[1])
            adapter_own, to_send, grad_spread = adapter_part(
                low_grad, tenants, adapter_down_maps, count, waiting[0]
            )
            came.append(swapped(to_send, 1))
            after, waiting = [to_send], []
        else:
            turns = later_hops[:1] if n < len(part_list) - 2 else later_hops
            later_hops = later_hops[len(turns) :]
            for hop in turns:
                low_grad = plus(low_grad, swapped(low_grad, hop))
        begin = sum(part.shape[1] for part in waiting)
        store, own_part, other_part = backward(
            slots, first, height, dgate, dup, store, fetches, after, waiting
        )
        own_parts.append(own_part)
        places.append((piece * depth + first, len(came), begin))
        waiting = [other_part]
        if not waits:
            came.append(swapped(other_part, 1))
            waiting = []

    keep, send = first_halves(own_parts, places, adapter_own, span, came)
    halvings = [block_owner(0, 1 << bit, count) for bit in reversed(range(2, len(hops) - 1))]
    for n, hop in enumerate(halvings):
        came = swapped(send, hop)
        beside = [send]
        if n == len(halvings) - 1:
            up_map_gradient, token = outer(input_spread, dgate, "up_maps", send, 4, (0, 3))
            keep, *sends = quarters(keep, came, [token])
        else:
            keep, send = halves(keep, came, beside)
    came = [swapped(sends[n - 1], block_owner(0, n, count)) for n in (3, 2, 1)]
    up_map_gradient, token = outer(
        input_spread, dgate, "up_maps", sends[0], 4, (3, 4), up_map_gradient
    )
    down_map_gradient, other_token = outer(input_span, grad_spread, "down_maps", sends[0])
    return (final(keep, came, [token, other_token]), down_map_gradient, up_map_gradient)


def solution(mesh):
    placed = (
        P(("groups", "tp"), None),
        P("groups", "tp"),
        P(None, "tp"),
        P(None, "tp"),
        P("tp", None),
        P(None, "tp"),
        P("groups"),
    )
    return jax.shard_map(
        local,
        mesh=mesh,
        in_specs=placed,
        out_specs=(P(("groups", "tp"), None), P("tp", "groups"), P("groups", "tp")),
        check_vma=False,
    )
```

```python
import jax
import jax.numpy as jnp
from jax import lax
from jax.experimental import pallas as pl
from jax.experimental.pallas import tpu as pltpu
from jax.sharding import PartitionSpec as P

ADAPTER_RANK = 64
TENANT_COUNT = 32
SPREAD = ADAPTER_RANK * TENANT_COUNT

adapter_scale = 2.0


def block_of(size, largest):
    block = largest
    while size % block:
        block //= 2
    return block


def contracted_rows(left, right):
    return lax.dot_general(
        left, right, (((0,), (0,)), ((), ())), preferred_element_type=jnp.float32
    )


def contracted_columns(left, right):
    return lax.dot_general(
        left, right, (((1,), (1,)), ((), ())), preferred_element_type=jnp.float32
    )


def tenant_mask(tenants, rows):
    columns = lax.broadcasted_iota(jnp.int32, (rows, SPREAD), 1) // ADAPTER_RANK
    return tenants == columns


def select_block(wide_rows, mask):
    kept = jnp.where(mask, wide_rows, 0.0)
    pair = 2 * ADAPTER_RANK
    total = kept[:, :pair]
    for start in range(pair, SPREAD, pair):
        total = total + kept[:, start : start + pair]
    return total[:, :ADAPTER_RANK] + total[:, ADAPTER_RANK:]


def spread_rows(low_rows, mask):
    pair = jnp.concatenate([low_rows, low_rows], axis=1)
    wide = jnp.concatenate([pair] * (TENANT_COUNT // 2), axis=1)
    return jnp.where(mask, wide, 0.0).astype(jnp.bfloat16)


VMEM = pl.BlockSpec(memory_space=pltpu.VMEM)
ANY = pl.BlockSpec(memory_space=pl.ANY)
CUTS = 4
COPIES = 8
STRIP = 256
SLOTS = 6
STORE_GRANT = 10 << 20


def store_call(kernel, store, fetches, operands, out_shapes, flops, name, after=()):
    new = isinstance(store, jax.ShapeDtypeStruct)
    depth = store.shape[0] // SLOTS
    part = depth // COPIES
    sources = []
    for array, *_ in fetches:
        if not any(array is known for known in sources):
            sources.append(array)
    places = [next(i for i, known in enumerate(sources) if known is f[0]) for f in fetches]
    n_in, n_out, n_hbm = len(operands), len(out_shapes), len(sources)

    def body(*refs):
        if not new:
            refs = refs[1:]
        ins, hbm = refs[:n_in], refs[n_in : n_in + n_hbm]
        rest = refs[n_in + n_hbm + len(after) :]
        store_ref, outs, scratch = rest[0], rest[1 : 1 + n_out], rest[1 + n_out :]
        copies = []
        for n, (place, (_, piece, slot, *half)) in enumerate(zip(places, fetches)):
            for k in range(COPIES):
                if half and k // (COPIES // 2) != half[0]:
                    continue
                copies.append(
                    pltpu.make_async_copy(
                        hbm[place].at[pl.ds(piece * depth + k * part, part)],
                        store_ref.at[pl.ds(slot * depth + k * part, part)],
                        scratch[0].at[n * COPIES + k],
                    )
                )
        for copy in copies:
            copy.start()
        def rows_of(slot, at=slice(0, depth)):
            return store_ref[slot * depth + at.start : slot * depth + at.stop, :]

        kernel(rows_of, *ins, *outs)
        for copy in copies:
            copy.wait()

    moved = 2 * depth * store.shape[1] * len(fetches)
    return pl.pallas_call(
        body,
        in_specs=[VMEM] * (n_in + (not new)) + [ANY] * (n_hbm + len(after)),
        out_specs=[VMEM] * (1 + n_out),
        out_shape=[pltpu.VMEM(store.shape, store.dtype), *out_shapes],
        input_output_aliases={} if new else {0: 0},
        scratch_shapes=[pltpu.SemaphoreType.DMA((COPIES * len(fetches),))] if fetches else [],
        compiler_params=pltpu.CompilerParams(vmem_limit_bytes=STORE_GRANT),
        cost_estimate=pl.CostEstimate(flops=flops, bytes_accessed=moved, transcendentals=0),
        name=name,
    )(
        *([] if new else [store]),
        *operands,
        *[pltpu.with_memory_space_constraint(array, pltpu.HBM) for array in sources],
        *after,
    )


def stacked(blocks, after=()):
    rows = sum(block.shape[0] for block in blocks)

    def stack_kernel(*refs):
        refs[-1][...] = jnp.concatenate([ref[...] for ref in refs[: len(blocks)]], axis=0)

    return pl.pallas_call(
        stack_kernel,
        in_specs=[VMEM] * len(blocks) + [ANY] * len(after),
        out_shape=jax.ShapeDtypeStruct((rows, blocks[0].shape[1]), blocks[0].dtype),
        compiler_params=pltpu.CompilerParams(vmem_limit_bytes=4 << 20),
        name="stacked",
    )(*blocks, *after)


def block_owner(own, block, count):
    bits = count.bit_length() - 1
    hops = [1 << (bits - 2), 1 << (bits - 1)] + [1 << bit for bit in reversed(range(bits - 2))]
    for n, hop in enumerate(hops):
        own = own ^ (((block >> n) & 1) * hop)
    return own


def source_of(own, row, rows, count):
    tokens = rows // count
    return block_owner(own, row // tokens, count) * tokens + row % tokens


def pick_held(own, rows, count):
    held = source_of(own, lax.broadcasted_iota(jnp.int32, (rows, rows), 0), rows, count)
    return held == lax.broadcasted_iota(jnp.int32, (rows, rows), 1)


def pick_given(own, rows, count):
    held = source_of(own, lax.broadcasted_iota(jnp.int32, (rows, rows), 1), rows, count)
    return held == lax.broadcasted_iota(jnp.int32, (rows, rows), 0)


def picked(pick, block):
    if block.dtype == jnp.bfloat16:
        return jnp.dot(pick.astype(jnp.bfloat16), block, preferred_element_type=jnp.float32)
    return jnp.dot(pick.astype(jnp.float32), block, precision=lax.Precision.HIGHEST)


def held_mask(pick, tenants_row):
    tenants = jnp.sum(jnp.where(pick, tenants_row, 0).astype(jnp.float32), axis=1, keepdims=True)
    return tenant_mask(tenants.astype(jnp.int32), pick.shape[0])


def low_kernel(count, aligned, down_ref, tenants_ref, *refs):
    x, (span_out, low_ref) = refs[:-3], refs[-2:]
    own = lax.axis_index("tp")
    if aligned:
        width = down_ref.shape[0]
        at = pl.ds(pl.multiple_of(own * width, width), width)
        span = jnp.concatenate([ref[:, at] for ref in x], axis=0)
    else:
        span = jnp.concatenate([ref[...] for ref in x], axis=0)
    span_out[...] = span
    rows = span.shape[0]
    wide = jnp.dot(span, down_ref[...], preferred_element_type=jnp.float32)
    low = select_block(wide, held_mask(pick_held(own, rows, count), tenants_ref[...]))
    low_ref[...] = picked(pick_given(own, rows, count), low)


def low_part(down, tenants, x, count, after):
    rows, span = sum(block.shape[0] for block in x), down.shape[0]
    aligned = span % 128 == 0
    if not aligned:
        x = [
            lax.dynamic_slice(
                block,
                (0, lax.axis_index("tp") * span),
                (block.shape[0], span),
                allow_negative_indices=False,
            )
            for block in x
        ]
    return pl.pallas_call(
        lambda *refs: low_kernel(count, aligned, *refs),
        in_specs=[VMEM] * (2 + len(x)) + [ANY],
        out_shape=[
            jax.ShapeDtypeStruct((rows, span), x[0].dtype),
            jax.ShapeDtypeStruct((rows, ADAPTER_RANK), jnp.float32),
        ],
        compiler_params=pltpu.CompilerParams(vmem_limit_bytes=4 << 20),
        cost_estimate=pl.CostEstimate(
            flops=2 * rows * down.size, bytes_accessed=2 * down.size, transcendentals=0
        ),
        name="low_part",
    )(down, tenants, *x, after)


def forward_kernel(cuts, slots, blocks, first, slot, *refs):
    x = refs[:blocks]
    gate_out, up_out = refs[-2:]
    gate, up = (0.0, 0.0) if first else (refs[blocks][...], refs[blocks + 1][...])
    for cut in cuts:
        gate_weight, up_weight = slot(slots[cut][0]), slot(slots[cut][1])
        depth = gate_weight.shape[0]
        at = slice(cut * depth, (cut + 1) * depth)
        rows = jnp.concatenate([ref[:, at] for ref in x], axis=0)
        gate = gate + jnp.dot(rows, gate_weight, preferred_element_type=jnp.float32)
        up = up + jnp.dot(rows, up_weight, preferred_element_type=jnp.float32)
    gate_out[...] = gate
    up_out[...] = up


def forward(cuts, slots, x, store, sums, fetches, after):
    rows = sum(block.shape[0] for block in x)
    depth, hidden = store.shape[0] // SLOTS, store.shape[1]
    result = jax.ShapeDtypeStruct((rows, hidden), jnp.float32)
    store, gate, up = store_call(
        lambda *refs: forward_kernel(cuts, slots, len(x), not sums, *refs),
        store,
        fetches,
        [*x, *sums],
        [result, result],
        4 * rows * depth * hidden * len(cuts),
        "forward",
        after=after,
    )
    return store, [gate, up]


def activation_kernel(
    count, maps_slot, slot, gate_ref, up_ref, hidden_ref, low_ref, tenants_ref,
    dgate_ref, dup_ref, part_ref, spread_ref,
):
    rows = gate_ref.shape[0]
    maps = slot(maps_slot)
    own = lax.axis_index("tp")
    pick = pick_held(own, rows, count)
    mask = held_mask(pick, tenants_ref[...])
    spread = spread_rows(picked(pick, low_ref[...]), mask)
    spread_ref[...] = spread
    gate = gate_ref[...] + adapter_scale * jnp.dot(
        spread, maps, preferred_element_type=jnp.float32
    )
    s = jax.nn.sigmoid(gate)
    hidden = picked(pick, hidden_ref[...])
    dgate = (hidden * up_ref[...] * s * (1.0 + gate * (1.0 - s))).astype(jnp.bfloat16)
    dgate_ref[...] = dgate
    dup_ref[...] = (hidden * gate * s).astype(jnp.bfloat16)
    part = select_block(contracted_columns(dgate, maps), mask)
    part_ref[...] = picked(pick_given(own, rows, count), part)


def activation(maps_slot, store, sums, hidden, low, tenants, count, fetches):
    rows, width = sums[0].shape
    value = jax.ShapeDtypeStruct((rows, width), jnp.bfloat16)
    return store_call(
        lambda *refs: activation_kernel(count, maps_slot, *refs),
        store,
        fetches,
        [*sums, hidden, low, tenants],
        [
            value,
            value,
            jax.ShapeDtypeStruct((rows, ADAPTER_RANK), jnp.float32),
            jax.ShapeDtypeStruct((rows, SPREAD), jnp.bfloat16),
        ],
        4 * rows * SPREAD * width,
        "activation",
    )


def adapter_kernel(count, low_ref, tenants_ref, down_ref, earlier, own_out, other_out, spread_ref):
    half = own_out.shape[0]
    before = earlier.shape[1]
    pick = pick_held(lax.axis_index("tp"), 2 * half, count)
    spread = spread_rows(picked(pick, low_ref[...]), held_mask(pick, tenants_ref[...]))
    spread_ref[...] = spread
    part = (adapter_scale * contracted_columns(spread, down_ref[...])).astype(jnp.bfloat16)
    own_out[...] = part[:half]
    other_out[:, :before] = earlier[...]
    other_out[:, before:] = part[half:]


def adapter_part(low, tenants, down, count, earlier):
    rows, span = low.shape[0], down.shape[0]
    return pl.pallas_call(
        lambda *refs: adapter_kernel(count, *refs),
        out_shape=[
            jax.ShapeDtypeStruct((rows // 2, span), jnp.bfloat16),
            jax.ShapeDtypeStruct((rows // 2, earlier.shape[1] + span), jnp.bfloat16),
            jax.ShapeDtypeStruct((rows, SPREAD), jnp.bfloat16),
        ],
        compiler_params=pltpu.CompilerParams(vmem_limit_bytes=4 << 20),
        cost_estimate=pl.CostEstimate(
            flops=2 * rows * down.size, bytes_accessed=2 * down.size, transcendentals=0
        ),
        name="adapter_part",
    )(low, tenants, down, earlier)


def backward_kernel(slots, start, height, slot, dgate_ref, dup_ref, *refs):
    own_out, other_out = refs[-2:]
    half = own_out.shape[0]
    before = other_out.shape[1] - height
    if before:
        other_out[:, :before] = refs[0][...]
    dgate, dup = dgate_ref[...], dup_ref[...]
    for strip in range(0, height, STRIP):
        at = slice(start + strip, start + strip + STRIP)
        part = contracted_columns(dgate, slot(slots[0], at))
        part = part + contracted_columns(dup, slot(slots[1], at))
        own_out[:, strip : strip + STRIP] = part[:half]
        other_out[:, before + strip : before + strip + STRIP] = part[half:].astype(jnp.bfloat16)


def backward(slots, start, height, dgate, dup, store, fetches, after, earlier=()):
    rows, hidden = dgate.shape
    other_width = height + sum(part.shape[1] for part in earlier)
    return store_call(
        lambda *refs: backward_kernel(slots, start, height, *refs),
        store,
        fetches,
        [dgate, dup, *earlier],
        [
            jax.ShapeDtypeStruct((rows // 2, height), jnp.float32),
            jax.ShapeDtypeStruct((rows // 2, other_width), jnp.bfloat16),
        ],
        4 * rows * hidden * height,
        "backward",
        after=after,
    )


def first_halves_kernel(places, span, adapter_own, *refs):
    keep_ref, send_ref, sums = refs[-3:]
    own, came = refs[: len(places)], refs[len(places) : -3]
    half = keep_ref.shape[0]
    device = lax.axis_index("tp")
    for part, (at, group, start) in zip(own, places):
        width = part.shape[1]
        other = came[group][:, start : start + width].astype(jnp.float32)
        sums[:, at : at + width] = part[...] + other
    mine = adapter_own[...].astype(jnp.float32)
    group, start = span
    other = came[group][:, start : start + mine.shape[1]].astype(jnp.float32)
    pair = jnp.where(
        device % 2 == 0,
        jnp.concatenate([mine, other], axis=1),
        jnp.concatenate([other, mine], axis=1),
    )
    width = pair.shape[1]
    sums[:, pl.ds(pl.multiple_of(device // 2 * width, width), width)] += pair
    keep_ref[...] = sums[:half, :]
    send_ref[...] = sums[half:, :].astype(jnp.bfloat16)


def first_halves(own, places, adapter_own, span, came):
    rows = adapter_own.shape[0]
    width = sum(part.shape[1] for part in own)
    return pl.pallas_call(
        lambda *refs: first_halves_kernel(places, span, *refs),
        out_shape=[
            jax.ShapeDtypeStruct((rows // 2, width), jnp.float32),
            jax.ShapeDtypeStruct((rows // 2, width), jnp.bfloat16),
        ],
        scratch_shapes=[pltpu.VMEM((rows, width), jnp.float32)],
        compiler_params=pltpu.CompilerParams(vmem_limit_bytes=40 << 20),
        name="first_halves",
    )(adapter_own, *own, *came)


def halves(keep, came, after):
    rows, width = keep.shape

    def halves_kernel(keep_ref, came_ref, *refs):
        keep_out, send_out = refs[-2:]
        total = keep_ref[...] + came_ref[...].astype(jnp.float32)
        keep_out[...] = total[: rows // 2]
        send_out[...] = total[rows // 2 :].astype(jnp.bfloat16)

    return pl.pallas_call(
        halves_kernel,
        in_specs=[VMEM, VMEM] + [ANY] * len(after),
        out_shape=[
            jax.ShapeDtypeStruct((rows // 2, width), jnp.float32),
            jax.ShapeDtypeStruct((rows // 2, width), jnp.bfloat16),
        ],
        compiler_params=pltpu.CompilerParams(vmem_limit_bytes=40 << 20),
        name="halves",
    )(keep, came, *after)


def quarters(keep, came, after):
    rows, width = keep.shape
    quarter = rows // 4

    def quarters_kernel(keep_ref, came_ref, *refs):
        keep_out, *sends = refs[-4:]
        total = keep_ref[...] + came_ref[...].astype(jnp.float32)
        keep_out[...] = total[:quarter]
        for n, send_out in enumerate(sends, 1):
            send_out[...] = total[n * quarter : (n + 1) * quarter].astype(jnp.bfloat16)

    return pl.pallas_call(
        quarters_kernel,
        in_specs=[VMEM, VMEM] + [ANY] * len(after),
        out_shape=[jax.ShapeDtypeStruct((quarter, width), jnp.float32)]
        + [jax.ShapeDtypeStruct((quarter, width), jnp.bfloat16)] * 3,
        compiler_params=pltpu.CompilerParams(vmem_limit_bytes=40 << 20),
        name="quarters",
    )(keep, came, *after)


def final(keep, came, after):
    def final_kernel(keep_ref, *refs):
        total = keep_ref[...]
        for ref in refs[: len(came)]:
            total = total + ref[...].astype(jnp.float32)
        refs[-1][...] = total.astype(jnp.bfloat16)

    return pl.pallas_call(
        final_kernel,
        in_specs=[VMEM] * (1 + len(came)) + [ANY] * len(after),
        out_shape=jax.ShapeDtypeStruct(keep.shape, jnp.bfloat16),
        compiler_params=pltpu.CompilerParams(vmem_limit_bytes=40 << 20),
        name="final",
    )(keep, *came, *after)


def outer_kernel(left_ref, right_ref, *refs):
    out_ref, token_ref = refs[-2:]
    out_ref[...] = contracted_rows(
        left_ref[...] * jnp.bfloat16(adapter_scale), right_ref[...]
    ).astype(jnp.bfloat16)
    token_ref[...] = jnp.zeros_like(token_ref)


def outer(left, right, name, after, largest):
    rows, height = left.shape
    width = right.shape[1]
    block = block_of(height, largest)
    if block % 128:
        block = height
    return pl.pallas_call(
        outer_kernel,
        grid=(height // block,),
        in_specs=[
            pl.BlockSpec((rows, block), lambda k: (0, k)),
            pl.BlockSpec((rows, width), lambda k: (0, 0)),
            ANY,
        ],
        out_specs=[
            pl.BlockSpec((block, width), lambda k: (k, 0)),
            pl.BlockSpec((8, 128), lambda k: (0, 0)),
        ],
        out_shape=[
            jax.ShapeDtypeStruct((height, width), jnp.bfloat16),
            jax.ShapeDtypeStruct((8, 128), jnp.float32),
        ],
        compiler_params=pltpu.CompilerParams(vmem_limit_bytes=24 << 20),
        cost_estimate=pl.CostEstimate(
            flops=2 * rows * height * width, bytes_accessed=2 * height * width, transcendentals=0
        ),
        name=name,
    )(left, right, after)


def add_kernel(left_ref, right_ref, out_ref):
    out_ref[...] = left_ref[...] + right_ref[...]


def plus(left, right):
    return pl.pallas_call(
        add_kernel,
        out_shape=jax.ShapeDtypeStruct(left.shape, left.dtype),
        compiler_params=pltpu.CompilerParams(vmem_limit_bytes=2 << 20),
        name="plus",
    )(left, right)


def swapped(block, hop):
    return lax.ppermute(block, "tp", [(i, i ^ hop) for i in range(lax.axis_size("tp"))])


def local(
    normed_layer_input,
    hidden_unit_gradient,
    gate_weight,
    up_weight,
    adapter_down_maps,
    adapter_up_maps,
    token_tenant_index,
):
    count = lax.axis_size("tp")
    own_rows, width = normed_layer_input.shape
    rows = own_rows * count
    hops = [1 << bit for bit in range(count.bit_length() - 1)]
    tenants = token_tenant_index.reshape(1, rows)

    def pair(cut, first, second):
        return [(gate_weight, cut, first), (up_weight, cut, second)]

    def mark(slot, token_ref):
        token_ref[...] = jnp.zeros_like(token_ref)

    mark_shape = jax.ShapeDtypeStruct((8, 128), jnp.float32)
    store = jax.ShapeDtypeStruct(
        (SLOTS * width // CUTS, gate_weight.shape[1]), gate_weight.dtype
    )
    far, near = hops[-1], hops[-2]
    came = [swapped(normed_layer_input, hop) for hop in (near, far, near | far)]
    store, token = store_call(mark, store, pair(0, 0, 1), [], [mark_shape], 0, "fetch")
    block = stacked([normed_layer_input, *came], [token])
    for hop in reversed(hops[2:-2]):
        block = stacked([block, swapped(block, hop)])
    other = swapped(block, hops[1])
    store, token = store_call(
        mark,
        store,
        [(gate_weight, 1, 2), (up_weight, 1, 3, 0)],
        [],
        [mark_shape],
        0,
        "fetch",
        after=[block],
    )
    block = stacked([block, other], [token])
    x = [block, swapped(block, 1)]
    store, token = store_call(
        mark, store, [(up_weight, 1, 3, 1)], [], [mark_shape], 0, "fetch", after=[block]
    )

    input_span, low = low_part(adapter_down_maps, tenants, x, count, token)
    sums = []
    slots = {0: (0, 1), 1: (2, 3), 2: (4, 5), 3: (0, 1)}
    step = 0
    for cuts, fetches in (
        ((0, 1), pair(2, 4, 5)), ((2,), pair(3, 0, 1)), ((3,), [(adapter_up_maps, 0, 2)])
    ):
        after = [low]
        if step < len(hops):
            low = plus(low, swapped(low, hops[step]))
            step += 1
        store, sums = forward(cuts, slots, x, store, sums, fetches, after)
    for hop in hops[step:]:
        low = plus(low, swapped(low, hop))
    store, dgate, dup, low_grad, input_spread = activation(
        2, store, sums, hidden_unit_gradient, low, tenants, count, []
    )

    later_hops = hops[1:] + hops[:1]
    depth = width // CUTS
    part_list = [
        (3, (0, 1), 0, depth, [(gate_weight, 1, 2)], True),
        (2, (4, 5), 0, depth, [(gate_weight, 0, 0)], False),
        (1, (2, 3), 0, depth, [(up_weight, 0, 1)], True),
        (0, (0, 1), depth // 2, depth // 2, [], True),
        (0, (0, 1), 0, depth // 2, [], False),
    ]
    own_parts, places, came, waiting = [], [], [], []
    for n, (piece, slots, first, height, fetches, waits) in enumerate(part_list):
        after = [low_grad]
        if n == len(part_list) - 1:
            span = (len(came), waiting[0].shape[1])
            adapter_own, to_send, grad_spread = adapter_part(
                low_grad, tenants, adapter_down_maps, count, waiting[0]
            )
            came.append(swapped(to_send, 1))
            after, waiting = [to_send], []
        else:
            turns = later_hops[:1] if n < len(part_list) - 2 else later_hops
            later_hops = later_hops[len(turns) :]
            for hop in turns:
                low_grad = plus(low_grad, swapped(low_grad, hop))
        begin = sum(part.shape[1] for part in waiting)
        store, own_part, other_part = backward(
            slots, first, height, dgate, dup, store, fetches, after, waiting
        )
        own_parts.append(own_part)
        places.append((piece * depth + first, len(came), begin))
        waiting = [other_part]
        if not waits:
            came.append(swapped(other_part, 1))
            waiting = []

    keep, send = first_halves(own_parts, places, adapter_own, span, came)
    halvings = [block_owner(0, 1 << bit, count) for bit in reversed(range(2, len(hops) - 1))]
    for n, hop in enumerate(halvings):
        came = swapped(send, hop)
        beside = [send]
        if n == len(halvings) - 1:
            up_map_gradient, token = outer(input_spread, dgate, "up_maps", send, 512)
            keep, *sends = quarters(keep, came, [token])
        else:
            keep, send = halves(keep, came, beside)
    came = [swapped(sends[n - 1], block_owner(0, n, count)) for n in (3, 2, 1)]
    down_map_gradient, token = outer(input_span, grad_spread, "down_maps", sends[0], 256)
    return (final(keep, came, [token]), down_map_gradient, up_map_gradient)


def solution(mesh):
    placed = (
        P(("groups", "tp"), None),
        P("groups", "tp"),
        P(None, "tp"),
        P(None, "tp"),
        P("tp", None),
        P(None, "tp"),
        P("groups"),
    )
    return jax.shard_map(
        local,
        mesh=mesh,
        in_specs=placed,
        out_specs=(P(("groups", "tp"), None), P("tp", "groups"), P("groups", "tp")),
        check_vma=False,
    )
```

```python
import jax
import jax.numpy as jnp
from jax import lax
from jax.experimental import pallas as pl
from jax.experimental.pallas import tpu as pltpu
from jax.sharding import PartitionSpec as P

ADAPTER_RANK = 64
TENANT_COUNT = 32
SPREAD = ADAPTER_RANK * TENANT_COUNT

adapter_scale = 2.0


def block_of(size, largest):
    block = largest
    while size % block:
        block //= 2
    return block


def contracted_rows(left, right):
    return lax.dot_general(
        left, right, (((0,), (0,)), ((), ())), preferred_element_type=jnp.float32
    )


def contracted_columns(left, right):
    return lax.dot_general(
        left, right, (((1,), (1,)), ((), ())), preferred_element_type=jnp.float32
    )


def tenant_mask(tenants, rows):
    columns = lax.broadcasted_iota(jnp.int32, (rows, SPREAD), 1) // ADAPTER_RANK
    return tenants == columns


def select_block(wide_rows, mask):
    kept = jnp.where(mask, wide_rows, 0.0)
    pair = 2 * ADAPTER_RANK
    total = kept[:, :pair]
    for start in range(pair, SPREAD, pair):
        total = total + kept[:, start : start + pair]
    return total[:, :ADAPTER_RANK] + total[:, ADAPTER_RANK:]


def spread_rows(low_rows, mask):
    pair = jnp.concatenate([low_rows, low_rows], axis=1)
    wide = jnp.concatenate([pair] * (TENANT_COUNT // 2), axis=1)
    return jnp.where(mask, wide, 0.0).astype(jnp.bfloat16)


VMEM = pl.BlockSpec(memory_space=pltpu.VMEM)
ANY = pl.BlockSpec(memory_space=pl.ANY)
CUTS = 4
COPIES = 16
STRIP = 256
SLOTS = 6
STORE_GRANT = 10 << 20


def store_call(kernel, store, fetches, operands, out_shapes, flops, name, after=()):
    new = isinstance(store, jax.ShapeDtypeStruct)
    depth = store.shape[0] // SLOTS
    part = depth // COPIES
    sources = []
    for array, *_ in fetches:
        if not any(array is known for known in sources):
            sources.append(array)
    places = [next(i for i, known in enumerate(sources) if known is f[0]) for f in fetches]
    n_in, n_out, n_hbm = len(operands), len(out_shapes), len(sources)

    def body(*refs):
        if not new:
            refs = refs[1:]
        ins, hbm = refs[:n_in], refs[n_in : n_in + n_hbm]
        rest = refs[n_in + n_hbm + len(after) :]
        store_ref, outs, scratch = rest[0], rest[1 : 1 + n_out], rest[1 + n_out :]
        copies = []
        for n, (place, (_, piece, slot, *half)) in enumerate(zip(places, fetches)):
            for k in range(COPIES):
                if half and k // (COPIES // 2) != half[0]:
                    continue
                copies.append(
                    pltpu.make_async_copy(
                        hbm[place].at[pl.ds(piece * depth + k * part, part)],
                        store_ref.at[pl.ds(slot * depth + k * part, part)],
                        scratch[0].at[n * COPIES + k],
                    )
                )
        for copy in copies:
            copy.start()
        def rows_of(slot, at=slice(0, depth)):
            return store_ref[slot * depth + at.start : slot * depth + at.stop, :]

        kernel(rows_of, *ins, *outs)
        for copy in copies:
            copy.wait()

    moved = 2 * depth * store.shape[1] * len(fetches)
    return pl.pallas_call(
        body,
        in_specs=[VMEM] * (n_in + (not new)) + [ANY] * (n_hbm + len(after)),
        out_specs=[VMEM] * (1 + n_out),
        out_shape=[pltpu.VMEM(store.shape, store.dtype), *out_shapes],
        input_output_aliases={} if new else {0: 0},
        scratch_shapes=[pltpu.SemaphoreType.DMA((COPIES * len(fetches),))] if fetches else [],
        compiler_params=pltpu.CompilerParams(vmem_limit_bytes=STORE_GRANT),
        cost_estimate=pl.CostEstimate(flops=flops, bytes_accessed=moved, transcendentals=0),
        name=name,
    )(
        *([] if new else [store]),
        *operands,
        *[pltpu.with_memory_space_constraint(array, pltpu.HBM) for array in sources],
        *after,
    )


def stacked(blocks, after=()):
    rows = sum(block.shape[0] for block in blocks)

    def stack_kernel(*refs):
        refs[-1][...] = jnp.concatenate([ref[...] for ref in refs[: len(blocks)]], axis=0)

    return pl.pallas_call(
        stack_kernel,
        in_specs=[VMEM] * len(blocks) + [ANY] * len(after),
        out_shape=jax.ShapeDtypeStruct((rows, blocks[0].shape[1]), blocks[0].dtype),
        compiler_params=pltpu.CompilerParams(vmem_limit_bytes=4 << 20),
        name="stacked",
    )(*blocks, *after)


def block_owner(own, block, count):
    bits = count.bit_length() - 1
    hops = [1 << (bits - 2), 1 << (bits - 1)] + [1 << bit for bit in reversed(range(bits - 2))]
    for n, hop in enumerate(hops):
        own = own ^ (((block >> n) & 1) * hop)
    return own


def source_of(own, row, rows, count):
    tokens = rows // count
    return block_owner(own, row // tokens, count) * tokens + row % tokens


def pick_held(own, rows, count):
    held = source_of(own, lax.broadcasted_iota(jnp.int32, (rows, rows), 0), rows, count)
    return held == lax.broadcasted_iota(jnp.int32, (rows, rows), 1)


def pick_given(own, rows, count):
    held = source_of(own, lax.broadcasted_iota(jnp.int32, (rows, rows), 1), rows, count)
    return held == lax.broadcasted_iota(jnp.int32, (rows, rows), 0)


def picked(pick, block):
    if block.dtype == jnp.bfloat16:
        return jnp.dot(pick.astype(jnp.bfloat16), block, preferred_element_type=jnp.float32)
    return jnp.dot(pick.astype(jnp.float32), block, precision=lax.Precision.HIGHEST)


def held_mask(pick, tenants_row):
    tenants = jnp.sum(jnp.where(pick, tenants_row, 0).astype(jnp.float32), axis=1, keepdims=True)
    return tenant_mask(tenants.astype(jnp.int32), pick.shape[0])


def low_kernel(count, aligned, down_ref, tenants_ref, *refs):
    x, (span_out, low_ref) = refs[:-3], refs[-2:]
    own = lax.axis_index("tp")
    if aligned:
        width = down_ref.shape[0]
        at = pl.ds(pl.multiple_of(own * width, width), width)
        span = jnp.concatenate([ref[:, at] for ref in x], axis=0)
    else:
        span = jnp.concatenate([ref[...] for ref in x], axis=0)
    span_out[...] = span
    rows = span.shape[0]
    wide = jnp.dot(span, down_ref[...], preferred_element_type=jnp.float32)
    low = select_block(wide, held_mask(pick_held(own, rows, count), tenants_ref[...]))
    low_ref[...] = picked(pick_given(own, rows, count), low)


def low_part(down, tenants, x, count, after):
    rows, span = sum(block.shape[0] for block in x), down.shape[0]
    aligned = span % 128 == 0
    if not aligned:
        x = [
            lax.dynamic_slice(
                block,
                (0, lax.axis_index("tp") * span),
                (block.shape[0], span),
                allow_negative_indices=False,
            )
            for block in x
        ]
    return pl.pallas_call(
        lambda *refs: low_kernel(count, aligned, *refs),
        in_specs=[VMEM] * (2 + len(x)) + [ANY],
        out_shape=[
            jax.ShapeDtypeStruct((rows, span), x[0].dtype),
            jax.ShapeDtypeStruct((rows, ADAPTER_RANK), jnp.float32),
        ],
        compiler_params=pltpu.CompilerParams(vmem_limit_bytes=4 << 20),
        cost_estimate=pl.CostEstimate(
            flops=2 * rows * down.size, bytes_accessed=2 * down.size, transcendentals=0
        ),
        name="low_part",
    )(down, tenants, *x, after)


def forward_kernel(cuts, slots, blocks, first, slot, *refs):
    x = refs[:blocks]
    gate_out, up_out = refs[-2:]
    gate, up = (0.0, 0.0) if first else (refs[blocks][...], refs[blocks + 1][...])
    for cut in cuts:
        gate_weight, up_weight = slot(slots[cut][0]), slot(slots[cut][1])
        depth = gate_weight.shape[0]
        at = slice(cut * depth, (cut + 1) * depth)
        rows = jnp.concatenate([ref[:, at] for ref in x], axis=0)
        gate = gate + jnp.dot(rows, gate_weight, preferred_element_type=jnp.float32)
        up = up + jnp.dot(rows, up_weight, preferred_element_type=jnp.float32)
    gate_out[...] = gate
    up_out[...] = up


def forward(cuts, slots, x, store, sums, fetches, after):
    rows = sum(block.shape[0] for block in x)
    depth, hidden = store.shape[0] // SLOTS, store.shape[1]
    result = jax.ShapeDtypeStruct((rows, hidden), jnp.float32)
    store, gate, up = store_call(
        lambda *refs: forward_kernel(cuts, slots, len(x), not sums, *refs),
        store,
        fetches,
        [*x, *sums],
        [result, result],
        4 * rows * depth * hidden * len(cuts),
        "forward",
        after=after,
    )
    return store, [gate, up]


def activation_kernel(
    count, maps_slot, slot, gate_ref, up_ref, hidden_ref, low_ref, tenants_ref,
    dgate_ref, dup_ref, part_ref, spread_ref,
):
    rows = gate_ref.shape[0]
    maps = slot(maps_slot)
    own = lax.axis_index("tp")
    pick = pick_held(own, rows, count)
    mask = held_mask(pick, tenants_ref[...])
    spread = spread_rows(picked(pick, low_ref[...]), mask)
    spread_ref[...] = spread
    gate = gate_ref[...] + adapter_scale * jnp.dot(
        spread, maps, preferred_element_type=jnp.float32
    )
    s = jax.nn.sigmoid(gate)
    hidden = picked(pick, hidden_ref[...])
    dgate = (hidden * up_ref[...] * s * (1.0 + gate * (1.0 - s))).astype(jnp.bfloat16)
    dgate_ref[...] = dgate
    dup_ref[...] = (hidden * gate * s).astype(jnp.bfloat16)
    part = select_block(contracted_columns(dgate, maps), mask)
    part_ref[...] = picked(pick_given(own, rows, count), part)


def activation(maps_slot, store, sums, hidden, low, tenants, count, fetches):
    rows, width = sums[0].shape
    value = jax.ShapeDtypeStruct((rows, width), jnp.bfloat16)
    return store_call(
        lambda *refs: activation_kernel(count, maps_slot, *refs),
        store,
        fetches,
        [*sums, hidden, low, tenants],
        [
            value,
            value,
            jax.ShapeDtypeStruct((rows, ADAPTER_RANK), jnp.float32),
            jax.ShapeDtypeStruct((rows, SPREAD), jnp.bfloat16),
        ],
        4 * rows * SPREAD * width,
        "activation",
    )


def adapter_kernel(count, low_ref, tenants_ref, down_ref, earlier, own_out, other_out, spread_ref):
    half = own_out.shape[0]
    before = earlier.shape[1]
    pick = pick_held(lax.axis_index("tp"), 2 * half, count)
    spread = spread_rows(picked(pick, low_ref[...]), held_mask(pick, tenants_ref[...]))
    spread_ref[...] = spread
    part = (adapter_scale * contracted_columns(spread, down_ref[...])).astype(jnp.bfloat16)
    own_out[...] = part[:half]
    other_out[:, :before] = earlier[...]
    other_out[:, before:] = part[half:]


def adapter_part(low, tenants, down, count, earlier):
    rows, span = low.shape[0], down.shape[0]
    return pl.pallas_call(
        lambda *refs: adapter_kernel(count, *refs),
        out_shape=[
            jax.ShapeDtypeStruct((rows // 2, span), jnp.bfloat16),
            jax.ShapeDtypeStruct((rows // 2, earlier.shape[1] + span), jnp.bfloat16),
            jax.ShapeDtypeStruct((rows, SPREAD), jnp.bfloat16),
        ],
        compiler_params=pltpu.CompilerParams(vmem_limit_bytes=4 << 20),
        cost_estimate=pl.CostEstimate(
            flops=2 * rows * down.size, bytes_accessed=2 * down.size, transcendentals=0
        ),
        name="adapter_part",
    )(low, tenants, down, earlier)


def backward_kernel(slots, start, height, slot, dgate_ref, dup_ref, *refs):
    own_out, other_out = refs[-2:]
    half = own_out.shape[0]
    before = other_out.shape[1] - height
    if before:
        other_out[:, :before] = refs[0][...]
    dgate, dup = dgate_ref[...], dup_ref[...]
    for strip in range(0, height, STRIP):
        at = slice(start + strip, start + strip + STRIP)
        part = contracted_columns(dgate, slot(slots[0], at))
        part = part + contracted_columns(dup, slot(slots[1], at))
        own_out[:, strip : strip + STRIP] = part[:half]
        other_out[:, before + strip : before + strip + STRIP] = part[half:].astype(jnp.bfloat16)


def backward(slots, start, height, dgate, dup, store, fetches, after, earlier=()):
    rows, hidden = dgate.shape
    other_width = height + sum(part.shape[1] for part in earlier)
    return store_call(
        lambda *refs: backward_kernel(slots, start, height, *refs),
        store,
        fetches,
        [dgate, dup, *earlier],
        [
            jax.ShapeDtypeStruct((rows // 2, height), jnp.float32),
            jax.ShapeDtypeStruct((rows // 2, other_width), jnp.bfloat16),
        ],
        4 * rows * hidden * height,
        "backward",
        after=after,
    )


def first_halves_kernel(places, span, adapter_own, *refs):
    keep_ref, send_ref, sums = refs[-3:]
    own, came = refs[: len(places)], refs[len(places) : -3]
    half = keep_ref.shape[0]
    device = lax.axis_index("tp")
    for part, (at, group, start) in zip(own, places):
        width = part.shape[1]
        other = came[group][:, start : start + width].astype(jnp.float32)
        sums[:, at : at + width] = part[...] + other
    mine = adapter_own[...].astype(jnp.float32)
    group, start = span
    other = came[group][:, start : start + mine.shape[1]].astype(jnp.float32)
    pair = jnp.where(
        device % 2 == 0,
        jnp.concatenate([mine, other], axis=1),
        jnp.concatenate([other, mine], axis=1),
    )
    width = pair.shape[1]
    sums[:, pl.ds(pl.multiple_of(device // 2 * width, width), width)] += pair
    keep_ref[...] = sums[:half, :]
    send_ref[...] = sums[half:, :].astype(jnp.bfloat16)


def first_halves(own, places, adapter_own, span, came):
    rows = adapter_own.shape[0]
    width = sum(part.shape[1] for part in own)
    return pl.pallas_call(
        lambda *refs: first_halves_kernel(places, span, *refs),
        out_shape=[
            jax.ShapeDtypeStruct((rows // 2, width), jnp.float32),
            jax.ShapeDtypeStruct((rows // 2, width), jnp.bfloat16),
        ],
        scratch_shapes=[pltpu.VMEM((rows, width), jnp.float32)],
        compiler_params=pltpu.CompilerParams(vmem_limit_bytes=40 << 20),
        name="first_halves",
    )(adapter_own, *own, *came)


def halves(keep, came, after):
    rows, width = keep.shape

    def halves_kernel(keep_ref, came_ref, *refs):
        keep_out, send_out = refs[-2:]
        total = keep_ref[...] + came_ref[...].astype(jnp.float32)
        keep_out[...] = total[: rows // 2]
        send_out[...] = total[rows // 2 :].astype(jnp.bfloat16)

    return pl.pallas_call(
        halves_kernel,
        in_specs=[VMEM, VMEM] + [ANY] * len(after),
        out_shape=[
            jax.ShapeDtypeStruct((rows // 2, width), jnp.float32),
            jax.ShapeDtypeStruct((rows // 2, width), jnp.bfloat16),
        ],
        compiler_params=pltpu.CompilerParams(vmem_limit_bytes=40 << 20),
        name="halves",
    )(keep, came, *after)


def quarters(keep, came, after):
    rows, width = keep.shape
    quarter = rows // 4

    def quarters_kernel(keep_ref, came_ref, *refs):
        keep_out, *sends = refs[-4:]
        total = keep_ref[...] + came_ref[...].astype(jnp.float32)
        keep_out[...] = total[:quarter]
        for n, send_out in enumerate(sends, 1):
            send_out[...] = total[n * quarter : (n + 1) * quarter].astype(jnp.bfloat16)

    return pl.pallas_call(
        quarters_kernel,
        in_specs=[VMEM, VMEM] + [ANY] * len(after),
        out_shape=[jax.ShapeDtypeStruct((quarter, width), jnp.float32)]
        + [jax.ShapeDtypeStruct((quarter, width), jnp.bfloat16)] * 3,
        compiler_params=pltpu.CompilerParams(vmem_limit_bytes=40 << 20),
        name="quarters",
    )(keep, came, *after)


def final(keep, came, after):
    def final_kernel(keep_ref, *refs):
        total = keep_ref[...]
        for ref in refs[: len(came)]:
            total = total + ref[...].astype(jnp.float32)
        refs[-1][...] = total.astype(jnp.bfloat16)

    return pl.pallas_call(
        final_kernel,
        in_specs=[VMEM] * (1 + len(came)) + [ANY] * len(after),
        out_shape=jax.ShapeDtypeStruct(keep.shape, jnp.bfloat16),
        compiler_params=pltpu.CompilerParams(vmem_limit_bytes=40 << 20),
        name="final",
    )(keep, *came, *after)


def outer_kernel(left_ref, right_ref, *refs):
    out_ref, token_ref = refs[-2:]
    out_ref[...] = contracted_rows(
        left_ref[...] * jnp.bfloat16(adapter_scale), right_ref[...]
    ).astype(jnp.bfloat16)
    token_ref[...] = jnp.zeros_like(token_ref)


def outer(left, right, name, after, largest):
    rows, height = left.shape
    width = right.shape[1]
    block = block_of(height, largest)
    if block % 128:
        block = height
    return pl.pallas_call(
        outer_kernel,
        grid=(height // block,),
        in_specs=[
            pl.BlockSpec((rows, block), lambda k: (0, k)),
            pl.BlockSpec((rows, width), lambda k: (0, 0)),
            ANY,
        ],
        out_specs=[
            pl.BlockSpec((block, width), lambda k: (k, 0)),
            pl.BlockSpec((8, 128), lambda k: (0, 0)),
        ],
        out_shape=[
            jax.ShapeDtypeStruct((height, width), jnp.bfloat16),
            jax.ShapeDtypeStruct((8, 128), jnp.float32),
        ],
        compiler_params=pltpu.CompilerParams(vmem_limit_bytes=24 << 20),
        cost_estimate=pl.CostEstimate(
            flops=2 * rows * height * width, bytes_accessed=2 * height * width, transcendentals=0
        ),
        name=name,
    )(left, right, after)


def add_kernel(left_ref, right_ref, out_ref):
    out_ref[...] = left_ref[...] + right_ref[...]


def plus(left, right):
    return pl.pallas_call(
        add_kernel,
        out_shape=jax.ShapeDtypeStruct(left.shape, left.dtype),
        compiler_params=pltpu.CompilerParams(vmem_limit_bytes=2 << 20),
        name="plus",
    )(left, right)


def swapped(block, hop):
    return lax.ppermute(block, "tp", [(i, i ^ hop) for i in range(lax.axis_size("tp"))])


def local(
    normed_layer_input,
    hidden_unit_gradient,
    gate_weight,
    up_weight,
    adapter_down_maps,
    adapter_up_maps,
    token_tenant_index,
):
    count = lax.axis_size("tp")
    own_rows, width = normed_layer_input.shape
    rows = own_rows * count
    hops = [1 << bit for bit in range(count.bit_length() - 1)]
    tenants = token_tenant_index.reshape(1, rows)

    def pair(cut, first, second):
        return [(gate_weight, cut, first), (up_weight, cut, second)]

    def mark(slot, token_ref):
        token_ref[...] = jnp.zeros_like(token_ref)

    mark_shape = jax.ShapeDtypeStruct((8, 128), jnp.float32)
    store = jax.ShapeDtypeStruct(
        (SLOTS * width // CUTS, gate_weight.shape[1]), gate_weight.dtype
    )
    far, near = hops[-1], hops[-2]
    came = [swapped(normed_layer_input, hop) for hop in (near, far, near | far)]
    store, token = store_call(mark, store, pair(0, 0, 1), [], [mark_shape], 0, "fetch")
    block = stacked([normed_layer_input, *came], [token])
    for hop in reversed(hops[2:-2]):
        block = stacked([block, swapped(block, hop)])
    x = [block] + [swapped(block, hop) for hop in (hops[1], 1, hops[1] | 1)]
    store, token = store_call(
        mark, store, pair(1, 2, 3), [], [mark_shape], 0, "fetch", after=[block]
    )

    input_span, low = low_part(adapter_down_maps, tenants, x, count, token)
    sums = []
    slots = {0: (0, 1), 1: (2, 3), 2: (4, 5), 3: (0, 1)}
    step = 0
    for cuts, fetches in (
        ((0, 1), pair(2, 4, 5)), ((2,), pair(3, 0, 1)), ((3,), [(adapter_up_maps, 0, 2)])
    ):
        after = [low]
        if step < len(hops):
            low = plus(low, swapped(low, hops[step]))
            step += 1
        store, sums = forward(cuts, slots, x, store, sums, fetches, after)
    for hop in hops[step:]:
        low = plus(low, swapped(low, hop))
    store, dgate, dup, low_grad, input_spread = activation(
        2, store, sums, hidden_unit_gradient, low, tenants, count, []
    )

    later_hops = hops[1:] + hops[:1]
    depth = width // CUTS
    part_list = [
        (3, (0, 1), 0, depth, [(gate_weight, 1, 2)], True),
        (2, (4, 5), 0, depth, [(gate_weight, 0, 0)], False),
        (1, (2, 3), 0, depth, [(up_weight, 0, 1)], True),
        (0, (0, 1), depth // 2, depth // 2, [], True),
        (0, (0, 1), 0, depth // 2, [], False),
    ]
    own_parts, places, came, waiting = [], [], [], []
    for n, (piece, slots, first, height, fetches, waits) in enumerate(part_list):
        after = [low_grad]
        if n == len(part_list) - 1:
            span = (len(came), waiting[0].shape[1])
            adapter_own, to_send, grad_spread = adapter_part(
                low_grad, tenants, adapter_down_maps, count, waiting[0]
            )
            came.append(swapped(to_send, 1))
            after, waiting = [to_send], []
        else:
            turns = later_hops[:1] if n < len(part_list) - 2 else later_hops
            later_hops = later_hops[len(turns) :]
            for hop in turns:
                low_grad = plus(low_grad, swapped(low_grad, hop))
        begin = sum(part.shape[1] for part in waiting)
        store, own_part, other_part = backward(
            slots, first, height, dgate, dup, store, fetches, after, waiting
        )
        own_parts.append(own_part)
        places.append((piece * depth + first, len(came), begin))
        waiting = [other_part]
        if not waits:
            came.append(swapped(other_part, 1))
            waiting = []

    keep, send = first_halves(own_parts, places, adapter_own, span, came)
    halvings = [block_owner(0, 1 << bit, count) for bit in reversed(range(2, len(hops) - 1))]
    for n, hop in enumerate(halvings):
        came = swapped(send, hop)
        beside = [send]
        if n == len(halvings) - 1:
            up_map_gradient, token = outer(input_spread, dgate, "up_maps", send, 512)
            keep, *sends = quarters(keep, came, [token])
        else:
            keep, send = halves(keep, came, beside)
    came = [swapped(sends[n - 1], block_owner(0, n, count)) for n in (3, 2, 1)]
    down_map_gradient, token = outer(input_span, grad_spread, "down_maps", sends[0], 256)
    return (final(keep, came, [token]), down_map_gradient, up_map_gradient)


def solution(mesh):
    placed = (
        P(("groups", "tp"), None),
        P("groups", "tp"),
        P(None, "tp"),
        P(None, "tp"),
        P("tp", None),
        P(None, "tp"),
        P("groups"),
    )
    return jax.shard_map(
        local,
        mesh=mesh,
        in_specs=placed,
        out_specs=(P(("groups", "tp"), None), P("tp", "groups"), P("groups", "tp")),
        check_vma=False,
    )
```

```python
import jax
import jax.numpy as jnp
from jax import lax
from jax.experimental import pallas as pl
from jax.experimental.pallas import tpu as pltpu
from jax.sharding import PartitionSpec as P

ADAPTER_RANK = 64
TENANT_COUNT = 32
SPREAD = ADAPTER_RANK * TENANT_COUNT

adapter_scale = 2.0


def block_of(size, largest):
    block = largest
    while size % block:
        block //= 2
    return block


def contracted_rows(left, right):
    return lax.dot_general(
        left, right, (((0,), (0,)), ((), ())), preferred_element_type=jnp.float32
    )


def contracted_columns(left, right):
    return lax.dot_general(
        left, right, (((1,), (1,)), ((), ())), preferred_element_type=jnp.float32
    )


def tenant_mask(tenants, rows):
    columns = lax.broadcasted_iota(jnp.int32, (rows, SPREAD), 1) // ADAPTER_RANK
    return tenants == columns


def select_block(wide_rows, mask):
    kept = jnp.where(mask, wide_rows, 0.0)
    pair = 2 * ADAPTER_RANK
    total = kept[:, :pair]
    for start in range(pair, SPREAD, pair):
        total = total + kept[:, start : start + pair]
    return total[:, :ADAPTER_RANK] + total[:, ADAPTER_RANK:]


def spread_rows(low_rows, mask):
    pair = jnp.concatenate([low_rows, low_rows], axis=1)
    wide = jnp.concatenate([pair] * (TENANT_COUNT // 2), axis=1)
    return jnp.where(mask, wide, 0.0).astype(jnp.bfloat16)


VMEM = pl.BlockSpec(memory_space=pltpu.VMEM)
ANY = pl.BlockSpec(memory_space=pl.ANY)
CUTS = 4
COPIES = 8
STRIP = 256
SLOTS = 6
STORE_GRANT = 10 << 20


def store_call(kernel, store, fetches, operands, out_shapes, flops, name, after=()):
    new = isinstance(store, jax.ShapeDtypeStruct)
    depth = store.shape[0] // SLOTS
    part = depth // COPIES
    sources = []
    for array, *_ in fetches:
        if not any(array is known for known in sources):
            sources.append(array)
    places = [next(i for i, known in enumerate(sources) if known is f[0]) for f in fetches]
    n_in, n_out, n_hbm = len(operands), len(out_shapes), len(sources)

    def body(*refs):
        if not new:
            refs = refs[1:]
        ins, hbm = refs[:n_in], refs[n_in : n_in + n_hbm]
        rest = refs[n_in + n_hbm + len(after) :]
        store_ref, outs, scratch = rest[0], rest[1 : 1 + n_out], rest[1 + n_out :]
        copies = []
        for n, (place, (_, piece, slot, *half)) in enumerate(zip(places, fetches)):
            for k in range(COPIES):
                if half and k // (COPIES // 2) != half[0]:
                    continue
                copies.append(
                    pltpu.make_async_copy(
                        hbm[place].at[pl.ds(piece * depth + k * part, part)],
                        store_ref.at[pl.ds(slot * depth + k * part, part)],
                        scratch[0].at[n * COPIES + k],
                    )
                )
        for copy in copies:
            copy.start()
        def rows_of(slot, at=slice(0, depth)):
            return store_ref[slot * depth + at.start : slot * depth + at.stop, :]

        kernel(rows_of, *ins, *outs)
        for copy in copies:
            copy.wait()

    moved = 2 * depth * store.shape[1] * len(fetches)
    return pl.pallas_call(
        body,
        in_specs=[VMEM] * (n_in + (not new)) + [ANY] * (n_hbm + len(after)),
        out_specs=[VMEM] * (1 + n_out),
        out_shape=[pltpu.VMEM(store.shape, store.dtype), *out_shapes],
        input_output_aliases={} if new else {0: 0},
        scratch_shapes=[pltpu.SemaphoreType.DMA((COPIES * len(fetches),))] if fetches else [],
        compiler_params=pltpu.CompilerParams(vmem_limit_bytes=STORE_GRANT),
        cost_estimate=pl.CostEstimate(flops=flops, bytes_accessed=moved, transcendentals=0),
        name=name,
    )(
        *([] if new else [store]),
        *operands,
        *[pltpu.with_memory_space_constraint(array, pltpu.HBM) for array in sources],
        *after,
    )


def stacked(blocks, after=()):
    rows = sum(block.shape[0] for block in blocks)

    def stack_kernel(*refs):
        refs[-1][...] = jnp.concatenate([ref[...] for ref in refs[: len(blocks)]], axis=0)

    return pl.pallas_call(
        stack_kernel,
        in_specs=[VMEM] * len(blocks) + [ANY] * len(after),
        out_shape=jax.ShapeDtypeStruct((rows, blocks[0].shape[1]), blocks[0].dtype),
        compiler_params=pltpu.CompilerParams(vmem_limit_bytes=4 << 20),
        name="stacked",
    )(*blocks, *after)


def block_owner(own, block, count):
    bits = count.bit_length() - 1
    hops = [1 << (bits - 2), 1 << (bits - 1)] + [1 << bit for bit in reversed(range(bits - 2))]
    for n, hop in enumerate(hops):
        own = own ^ (((block >> n) & 1) * hop)
    return own


def source_of(own, row, rows, count):
    tokens = rows // count
    return block_owner(own, row // tokens, count) * tokens + row % tokens


def pick_held(own, rows, count):
    held = source_of(own, lax.broadcasted_iota(jnp.int32, (rows, rows), 0), rows, count)
    return held == lax.broadcasted_iota(jnp.int32, (rows, rows), 1)


def pick_given(own, rows, count):
    held = source_of(own, lax.broadcasted_iota(jnp.int32, (rows, rows), 1), rows, count)
    return held == lax.broadcasted_iota(jnp.int32, (rows, rows), 0)


def picked(pick, block):
    if block.dtype == jnp.bfloat16:
        return jnp.dot(pick.astype(jnp.bfloat16), block, preferred_element_type=jnp.float32)
    return jnp.dot(pick.astype(jnp.float32), block, precision=lax.Precision.HIGHEST)


def held_mask(pick, tenants_row):
    tenants = jnp.sum(jnp.where(pick, tenants_row, 0).astype(jnp.float32), axis=1, keepdims=True)
    return tenant_mask(tenants.astype(jnp.int32), pick.shape[0])


def low_kernel(count, aligned, down_ref, tenants_ref, *refs):
    x, (span_out, low_ref) = refs[:-3], refs[-2:]
    own = lax.axis_index("tp")
    if aligned:
        width = down_ref.shape[0]
        at = pl.ds(pl.multiple_of(own * width, width), width)
        span = jnp.concatenate([ref[:, at] for ref in x], axis=0)
    else:
        span = jnp.concatenate([ref[...] for ref in x], axis=0)
    span_out[...] = span
    rows = span.shape[0]
    wide = jnp.dot(span, down_ref[...], preferred_element_type=jnp.float32)
    low = select_block(wide, held_mask(pick_held(own, rows, count), tenants_ref[...]))
    low_ref[...] = picked(pick_given(own, rows, count), low)


def low_part(down, tenants, x, count, after):
    rows, span = sum(block.shape[0] for block in x), down.shape[0]
    aligned = span % 128 == 0
    if not aligned:
        x = [
            lax.dynamic_slice(
                block,
                (0, lax.axis_index("tp") * span),
                (block.shape[0], span),
                allow_negative_indices=False,
            )
            for block in x
        ]
    return pl.pallas_call(
        lambda *refs: low_kernel(count, aligned, *refs),
        in_specs=[VMEM] * (2 + len(x)) + [ANY],
        out_shape=[
            jax.ShapeDtypeStruct((rows, span), x[0].dtype),
            jax.ShapeDtypeStruct((rows, ADAPTER_RANK), jnp.float32),
        ],
        compiler_params=pltpu.CompilerParams(vmem_limit_bytes=4 << 20),
        cost_estimate=pl.CostEstimate(
            flops=2 * rows * down.size, bytes_accessed=2 * down.size, transcendentals=0
        ),
        name="low_part",
    )(down, tenants, *x, after)


def forward_kernel(cuts, slots, blocks, first, slot, *refs):
    x = refs[:blocks]
    gate_out, up_out = refs[-2:]
    gate, up = (0.0, 0.0) if first else (refs[blocks][...], refs[blocks + 1][...])
    for cut in cuts:
        gate_weight, up_weight = slot(slots[cut][0]), slot(slots[cut][1])
        depth = gate_weight.shape[0]
        at = slice(cut * depth, (cut + 1) * depth)
        rows = jnp.concatenate([ref[:, at] for ref in x], axis=0)
        gate = gate + jnp.dot(rows, gate_weight, preferred_element_type=jnp.float32)
        up = up + jnp.dot(rows, up_weight, preferred_element_type=jnp.float32)
    gate_out[...] = gate
    up_out[...] = up


def forward(cuts, slots, x, store, sums, fetches, after):
    rows = sum(block.shape[0] for block in x)
    depth, hidden = store.shape[0] // SLOTS, store.shape[1]
    result = jax.ShapeDtypeStruct((rows, hidden), jnp.float32)
    store, gate, up = store_call(
        lambda *refs: forward_kernel(cuts, slots, len(x), not sums, *refs),
        store,
        fetches,
        [*x, *sums],
        [result, result],
        4 * rows * depth * hidden * len(cuts),
        "forward",
        after=after,
    )
    return store, [gate, up]


def activation_kernel(
    count, maps_slot, slot, gate_ref, up_ref, hidden_ref, low_ref, tenants_ref,
    dgate_ref, dup_ref, part_ref, spread_ref,
):
    rows = gate_ref.shape[0]
    maps = slot(maps_slot)
    own = lax.axis_index("tp")
    pick = pick_held(own, rows, count)
    mask = held_mask(pick, tenants_ref[...])
    spread = spread_rows(picked(pick, low_ref[...]), mask)
    spread_ref[...] = spread
    gate = gate_ref[...] + adapter_scale * jnp.dot(
        spread, maps, preferred_element_type=jnp.float32
    )
    s = jax.nn.sigmoid(gate)
    hidden = picked(pick, hidden_ref[...])
    dgate = (hidden * up_ref[...] * s * (1.0 + gate * (1.0 - s))).astype(jnp.bfloat16)
    dgate_ref[...] = dgate
    dup_ref[...] = (hidden * gate * s).astype(jnp.bfloat16)
    part = select_block(contracted_columns(dgate, maps), mask)
    part_ref[...] = picked(pick_given(own, rows, count), part)


def activation(maps_slot, store, sums, hidden, low, tenants, count, fetches):
    rows, width = sums[0].shape
    value = jax.ShapeDtypeStruct((rows, width), jnp.bfloat16)
    return store_call(
        lambda *refs: activation_kernel(count, maps_slot, *refs),
        store,
        fetches,
        [*sums, hidden, low, tenants],
        [
            value,
            value,
            jax.ShapeDtypeStruct((rows, ADAPTER_RANK), jnp.float32),
            jax.ShapeDtypeStruct((rows, SPREAD), jnp.bfloat16),
        ],
        4 * rows * SPREAD * width,
        "activation",
    )


def adapter_kernel(count, low_ref, tenants_ref, down_ref, earlier, own_out, other_out, spread_ref):
    half = own_out.shape[0]
    before = earlier.shape[1]
    pick = pick_held(lax.axis_index("tp"), 2 * half, count)
    spread = spread_rows(picked(pick, low_ref[...]), held_mask(pick, tenants_ref[...]))
    spread_ref[...] = spread
    part = (adapter_scale * contracted_columns(spread, down_ref[...])).astype(jnp.bfloat16)
    own_out[...] = part[:half]
    other_out[:, :before] = earlier[...]
    other_out[:, before:] = part[half:]


def adapter_part(low, tenants, down, count, earlier):
    rows, span = low.shape[0], down.shape[0]
    return pl.pallas_call(
        lambda *refs: adapter_kernel(count, *refs),
        out_shape=[
            jax.ShapeDtypeStruct((rows // 2, span), jnp.bfloat16),
            jax.ShapeDtypeStruct((rows // 2, earlier.shape[1] + span), jnp.bfloat16),
            jax.ShapeDtypeStruct((rows, SPREAD), jnp.bfloat16),
        ],
        compiler_params=pltpu.CompilerParams(vmem_limit_bytes=4 << 20),
        cost_estimate=pl.CostEstimate(
            flops=2 * rows * down.size, bytes_accessed=2 * down.size, transcendentals=0
        ),
        name="adapter_part",
    )(low, tenants, down, earlier)


def backward_kernel(slots, start, height, slot, dgate_ref, dup_ref, *refs):
    own_out, other_out = refs[-2:]
    half = own_out.shape[0]
    before = other_out.shape[1] - height
    if before:
        other_out[:, :before] = refs[0][...]
    dgate, dup = dgate_ref[...], dup_ref[...]
    for strip in range(0, height, STRIP):
        at = slice(start + strip, start + strip + STRIP)
        part = contracted_columns(dgate, slot(slots[0], at))
        part = part + contracted_columns(dup, slot(slots[1], at))
        own_out[:, strip : strip + STRIP] = part[:half]
        other_out[:, before + strip : before + strip + STRIP] = part[half:].astype(jnp.bfloat16)


def backward(slots, start, height, dgate, dup, store, fetches, after, earlier=()):
    rows, hidden = dgate.shape
    other_width = height + sum(part.shape[1] for part in earlier)
    return store_call(
        lambda *refs: backward_kernel(slots, start, height, *refs),
        store,
        fetches,
        [dgate, dup, *earlier],
        [
            jax.ShapeDtypeStruct((rows // 2, height), jnp.float32),
            jax.ShapeDtypeStruct((rows // 2, other_width), jnp.bfloat16),
        ],
        4 * rows * hidden * height,
        "backward",
        after=after,
    )


def first_halves_kernel(places, span, adapter_own, *refs):
    keep_ref, send_ref, sums = refs[-3:]
    own, came = refs[: len(places)], refs[len(places) : -3]
    half = keep_ref.shape[0]
    device = lax.axis_index("tp")
    for part, (at, group, start) in zip(own, places):
        width = part.shape[1]
        other = came[group][:, start : start + width].astype(jnp.float32)
        sums[:, at : at + width] = part[...] + other
    mine = adapter_own[...].astype(jnp.float32)
    group, start = span
    other = came[group][:, start : start + mine.shape[1]].astype(jnp.float32)
    pair = jnp.where(
        device % 2 == 0,
        jnp.concatenate([mine, other], axis=1),
        jnp.concatenate([other, mine], axis=1),
    )
    width = pair.shape[1]
    sums[:, pl.ds(pl.multiple_of(device // 2 * width, width), width)] += pair
    keep_ref[...] = sums[:half, :]
    send_ref[...] = sums[half:, :].astype(jnp.bfloat16)


def first_halves(own, places, adapter_own, span, came):
    rows = adapter_own.shape[0]
    width = sum(part.shape[1] for part in own)
    return pl.pallas_call(
        lambda *refs: first_halves_kernel(places, span, *refs),
        out_shape=[
            jax.ShapeDtypeStruct((rows // 2, width), jnp.float32),
            jax.ShapeDtypeStruct((rows // 2, width), jnp.bfloat16),
        ],
        scratch_shapes=[pltpu.VMEM((rows, width), jnp.float32)],
        compiler_params=pltpu.CompilerParams(vmem_limit_bytes=40 << 20),
        name="first_halves",
    )(adapter_own, *own, *came)


def halves(keep, came, after):
    rows, width = keep.shape

    def halves_kernel(keep_ref, came_ref, *refs):
        keep_out, send_out = refs[-2:]
        total = keep_ref[...] + came_ref[...].astype(jnp.float32)
        keep_out[...] = total[: rows // 2]
        send_out[...] = total[rows // 2 :].astype(jnp.bfloat16)

    return pl.pallas_call(
        halves_kernel,
        in_specs=[VMEM, VMEM] + [ANY] * len(after),
        out_shape=[
            jax.ShapeDtypeStruct((rows // 2, width), jnp.float32),
            jax.ShapeDtypeStruct((rows // 2, width), jnp.bfloat16),
        ],
        compiler_params=pltpu.CompilerParams(vmem_limit_bytes=40 << 20),
        name="halves",
    )(keep, came, *after)


def quarters(keep, came, after):
    rows, width = keep.shape
    quarter = rows // 4

    def quarters_kernel(keep_ref, came_ref, *refs):
        keep_out, *sends = refs[-4:]
        total = keep_ref[...] + came_ref[...].astype(jnp.float32)
        keep_out[...] = total[:quarter]
        for n, send_out in enumerate(sends, 1):
            send_out[...] = total[n * quarter : (n + 1) * quarter].astype(jnp.bfloat16)

    return pl.pallas_call(
        quarters_kernel,
        in_specs=[VMEM, VMEM] + [ANY] * len(after),
        out_shape=[jax.ShapeDtypeStruct((quarter, width), jnp.float32)]
        + [jax.ShapeDtypeStruct((quarter, width), jnp.bfloat16)] * 3,
        compiler_params=pltpu.CompilerParams(vmem_limit_bytes=40 << 20),
        name="quarters",
    )(keep, came, *after)


def final(keep, came, after):
    def final_kernel(keep_ref, *refs):
        total = keep_ref[...]
        for ref in refs[: len(came)]:
            total = total + ref[...].astype(jnp.float32)
        refs[-1][...] = total.astype(jnp.bfloat16)

    return pl.pallas_call(
        final_kernel,
        in_specs=[VMEM] * (1 + len(came)) + [ANY] * len(after),
        out_shape=jax.ShapeDtypeStruct(keep.shape, jnp.bfloat16),
        compiler_params=pltpu.CompilerParams(vmem_limit_bytes=40 << 20),
        name="final",
    )(keep, *came, *after)


def outer_kernel(left_ref, right_ref, *refs):
    out_ref, token_ref = refs[-2:]
    out_ref[...] = contracted_rows(
        left_ref[...] * jnp.bfloat16(adapter_scale), right_ref[...]
    ).astype(jnp.bfloat16)
    token_ref[...] = jnp.zeros_like(token_ref)


def outer(left, right, name, after, largest):
    rows, height = left.shape
    width = right.shape[1]
    block = block_of(height, largest)
    if block % 128:
        block = height
    return pl.pallas_call(
        outer_kernel,
        grid=(height // block,),
        in_specs=[
            pl.BlockSpec((rows, block), lambda k: (0, k)),
            pl.BlockSpec((rows, width), lambda k: (0, 0)),
            ANY,
        ],
        out_specs=[
            pl.BlockSpec((block, width), lambda k: (k, 0)),
            pl.BlockSpec((8, 128), lambda k: (0, 0)),
        ],
        out_shape=[
            jax.ShapeDtypeStruct((height, width), jnp.bfloat16),
            jax.ShapeDtypeStruct((8, 128), jnp.float32),
        ],
        compiler_params=pltpu.CompilerParams(vmem_limit_bytes=24 << 20),
        cost_estimate=pl.CostEstimate(
            flops=2 * rows * height * width, bytes_accessed=2 * height * width, transcendentals=0
        ),
        name=name,
    )(left, right, after)


def add_kernel(left_ref, right_ref, out_ref):
    out_ref[...] = left_ref[...] + right_ref[...]


def plus(left, right):
    return pl.pallas_call(
        add_kernel,
        out_shape=jax.ShapeDtypeStruct(left.shape, left.dtype),
        compiler_params=pltpu.CompilerParams(vmem_limit_bytes=2 << 20),
        name="plus",
    )(left, right)


def swapped(block, hop):
    return lax.ppermute(block, "tp", [(i, i ^ hop) for i in range(lax.axis_size("tp"))])


def local(
    normed_layer_input,
    hidden_unit_gradient,
    gate_weight,
    up_weight,
    adapter_down_maps,
    adapter_up_maps,
    token_tenant_index,
):
    count = lax.axis_size("tp")
    own_rows, width = normed_layer_input.shape
    rows = own_rows * count
    hops = [1 << bit for bit in range(count.bit_length() - 1)]
    tenants = token_tenant_index.reshape(1, rows)

    def pair(cut, first, second):
        return [(gate_weight, cut, first), (up_weight, cut, second)]

    def mark(slot, token_ref):
        token_ref[...] = jnp.zeros_like(token_ref)

    mark_shape = jax.ShapeDtypeStruct((8, 128), jnp.float32)
    store = jax.ShapeDtypeStruct(
        (SLOTS * width // CUTS, gate_weight.shape[1]), gate_weight.dtype
    )
    far, near = hops[-1], hops[-2]
    came = [swapped(normed_layer_input, hop) for hop in (near, far, near | far)]
    store, token = store_call(mark, store, pair(0, 0, 1), [], [mark_shape], 0, "fetch")
    block = stacked([normed_layer_input, *came], [token])
    for hop in reversed(hops[2:-2]):
        block = stacked([block, swapped(block, hop)])
    x = [block] + [swapped(block, hop) for hop in (hops[1], 1, hops[1] | 1)]
    store, token = store_call(
        mark, store, pair(1, 2, 3), [], [mark_shape], 0, "fetch", after=[block]
    )

    input_span, low = low_part(adapter_down_maps, tenants, x, count, token)
    sums = []
    slots = {0: (0, 1), 1: (2, 3), 2: (4, 5), 3: (0, 1)}
    step = 0
    for cuts, fetches in (
        ((0, 1), pair(2, 4, 5)), ((2,), pair(3, 0, 1)), ((3,), [(adapter_up_maps, 0, 2)])
    ):
        after = [low]
        if step < len(hops):
            low = plus(low, swapped(low, hops[step]))
            step += 1
        store, sums = forward(cuts, slots, x, store, sums, fetches, after)
    for hop in hops[step:]:
        low = plus(low, swapped(low, hop))
    store, dgate, dup, low_grad, input_spread = activation(
        2, store, sums, hidden_unit_gradient, low, tenants, count, []
    )

    later_hops = hops[1:] + hops[:1]
    depth = width // CUTS
    part_list = [
        (3, (0, 1), 0, depth, [(gate_weight, 1, 2)], True),
        (2, (4, 5), 0, depth, [(gate_weight, 0, 0)], False),
        (1, (2, 3), 0, depth, [(up_weight, 0, 1)], True),
        (0, (0, 1), depth // 2, depth // 2, [], True),
        (0, (0, 1), 0, depth // 2, [], False),
    ]
    own_parts, places, came, waiting = [], [], [], []
    for n, (piece, slots, first, height, fetches, waits) in enumerate(part_list):
        after = [low_grad]
        if n == len(part_list) - 1:
            span = (len(came), waiting[0].shape[1])
            adapter_own, to_send, grad_spread = adapter_part(
                low_grad, tenants, adapter_down_maps, count, waiting[0]
            )
            came.append(swapped(to_send, 1))
            after, waiting = [to_send], []
        else:
            turns = later_hops[:1] if n < len(part_list) - 2 else later_hops
            later_hops = later_hops[len(turns) :]
            for hop in turns:
                low_grad = plus(low_grad, swapped(low_grad, hop))
        begin = sum(part.shape[1] for part in waiting)
        store, own_part, other_part = backward(
            slots, first, height, dgate, dup, store, fetches, after, waiting
        )
        own_parts.append(own_part)
        places.append((piece * depth + first, len(came), begin))
        waiting = [other_part]
        if not waits:
            came.append(swapped(other_part, 1))
            waiting = []

    keep, send = first_halves(own_parts, places, adapter_own, span, came)
    halvings = [block_owner(0, 1 << bit, count) for bit in reversed(range(2, len(hops) - 1))]
    for n, hop in enumerate(halvings):
        came = swapped(send, hop)
        beside = [send]
        if n == len(halvings) - 1:
            up_map_gradient, token = outer(input_spread, dgate, "up_maps", send, 512)
            keep, *sends = quarters(keep, came, [token])
        else:
            keep, send = halves(keep, came, beside)
    came = [swapped(sends[n - 1], block_owner(0, n, count)) for n in (3, 2, 1)]
    down_map_gradient, token = outer(input_span, grad_spread, "down_maps", sends[0], 256)
    return (final(keep, came, [token]), down_map_gradient, up_map_gradient)


def solution(mesh):
    placed = (
        P(("groups", "tp"), None),
        P("groups", "tp"),
        P(None, "tp"),
        P(None, "tp"),
        P("tp", None),
        P(None, "tp"),
        P("groups"),
    )
    return jax.shard_map(
        local,
        mesh=mesh,
        in_specs=placed,
        out_specs=(P(("groups", "tp"), None), P("tp", "groups"), P("groups", "tp")),
        check_vma=False,
    )
```

```python
import jax
import jax.numpy as jnp
from jax import lax
from jax.experimental import pallas as pl
from jax.experimental.pallas import tpu as pltpu
from jax.sharding import PartitionSpec as P

ADAPTER_RANK = 64
TENANT_COUNT = 32
SPREAD = ADAPTER_RANK * TENANT_COUNT

adapter_scale = 2.0


def block_of(size, largest):
    block = largest
    while size % block:
        block //= 2
    return block


def contracted_rows(left, right):
    return lax.dot_general(
        left, right, (((0,), (0,)), ((), ())), preferred_element_type=jnp.float32
    )


def contracted_columns(left, right):
    return lax.dot_general(
        left, right, (((1,), (1,)), ((), ())), preferred_element_type=jnp.float32
    )


def tenant_mask(tenants, rows):
    columns = lax.broadcasted_iota(jnp.int32, (rows, SPREAD), 1) // ADAPTER_RANK
    return tenants == columns


def select_block(wide_rows, mask):
    kept = jnp.where(mask, wide_rows, 0.0)
    pair = 2 * ADAPTER_RANK
    total = kept[:, :pair]
    for start in range(pair, SPREAD, pair):
        total = total + kept[:, start : start + pair]
    return total[:, :ADAPTER_RANK] + total[:, ADAPTER_RANK:]


def spread_rows(low_rows, mask):
    pair = jnp.concatenate([low_rows, low_rows], axis=1)
    wide = jnp.concatenate([pair] * (TENANT_COUNT // 2), axis=1)
    return jnp.where(mask, wide, 0.0).astype(jnp.bfloat16)


VMEM = pl.BlockSpec(memory_space=pltpu.VMEM)
ANY = pl.BlockSpec(memory_space=pl.ANY)
CUTS = 4
COPIES = 8
STRIP = 256
SLOTS = 6
STORE_GRANT = 10 << 20


def store_call(kernel, store, fetches, operands, out_shapes, flops, name, after=()):
    new = isinstance(store, jax.ShapeDtypeStruct)
    depth = store.shape[0] // SLOTS
    part = depth // COPIES
    sources = []
    for array, *_ in fetches:
        if not any(array is known for known in sources):
            sources.append(array)
    places = [next(i for i, known in enumerate(sources) if known is f[0]) for f in fetches]
    n_in, n_out, n_hbm = len(operands), len(out_shapes), len(sources)

    def body(*refs):
        if not new:
            refs = refs[1:]
        ins, hbm = refs[:n_in], refs[n_in : n_in + n_hbm]
        rest = refs[n_in + n_hbm + len(after) :]
        store_ref, outs, scratch = rest[0], rest[1 : 1 + n_out], rest[1 + n_out :]
        copies = []
        for n, (place, (_, piece, slot, *half)) in enumerate(zip(places, fetches)):
            for k in range(COPIES):
                if half and k // (COPIES // 2) != half[0]:
                    continue
                copies.append(
                    pltpu.make_async_copy(
                        hbm[place].at[pl.ds(piece * depth + k * part, part)],
                        store_ref.at[pl.ds(slot * depth + k * part, part)],
                        scratch[0].at[n * COPIES + k],
                    )
                )
        for copy in copies:
            copy.start()
        def rows_of(slot, at=slice(0, depth)):
            return store_ref[slot * depth + at.start : slot * depth + at.stop, :]

        kernel(rows_of, *ins, *outs)
        for copy in copies:
            copy.wait()

    moved = 2 * depth * store.shape[1] * len(fetches)
    return pl.pallas_call(
        body,
        in_specs=[VMEM] * (n_in + (not new)) + [ANY] * (n_hbm + len(after)),
        out_specs=[VMEM] * (1 + n_out),
        out_shape=[pltpu.VMEM(store.shape, store.dtype), *out_shapes],
        input_output_aliases={} if new else {0: 0},
        scratch_shapes=[pltpu.SemaphoreType.DMA((COPIES * len(fetches),))] if fetches else [],
        compiler_params=pltpu.CompilerParams(vmem_limit_bytes=STORE_GRANT),
        cost_estimate=pl.CostEstimate(flops=flops, bytes_accessed=moved, transcendentals=0),
        name=name,
    )(
        *([] if new else [store]),
        *operands,
        *[pltpu.with_memory_space_constraint(array, pltpu.HBM) for array in sources],
        *after,
    )


def stacked(blocks, after=()):
    rows = sum(block.shape[0] for block in blocks)

    def stack_kernel(*refs):
        refs[-1][...] = jnp.concatenate([ref[...] for ref in refs[: len(blocks)]], axis=0)

    return pl.pallas_call(
        stack_kernel,
        in_specs=[VMEM] * len(blocks) + [ANY] * len(after),
        out_shape=jax.ShapeDtypeStruct((rows, blocks[0].shape[1]), blocks[0].dtype),
        compiler_params=pltpu.CompilerParams(vmem_limit_bytes=4 << 20),
        name="stacked",
    )(*blocks, *after)


def block_owner(own, block, count):
    bits = count.bit_length() - 1
    hops = [1 << (bits - 2), 1 << (bits - 1)] + [1 << bit for bit in reversed(range(bits - 2))]
    for n, hop in enumerate(hops):
        own = own ^ (((block >> n) & 1) * hop)
    return own


def source_of(own, row, rows, count):
    tokens = rows // count
    return block_owner(own, row // tokens, count) * tokens + row % tokens


def pick_held(own, rows, count):
    held = source_of(own, lax.broadcasted_iota(jnp.int32, (rows, rows), 0), rows, count)
    return held == lax.broadcasted_iota(jnp.int32, (rows, rows), 1)


def pick_given(own, rows, count):
    held = source_of(own, lax.broadcasted_iota(jnp.int32, (rows, rows), 1), rows, count)
    return held == lax.broadcasted_iota(jnp.int32, (rows, rows), 0)


def picked(pick, block):
    if block.dtype == jnp.bfloat16:
        return jnp.dot(pick.astype(jnp.bfloat16), block, preferred_element_type=jnp.float32)
    return jnp.dot(pick.astype(jnp.float32), block, precision=lax.Precision.HIGHEST)


def held_mask(pick, tenants_row):
    tenants = jnp.sum(jnp.where(pick, tenants_row, 0).astype(jnp.float32), axis=1, keepdims=True)
    return tenant_mask(tenants.astype(jnp.int32), pick.shape[0])


def low_kernel(count, aligned, down_ref, other_down_ref, tenants_ref, *refs):
    x, (span_out, low_ref) = refs[:-3], refs[-2:]
    own = lax.axis_index("tp")
    width = down_ref.shape[0]
    spans = []
    for n, device in enumerate((own, own ^ 1)):
        if aligned:
            at = pl.ds(pl.multiple_of(device * width, width), width)
            spans.append(jnp.concatenate([ref[:, at] for ref in x], axis=0))
        else:
            spans.append(jnp.concatenate([ref[...] for ref in x[n::2]], axis=0))
    span_out[...] = spans[0]
    rows = spans[0].shape[0]
    wide = jnp.dot(spans[0], down_ref[...], preferred_element_type=jnp.float32)
    wide = wide + jnp.dot(spans[1], other_down_ref[...], preferred_element_type=jnp.float32)
    low = select_block(wide, held_mask(pick_held(own, rows, count), tenants_ref[...]))
    low_ref[...] = picked(pick_given(own, rows, count), low)


def low_part(down, other_down, tenants, x, count, after):
    rows, span = sum(block.shape[0] for block in x), down.shape[0]
    aligned = span % 128 == 0
    if not aligned:
        own = lax.axis_index("tp")
        x = [
            lax.dynamic_slice(
                block, (0, device * span), (block.shape[0], span), allow_negative_indices=False
            )
            for block in x
            for device in (own, own ^ 1)
        ]
    return pl.pallas_call(
        lambda *refs: low_kernel(count, aligned, *refs),
        in_specs=[VMEM] * (3 + len(x)) + [ANY],
        out_shape=[
            jax.ShapeDtypeStruct((rows, span), x[0].dtype),
            jax.ShapeDtypeStruct((rows, ADAPTER_RANK), jnp.float32),
        ],
        compiler_params=pltpu.CompilerParams(vmem_limit_bytes=5 << 20),
        cost_estimate=pl.CostEstimate(
            flops=4 * rows * down.size, bytes_accessed=4 * down.size, transcendentals=0
        ),
        name="low_part",
    )(down, other_down, tenants, *x, after)


def forward_kernel(cuts, slots, blocks, first, slot, *refs):
    x = refs[:blocks]
    gate_out, up_out = refs[-2:]
    gate, up = (0.0, 0.0) if first else (refs[blocks][...], refs[blocks + 1][...])
    for cut in cuts:
        gate_weight, up_weight = slot(slots[cut][0]), slot(slots[cut][1])
        depth = gate_weight.shape[0]
        at = slice(cut * depth, (cut + 1) * depth)
        rows = jnp.concatenate([ref[:, at] for ref in x], axis=0)
        gate = gate + jnp.dot(rows, gate_weight, preferred_element_type=jnp.float32)
        up = up + jnp.dot(rows, up_weight, preferred_element_type=jnp.float32)
    gate_out[...] = gate
    up_out[...] = up


def forward(cuts, slots, x, store, sums, fetches, after):
    rows = sum(block.shape[0] for block in x)
    depth, hidden = store.shape[0] // SLOTS, store.shape[1]
    result = jax.ShapeDtypeStruct((rows, hidden), jnp.float32)
    store, gate, up = store_call(
        lambda *refs: forward_kernel(cuts, slots, len(x), not sums, *refs),
        store,
        fetches,
        [*x, *sums],
        [result, result],
        4 * rows * depth * hidden * len(cuts),
        "forward",
        after=after,
    )
    return store, [gate, up]


def activation_kernel(
    count, maps_slot, slot, gate_ref, up_ref, hidden_ref, low_ref, tenants_ref,
    dgate_ref, dup_ref, part_ref, spread_ref,
):
    rows = gate_ref.shape[0]
    maps = slot(maps_slot)
    own = lax.axis_index("tp")
    pick = pick_held(own, rows, count)
    mask = held_mask(pick, tenants_ref[...])
    spread = spread_rows(picked(pick, low_ref[...]), mask)
    spread_ref[...] = spread
    gate = gate_ref[...] + adapter_scale * jnp.dot(
        spread, maps, preferred_element_type=jnp.float32
    )
    s = jax.nn.sigmoid(gate)
    hidden = picked(pick, hidden_ref[...])
    dgate = (hidden * up_ref[...] * s * (1.0 + gate * (1.0 - s))).astype(jnp.bfloat16)
    dgate_ref[...] = dgate
    dup_ref[...] = (hidden * gate * s).astype(jnp.bfloat16)
    part = select_block(contracted_columns(dgate, maps), mask)
    part_ref[...] = picked(pick_given(own, rows, count), part)


def activation(maps_slot, store, sums, hidden, low, tenants, count, fetches):
    rows, width = sums[0].shape
    value = jax.ShapeDtypeStruct((rows, width), jnp.bfloat16)
    return store_call(
        lambda *refs: activation_kernel(count, maps_slot, *refs),
        store,
        fetches,
        [*sums, hidden, low, tenants],
        [
            value,
            value,
            jax.ShapeDtypeStruct((rows, ADAPTER_RANK), jnp.float32),
            jax.ShapeDtypeStruct((rows, SPREAD), jnp.bfloat16),
        ],
        4 * rows * SPREAD * width,
        "activation",
    )


def adapter_kernel(count, low_ref, tenants_ref, down_ref, earlier, own_out, other_out, spread_ref):
    half = own_out.shape[0]
    before = earlier.shape[1]
    pick = pick_held(lax.axis_index("tp"), 2 * half, count)
    spread = spread_rows(picked(pick, low_ref[...]), held_mask(pick, tenants_ref[...]))
    spread_ref[...] = spread
    part = (adapter_scale * contracted_columns(spread, down_ref[...])).astype(jnp.bfloat16)
    own_out[...] = part[:half]
    other_out[:, :before] = earlier[...]
    other_out[:, before:] = part[half:]


def adapter_part(low, tenants, down, count, earlier):
    rows, span = low.shape[0], down.shape[0]
    return pl.pallas_call(
        lambda *refs: adapter_kernel(count, *refs),
        out_shape=[
            jax.ShapeDtypeStruct((rows // 2, span), jnp.bfloat16),
            jax.ShapeDtypeStruct((rows // 2, earlier.shape[1] + span), jnp.bfloat16),
            jax.ShapeDtypeStruct((rows, SPREAD), jnp.bfloat16),
        ],
        compiler_params=pltpu.CompilerParams(vmem_limit_bytes=4 << 20),
        cost_estimate=pl.CostEstimate(
            flops=2 * rows * down.size, bytes_accessed=2 * down.size, transcendentals=0
        ),
        name="adapter_part",
    )(low, tenants, down, earlier)


def backward_kernel(slots, start, height, slot, dgate_ref, dup_ref, *refs):
    own_out, other_out = refs[-2:]
    half = own_out.shape[0]
    before = other_out.shape[1] - height
    if before:
        other_out[:, :before] = refs[0][...]
    dgate, dup = dgate_ref[...], dup_ref[...]
    for strip in range(0, height, STRIP):
        at = slice(start + strip, start + strip + STRIP)
        part = contracted_columns(dgate, slot(slots[0], at))
        part = part + contracted_columns(dup, slot(slots[1], at))
        own_out[:, strip : strip + STRIP] = part[:half]
        other_out[:, before + strip : before + strip + STRIP] = part[half:].astype(jnp.bfloat16)


def backward(slots, start, height, dgate, dup, store, fetches, after, earlier=()):
    rows, hidden = dgate.shape
    other_width = height + sum(part.shape[1] for part in earlier)
    return store_call(
        lambda *refs: backward_kernel(slots, start, height, *refs),
        store,
        fetches,
        [dgate, dup, *earlier],
        [
            jax.ShapeDtypeStruct((rows // 2, height), jnp.float32),
            jax.ShapeDtypeStruct((rows // 2, other_width), jnp.bfloat16),
        ],
        4 * rows * hidden * height,
        "backward",
        after=after,
    )


def first_halves_kernel(places, span, adapter_own, *refs):
    keep_ref, send_ref, sums = refs[-3:]
    own, came = refs[: len(places)], refs[len(places) : -3]
    half = keep_ref.shape[0]
    device = lax.axis_index("tp")
    for part, (at, group, start) in zip(own, places):
        width = part.shape[1]
        other = came[group][:, start : start + width].astype(jnp.float32)
        sums[:, at : at + width] = part[...] + other
    mine = adapter_own[...].astype(jnp.float32)
    group, start = span
    other = came[group][:, start : start + mine.shape[1]].astype(jnp.float32)
    pair = jnp.where(
        device % 2 == 0,
        jnp.concatenate([mine, other], axis=1),
        jnp.concatenate([other, mine], axis=1),
    )
    width = pair.shape[1]
    sums[:, pl.ds(pl.multiple_of(device // 2 * width, width), width)] += pair
    keep_ref[...] = sums[:half, :]
    send_ref[...] = sums[half:, :].astype(jnp.bfloat16)


def first_halves(own, places, adapter_own, span, came):
    rows = adapter_own.shape[0]
    width = sum(part.shape[1] for part in own)
    return pl.pallas_call(
        lambda *refs: first_halves_kernel(places, span, *refs),
        out_shape=[
            jax.ShapeDtypeStruct((rows // 2, width), jnp.float32),
            jax.ShapeDtypeStruct((rows // 2, width), jnp.bfloat16),
        ],
        scratch_shapes=[pltpu.VMEM((rows, width), jnp.float32)],
        compiler_params=pltpu.CompilerParams(vmem_limit_bytes=40 << 20),
        name="first_halves",
    )(adapter_own, *own, *came)


def halves(keep, came, after):
    rows, width = keep.shape

    def halves_kernel(keep_ref, came_ref, *refs):
        keep_out, send_out = refs[-2:]
        total = keep_ref[...] + came_ref[...].astype(jnp.float32)
        keep_out[...] = total[: rows // 2]
        send_out[...] = total[rows // 2 :].astype(jnp.bfloat16)

    return pl.pallas_call(
        halves_kernel,
        in_specs=[VMEM, VMEM] + [ANY] * len(after),
        out_shape=[
            jax.ShapeDtypeStruct((rows // 2, width), jnp.float32),
            jax.ShapeDtypeStruct((rows // 2, width), jnp.bfloat16),
        ],
        compiler_params=pltpu.CompilerParams(vmem_limit_bytes=40 << 20),
        name="halves",
    )(keep, came, *after)


def quarters(keep, came, after):
    rows, width = keep.shape
    quarter = rows // 4

    def quarters_kernel(keep_ref, came_ref, *refs):
        keep_out, *sends = refs[-4:]
        total = keep_ref[...] + came_ref[...].astype(jnp.float32)
        keep_out[...] = total[:quarter]
        for n, send_out in enumerate(sends, 1):
            send_out[...] = total[n * quarter : (n + 1) * quarter].astype(jnp.bfloat16)

    return pl.pallas_call(
        quarters_kernel,
        in_specs=[VMEM, VMEM] + [ANY] * len(after),
        out_shape=[jax.ShapeDtypeStruct((quarter, width), jnp.float32)]
        + [jax.ShapeDtypeStruct((quarter, width), jnp.bfloat16)] * 3,
        compiler_params=pltpu.CompilerParams(vmem_limit_bytes=40 << 20),
        name="quarters",
    )(keep, came, *after)


def final(keep, came, after):
    def final_kernel(keep_ref, *refs):
        total = keep_ref[...]
        for ref in refs[: len(came)]:
            total = total + ref[...].astype(jnp.float32)
        refs[-1][...] = total.astype(jnp.bfloat16)

    return pl.pallas_call(
        final_kernel,
        in_specs=[VMEM] * (1 + len(came)) + [ANY] * len(after),
        out_shape=jax.ShapeDtypeStruct(keep.shape, jnp.bfloat16),
        compiler_params=pltpu.CompilerParams(vmem_limit_bytes=40 << 20),
        name="final",
    )(keep, *came, *after)


def outer_kernel(left_ref, right_ref, *refs):
    out_ref, token_ref = refs[-2:]
    out_ref[...] = contracted_rows(
        left_ref[...] * jnp.bfloat16(adapter_scale), right_ref[...]
    ).astype(jnp.bfloat16)
    token_ref[...] = jnp.zeros_like(token_ref)


def outer(left, right, name, after, largest):
    rows, height = left.shape
    width = right.shape[1]
    block = block_of(height, largest)
    if block % 128:
        block = height
    return pl.pallas_call(
        outer_kernel,
        grid=(height // block,),
        in_specs=[
            pl.BlockSpec((rows, block), lambda k: (0, k)),
            pl.BlockSpec((rows, width), lambda k: (0, 0)),
            ANY,
        ],
        out_specs=[
            pl.BlockSpec((block, width), lambda k: (k, 0)),
            pl.BlockSpec((8, 128), lambda k: (0, 0)),
        ],
        out_shape=[
            jax.ShapeDtypeStruct((height, width), jnp.bfloat16),
            jax.ShapeDtypeStruct((8, 128), jnp.float32),
        ],
        compiler_params=pltpu.CompilerParams(vmem_limit_bytes=24 << 20),
        cost_estimate=pl.CostEstimate(
            flops=2 * rows * height * width, bytes_accessed=2 * height * width, transcendentals=0
        ),
        name=name,
    )(left, right, after)


def add_kernel(left_ref, right_ref, out_ref):
    out_ref[...] = left_ref[...] + right_ref[...]


def plus(left, right):
    return pl.pallas_call(
        add_kernel,
        out_shape=jax.ShapeDtypeStruct(left.shape, left.dtype),
        compiler_params=pltpu.CompilerParams(vmem_limit_bytes=2 << 20),
        name="plus",
    )(left, right)


def swapped(block, hop):
    return lax.ppermute(block, "tp", [(i, i ^ hop) for i in range(lax.axis_size("tp"))])


def local(
    normed_layer_input,
    hidden_unit_gradient,
    gate_weight,
    up_weight,
    adapter_down_maps,
    adapter_up_maps,
    token_tenant_index,
):
    count = lax.axis_size("tp")
    own_rows, width = normed_layer_input.shape
    rows = own_rows * count
    hops = [1 << bit for bit in range(count.bit_length() - 1)]
    tenants = token_tenant_index.reshape(1, rows)

    def pair(cut, first, second):
        return [(gate_weight, cut, first), (up_weight, cut, second)]

    def mark(slot, token_ref):
        token_ref[...] = jnp.zeros_like(token_ref)

    mark_shape = jax.ShapeDtypeStruct((8, 128), jnp.float32)
    store = jax.ShapeDtypeStruct(
        (SLOTS * width // CUTS, gate_weight.shape[1]), gate_weight.dtype
    )
    far, near = hops[-1], hops[-2]
    came = [swapped(normed_layer_input, hop) for hop in (near, far, near | far)]
    other_down_maps = swapped(adapter_down_maps, 1)
    store, token = store_call(mark, store, pair(0, 0, 1), [], [mark_shape], 0, "fetch")
    block = stacked([normed_layer_input, *came], [token])
    for hop in reversed(hops[2:-2]):
        block = stacked([block, swapped(block, hop)])
    x = [block] + [swapped(block, hop) for hop in (hops[1], 1, hops[1] | 1)]
    store, token = store_call(
        mark, store, pair(1, 2, 3), [], [mark_shape], 0, "fetch", after=[block]
    )

    input_span, low = low_part(adapter_down_maps, other_down_maps, tenants, x, count, token)
    sums = []
    slots = {0: (0, 1), 1: (2, 3), 2: (4, 5), 3: (0, 1)}
    step = 1
    for cuts, fetches in (
        ((0, 1), pair(2, 4, 5)), ((2,), pair(3, 0, 1)), ((3,), [(adapter_up_maps, 0, 2)])
    ):
        after = [low]
        if step < len(hops):
            low = plus(low, swapped(low, hops[step]))
            step += 1
        store, sums = forward(cuts, slots, x, store, sums, fetches, after)
    for hop in hops[step:]:
        low = plus(low, swapped(low, hop))
    store, dgate, dup, low_grad, input_spread = activation(
        2, store, sums, hidden_unit_gradient, low, tenants, count, []
    )

    later_hops = hops[1:] + hops[:1]
    depth = width // CUTS
    part_list = [
        (3, (0, 1), 0, depth, [(gate_weight, 1, 2)], True),
        (2, (4, 5), 0, depth, [(gate_weight, 0, 0)], False),
        (1, (2, 3), 0, depth, [(up_weight, 0, 1)], True),
        (0, (0, 1), depth // 2, depth // 2, [], True),
        (0, (0, 1), 0, depth // 2, [], False),
    ]
    own_parts, places, came, waiting = [], [], [], []
    for n, (piece, slots, first, height, fetches, waits) in enumerate(part_list):
        after = [low_grad]
        if n == len(part_list) - 1:
            span = (len(came), waiting[0].shape[1])
            adapter_own, to_send, grad_spread = adapter_part(
                low_grad, tenants, adapter_down_maps, count, waiting[0]
            )
            came.append(swapped(to_send, 1))
            after, waiting = [to_send], []
        else:
            turns = later_hops[:1] if n < len(part_list) - 2 else later_hops
            later_hops = later_hops[len(turns) :]
            for hop in turns:
                low_grad = plus(low_grad, swapped(low_grad, hop))
        begin = sum(part.shape[1] for part in waiting)
        store, own_part, other_part = backward(
            slots, first, height, dgate, dup, store, fetches, after, waiting
        )
        own_parts.append(own_part)
        places.append((piece * depth + first, len(came), begin))
        waiting = [other_part]
        if not waits:
            came.append(swapped(other_part, 1))
            waiting = []

    keep, send = first_halves(own_parts, places, adapter_own, span, came)
    halvings = [block_owner(0, 1 << bit, count) for bit in reversed(range(2, len(hops) - 1))]
    for n, hop in enumerate(halvings):
        came = swapped(send, hop)
        beside = [send]
        if n == len(halvings) - 1:
            up_map_gradient, token = outer(input_spread, dgate, "up_maps", send, 512)
            keep, *sends = quarters(keep, came, [token])
        else:
            keep, send = halves(keep, came, beside)
    came = [swapped(sends[n - 1], block_owner(0, n, count)) for n in (3, 2, 1)]
    down_map_gradient, token = outer(input_span, grad_spread, "down_maps", sends[0], 256)
    return (final(keep, came, [token]), down_map_gradient, up_map_gradient)


def solution(mesh):
    placed = (
        P(("groups", "tp"), None),
        P("groups", "tp"),
        P(None, "tp"),
        P(None, "tp"),
        P("tp", None),
        P(None, "tp"),
        P("groups"),
    )
    return jax.shard_map(
        local,
        mesh=mesh,
        in_specs=placed,
        out_specs=(P(("groups", "tp"), None), P("tp", "groups"), P("groups", "tp")),
        check_vma=False,
    )
```

```python
import jax
import jax.numpy as jnp
from jax import lax
from jax.experimental import pallas as pl
from jax.experimental.pallas import tpu as pltpu
from jax.sharding import PartitionSpec as P

ADAPTER_RANK = 64
TENANT_COUNT = 32
SPREAD = ADAPTER_RANK * TENANT_COUNT

adapter_scale = 2.0


def block_of(size, largest):
    block = largest
    while size % block:
        block //= 2
    return block


def contracted_rows(left, right):
    return lax.dot_general(
        left, right, (((0,), (0,)), ((), ())), preferred_element_type=jnp.float32
    )


def contracted_columns(left, right):
    return lax.dot_general(
        left, right, (((1,), (1,)), ((), ())), preferred_element_type=jnp.float32
    )


def tenant_mask(tenants, rows):
    columns = lax.broadcasted_iota(jnp.int32, (rows, SPREAD), 1) // ADAPTER_RANK
    return tenants == columns


def select_block(wide_rows, mask):
    kept = jnp.where(mask, wide_rows, 0.0)
    pair = 2 * ADAPTER_RANK
    total = kept[:, :pair]
    for start in range(pair, SPREAD, pair):
        total = total + kept[:, start : start + pair]
    return total[:, :ADAPTER_RANK] + total[:, ADAPTER_RANK:]


def spread_rows(low_rows, mask):
    pair = jnp.concatenate([low_rows, low_rows], axis=1)
    wide = jnp.concatenate([pair] * (TENANT_COUNT // 2), axis=1)
    return jnp.where(mask, wide, 0.0).astype(jnp.bfloat16)


VMEM = pl.BlockSpec(memory_space=pltpu.VMEM)
ANY = pl.BlockSpec(memory_space=pl.ANY)
CUTS = 4
COPIES = 8
STRIP = 256
SLOTS = 6
STORE_GRANT = 10 << 20


def store_call(kernel, store, fetches, operands, out_shapes, flops, name, after=()):
    new = isinstance(store, jax.ShapeDtypeStruct)
    depth = store.shape[0] // SLOTS
    part = depth // COPIES
    sources = []
    for array, *_ in fetches:
        if not any(array is known for known in sources):
            sources.append(array)
    places = [next(i for i, known in enumerate(sources) if known is f[0]) for f in fetches]
    n_in, n_out, n_hbm = len(operands), len(out_shapes), len(sources)

    def body(*refs):
        if not new:
            refs = refs[1:]
        ins, hbm = refs[:n_in], refs[n_in : n_in + n_hbm]
        rest = refs[n_in + n_hbm + len(after) :]
        store_ref, outs, scratch = rest[0], rest[1 : 1 + n_out], rest[1 + n_out :]
        copies = []
        for n, (place, (_, piece, slot, *half)) in enumerate(zip(places, fetches)):
            for k in range(COPIES):
                if half and k // (COPIES // 2) != half[0]:
                    continue
                copies.append(
                    pltpu.make_async_copy(
                        hbm[place].at[pl.ds(piece * depth + k * part, part)],
                        store_ref.at[pl.ds(slot * depth + k * part, part)],
                        scratch[0].at[n * COPIES + k],
                    )
                )
        for copy in copies:
            copy.start()
        def rows_of(slot, at=slice(0, depth)):
            return store_ref[slot * depth + at.start : slot * depth + at.stop, :]

        kernel(rows_of, *ins, *outs)
        for copy in copies:
            copy.wait()

    moved = 2 * depth * store.shape[1] * len(fetches)
    return pl.pallas_call(
        body,
        in_specs=[VMEM] * (n_in + (not new)) + [ANY] * (n_hbm + len(after)),
        out_specs=[VMEM] * (1 + n_out),
        out_shape=[pltpu.VMEM(store.shape, store.dtype), *out_shapes],
        input_output_aliases={} if new else {0: 0},
        scratch_shapes=[pltpu.SemaphoreType.DMA((COPIES * len(fetches),))] if fetches else [],
        compiler_params=pltpu.CompilerParams(vmem_limit_bytes=STORE_GRANT),
        cost_estimate=pl.CostEstimate(flops=flops, bytes_accessed=moved, transcendentals=0),
        name=name,
    )(
        *([] if new else [store]),
        *operands,
        *[pltpu.with_memory_space_constraint(array, pltpu.HBM) for array in sources],
        *after,
    )


def stacked(blocks, after=()):
    rows = sum(block.shape[0] for block in blocks)

    def stack_kernel(*refs):
        refs[-1][...] = jnp.concatenate([ref[...] for ref in refs[: len(blocks)]], axis=0)

    return pl.pallas_call(
        stack_kernel,
        in_specs=[VMEM] * len(blocks) + [ANY] * len(after),
        out_shape=jax.ShapeDtypeStruct((rows, blocks[0].shape[1]), blocks[0].dtype),
        compiler_params=pltpu.CompilerParams(vmem_limit_bytes=4 << 20),
        name="stacked",
    )(*blocks, *after)


def block_owner(own, block, count):
    bits = count.bit_length() - 1
    hops = [1 << (bits - 2), 1 << (bits - 1)] + [1 << bit for bit in reversed(range(bits - 2))]
    for n, hop in enumerate(hops):
        own = own ^ (((block >> n) & 1) * hop)
    return own


def source_of(own, row, rows, count):
    tokens = rows // count
    return block_owner(own, row // tokens, count) * tokens + row % tokens


def pick_held(own, rows, count):
    held = source_of(own, lax.broadcasted_iota(jnp.int32, (rows, rows), 0), rows, count)
    return held == lax.broadcasted_iota(jnp.int32, (rows, rows), 1)


def pick_given(own, rows, count):
    held = source_of(own, lax.broadcasted_iota(jnp.int32, (rows, rows), 1), rows, count)
    return held == lax.broadcasted_iota(jnp.int32, (rows, rows), 0)


def picked(pick, block):
    if block.dtype == jnp.bfloat16:
        return jnp.dot(pick.astype(jnp.bfloat16), block, preferred_element_type=jnp.float32)
    return jnp.dot(pick.astype(jnp.float32), block, precision=lax.Precision.HIGHEST)


def held_mask(pick, tenants_row):
    tenants = jnp.sum(jnp.where(pick, tenants_row, 0).astype(jnp.float32), axis=1, keepdims=True)
    return tenant_mask(tenants.astype(jnp.int32), pick.shape[0])


def low_kernel(count, aligned, down_ref, other_down_ref, tenants_ref, *refs):
    x, (span_out, low_ref) = refs[:-3], refs[-2:]
    own = lax.axis_index("tp")
    width = down_ref.shape[0]
    spans = []
    for n, device in enumerate((own, own ^ 1)):
        if aligned:
            at = pl.ds(pl.multiple_of(device * width, width), width)
            spans.append(jnp.concatenate([ref[:, at] for ref in x], axis=0))
        else:
            spans.append(jnp.concatenate([ref[...] for ref in x[n::2]], axis=0))
    span_out[...] = spans[0]
    rows = spans[0].shape[0]
    wide = jnp.dot(spans[0], down_ref[...], preferred_element_type=jnp.float32)
    wide = wide + jnp.dot(spans[1], other_down_ref[...], preferred_element_type=jnp.float32)
    low = select_block(wide, held_mask(pick_held(own, rows, count), tenants_ref[...]))
    low_ref[...] = picked(pick_given(own, rows, count), low)


def low_part(down, other_down, tenants, x, count, after):
    rows, span = sum(block.shape[0] for block in x), down.shape[0]
    aligned = span % 128 == 0
    if not aligned:
        own = lax.axis_index("tp")
        x = [
            lax.dynamic_slice(
                block, (0, device * span), (block.shape[0], span), allow_negative_indices=False
            )
            for block in x
            for device in (own, own ^ 1)
        ]
    return pl.pallas_call(
        lambda *refs: low_kernel(count, aligned, *refs),
        in_specs=[VMEM] * (3 + len(x)) + [ANY],
        out_shape=[
            jax.ShapeDtypeStruct((rows, span), x[0].dtype),
            jax.ShapeDtypeStruct((rows, ADAPTER_RANK), jnp.float32),
        ],
        compiler_params=pltpu.CompilerParams(vmem_limit_bytes=5 << 20),
        cost_estimate=pl.CostEstimate(
            flops=4 * rows * down.size, bytes_accessed=4 * down.size, transcendentals=0
        ),
        name="low_part",
    )(down, other_down, tenants, *x, after)


def forward_kernel(cuts, slots, blocks, first, slot, *refs):
    x = refs[:blocks]
    gate_out, up_out = refs[-2:]
    gate, up = (0.0, 0.0) if first else (refs[blocks][...], refs[blocks + 1][...])
    for cut in cuts:
        gate_weight, up_weight = slot(slots[cut][0]), slot(slots[cut][1])
        depth = gate_weight.shape[0]
        at = slice(cut * depth, (cut + 1) * depth)
        rows = jnp.concatenate([ref[:, at] for ref in x], axis=0)
        gate = gate + jnp.dot(rows, gate_weight, preferred_element_type=jnp.float32)
        up = up + jnp.dot(rows, up_weight, preferred_element_type=jnp.float32)
    gate_out[...] = gate
    up_out[...] = up


def forward(cuts, slots, x, store, sums, fetches, after):
    rows = sum(block.shape[0] for block in x)
    depth, hidden = store.shape[0] // SLOTS, store.shape[1]
    result = jax.ShapeDtypeStruct((rows, hidden), jnp.float32)
    store, gate, up = store_call(
        lambda *refs: forward_kernel(cuts, slots, len(x), not sums, *refs),
        store,
        fetches,
        [*x, *sums],
        [result, result],
        4 * rows * depth * hidden * len(cuts),
        "forward",
        after=after,
    )
    return store, [gate, up]


def activation_kernel(
    count, maps_slot, slot, gate_ref, up_ref, hidden_ref, low_ref, came_ref, tenants_ref,
    dgate_ref, dup_ref, part_ref, spread_ref,
):
    rows = gate_ref.shape[0]
    maps = slot(maps_slot)
    own = lax.axis_index("tp")
    pick = pick_held(own, rows, count)
    mask = held_mask(pick, tenants_ref[...])
    spread = spread_rows(picked(pick, low_ref[...] + came_ref[...]), mask)
    spread_ref[...] = spread
    gate = gate_ref[...] + adapter_scale * jnp.dot(
        spread, maps, preferred_element_type=jnp.float32
    )
    s = jax.nn.sigmoid(gate)
    hidden = picked(pick, hidden_ref[...])
    dgate = (hidden * up_ref[...] * s * (1.0 + gate * (1.0 - s))).astype(jnp.bfloat16)
    dgate_ref[...] = dgate
    dup_ref[...] = (hidden * gate * s).astype(jnp.bfloat16)
    part = select_block(contracted_columns(dgate, maps), mask)
    part_ref[...] = picked(pick_given(own, rows, count), part)


def activation(maps_slot, store, sums, hidden, low, came, tenants, count, fetches):
    rows, width = sums[0].shape
    value = jax.ShapeDtypeStruct((rows, width), jnp.bfloat16)
    return store_call(
        lambda *refs: activation_kernel(count, maps_slot, *refs),
        store,
        fetches,
        [*sums, hidden, low, came, tenants],
        [
            value,
            value,
            jax.ShapeDtypeStruct((rows, ADAPTER_RANK), jnp.float32),
            jax.ShapeDtypeStruct((rows, SPREAD), jnp.bfloat16),
        ],
        4 * rows * SPREAD * width,
        "activation",
    )


def adapter_kernel(
    count, low_ref, came_ref, tenants_ref, down_ref, earlier, own_out, other_out, spread_ref
):
    half = own_out.shape[0]
    before = earlier.shape[1]
    pick = pick_held(lax.axis_index("tp"), 2 * half, count)
    low = low_ref[...] + came_ref[...]
    spread = spread_rows(picked(pick, low), held_mask(pick, tenants_ref[...]))
    spread_ref[...] = spread
    part = (adapter_scale * contracted_columns(spread, down_ref[...])).astype(jnp.bfloat16)
    own_out[...] = part[:half]
    other_out[:, :before] = earlier[...]
    other_out[:, before:] = part[half:]


def adapter_part(low, came, tenants, down, count, earlier):
    rows, span = low.shape[0], down.shape[0]
    return pl.pallas_call(
        lambda *refs: adapter_kernel(count, *refs),
        out_shape=[
            jax.ShapeDtypeStruct((rows // 2, span), jnp.bfloat16),
            jax.ShapeDtypeStruct((rows // 2, earlier.shape[1] + span), jnp.bfloat16),
            jax.ShapeDtypeStruct((rows, SPREAD), jnp.bfloat16),
        ],
        compiler_params=pltpu.CompilerParams(vmem_limit_bytes=4 << 20),
        cost_estimate=pl.CostEstimate(
            flops=2 * rows * down.size, bytes_accessed=2 * down.size, transcendentals=0
        ),
        name="adapter_part",
    )(low, came, tenants, down, earlier)


def backward_kernel(slots, start, height, slot, dgate_ref, dup_ref, *refs):
    own_out, other_out = refs[-2:]
    half = own_out.shape[0]
    before = other_out.shape[1] - height
    if before:
        other_out[:, :before] = refs[0][...]
    dgate, dup = dgate_ref[...], dup_ref[...]
    for strip in range(0, height, STRIP):
        at = slice(start + strip, start + strip + STRIP)
        part = contracted_columns(dgate, slot(slots[0], at))
        part = part + contracted_columns(dup, slot(slots[1], at))
        own_out[:, strip : strip + STRIP] = part[:half]
        other_out[:, before + strip : before + strip + STRIP] = part[half:].astype(jnp.bfloat16)


def backward(slots, start, height, dgate, dup, store, fetches, after, earlier=()):
    rows, hidden = dgate.shape
    other_width = height + sum(part.shape[1] for part in earlier)
    return store_call(
        lambda *refs: backward_kernel(slots, start, height, *refs),
        store,
        fetches,
        [dgate, dup, *earlier],
        [
            jax.ShapeDtypeStruct((rows // 2, height), jnp.float32),
            jax.ShapeDtypeStruct((rows // 2, other_width), jnp.bfloat16),
        ],
        4 * rows * hidden * height,
        "backward",
        after=after,
    )


def first_halves_kernel(places, span, adapter_own, *refs):
    keep_ref, send_ref, sums = refs[-3:]
    own, came = refs[: len(places)], refs[len(places) : -3]
    half = keep_ref.shape[0]
    device = lax.axis_index("tp")
    for part, (at, group, start) in zip(own, places):
        width = part.shape[1]
        other = came[group][:, start : start + width].astype(jnp.float32)
        sums[:, at : at + width] = part[...] + other
    mine = adapter_own[...].astype(jnp.float32)
    group, start = span
    other = came[group][:, start : start + mine.shape[1]].astype(jnp.float32)
    pair = jnp.where(
        device % 2 == 0,
        jnp.concatenate([mine, other], axis=1),
        jnp.concatenate([other, mine], axis=1),
    )
    width = pair.shape[1]
    sums[:, pl.ds(pl.multiple_of(device // 2 * width, width), width)] += pair
    keep_ref[...] = sums[:half, :]
    send_ref[...] = sums[half:, :].astype(jnp.bfloat16)


def first_halves(own, places, adapter_own, span, came):
    rows = adapter_own.shape[0]
    width = sum(part.shape[1] for part in own)
    return pl.pallas_call(
        lambda *refs: first_halves_kernel(places, span, *refs),
        out_shape=[
            jax.ShapeDtypeStruct((rows // 2, width), jnp.float32),
            jax.ShapeDtypeStruct((rows // 2, width), jnp.bfloat16),
        ],
        scratch_shapes=[pltpu.VMEM((rows, width), jnp.float32)],
        compiler_params=pltpu.CompilerParams(vmem_limit_bytes=40 << 20),
        name="first_halves",
    )(adapter_own, *own, *came)


def halves(keep, came, after):
    rows, width = keep.shape

    def halves_kernel(keep_ref, came_ref, *refs):
        keep_out, send_out = refs[-2:]
        total = keep_ref[...] + came_ref[...].astype(jnp.float32)
        keep_out[...] = total[: rows // 2]
        send_out[...] = total[rows // 2 :].astype(jnp.bfloat16)

    return pl.pallas_call(
        halves_kernel,
        in_specs=[VMEM, VMEM] + [ANY] * len(after),
        out_shape=[
            jax.ShapeDtypeStruct((rows // 2, width), jnp.float32),
            jax.ShapeDtypeStruct((rows // 2, width), jnp.bfloat16),
        ],
        compiler_params=pltpu.CompilerParams(vmem_limit_bytes=40 << 20),
        name="halves",
    )(keep, came, *after)


def quarters(keep, came, after):
    rows, width = keep.shape
    quarter = rows // 4

    def quarters_kernel(keep_ref, came_ref, *refs):
        keep_out, *sends = refs[-4:]
        total = keep_ref[...] + came_ref[...].astype(jnp.float32)
        keep_out[...] = total[:quarter]
        for n, send_out in enumerate(sends, 1):
            send_out[...] = total[n * quarter : (n + 1) * quarter].astype(jnp.bfloat16)

    return pl.pallas_call(
        quarters_kernel,
        in_specs=[VMEM, VMEM] + [ANY] * len(after),
        out_shape=[jax.ShapeDtypeStruct((quarter, width), jnp.float32)]
        + [jax.ShapeDtypeStruct((quarter, width), jnp.bfloat16)] * 3,
        compiler_params=pltpu.CompilerParams(vmem_limit_bytes=40 << 20),
        name="quarters",
    )(keep, came, *after)


def final(keep, came, after):
    def final_kernel(keep_ref, *refs):
        total = keep_ref[...]
        for ref in refs[: len(came)]:
            total = total + ref[...].astype(jnp.float32)
        refs[-1][...] = total.astype(jnp.bfloat16)

    return pl.pallas_call(
        final_kernel,
        in_specs=[VMEM] * (1 + len(came)) + [ANY] * len(after),
        out_shape=jax.ShapeDtypeStruct(keep.shape, jnp.bfloat16),
        compiler_params=pltpu.CompilerParams(vmem_limit_bytes=40 << 20),
        name="final",
    )(keep, *came, *after)


def outer_kernel(left_ref, right_ref, *refs):
    out_ref, token_ref = refs[-2:]
    out_ref[...] = contracted_rows(
        left_ref[...] * jnp.bfloat16(adapter_scale), right_ref[...]
    ).astype(jnp.bfloat16)
    token_ref[...] = jnp.zeros_like(token_ref)


def outer(left, right, name, after, largest):
    rows, height = left.shape
    width = right.shape[1]
    block = block_of(height, largest)
    if block % 128:
        block = height
    return pl.pallas_call(
        outer_kernel,
        grid=(height // block,),
        in_specs=[
            pl.BlockSpec((rows, block), lambda k: (0, k)),
            pl.BlockSpec((rows, width), lambda k: (0, 0)),
            ANY,
        ],
        out_specs=[
            pl.BlockSpec((block, width), lambda k: (k, 0)),
            pl.BlockSpec((8, 128), lambda k: (0, 0)),
        ],
        out_shape=[
            jax.ShapeDtypeStruct((height, width), jnp.bfloat16),
            jax.ShapeDtypeStruct((8, 128), jnp.float32),
        ],
        compiler_params=pltpu.CompilerParams(vmem_limit_bytes=24 << 20),
        cost_estimate=pl.CostEstimate(
            flops=2 * rows * height * width, bytes_accessed=2 * height * width, transcendentals=0
        ),
        name=name,
    )(left, right, after)


def add_kernel(left_ref, right_ref, out_ref):
    out_ref[...] = left_ref[...] + right_ref[...]


def plus(left, right):
    return pl.pallas_call(
        add_kernel,
        out_shape=jax.ShapeDtypeStruct(left.shape, left.dtype),
        compiler_params=pltpu.CompilerParams(vmem_limit_bytes=2 << 20),
        name="plus",
    )(left, right)


def swapped(block, hop):
    return lax.ppermute(block, "tp", [(i, i ^ hop) for i in range(lax.axis_size("tp"))])


def local(
    normed_layer_input,
    hidden_unit_gradient,
    gate_weight,
    up_weight,
    adapter_down_maps,
    adapter_up_maps,
    token_tenant_index,
):
    count = lax.axis_size("tp")
    own_rows, width = normed_layer_input.shape
    rows = own_rows * count
    hops = [1 << bit for bit in range(count.bit_length() - 1)]
    tenants = token_tenant_index.reshape(1, rows)

    def pair(cut, first, second):
        return [(gate_weight, cut, first), (up_weight, cut, second)]

    def mark(slot, token_ref):
        token_ref[...] = jnp.zeros_like(token_ref)

    mark_shape = jax.ShapeDtypeStruct((8, 128), jnp.float32)
    store = jax.ShapeDtypeStruct(
        (SLOTS * width // CUTS, gate_weight.shape[1]), gate_weight.dtype
    )
    far, near = hops[-1], hops[-2]
    came = [swapped(normed_layer_input, hop) for hop in (near, far, near | far)]
    other_down_maps = swapped(adapter_down_maps, 1)
    store, token = store_call(mark, store, pair(0, 0, 1), [], [mark_shape], 0, "fetch")
    block = stacked([normed_layer_input, *came], [token])
    for hop in reversed(hops[2:-2]):
        block = stacked([block, swapped(block, hop)])
    x = [block] + [swapped(block, hop) for hop in (hops[1], 1, hops[1] | 1)]
    store, token = store_call(
        mark, store, pair(1, 2, 3), [], [mark_shape], 0, "fetch", after=[block]
    )

    input_span, low = low_part(adapter_down_maps, other_down_maps, tenants, x, count, token)
    sums = []
    slots = {0: (0, 1), 1: (2, 3), 2: (4, 5), 3: (0, 1)}
    step = 1
    for cuts, fetches in (
        ((0, 1), pair(2, 4, 5)), ((2,), pair(3, 0, 1)), ((3,), [(adapter_up_maps, 0, 2)])
    ):
        after = [low]
        if step < len(hops):
            came_low = swapped(low, hops[step])
            if step < len(hops) - 1:
                low = plus(low, came_low)
            step += 1
        store, sums = forward(cuts, slots, x, store, sums, fetches, after)
    for hop in hops[step:]:
        came_low = swapped(low, hop)
        if hop != hops[-1]:
            low = plus(low, came_low)
    store, dgate, dup, low_grad, input_spread = activation(
        2, store, sums, hidden_unit_gradient, low, came_low, tenants, count, []
    )

    later_hops = hops[1:] + hops[:1]
    depth = width // CUTS
    part_list = [
        (3, (0, 1), 0, depth, [(gate_weight, 1, 2)], True),
        (2, (4, 5), 0, depth, [(gate_weight, 0, 0)], False),
        (1, (2, 3), 0, depth, [(up_weight, 0, 1)], True),
        (0, (0, 1), depth // 2, depth // 2, [], True),
        (0, (0, 1), 0, depth // 2, [], False),
    ]
    own_parts, places, came, waiting = [], [], [], []
    for n, (piece, slots, first, height, fetches, waits) in enumerate(part_list):
        after = [low_grad]
        if n == len(part_list) - 1:
            span = (len(came), waiting[0].shape[1])
            adapter_own, to_send, grad_spread = adapter_part(
                low_grad, came_grad, tenants, adapter_down_maps, count, waiting[0]
            )
            came.append(swapped(to_send, 1))
            after, waiting = [to_send], []
        else:
            turns = later_hops[:1] if n < len(part_list) - 2 else later_hops
            later_hops = later_hops[len(turns) :]
            for hop in turns:
                came_grad = swapped(low_grad, hop)
                if hop != hops[0]:
                    low_grad = plus(low_grad, came_grad)
        begin = sum(part.shape[1] for part in waiting)
        store, own_part, other_part = backward(
            slots, first, height, dgate, dup, store, fetches, after, waiting
        )
        own_parts.append(own_part)
        places.append((piece * depth + first, len(came), begin))
        waiting = [other_part]
        if not waits:
            came.append(swapped(other_part, 1))
            waiting = []

    keep, send = first_halves(own_parts, places, adapter_own, span, came)
    halvings = [block_owner(0, 1 << bit, count) for bit in reversed(range(2, len(hops) - 1))]
    for n, hop in enumerate(halvings):
        came = swapped(send, hop)
        beside = [send]
        if n == len(halvings) - 1:
            up_map_gradient, token = outer(input_spread, dgate, "up_maps", send, 512)
            keep, *sends = quarters(keep, came, [token])
        else:
            keep, send = halves(keep, came, beside)
    came = [swapped(sends[n - 1], block_owner(0, n, count)) for n in (3, 2, 1)]
    down_map_gradient, token = outer(input_span, grad_spread, "down_maps", sends[0], 128)
    return (final(keep, came, [token]), down_map_gradient, up_map_gradient)


def solution(mesh):
    placed = (
        P(("groups", "tp"), None),
        P("groups", "tp"),
        P(None, "tp"),
        P(None, "tp"),
        P("tp", None),
        P(None, "tp"),
        P("groups"),
    )
    return jax.shard_map(
        local,
        mesh=mesh,
        in_specs=placed,
        out_specs=(P(("groups", "tp"), None), P("tp", "groups"), P("groups", "tp")),
        check_vma=False,
    )
```
